32 devices in a mesh: seq: 8 (over y, x, core), head: 4 (over z).
Axes of the slice: x: 2, y: 2, z: 4, core: 2. Of those that a mesh axis runs over, the one named last changes fastest.
Arguments:
- normed_input: bfloat16 [1024, 2304], P('seq'), may hold values from -6 to 6
- stored_queries: bfloat16 [1024, 2048], P('seq', 'head'), may hold values from -50 to 50
- stored_keys: bfloat16 [1024, 1024], P('seq', 'head'), may hold values from -4 to 4
- stored_values: bfloat16 [1024, 1024], P('seq', 'head'), may hold values from -6 to 6
- query_weight: bfloat16 [2304, 2048], P(None, 'head'), may hold values from -0.125 to 0.125
- key_matrix: bfloat16 [2304, 1024], P(None, 'head'), may hold values from -0.125 to 0.125
- value_matrix: bfloat16 [2304, 1024], P(None, 'head'), may hold values from -0.125 to 0.125
- output_weight: bfloat16 [2048, 2304], P('head'), may hold values from -0.125 to 0.125
- out_cotangent: bfloat16 [1024, 2304], P('seq'), may hold values from -48 to 48
Outputs:
- grad_input: bfloat16 [1024, 2304], P('seq', 'head')
- grad_wvalue: float32 [2304, 1024], P('seq', 'head')
- grad_woutput: float32 [2048, 2304], P('head', 'seq')
The draws below stay inside these ranges and needn't reach their ends.
All inputs are finite; a program needn't handle non-finite values.
Results may differ from the reference program's by a relative error of at most 0.033.
Values may be sent and summed in bfloat16 or wider, within the bound.
No kernel may reach another device: no remote copies, remote signals or barrier semaphores. Data moves between devices by JAX's collectives and lax.ppermute only.
A program may use at most 128 MiB of HBM per device.

```python
import jax
import jax.numpy as jnp
from jax import lax

MODEL_DIMENSION = 2304
QUERY_HEADS = 16
KEY_VALUE_HEADS = 8
HEAD_SIZE = 128
WINDOW_LENGTH = 4096
BLOCK_TOKENS = 128
QUERIES_PER_KEY = 2
SEQUENCE_TOKENS = 1024


def paired_fields(key):
    query_key, key_random_seed = jax.random.split(jax.random.fold_in(key, 11))
    key_base_offset = jnp.clip(jax.random.normal(key_random_seed, (SEQUENCE_TOKENS, KEY_VALUE_HEADS * HEAD_SIZE), jnp.float32), -4.0, 4.0)
    query_base = jnp.clip(jax.random.normal(query_key, (SEQUENCE_TOKENS, QUERY_HEADS * HEAD_SIZE), jnp.float32), -4.0, 4.0)
    return (query_base, key_base_offset)


def draw_stored_queries(key, part):
    return paired_fields(key)[0].astype(jnp.bfloat16)


def draw_stored_keys(key, part):
    return paired_fields(key)[1].astype(jnp.bfloat16)


def with_spikes(result, own_key, source, target, shards_of, factor):
    def block_of(dim):
        return (jnp.arange(result.shape[dim]) // (result.shape[dim] // shards_of)).reshape((-1,) + (1,) * (result.ndim - 1 - dim))

    one_side = jax.random.permutation(own_key, shards_of)[block_of(target)]
    far = (block_of(target) + shards_of // 2) % shards_of
    return jnp.where((block_of(source) == one_side) | (block_of(source) == far), factor * result, result)


def shard_levels(own_key, extent, cuts, least, top_value):
    def one(dim, shards_of):
        steps = jax.random.uniform(jax.random.fold_in(jax.random.fold_in(own_key, 6), dim), (shards_of,), jnp.float32, least / len(cuts), top_value / len(cuts))
        return jnp.repeat(jnp.exp(steps), extent[dim] // shards_of).reshape((-1,) + (1,) * (len(extent) - dim - 1))

    level = one(*cuts[0])
    for cut in cuts[1:]:
        level = level * one(*cut)
    return level


def gaussian(rng, extent, scale, most, cuts=(), held_as=jnp.bfloat16):
    array = scale * jax.random.normal(rng, extent, jnp.float32)
    if cuts:
        array = array * shard_levels(rng, extent, cuts, -0.22, 0.18)
    return jnp.clip(array, -most, most).astype(held_as)


def noise_with(key, dims, deviation, reach, shards, heavy, kind=jnp.bfloat16):
    result = deviation * jax.random.normal(key, dims, jnp.float32)
    if shards:
        result = result * shard_levels(key, dims, shards, -0.22, 0.18)
    return jnp.clip(with_spikes(result, jax.random.fold_in(key, 3), *heavy), -reach, reach).astype(kind)


def setup_inputs(seed: int = 0) -> dict:
    keys = jax.random.split(jax.random.key(seed), 10)
    normed_input = noise_with(keys[0], (SEQUENCE_TOKENS, MODEL_DIMENSION), 1.0, 6.0, ((0, 8),), (0, 1, 8, 2.0))
    stored_queries = draw_stored_queries(jax.random.fold_in(keys[9], 71), 0)
    stored_keys = draw_stored_keys(jax.random.fold_in(keys[9], 71), 0)
    stored_values = gaussian(keys[3], (SEQUENCE_TOKENS, KEY_VALUE_HEADS * HEAD_SIZE), 1.0, 6.0, ((0, 8), (1, 4)))
    query_weight = gaussian(keys[4], (MODEL_DIMENSION, QUERY_HEADS * HEAD_SIZE), MODEL_DIMENSION ** -0.5, 0.125, ((1, 4),))
    key_matrix = gaussian(keys[5], (MODEL_DIMENSION, KEY_VALUE_HEADS * HEAD_SIZE), MODEL_DIMENSION ** -0.5, 0.125, ((1, 4),))
    value_matrix = gaussian(keys[6], (MODEL_DIMENSION, KEY_VALUE_HEADS * HEAD_SIZE), MODEL_DIMENSION ** -0.5, 0.125, ((1, 4),))
    output_weight = gaussian(keys[7], (QUERY_HEADS * HEAD_SIZE, MODEL_DIMENSION), MODEL_DIMENSION ** -0.5, 0.125, ((0, 4),))
    out_cotangent = noise_with(keys[8], (SEQUENCE_TOKENS, MODEL_DIMENSION), 8.0, 48.0, ((0, 8),), (0, 1, 8, 2.0))
    return dict(normed_input=normed_input, stored_queries=stored_queries, stored_keys=stored_keys, stored_values=stored_values, query_weight=query_weight, key_matrix=key_matrix, value_matrix=value_matrix, output_weight=output_weight, out_cotangent=out_cotangent)


logit_scale = 1.0 / 12.0


def reference(normed_input, stored_queries, stored_keys, stored_values, query_weight, key_matrix, value_matrix, output_weight, out_cotangent):
    token_positions = normed_input.shape[0]
    blocks = token_positions // BLOCK_TOKENS
    window_extent = WINDOW_LENGTH + BLOCK_TOKENS
    output_gradient = jnp.dot(out_cotangent, output_weight.T, preferred_element_type=jnp.float32).astype(jnp.bfloat16)
    empty_rows = jnp.zeros((WINDOW_LENGTH, KEY_VALUE_HEADS * HEAD_SIZE), stored_keys.dtype)
    padded_keys = jnp.concatenate([empty_rows, stored_keys], axis=0)
    padded_values = jnp.concatenate([empty_rows, stored_values], axis=0)

    def one_block(carry_pair, block_index):
        first_row_offset = (block_index * BLOCK_TOKENS).astype(jnp.int32)
        key_running_total, value_running_total = carry_pair
        block_of_queries = lax.dynamic_slice_in_dim(stored_queries, first_row_offset, BLOCK_TOKENS, 0).reshape(BLOCK_TOKENS, KEY_VALUE_HEADS, QUERIES_PER_KEY, HEAD_SIZE).astype(jnp.float32)
        block_gradient = lax.dynamic_slice_in_dim(output_gradient, first_row_offset, BLOCK_TOKENS, 0).reshape(BLOCK_TOKENS, KEY_VALUE_HEADS, QUERIES_PER_KEY, HEAD_SIZE).astype(jnp.float32)
        block_of_keys = lax.dynamic_slice_in_dim(padded_keys, first_row_offset, window_extent, 0).reshape(window_extent, KEY_VALUE_HEADS, HEAD_SIZE).astype(jnp.float32)
        block_of_values = lax.dynamic_slice_in_dim(padded_values, first_row_offset, window_extent, 0).reshape(window_extent, KEY_VALUE_HEADS, HEAD_SIZE).astype(jnp.float32)
        query_pos = first_row_offset + jnp.arange(BLOCK_TOKENS, dtype=jnp.int32)
        key_pos = first_row_offset - WINDOW_LENGTH + jnp.arange(window_extent, dtype=jnp.int32)
        pos_gap = query_pos[:, None] - key_pos[None, :]
        allowed = (pos_gap >= 0) & (pos_gap < WINDOW_LENGTH) & (key_pos >= 0)[None, :]
        attention_logits = logit_scale * jnp.einsum("eial,cil->iaec", block_of_queries, block_of_keys)
        masked = jnp.where(allowed[None, None], attention_logits, -jnp.inf)
        row_top = jnp.max(masked, axis=-1, keepdims=True)
        exp_scores = jnp.exp(masked - row_top)
        attn_prob = exp_scores / jnp.sum(exp_scores, axis=-1, keepdims=True)
        probability_halfwidth = attn_prob.astype(jnp.bfloat16)
        attention_output = jnp.einsum("kbxh,hkj->xkbj", probability_halfwidth.astype(jnp.float32), block_of_values).astype(jnp.bfloat16)
        row_delta = jnp.sum(block_gradient * attention_output.astype(jnp.float32), axis=-1)
        row_delta = jnp.transpose(row_delta, (1, 2, 0))
        probability_gradient = jnp.einsum("eial,cil->iaec", block_gradient, block_of_values)
        score_gradient = (attn_prob * (probability_gradient - row_delta[..., None])).astype(jnp.bfloat16).astype(jnp.float32)
        query_gradient = (logit_scale * jnp.einsum("kbxh,hkj->xkbj", score_gradient, block_of_keys)).astype(jnp.bfloat16)
        key_partial = logit_scale * jnp.einsum("ozpn,pozw->now", score_gradient, block_of_queries)
        value_partial = jnp.einsum("ozpn,pozw->now", probability_halfwidth.astype(jnp.float32), block_gradient)
        previous_key = lax.dynamic_slice_in_dim(key_running_total, first_row_offset, window_extent, 0)
        previous_value = lax.dynamic_slice_in_dim(value_running_total, first_row_offset, window_extent, 0)
        key_running_total = lax.dynamic_update_slice_in_dim(key_running_total, previous_key + key_partial.reshape(window_extent, KEY_VALUE_HEADS * HEAD_SIZE), first_row_offset, 0)
        value_running_total = lax.dynamic_update_slice_in_dim(value_running_total, previous_value + value_partial.reshape(window_extent, KEY_VALUE_HEADS * HEAD_SIZE), first_row_offset, 0)
        return (key_running_total, value_running_total), (attention_output.reshape(BLOCK_TOKENS, QUERY_HEADS * HEAD_SIZE), query_gradient.reshape(BLOCK_TOKENS, QUERY_HEADS * HEAD_SIZE))

    initial_carry_pair = (jnp.zeros((WINDOW_LENGTH + token_positions, KEY_VALUE_HEADS * HEAD_SIZE), jnp.float32), jnp.zeros((WINDOW_LENGTH + token_positions, KEY_VALUE_HEADS * HEAD_SIZE), jnp.float32))
    (key_running_total, value_running_total), (attention_output, query_gradient) = lax.scan(one_block, initial_carry_pair, jnp.arange(blocks, dtype=jnp.int32))
    attention_output = attention_output.reshape(token_positions, QUERY_HEADS * HEAD_SIZE)
    query_gradient = query_gradient.reshape(token_positions, QUERY_HEADS * HEAD_SIZE)
    grad_key = key_running_total[WINDOW_LENGTH:].astype(jnp.bfloat16)
    grad_value = value_running_total[WINDOW_LENGTH:].astype(jnp.bfloat16)
    grad_input = jnp.dot(query_gradient, query_weight.T, preferred_element_type=jnp.float32)
    grad_input = grad_input + jnp.dot(grad_key, key_matrix.T, preferred_element_type=jnp.float32)
    grad_input = (grad_input + jnp.dot(grad_value, value_matrix.T, preferred_element_type=jnp.float32)).astype(jnp.bfloat16)
    grad_wvalue = jnp.dot(normed_input.T, grad_value, preferred_element_type=jnp.float32)
    grad_woutput = jnp.dot(attention_output.T, out_cotangent, preferred_element_type=jnp.float32)
    return grad_input, grad_wvalue, grad_woutput
```

```python
import functools

import jax
import jax.numpy as jnp
from jax import lax
from jax.experimental import pallas as pl
from jax.experimental.pallas import tpu as pltpu
from jax.sharding import PartitionSpec as P

HEAD_SIZE = 128
WINDOW_LENGTH = 4096
QUERIES_PER_KEY = 2


logit_scale = 1.0 / 12.0
log2_scale = 1.4426950408889634 / 12.0
excluded = -1e30


def passed_along(value, axis, steps):
    count = lax.axis_size(axis)
    leading, last = (max(0, -steps), min(count, count - steps))
    return lax.ppermute(value, axis, [(source, source + steps) for source in range(leading, last)])


NT = (((1,), (1,)), ((), ()))


def dot_nt(left, right):
    return lax.dot_general(left, right, NT, preferred_element_type=jnp.float32)


def dot_nn(left, right):
    return jnp.dot(left, right, preferred_element_type=jnp.float32)


def out_grad_kernel(cot_ref, weight_ref, q_ref, k_ref, v_ref, packed_ref):
    q_cols = q_ref.shape[1]
    kv_cols = k_ref.shape[1]
    packed_ref[:, :q_cols] = q_ref[...]
    packed_ref[:, q_cols : q_cols + kv_cols] = k_ref[...]
    packed_ref[:, q_cols + kv_cols : q_cols + 2 * kv_cols] = v_ref[...]
    packed_ref[:, q_cols + 2 * kv_cols :] = dot_nt(cot_ref[...], weight_ref[...]).astype(
        jnp.bfloat16
    )


def turn_kernel(parts, normed_ref, cot_ref, turned_ref):
    cut = normed_ref.shape[1] // parts
    for which, ref in enumerate((normed_ref, cot_ref)):
        turned = ref[...].astype(jnp.float32).T.astype(jnp.bfloat16)
        for part in range(parts):
            turned_ref[part, which] = turned[part * cut : (part + 1) * cut]


def attention_kernel(
    gathered_ref,
    wq_hbm,
    wk_hbm,
    wv_hbm,
    terms_ref,
    attn_ref,
    dv_ref,
    wq_ref,
    wk_ref,
    wv_ref,
    score_ref,
    prob_ref,
    grad_ref,
    value_t_ref,
    key_t_ref,
    dk_ref,
    dx_ref,
    weight_sem,
):
    me = lax.axis_index("seq")
    copies = [
        pltpu.make_async_copy(source, target, weight_sem.at[place])
        for place, (source, target) in enumerate(
            ((wq_hbm, wq_ref), (wk_hbm, wk_ref), (wv_hbm, wv_ref))
        )
    ]
    for copy in copies:
        copy.start()
    tokens = gathered_ref.shape[0]
    rows = dx_ref.shape[0]
    blocks = tokens // rows
    kv_cols = dv_ref.shape[1]
    kv_heads = kv_cols // HEAD_SIZE
    q_cols = attn_ref.shape[0]
    key_base = q_cols
    value_base = q_cols + kv_cols
    grad_base = q_cols + 2 * kv_cols
    wide = QUERIES_PER_KEY * rows

    def stacked(block, base, kv_head):
        return jnp.concatenate(
            [
                gathered_ref[
                    block * rows : (block + 1) * rows,
                    base + h * HEAD_SIZE : base + (h + 1) * HEAD_SIZE,
                ]
                for h in range(kv_head * QUERIES_PER_KEY, (kv_head + 1) * QUERIES_PER_KEY)
            ],
            axis=0,
        )

    def columns(base, kv_head):
        return slice(base + kv_head * HEAD_SIZE, base + (kv_head + 1) * HEAD_SIZE)

    dk_ref[...] = jnp.zeros_like(dk_ref)
    for kv_head in range(kv_heads):
        value_t_ref[kv_head] = gathered_ref[:, columns(value_base, kv_head)].T
        key_t_ref[kv_head] = gathered_ref[:, columns(key_base, kv_head)].T
    key_place = lax.broadcasted_iota(jnp.int32, (rows, wide), 0)
    query_place = lax.broadcasted_iota(jnp.int32, (rows, wide), 1) % rows
    allowed = key_place <= query_place

    for block in range(blocks):
        span = (block + 1) * rows
        kept = []
        for kv_head in range(kv_heads):
            queries = stacked(block, 0, kv_head)
            grads = stacked(block, grad_base, kv_head)
            grad_ref[kv_head, block * wide : (block + 1) * wide] = grads
            scores = dot_nt(gathered_ref[:span, columns(key_base, kv_head)], queries)
            diagonal = jnp.where(allowed, scores[block * rows :], excluded)
            if block:
                scores = jnp.concatenate([scores[: block * rows], diagonal], axis=0)
            else:
                scores = diagonal
            score_ref[kv_head, :span] = scores
            top = jnp.max(scores, axis=0, keepdims=True)
            weights = jnp.exp2((score_ref[kv_head, :span] - top) * log2_scale)
            score_ref[kv_head, :span] = weights
            inverse = 1.0 / jnp.sum(weights, axis=0, keepdims=True)
            prob_b = (score_ref[kv_head, :span] * inverse).astype(jnp.bfloat16)
            prob_ref[kv_head, :span, block * wide : (block + 1) * wide] = prob_b
            attn = dot_nn(value_t_ref[kv_head, :, :span], prob_b).astype(jnp.bfloat16)
            for h in range(QUERIES_PER_KEY):
                first = (kv_head * QUERIES_PER_KEY + h) * HEAD_SIZE
                attn_ref[first : first + HEAD_SIZE, block * rows : (block + 1) * rows] = attn[
                    :, h * rows : (h + 1) * rows
                ]
            delta = jnp.sum(
                grads.T.astype(jnp.float32) * attn.astype(jnp.float32), axis=0, keepdims=True
            )
            kept.append((queries, grads, inverse, delta))

        @pl.when(me <= block)
        def _():
            own = pl.ds(pl.multiple_of(me * rows, rows), rows)
            for kv_head, (queries, grads, inverse, delta) in enumerate(kept):
                dprob = dot_nt(gathered_ref[own, columns(value_base, kv_head)], grads)
                dscore = score_ref[kv_head, own] * inverse * (dprob - delta)
                dk_ref[kv_head] += dot_nn(dscore.astype(jnp.bfloat16), queries)

        @pl.when(me == block)
        def _():
            for kv_head, (queries, grads, inverse, delta) in enumerate(kept):
                dprob = dot_nt(gathered_ref[:span, columns(value_base, kv_head)], grads)
                dscore = score_ref[kv_head, :span] * inverse * (dprob - delta)
                dq_t = logit_scale * dot_nn(
                    key_t_ref[kv_head, :, :span], dscore.astype(jnp.bfloat16)
                )
                for h in range(QUERIES_PER_KEY):
                    first = (kv_head * QUERIES_PER_KEY + h) * HEAD_SIZE
                    dx_ref[:, first : first + HEAD_SIZE] = dq_t[
                        :, h * rows : (h + 1) * rows
                    ].T.astype(jnp.bfloat16)

    for kv_head in range(kv_heads):
        for block in range(blocks):
            dv_ref[block * rows : (block + 1) * rows, columns(0, kv_head)] = dot_nn(
                prob_ref[kv_head, block * rows : (block + 1) * rows, block * wide :],
                grad_ref[kv_head, block * wide :],
            ).astype(jnp.bfloat16)
        dx_ref[:, columns(key_base, kv_head)] = (logit_scale * dk_ref[kv_head]).astype(
            jnp.bfloat16
        )
    dx_ref[:, value_base : value_base + kv_cols] = dv_ref[
        pl.ds(pl.multiple_of(me * rows, rows), rows)
    ]
    for copy in copies:
        copy.wait()
    parts, _, cut = terms_ref.shape
    for part in range(parts):
        out_rows = slice(part * cut, (part + 1) * cut)
        terms_ref[part] = (
            dot_nt(dx_ref[:, :key_base], wq_ref[out_rows])
            + dot_nt(dx_ref[:, key_base:value_base], wk_ref[out_rows])
            + dot_nt(dx_ref[:, value_base:], wv_ref[out_rows])
        ).astype(jnp.bfloat16)


def weight_grad_kernel(turned_ref, attn_ref, dv_ref, wvalue_ref, woutput_ref, joined_ref):
    parts = turned_ref.shape[0]
    rows = turned_ref.shape[3]
    for part in range(parts):
        joined_ref[:, :, part * rows : (part + 1) * rows] = turned_ref[part]
    wvalue_ref[...] = dot_nn(joined_ref[0], dv_ref[...])
    woutput_ref[...] = dot_nt(attn_ref[...], joined_ref[1])


def kernel_call(body, outs, operands, in_specs=None, scratch=(), flops=0, moved=0):
    vmem = pl.BlockSpec(memory_space=pltpu.VMEM)
    return pl.pallas_call(
        body,
        out_shape=outs,
        in_specs=in_specs or [vmem] * len(operands),
        out_specs=jax.tree.map(lambda _: vmem, outs),
        scratch_shapes=list(scratch),
        compiler_params=pltpu.CompilerParams(vmem_limit_bytes=48 * 1024 * 1024),
        cost_estimate=pl.CostEstimate(flops=flops, bytes_accessed=moved, transcendentals=0),
    )(*operands)


def gathered_plan(
    normed_input,
    stored_queries,
    stored_keys,
    stored_values,
    query_weight,
    key_matrix,
    value_matrix,
    output_weight,
    out_cotangent,
):
    bf16, f32 = jnp.bfloat16, jnp.float32
    rows, model = normed_input.shape
    blocks = lax.axis_size("seq")
    groups = lax.axis_size("head")
    tokens = rows * blocks
    q_cols = stored_queries.shape[1]
    kv_cols = stored_keys.shape[1]
    kv_heads = kv_cols // HEAD_SIZE
    wide = QUERIES_PER_KEY * rows
    packed_cols = 2 * q_cols + 2 * kv_cols
    packed = kernel_call(
        out_grad_kernel,
        jax.ShapeDtypeStruct((rows, packed_cols), bf16),
        (out_cotangent, output_weight, stored_queries, stored_keys, stored_values),
        flops=2 * rows * model * q_cols,
        moved=2 * model * (rows + q_cols),
    )
    gathered = lax.all_gather(packed, "seq", axis=0, tiled=True)
    turned = kernel_call(
        functools.partial(turn_kernel, blocks),
        jax.ShapeDtypeStruct((blocks, 2, model // blocks, rows), bf16),
        (normed_input, out_cotangent),
        moved=8 * rows * model,
    )
    turned = lax.all_to_all(turned, "seq", 0, 0)
    anywhere = pl.BlockSpec(memory_space=pl.ANY)
    terms, attn, dv = kernel_call(
        attention_kernel,
        (
            jax.ShapeDtypeStruct((groups, rows, model // groups), bf16),
            jax.ShapeDtypeStruct((q_cols, tokens), bf16),
            jax.ShapeDtypeStruct((tokens, kv_cols), bf16),
        ),
        (gathered, query_weight, key_matrix, value_matrix),
        in_specs=[pl.BlockSpec(memory_space=pltpu.VMEM)] + [anywhere] * 3,
        scratch=(
            pltpu.VMEM(query_weight.shape, bf16),
            pltpu.VMEM(key_matrix.shape, bf16),
            pltpu.VMEM(value_matrix.shape, bf16),
            pltpu.VMEM((kv_heads, tokens, wide), f32),
            pltpu.VMEM((kv_heads, tokens, blocks * wide), bf16),
            pltpu.VMEM((kv_heads, blocks * wide, HEAD_SIZE), bf16),
            pltpu.VMEM((kv_heads, HEAD_SIZE, tokens), bf16),
            pltpu.VMEM((kv_heads, HEAD_SIZE, tokens), bf16),
            pltpu.VMEM((kv_heads, rows, HEAD_SIZE), f32),
            pltpu.VMEM((rows, q_cols + 2 * kv_cols), bf16),
            pltpu.SemaphoreType.DMA((3,)),
        ),
        flops=8 * tokens * tokens * q_cols,
        moved=2 * (tokens * packed_cols + model * (q_cols + 2 * kv_cols)),
    )
    arrived = lax.all_to_all(terms, "head", 0, 0)
    grad_wvalue, grad_woutput = kernel_call(
        weight_grad_kernel,
        (
            jax.ShapeDtypeStruct((model // blocks, kv_cols), f32),
            jax.ShapeDtypeStruct((q_cols, model // blocks), f32),
        ),
        (turned, attn, dv),
        scratch=(pltpu.VMEM((2, model // blocks, tokens), bf16),),
        flops=2 * tokens * (model // blocks) * (q_cols + kv_cols),
        moved=4 * (model // blocks) * (tokens + q_cols + kv_cols),
    )
    grad_input = jnp.sum(arrived.astype(f32), axis=0).astype(bf16)
    return (grad_input, grad_wvalue, grad_woutput)


def local(normed_input, *others):
    if normed_input.shape[0] * lax.axis_size("seq") <= WINDOW_LENGTH:
        return gathered_plan(normed_input, *others)
    return windowed_plan(normed_input, *others)


def windowed_plan(
    normed_input,
    stored_queries,
    stored_keys,
    stored_values,
    query_weight,
    key_matrix,
    value_matrix,
    output_weight,
    out_cotangent,
):
    tok_rows = normed_input.shape[0]
    blocks_seq = lax.axis_size("seq")
    seq_place = lax.axis_index("seq")
    reach_blocks = min(WINDOW_LENGTH // tok_rows, blocks_seq - 1)
    kv_heads = stored_keys.shape[1] // HEAD_SIZE
    output_gradient = jnp.dot(
        out_cotangent, output_weight.T, preferred_element_type=jnp.float32
    ).astype(jnp.bfloat16)
    pieces = [(stored_keys, stored_values)]
    current = (stored_keys, stored_values)
    for relay_step in range(reach_blocks):
        current = passed_along((current[0], current[1]), "seq", 1)
        pieces = [current] + pieces
    key_window = jnp.concatenate([piece[0] for piece in pieces], axis=0)
    value_window = jnp.concatenate([piece[1] for piece in pieces], axis=0)
    key_span = key_window.shape[0]
    query_pos = seq_place * tok_rows + jnp.arange(tok_rows, dtype=jnp.int32)
    key_pos = (seq_place - reach_blocks) * tok_rows + jnp.arange(key_span, dtype=jnp.int32)
    pos_gap = query_pos[:, None] - key_pos[None, :]
    allowed = (pos_gap >= 0) & (pos_gap < WINDOW_LENGTH) & (key_pos >= 0)[None, :]
    allowed_rows = jnp.tile(allowed, (QUERIES_PER_KEY, 1))
    query_stack = (
        stored_queries.reshape(tok_rows, kv_heads, QUERIES_PER_KEY, HEAD_SIZE)
        .transpose(1, 2, 0, 3)
        .reshape(kv_heads, QUERIES_PER_KEY * tok_rows, HEAD_SIZE)
    )
    grad_stack = (
        output_gradient.reshape(tok_rows, kv_heads, QUERIES_PER_KEY, HEAD_SIZE)
        .transpose(1, 2, 0, 3)
        .reshape(kv_heads, QUERIES_PER_KEY * tok_rows, HEAD_SIZE)
    )
    key_stack = key_window.reshape(key_span, kv_heads, HEAD_SIZE).transpose(1, 0, 2)
    value_stack = value_window.reshape(key_span, kv_heads, HEAD_SIZE).transpose(1, 0, 2)

    def per_head(head_items):
        query_head, key_head, value_head, grad_head = head_items
        attention_logits = logit_scale * jnp.dot(
            query_head, key_head.T, preferred_element_type=jnp.float32
        )
        masked = jnp.where(allowed_rows, attention_logits, -jnp.inf)
        row_top = jnp.max(masked, axis=1, keepdims=True)
        exp_scores = jnp.exp(masked - row_top)
        attn_prob = exp_scores / jnp.sum(exp_scores, axis=1, keepdims=True)
        probability_halfwidth = attn_prob.astype(jnp.bfloat16)
        attn_head = jnp.dot(
            probability_halfwidth, value_head, preferred_element_type=jnp.float32
        ).astype(jnp.bfloat16)
        row_delta = jnp.sum(
            grad_head.astype(jnp.float32) * attn_head.astype(jnp.float32), axis=1, keepdims=True
        )
        probability_gradient = jnp.dot(grad_head, value_head.T, preferred_element_type=jnp.float32)
        score_gradient = (attn_prob * (probability_gradient - row_delta)).astype(jnp.bfloat16)
        qgrad_head = (
            logit_scale * jnp.dot(score_gradient, key_head, preferred_element_type=jnp.float32)
        ).astype(jnp.bfloat16)
        key_partial = logit_scale * jnp.dot(
            score_gradient.T, query_head, preferred_element_type=jnp.float32
        )
        value_partial = jnp.dot(
            probability_halfwidth.T, grad_head, preferred_element_type=jnp.float32
        )
        return (attn_head, qgrad_head, key_partial, value_partial)

    attn_all, qgrad_all, key_all, value_all = lax.map(
        per_head, (query_stack, key_stack, value_stack, grad_stack)
    )
    attention_output = (
        attn_all.reshape(kv_heads, QUERIES_PER_KEY, tok_rows, HEAD_SIZE)
        .transpose(2, 0, 1, 3)
        .reshape(tok_rows, kv_heads * QUERIES_PER_KEY * HEAD_SIZE)
    )
    query_gradient = (
        qgrad_all.reshape(kv_heads, QUERIES_PER_KEY, tok_rows, HEAD_SIZE)
        .transpose(2, 0, 1, 3)
        .reshape(tok_rows, kv_heads * QUERIES_PER_KEY * HEAD_SIZE)
    )
    key_terms = key_all.transpose(1, 0, 2).reshape(key_span, kv_heads * HEAD_SIZE)
    value_terms = value_all.transpose(1, 0, 2).reshape(key_span, kv_heads * HEAD_SIZE)

    def take_slot(terms, slot_index):
        return terms[slot_index * tok_rows : (slot_index + 1) * tok_rows]

    key_sum = take_slot(key_terms, reach_blocks)
    value_sum = take_slot(value_terms, reach_blocks)
    for distance in range(1, reach_blocks + 1):
        received = passed_along(
            (
                take_slot(key_terms, reach_blocks - distance),
                take_slot(value_terms, reach_blocks - distance),
            ),
            "seq",
            -distance,
        )
        key_sum = key_sum + received[0]
        value_sum = value_sum + received[1]
    grad_key = key_sum.astype(jnp.bfloat16)
    grad_value = value_sum.astype(jnp.bfloat16)
    input_terms = jnp.dot(query_gradient, query_weight.T, preferred_element_type=jnp.float32)
    input_terms = input_terms + jnp.dot(grad_key, key_matrix.T, preferred_element_type=jnp.float32)
    input_terms = input_terms + jnp.dot(
        grad_value, value_matrix.T, preferred_element_type=jnp.float32
    )
    grad_input = lax.psum_scatter(input_terms, "head", scatter_dimension=1, tiled=True).astype(
        jnp.bfloat16
    )
    value_cols = grad_value.shape[1]
    input_cols = normed_input.T
    cot_cols = out_cotangent.T
    gathered = lax.psum_scatter(
        jnp.concatenate(
            [
                jnp.dot(input_cols, grad_value, preferred_element_type=jnp.float32),
                jnp.dot(cot_cols, attention_output, preferred_element_type=jnp.float32),
            ],
            axis=1,
        ),
        "seq",
        scatter_dimension=0,
        tiled=True,
    )
    grad_wvalue = gathered[:, :value_cols]
    grad_woutput = gathered[:, value_cols:].T
    return (grad_input, grad_wvalue, grad_woutput)


def solution(mesh):
    placed = (
        P("seq", None),
        P("seq", "head"),
        P("seq", "head"),
        P("seq", "head"),
        P(None, "head"),
        P(None, "head"),
        P(None, "head"),
        P("head", None),
        P("seq", None),
    )
    return jax.shard_map(
        local,
        mesh=mesh,
        in_specs=placed,
        out_specs=(P("seq", "head"), P("seq", "head"), P("head", "seq")),
        check_vma=False,
    )
```

```python
import functools

import jax
import jax.numpy as jnp
from jax import lax
from jax.experimental import pallas as pl
from jax.experimental.pallas import tpu as pltpu
from jax.sharding import PartitionSpec as P

HEAD_SIZE = 128
WINDOW_LENGTH = 4096
QUERIES_PER_KEY = 2


logit_scale = 1.0 / 12.0
log2_scale = 1.4426950408889634 / 12.0
excluded = -1e30


def passed_along(value, axis, steps):
    count = lax.axis_size(axis)
    leading, last = (max(0, -steps), min(count, count - steps))
    return lax.ppermute(value, axis, [(source, source + steps) for source in range(leading, last)])


NT = (((1,), (1,)), ((), ()))


def dot_nt(left, right):
    return lax.dot_general(left, right, NT, preferred_element_type=jnp.float32)


def dot_nn(left, right):
    return jnp.dot(left, right, preferred_element_type=jnp.float32)


def out_grad_kernel(
    cot_hbm, weight_hbm, q_hbm, k_hbm, v_hbm, packed_ref, cot_ref, weight_ref, sem
):
    q_cols = q_hbm.shape[1]
    kv_cols = k_hbm.shape[1]
    pieces = sem.shape[0] - 4
    cut = weight_ref.shape[0] // pieces
    cot_copy = pltpu.make_async_copy(cot_hbm, cot_ref, sem.at[pieces])
    cot_copy.start()
    weight_copies = [
        pltpu.make_async_copy(
            weight_hbm.at[pl.ds(piece * cut, cut)],
            weight_ref.at[pl.ds(piece * cut, cut)],
            sem.at[piece],
        )
        for piece in range(pieces)
    ]
    for copy in weight_copies:
        copy.start()
    first = 0
    packed_copies = []
    for place, source in enumerate((q_hbm, k_hbm, v_hbm)):
        cols = source.shape[1]
        packed_copies.append(
            pltpu.make_async_copy(
                source, packed_ref.at[:, pl.ds(first, cols)], sem.at[pieces + 1 + place]
            )
        )
        packed_copies[-1].start()
        first += cols
    cot_copy.wait()
    for piece, copy in enumerate(weight_copies):
        copy.wait()
        packed_ref[:, first + piece * cut : first + (piece + 1) * cut] = dot_nt(
            cot_ref[...], weight_ref[piece * cut : (piece + 1) * cut]
        ).astype(jnp.bfloat16)
    for copy in packed_copies:
        copy.wait()


def turn_kernel(parts, normed_hbm, cot_hbm, turned_ref, normed_ref, cot_ref, sem):
    cut = normed_ref.shape[1] // parts
    copies = []
    for which, (source, target) in enumerate(((normed_hbm, normed_ref), (cot_hbm, cot_ref))):
        copies.append(pltpu.make_async_copy(source, target, sem.at[which]))
        copies[-1].start()
    for which, ref in enumerate((normed_ref, cot_ref)):
        copies[which].wait()
        turned = ref[...].astype(jnp.float32).T.astype(jnp.bfloat16)
        for part in range(parts):
            turned_ref[part, which] = turned[part * cut : (part + 1) * cut]


def attention_kernel(
    blocks,
    *refs,
):
    attention_body(refs[:blocks], *refs[blocks:])


def attention_body(
    block_refs,
    wq_hbm,
    wk_hbm,
    wv_hbm,
    terms_ref,
    attn_ref,
    dv_ref,
    wq_ref,
    wk_ref,
    wv_ref,
    score_ref,
    prob_ref,
    grad_ref,
    value_t_ref,
    key_t_ref,
    dk_ref,
    dx_ref,
    gathered_ref,
    weight_sem,
    block_sem,
):
    me = lax.axis_index("seq")
    copies = [
        pltpu.make_async_copy(source, target, weight_sem.at[place])
        for place, (source, target) in enumerate(
            ((wq_hbm, wq_ref), (wk_hbm, wk_ref), (wv_hbm, wv_ref))
        )
    ]
    rows = dx_ref.shape[0]
    arrivals = []
    for apart, source in enumerate(block_refs):
        place = pl.ds(pl.multiple_of((me ^ apart) * rows, rows), rows)
        arrivals.append(
            pltpu.make_async_copy(source, gathered_ref.at[place], block_sem.at[apart])
        )
        arrivals[-1].start()
    for copy in copies:
        copy.start()
    for copy in arrivals:
        copy.wait()
    tokens = gathered_ref.shape[0]
    blocks = tokens // rows
    kv_cols = dv_ref.shape[1]
    kv_heads = kv_cols // HEAD_SIZE
    q_cols = attn_ref.shape[0]
    key_base = q_cols
    value_base = q_cols + kv_cols
    grad_base = q_cols + 2 * kv_cols
    wide = QUERIES_PER_KEY * rows

    def stacked(block, base, kv_head):
        return jnp.concatenate(
            [
                gathered_ref[
                    block * rows : (block + 1) * rows,
                    base + h * HEAD_SIZE : base + (h + 1) * HEAD_SIZE,
                ]
                for h in range(kv_head * QUERIES_PER_KEY, (kv_head + 1) * QUERIES_PER_KEY)
            ],
            axis=0,
        )

    def columns(base, kv_head):
        return slice(base + kv_head * HEAD_SIZE, base + (kv_head + 1) * HEAD_SIZE)

    dk_ref[...] = jnp.zeros_like(dk_ref)
    for kv_head in range(kv_heads):
        value_t_ref[kv_head] = gathered_ref[:, columns(value_base, kv_head)].T
        key_t_ref[kv_head] = gathered_ref[:, columns(key_base, kv_head)].T
    key_place = lax.broadcasted_iota(jnp.int32, (rows, wide), 0)
    query_place = lax.broadcasted_iota(jnp.int32, (rows, wide), 1) % rows
    allowed = key_place <= query_place

    for block in range(blocks):
        span = (block + 1) * rows
        kept = []
        for kv_head in range(kv_heads):
            queries = stacked(block, 0, kv_head)
            grads = stacked(block, grad_base, kv_head)
            grad_ref[kv_head, block * wide : (block + 1) * wide] = grads
            scores = dot_nt(gathered_ref[:span, columns(key_base, kv_head)], queries)
            diagonal = jnp.where(allowed, scores[block * rows :], excluded)
            if block:
                scores = jnp.concatenate([scores[: block * rows], diagonal], axis=0)
            else:
                scores = diagonal
            score_ref[kv_head, :span] = scores
            top = jnp.max(scores, axis=0, keepdims=True)
            weights = jnp.exp2((score_ref[kv_head, :span] - top) * log2_scale)
            score_ref[kv_head, :span] = weights
            inverse = 1.0 / jnp.sum(weights, axis=0, keepdims=True)
            prob_b = (score_ref[kv_head, :span] * inverse).astype(jnp.bfloat16)
            prob_ref[kv_head, :span, block * wide : (block + 1) * wide] = prob_b
            attn = dot_nn(value_t_ref[kv_head, :, :span], prob_b).astype(jnp.bfloat16)
            for h in range(QUERIES_PER_KEY):
                first = (kv_head * QUERIES_PER_KEY + h) * HEAD_SIZE
                attn_ref[first : first + HEAD_SIZE, block * rows : (block + 1) * rows] = attn[
                    :, h * rows : (h + 1) * rows
                ]
            delta = jnp.sum(
                grads.T.astype(jnp.float32) * attn.astype(jnp.float32), axis=0, keepdims=True
            )
            kept.append((queries, grads, inverse, delta))

        @pl.when(me <= block)
        def _():
            own = pl.ds(pl.multiple_of(me * rows, rows), rows)
            for kv_head, (queries, grads, inverse, delta) in enumerate(kept):
                dprob = dot_nt(gathered_ref[own, columns(value_base, kv_head)], grads)
                dscore = score_ref[kv_head, own] * inverse * (dprob - delta)
                dk_ref[kv_head] += dot_nn(dscore.astype(jnp.bfloat16), queries)

        @pl.when(me == block)
        def _():
            for kv_head, (queries, grads, inverse, delta) in enumerate(kept):
                dprob = dot_nt(gathered_ref[:span, columns(value_base, kv_head)], grads)
                dscore = score_ref[kv_head, :span] * inverse * (dprob - delta)
                dq_t = logit_scale * dot_nn(
                    key_t_ref[kv_head, :, :span], dscore.astype(jnp.bfloat16)
                )
                for h in range(QUERIES_PER_KEY):
                    first = (kv_head * QUERIES_PER_KEY + h) * HEAD_SIZE
                    dx_ref[:, first : first + HEAD_SIZE] = dq_t[
                        :, h * rows : (h + 1) * rows
                    ].T.astype(jnp.bfloat16)

    for kv_head in range(kv_heads):
        for block in range(blocks):
            dv_ref[block * rows : (block + 1) * rows, columns(0, kv_head)] = dot_nn(
                prob_ref[kv_head, block * rows : (block + 1) * rows, block * wide :],
                grad_ref[kv_head, block * wide :],
            ).astype(jnp.bfloat16)
        dx_ref[:, columns(key_base, kv_head)] = (logit_scale * dk_ref[kv_head]).astype(
            jnp.bfloat16
        )
    dx_ref[:, value_base : value_base + kv_cols] = dv_ref[
        pl.ds(pl.multiple_of(me * rows, rows), rows)
    ]
    for copy in copies:
        copy.wait()
    parts, cut, _ = terms_ref.shape
    for part in range(parts):
        out_rows = slice(part * cut, (part + 1) * cut)
        terms_ref[part] = (
            dot_nt(wq_ref[out_rows], dx_ref[:, :key_base])
            + dot_nt(wk_ref[out_rows], dx_ref[:, key_base:value_base])
            + dot_nt(wv_ref[out_rows], dx_ref[:, value_base:])
        ).astype(jnp.bfloat16)


def weight_grad_kernel(turned_ref, attn_ref, dv_ref, wvalue_ref, woutput_ref, joined_ref):
    parts = turned_ref.shape[0]
    rows = turned_ref.shape[3]
    for part in range(parts):
        joined_ref[:, :, part * rows : (part + 1) * rows] = turned_ref[part]
    wvalue_ref[...] = dot_nn(joined_ref[0], dv_ref[...])
    woutput_ref[...] = dot_nt(joined_ref[1], attn_ref[...])


def kernel_call(body, outs, operands, in_vmem=(), scratch=(), flops=0, moved=0, room=48):
    vmem = pl.BlockSpec(memory_space=pltpu.VMEM)
    hbm = pl.BlockSpec(memory_space=pltpu.HBM)
    return pl.pallas_call(
        body,
        out_shape=outs,
        in_specs=[vmem if place in in_vmem else hbm for place in range(len(operands))],
        out_specs=jax.tree.map(lambda _: vmem, outs),
        scratch_shapes=list(scratch),
        compiler_params=pltpu.CompilerParams(vmem_limit_bytes=room * 1024 * 1024),
        cost_estimate=pl.CostEstimate(flops=flops, bytes_accessed=moved, transcendentals=0),
    )(*operands)


def swapped(value, apart):
    count = lax.axis_size("seq")
    return lax.ppermute(value, "seq", [(place, place ^ apart) for place in range(count)])


def gathered_plan(
    normed_input,
    stored_queries,
    stored_keys,
    stored_values,
    query_weight,
    key_matrix,
    value_matrix,
    output_weight,
    out_cotangent,
):
    bf16, f32 = jnp.bfloat16, jnp.float32
    rows, model = normed_input.shape
    blocks = lax.axis_size("seq")
    groups = lax.axis_size("head")
    tokens = rows * blocks
    q_cols = stored_queries.shape[1]
    kv_cols = stored_keys.shape[1]
    kv_heads = kv_cols // HEAD_SIZE
    wide = QUERIES_PER_KEY * rows
    packed_cols = 2 * q_cols + 2 * kv_cols
    packed = kernel_call(
        out_grad_kernel,
        jax.ShapeDtypeStruct((rows, packed_cols), bf16),
        (out_cotangent, output_weight, stored_queries, stored_keys, stored_values),
        scratch=(
            pltpu.VMEM(out_cotangent.shape, bf16),
            pltpu.VMEM(output_weight.shape, bf16),
            pltpu.SemaphoreType.DMA((q_cols // HEAD_SIZE + 4,)),
        ),
        flops=2 * rows * model * q_cols,
        moved=2 * model * (rows + q_cols),
        room=63,
    )
    held = {0: packed}
    for apart in range(2, blocks, 2):
        held[apart] = swapped(packed, apart)
    for apart in range(0, blocks, 2):
        held[apart + 1] = swapped(held[apart], 1)
    turned = kernel_call(
        functools.partial(turn_kernel, blocks),
        jax.ShapeDtypeStruct((blocks, 2, model // blocks, rows), bf16),
        (normed_input, out_cotangent),
        scratch=(
            pltpu.VMEM(normed_input.shape, bf16),
            pltpu.VMEM(out_cotangent.shape, bf16),
            pltpu.SemaphoreType.DMA((2,)),
        ),
        moved=8 * rows * model,
    )
    turned = lax.all_to_all(turned, "seq", 0, 0)
    terms, attn, dv = kernel_call(
        functools.partial(attention_kernel, blocks),
        (
            jax.ShapeDtypeStruct((groups, model // groups, rows), bf16),
            jax.ShapeDtypeStruct((q_cols, tokens), bf16),
            jax.ShapeDtypeStruct((tokens, kv_cols), bf16),
        ),
        (*(held[apart] for apart in range(blocks)), query_weight, key_matrix, value_matrix),
        scratch=(
            pltpu.VMEM(query_weight.shape, bf16),
            pltpu.VMEM(key_matrix.shape, bf16),
            pltpu.VMEM(value_matrix.shape, bf16),
            pltpu.VMEM((kv_heads, tokens, wide), f32),
            pltpu.VMEM((kv_heads, tokens, blocks * wide), bf16),
            pltpu.VMEM((kv_heads, blocks * wide, HEAD_SIZE), bf16),
            pltpu.VMEM((kv_heads, HEAD_SIZE, tokens), bf16),
            pltpu.VMEM((kv_heads, HEAD_SIZE, tokens), bf16),
            pltpu.VMEM((kv_heads, rows, HEAD_SIZE), f32),
            pltpu.VMEM((rows, q_cols + 2 * kv_cols), bf16),
            pltpu.VMEM((tokens, packed_cols), bf16),
            pltpu.SemaphoreType.DMA((3,)),
            pltpu.SemaphoreType.DMA((blocks,)),
        ),
        flops=8 * tokens * tokens * q_cols,
        moved=2 * (tokens * packed_cols + model * (q_cols + 2 * kv_cols)),
    )
    arrived = lax.all_to_all(terms, "head", 0, 0)
    grad_wvalue, grad_woutput = kernel_call(
        weight_grad_kernel,
        (
            jax.ShapeDtypeStruct((model // blocks, kv_cols), f32),
            jax.ShapeDtypeStruct((model // blocks, q_cols), f32),
        ),
        (turned, attn, dv),
        in_vmem=(0, 1, 2),
        scratch=(pltpu.VMEM((2, model // blocks, tokens), bf16),),
        flops=2 * tokens * (model // blocks) * (q_cols + kv_cols),
        moved=4 * (model // blocks) * (tokens + q_cols + kv_cols),
    )
    grad_input = jnp.sum(arrived.astype(f32), axis=0).astype(bf16)
    return (grad_input.T, grad_wvalue, grad_woutput.T)


def local(normed_input, *others):
    blocks = lax.axis_size("seq")
    fits = normed_input.shape[0] * blocks <= WINDOW_LENGTH
    if fits and blocks % 2 == 0 and blocks & (blocks - 1) == 0:
        return gathered_plan(normed_input, *others)
    return windowed_plan(normed_input, *others)


def windowed_plan(
    normed_input,
    stored_queries,
    stored_keys,
    stored_values,
    query_weight,
    key_matrix,
    value_matrix,
    output_weight,
    out_cotangent,
):
    tok_rows = normed_input.shape[0]
    blocks_seq = lax.axis_size("seq")
    seq_place = lax.axis_index("seq")
    reach_blocks = min(WINDOW_LENGTH // tok_rows, blocks_seq - 1)
    kv_heads = stored_keys.shape[1] // HEAD_SIZE
    output_gradient = jnp.dot(
        out_cotangent, output_weight.T, preferred_element_type=jnp.float32
    ).astype(jnp.bfloat16)
    pieces = [(stored_keys, stored_values)]
    current = (stored_keys, stored_values)
    for relay_step in range(reach_blocks):
        current = passed_along((current[0], current[1]), "seq", 1)
        pieces = [current] + pieces
    key_window = jnp.concatenate([piece[0] for piece in pieces], axis=0)
    value_window = jnp.concatenate([piece[1] for piece in pieces], axis=0)
    key_span = key_window.shape[0]
    query_pos = seq_place * tok_rows + jnp.arange(tok_rows, dtype=jnp.int32)
    key_pos = (seq_place - reach_blocks) * tok_rows + jnp.arange(key_span, dtype=jnp.int32)
    pos_gap = query_pos[:, None] - key_pos[None, :]
    allowed = (pos_gap >= 0) & (pos_gap < WINDOW_LENGTH) & (key_pos >= 0)[None, :]
    allowed_rows = jnp.tile(allowed, (QUERIES_PER_KEY, 1))
    query_stack = (
        stored_queries.reshape(tok_rows, kv_heads, QUERIES_PER_KEY, HEAD_SIZE)
        .transpose(1, 2, 0, 3)
        .reshape(kv_heads, QUERIES_PER_KEY * tok_rows, HEAD_SIZE)
    )
    grad_stack = (
        output_gradient.reshape(tok_rows, kv_heads, QUERIES_PER_KEY, HEAD_SIZE)
        .transpose(1, 2, 0, 3)
        .reshape(kv_heads, QUERIES_PER_KEY * tok_rows, HEAD_SIZE)
    )
    key_stack = key_window.reshape(key_span, kv_heads, HEAD_SIZE).transpose(1, 0, 2)
    value_stack = value_window.reshape(key_span, kv_heads, HEAD_SIZE).transpose(1, 0, 2)

    def per_head(head_items):
        query_head, key_head, value_head, grad_head = head_items
        attention_logits = logit_scale * jnp.dot(
            query_head, key_head.T, preferred_element_type=jnp.float32
        )
        masked = jnp.where(allowed_rows, attention_logits, -jnp.inf)
        row_top = jnp.max(masked, axis=1, keepdims=True)
        exp_scores = jnp.exp(masked - row_top)
        attn_prob = exp_scores / jnp.sum(exp_scores, axis=1, keepdims=True)
        probability_halfwidth = attn_prob.astype(jnp.bfloat16)
        attn_head = jnp.dot(
            probability_halfwidth, value_head, preferred_element_type=jnp.float32
        ).astype(jnp.bfloat16)
        row_delta = jnp.sum(
            grad_head.astype(jnp.float32) * attn_head.astype(jnp.float32), axis=1, keepdims=True
        )
        probability_gradient = jnp.dot(grad_head, value_head.T, preferred_element_type=jnp.float32)
        score_gradient = (attn_prob * (probability_gradient - row_delta)).astype(jnp.bfloat16)
        qgrad_head = (
            logit_scale * jnp.dot(score_gradient, key_head, preferred_element_type=jnp.float32)
        ).astype(jnp.bfloat16)
        key_partial = logit_scale * jnp.dot(
            score_gradient.T, query_head, preferred_element_type=jnp.float32
        )
        value_partial = jnp.dot(
            probability_halfwidth.T, grad_head, preferred_element_type=jnp.float32
        )
        return (attn_head, qgrad_head, key_partial, value_partial)

    attn_all, qgrad_all, key_all, value_all = lax.map(
        per_head, (query_stack, key_stack, value_stack, grad_stack)
    )
    attention_output = (
        attn_all.reshape(kv_heads, QUERIES_PER_KEY, tok_rows, HEAD_SIZE)
        .transpose(2, 0, 1, 3)
        .reshape(tok_rows, kv_heads * QUERIES_PER_KEY * HEAD_SIZE)
    )
    query_gradient = (
        qgrad_all.reshape(kv_heads, QUERIES_PER_KEY, tok_rows, HEAD_SIZE)
        .transpose(2, 0, 1, 3)
        .reshape(tok_rows, kv_heads * QUERIES_PER_KEY * HEAD_SIZE)
    )
    key_terms = key_all.transpose(1, 0, 2).reshape(key_span, kv_heads * HEAD_SIZE)
    value_terms = value_all.transpose(1, 0, 2).reshape(key_span, kv_heads * HEAD_SIZE)

    def take_slot(terms, slot_index):
        return terms[slot_index * tok_rows : (slot_index + 1) * tok_rows]

    key_sum = take_slot(key_terms, reach_blocks)
    value_sum = take_slot(value_terms, reach_blocks)
    for distance in range(1, reach_blocks + 1):
        received = passed_along(
            (
                take_slot(key_terms, reach_blocks - distance),
                take_slot(value_terms, reach_blocks - distance),
            ),
            "seq",
            -distance,
        )
        key_sum = key_sum + received[0]
        value_sum = value_sum + received[1]
    grad_key = key_sum.astype(jnp.bfloat16)
    grad_value = value_sum.astype(jnp.bfloat16)
    input_terms = jnp.dot(query_gradient, query_weight.T, preferred_element_type=jnp.float32)
    input_terms = input_terms + jnp.dot(grad_key, key_matrix.T, preferred_element_type=jnp.float32)
    input_terms = input_terms + jnp.dot(
        grad_value, value_matrix.T, preferred_element_type=jnp.float32
    )
    grad_input = lax.psum_scatter(input_terms, "head", scatter_dimension=1, tiled=True).astype(
        jnp.bfloat16
    )
    value_cols = grad_value.shape[1]
    input_cols = normed_input.T
    cot_cols = out_cotangent.T
    gathered = lax.psum_scatter(
        jnp.concatenate(
            [
                jnp.dot(input_cols, grad_value, preferred_element_type=jnp.float32),
                jnp.dot(cot_cols, attention_output, preferred_element_type=jnp.float32),
            ],
            axis=1,
        ),
        "seq",
        scatter_dimension=0,
        tiled=True,
    )
    grad_wvalue = gathered[:, :value_cols]
    grad_woutput = gathered[:, value_cols:].T
    return (grad_input, grad_wvalue, grad_woutput)


def solution(mesh):
    placed = (
        P("seq", None),
        P("seq", "head"),
        P("seq", "head"),
        P("seq", "head"),
        P(None, "head"),
        P(None, "head"),
        P(None, "head"),
        P("head", None),
        P("seq", None),
    )
    return jax.shard_map(
        local,
        mesh=mesh,
        in_specs=placed,
        out_specs=(P("seq", "head"), P("seq", "head"), P("head", "seq")),
        check_vma=False,
    )
```

```python
import functools

import jax
import jax.numpy as jnp
from jax import lax
from jax.experimental import pallas as pl
from jax.experimental.pallas import tpu as pltpu
from jax.sharding import PartitionSpec as P

HEAD_SIZE = 128
WINDOW_LENGTH = 4096
QUERIES_PER_KEY = 2


logit_scale = 1.0 / 12.0
log2_scale = 1.4426950408889634 / 12.0
excluded = -1e30


def passed_along(value, axis, steps):
    count = lax.axis_size(axis)
    leading, last = (max(0, -steps), min(count, count - steps))
    return lax.ppermute(value, axis, [(source, source + steps) for source in range(leading, last)])


NT = (((1,), (1,)), ((), ()))


def dot_nt(left, right):
    return lax.dot_general(left, right, NT, preferred_element_type=jnp.float32)


def dot_nn(left, right):
    return jnp.dot(left, right, preferred_element_type=jnp.float32)


def at(place, size):
    return pl.ds(pl.multiple_of(place * size, size), size)


def out_grad_kernel(
    cot_hbm, weight_hbm, q_hbm, k_hbm, v_hbm, same_ref, other_ref, cot_ref, weight_ref, sem
):
    core = lax.axis_index("seq") % 2
    cut = weight_ref.shape[0] // 2
    cot_copy = pltpu.make_async_copy(cot_hbm, cot_ref, sem.at[0])
    cot_copy.start()
    halves = ((other_ref, 1 - core), (same_ref, core))
    weight_copies = []
    for place, (_, half) in enumerate(halves):
        weight_copies.append(
            pltpu.make_async_copy(
                weight_hbm.at[at(half, cut)], weight_ref.at[at(place, cut)], sem.at[1 + place]
            )
        )
        weight_copies[-1].start()
    plain_copies = []
    for place, (target, half) in enumerate(halves):
        first = 0
        for which, source in enumerate((q_hbm, k_hbm, v_hbm)):
            cols = source.shape[1] // 2
            plain_copies.append(
                pltpu.make_async_copy(
                    source.at[:, at(half, cols)],
                    target.at[:, pl.ds(first, cols)],
                    sem.at[3 + 3 * place + which],
                )
            )
            plain_copies[-1].start()
            first += cols
    cot_copy.wait()
    for place, (target, _) in enumerate(halves):
        weight_copies[place].wait()
        target[:, first:] = dot_nt(
            cot_ref[...], weight_ref[place * cut : (place + 1) * cut]
        ).astype(jnp.bfloat16)
    for copy in plain_copies:
        copy.wait()


def turn_kernel(parts, normed_hbm, cot_hbm, turned_ref, normed_ref, cot_ref, sem):
    cut = normed_ref.shape[1] // parts
    copies = []
    for which, (source, target) in enumerate(((normed_hbm, normed_ref), (cot_hbm, cot_ref))):
        copies.append(pltpu.make_async_copy(source, target, sem.at[which]))
        copies[-1].start()
    for which, ref in enumerate((normed_ref, cot_ref)):
        copies[which].wait()
        turned = ref[...].astype(jnp.float32).T.astype(jnp.bfloat16)
        for part in range(parts):
            turned_ref[part, which] = turned[part * cut : (part + 1) * cut]


def attention_kernel(blocks, *refs):
    attention_body(refs[:blocks], *refs[blocks:])


def attention_body(
    block_refs,
    dx_own_ref,
    dx_far_ref,
    attn_ref,
    dv_ref,
    gathered_ref,
    score_even_ref,
    score_odd_ref,
    prob_ref,
    grad_t_ref,
    delta_ref,
    query_ref,
    value_t_ref,
    key_t_ref,
    dq_t_ref,
    dk_ref,
    sem,
):
    me = lax.axis_index("seq")
    core, chip = me % 2, me // 2
    rows = dx_own_ref.shape[0]
    arrivals = []
    for apart, source in enumerate(block_refs):
        arrivals.append(
            pltpu.make_async_copy(source, gathered_ref.at[at(me ^ apart, rows)], sem.at[apart])
        )
        arrivals[-1].start()
    for copy in arrivals:
        copy.wait()
    tokens = gathered_ref.shape[0]
    size = 2 * rows
    steps = tokens // size
    wide = QUERIES_PER_KEY * size
    heads = QUERIES_PER_KEY
    key_cols = slice(heads * HEAD_SIZE, (heads + 1) * HEAD_SIZE)
    value_cols = slice((heads + 1) * HEAD_SIZE, (heads + 2) * HEAD_SIZE)
    grad_base = (heads + 2) * HEAD_SIZE
    value_t_ref[...] = gathered_ref[:, value_cols].T
    key_t_ref[...] = gathered_ref[:, key_cols].T
    key_place = lax.broadcasted_iota(jnp.int32, (size, wide), 0)
    query_place = lax.broadcasted_iota(jnp.int32, (size, wide), 1) % size
    allowed = key_place <= query_place

    for step in range(steps):
        span = (step + 1) * size
        own = slice(step * size, span)
        lanes = slice(step * wide, (step + 1) * wide)
        score_ref = score_odd_ref if step % 2 else score_even_ref
        queries = jnp.concatenate(
            [gathered_ref[own, h * HEAD_SIZE : (h + 1) * HEAD_SIZE] for h in range(heads)], axis=0
        )
        query_ref[lanes] = queries
        top = None
        for piece in range(step + 1):
            part = slice(piece * size, (piece + 1) * size)
            scores = dot_nt(gathered_ref[part, key_cols], queries)
            if piece == step:
                scores = jnp.where(allowed, scores, excluded)
            score_ref[part] = scores
            largest = jnp.max(scores.reshape(size // 8, 8, wide), axis=0)
            top = largest if top is None else jnp.maximum(top, largest)
        top = jnp.max(top, axis=0, keepdims=True)
        total = None
        for piece in range(step + 1):
            part = slice(piece * size, (piece + 1) * size)
            weights = jnp.exp2((score_ref[part] - top) * log2_scale)
            prob_ref[part, lanes] = weights.astype(jnp.bfloat16)
            summed = jnp.sum(weights.reshape(size // 8, 8, wide), axis=0)
            total = summed if total is None else total + summed
        inverse = 1.0 / jnp.sum(total, axis=0, keepdims=True)
        attn = dot_nn(value_t_ref[:, :span], prob_ref[:span, lanes]) * inverse
        for h in range(heads):
            attn_ref[h * HEAD_SIZE : (h + 1) * HEAD_SIZE, own] = attn[
                :, h * size : (h + 1) * size
            ].astype(jnp.bfloat16)
        grads_t = jnp.concatenate(
            [
                gathered_ref[
                    own, grad_base + h * HEAD_SIZE : grad_base + (h + 1) * HEAD_SIZE
                ].T
                for h in range(heads)
            ],
            axis=1,
        )
        grads_t = (grads_t.astype(jnp.float32) * inverse).astype(jnp.bfloat16)
        grad_t_ref[:, lanes] = grads_t
        delta_ref[:, lanes] = jnp.sum(grads_t.astype(jnp.float32) * attn, axis=0, keepdims=True)

    for step in range(steps):
        own = slice(step * size, (step + 1) * size)
        dv_ref[own] = dot_nt(prob_ref[own, step * wide :], grad_t_ref[:, step * wide :]).astype(
            jnp.bfloat16
        )

    dq_t_ref[...] = jnp.zeros_like(dq_t_ref)
    dk_ref[...] = jnp.zeros_like(dk_ref)
    for step in range(steps):
        key_step = jnp.minimum(chip, step)
        query_step = jnp.maximum(chip, step)
        dprob = dot_nn(
            gathered_ref[at(key_step, size), value_cols], grad_t_ref[:, at(query_step, wide)]
        )
        dscore = (
            prob_ref[at(key_step, size), at(query_step, wide)].astype(jnp.float32)
            * (dprob - delta_ref[:, at(query_step, wide)])
        ).astype(jnp.bfloat16)

        @pl.when(step <= chip)
        def _():
            dq_t_ref[...] += dot_nn(key_t_ref[:, at(key_step, size)], dscore)

        @pl.when(step >= chip)
        def _():
            dk_ref[...] += dot_nn(dscore, query_ref[at(query_step, wide)])

    for target, half in ((dx_far_ref, 1 - core), (dx_own_ref, core)):
        for h in range(heads):
            target[:, h * HEAD_SIZE : (h + 1) * HEAD_SIZE] = (
                (logit_scale * dq_t_ref[:, at(2 * h + half, rows)])
                .T.astype(jnp.bfloat16)
            )
        target[:, key_cols] = (logit_scale * dk_ref[at(half, rows)]).astype(jnp.bfloat16)
        target[:, value_cols] = dv_ref[at(2 * chip + half, rows)]


def input_terms_kernel(
    apart_groups, own_ref, far_ref, wq_ref, wk_ref, wv_ref, *refs
):
    terms, dx_ref = refs[:-1], refs[-1]
    core = lax.axis_index("seq") % 2
    group = lax.axis_index("head")
    q_cols = wq_ref.shape[1] // 2
    kv_cols = wk_ref.shape[1] // 2
    for source, half in ((own_ref, core), (far_ref, 1 - core)):
        dx_ref[:, at(half, q_cols)] = source[:, :q_cols]
        dx_ref[:, pl.ds(pl.multiple_of(2 * q_cols + half * kv_cols, kv_cols), kv_cols)] = source[
            :, q_cols : q_cols + kv_cols
        ]
        dx_ref[
            :, pl.ds(pl.multiple_of(2 * q_cols + (2 + half) * kv_cols, kv_cols), kv_cols)
        ] = source[:, q_cols + kv_cols :]
    for apart, target in zip(apart_groups, terms):
        cut = target.shape[0]
        place = at(group ^ apart, cut)
        target[...] = (
            dot_nt(wq_ref[place], dx_ref[:, : 2 * q_cols])
            + dot_nt(wk_ref[place], dx_ref[:, 2 * q_cols : 2 * q_cols + 2 * kv_cols])
            + dot_nt(wv_ref[place], dx_ref[:, 2 * q_cols + 2 * kv_cols :])
        ).astype(target.dtype)


def weight_grad_kernel(
    turned_ref, attn_ref, far_attn_ref, dv_ref, far_dv_ref, wvalue_ref, woutput_ref, joined_ref
):
    core = lax.axis_index("seq") % 2
    parts = turned_ref.shape[0]
    rows = turned_ref.shape[3]
    for part in range(parts):
        joined_ref[:, :, part * rows : (part + 1) * rows] = turned_ref[part]
    for half, attn, dv in ((core, attn_ref, dv_ref), (1 - core, far_attn_ref, far_dv_ref)):
        wvalue_ref[:, at(half, dv.shape[1])] = dot_nn(joined_ref[0], dv[...])
        woutput_ref[:, at(half, attn.shape[0])] = dot_nt(joined_ref[1], attn[...])


def kernel_call(body, outs, operands, in_vmem=(), scratch=(), flops=0, moved=0, room=32):
    vmem = pl.BlockSpec(memory_space=pltpu.VMEM)
    hbm = pl.BlockSpec(memory_space=pltpu.HBM)
    return pl.pallas_call(
        body,
        out_shape=outs,
        in_specs=[vmem if place in in_vmem else hbm for place in range(len(operands))],
        out_specs=jax.tree.map(lambda _: vmem, outs),
        scratch_shapes=list(scratch),
        compiler_params=pltpu.CompilerParams(vmem_limit_bytes=room * 1024 * 1024),
        cost_estimate=pl.CostEstimate(flops=flops, bytes_accessed=moved, transcendentals=0),
    )(*operands)


def swapped(value, axis, apart):
    count = lax.axis_size(axis)
    return lax.ppermute(value, axis, [(place, place ^ apart) for place in range(count)])


def gathered_plan(
    normed_input,
    stored_queries,
    stored_keys,
    stored_values,
    query_weight,
    key_matrix,
    value_matrix,
    output_weight,
    out_cotangent,
):
    bf16, f32 = jnp.bfloat16, jnp.float32
    rows, model = normed_input.shape
    blocks = lax.axis_size("seq")
    groups = lax.axis_size("head")
    tokens = rows * blocks
    q_cols = stored_queries.shape[1] // 2
    kv_cols = HEAD_SIZE
    wide = 2 * QUERIES_PER_KEY * rows
    packed_cols = 2 * q_cols + 2 * kv_cols
    shape = jax.ShapeDtypeStruct
    same, other = kernel_call(
        out_grad_kernel,
        (shape((rows, packed_cols), bf16),) * 2,
        (out_cotangent, output_weight, stored_queries, stored_keys, stored_values),
        scratch=(
            pltpu.VMEM(out_cotangent.shape, bf16),
            pltpu.VMEM(output_weight.shape, bf16),
            pltpu.SemaphoreType.DMA((9,)),
        ),
        flops=4 * rows * model * q_cols,
        moved=2 * model * (rows + 2 * q_cols),
        room=63,
    )
    held = [same] + [
        swapped(other if apart % 2 else same, "seq", apart) for apart in range(1, blocks)
    ]
    turned = kernel_call(
        functools.partial(turn_kernel, blocks),
        shape((blocks, 2, model // blocks, rows), bf16),
        (normed_input, out_cotangent),
        scratch=(
            pltpu.VMEM(normed_input.shape, bf16),
            pltpu.VMEM(out_cotangent.shape, bf16),
            pltpu.SemaphoreType.DMA((2,)),
        ),
        moved=8 * rows * model,
    )
    turned = lax.all_to_all(turned, "seq", 0, 0)
    dx_own, dx_far, attn, dv = kernel_call(
        functools.partial(attention_kernel, blocks),
        (
            shape((rows, q_cols + 2 * kv_cols), bf16),
            shape((rows, q_cols + 2 * kv_cols), bf16),
            shape((q_cols, tokens), bf16),
            shape((tokens, kv_cols), bf16),
        ),
        held,
        scratch=(
            pltpu.VMEM((tokens, packed_cols), bf16),
            pltpu.VMEM((tokens, wide), f32),
            pltpu.VMEM((tokens, wide), f32),
            pltpu.VMEM((tokens, tokens * QUERIES_PER_KEY), bf16),
            pltpu.VMEM((HEAD_SIZE, tokens * QUERIES_PER_KEY), bf16),
            pltpu.VMEM((1, tokens * QUERIES_PER_KEY), f32),
            pltpu.VMEM((tokens * QUERIES_PER_KEY, HEAD_SIZE), bf16),
            pltpu.VMEM((HEAD_SIZE, tokens), bf16),
            pltpu.VMEM((HEAD_SIZE, tokens), bf16),
            pltpu.VMEM((HEAD_SIZE, wide), f32),
            pltpu.VMEM((2 * rows, HEAD_SIZE), f32),
            pltpu.SemaphoreType.DMA((blocks,)),
        ),
        flops=8 * tokens * tokens * q_cols,
        moved=2 * tokens * packed_cols,
    )
    dx_got = swapped(dx_far, "seq", 1)
    aparts = tuple(range(groups - 1, -1, -1))
    terms = kernel_call(
        functools.partial(input_terms_kernel, aparts),
        tuple(shape((model // groups, rows), bf16 if apart else f32) for apart in aparts),
        (dx_own, dx_got, query_weight, key_matrix, value_matrix),
        in_vmem=range(5),
        scratch=(pltpu.VMEM((rows, 2 * (q_cols + 2 * kv_cols)), bf16),),
        flops=4 * rows * model * (q_cols + 2 * kv_cols),
        moved=4 * model * (q_cols + 2 * kv_cols),
    )
    grad_input = terms[-1]
    for apart, term in zip(aparts[:-1], terms[:-1]):
        grad_input = grad_input + swapped(term, "head", apart).astype(f32)
    grad_wvalue, grad_woutput = kernel_call(
        weight_grad_kernel,
        (
            shape((model // blocks, 2 * kv_cols), f32),
            shape((model // blocks, 2 * q_cols), f32),
        ),
        (turned, attn, swapped(attn, "seq", 1), dv, swapped(dv, "seq", 1)),
        in_vmem=range(5),
        scratch=(pltpu.VMEM((2, model // blocks, tokens), bf16),),
        flops=4 * tokens * (model // blocks) * (q_cols + kv_cols),
        moved=4 * (model // blocks) * (tokens + 2 * q_cols + 2 * kv_cols),
    )
    return (grad_input.astype(bf16).T, grad_wvalue, grad_woutput.T)


def power_of_two(count):
    return count & (count - 1) == 0


def local(normed_input, stored_queries, stored_keys, *others):
    blocks, groups = lax.axis_size("seq"), lax.axis_size("head")
    whole_window = normed_input.shape[0] * blocks <= WINDOW_LENGTH
    two_heads = stored_keys.shape[1] == 2 * HEAD_SIZE
    paired = blocks > 1 and power_of_two(blocks) and power_of_two(groups)
    plan = gathered_plan if whole_window and two_heads and paired else windowed_plan
    return plan(normed_input, stored_queries, stored_keys, *others)


def windowed_plan(
    normed_input,
    stored_queries,
    stored_keys,
    stored_values,
    query_weight,
    key_matrix,
    value_matrix,
    output_weight,
    out_cotangent,
):
    tok_rows = normed_input.shape[0]
    blocks_seq = lax.axis_size("seq")
    seq_place = lax.axis_index("seq")
    reach_blocks = min(WINDOW_LENGTH // tok_rows, blocks_seq - 1)
    kv_heads = stored_keys.shape[1] // HEAD_SIZE
    output_gradient = jnp.dot(
        out_cotangent, output_weight.T, preferred_element_type=jnp.float32
    ).astype(jnp.bfloat16)
    pieces = [(stored_keys, stored_values)]
    current = (stored_keys, stored_values)
    for relay_step in range(reach_blocks):
        current = passed_along((current[0], current[1]), "seq", 1)
        pieces = [current] + pieces
    key_window = jnp.concatenate([piece[0] for piece in pieces], axis=0)
    value_window = jnp.concatenate([piece[1] for piece in pieces], axis=0)
    key_span = key_window.shape[0]
    query_pos = seq_place * tok_rows + jnp.arange(tok_rows, dtype=jnp.int32)
    key_pos = (seq_place - reach_blocks) * tok_rows + jnp.arange(key_span, dtype=jnp.int32)
    pos_gap = query_pos[:, None] - key_pos[None, :]
    allowed = (pos_gap >= 0) & (pos_gap < WINDOW_LENGTH) & (key_pos >= 0)[None, :]
    allowed_rows = jnp.tile(allowed, (QUERIES_PER_KEY, 1))
    query_stack = (
        stored_queries.reshape(tok_rows, kv_heads, QUERIES_PER_KEY, HEAD_SIZE)
        .transpose(1, 2, 0, 3)
        .reshape(kv_heads, QUERIES_PER_KEY * tok_rows, HEAD_SIZE)
    )
    grad_stack = (
        output_gradient.reshape(tok_rows, kv_heads, QUERIES_PER_KEY, HEAD_SIZE)
        .transpose(1, 2, 0, 3)
        .reshape(kv_heads, QUERIES_PER_KEY * tok_rows, HEAD_SIZE)
    )
    key_stack = key_window.reshape(key_span, kv_heads, HEAD_SIZE).transpose(1, 0, 2)
    value_stack = value_window.reshape(key_span, kv_heads, HEAD_SIZE).transpose(1, 0, 2)

    def per_head(head_items):
        query_head, key_head, value_head, grad_head = head_items
        attention_logits = logit_scale * jnp.dot(
            query_head, key_head.T, preferred_element_type=jnp.float32
        )
        masked = jnp.where(allowed_rows, attention_logits, -jnp.inf)
        row_top = jnp.max(masked, axis=1, keepdims=True)
        exp_scores = jnp.exp(masked - row_top)
        attn_prob = exp_scores / jnp.sum(exp_scores, axis=1, keepdims=True)
        probability_halfwidth = attn_prob.astype(jnp.bfloat16)
        attn_head = jnp.dot(
            probability_halfwidth, value_head, preferred_element_type=jnp.float32
        ).astype(jnp.bfloat16)
        row_delta = jnp.sum(
            grad_head.astype(jnp.float32) * attn_head.astype(jnp.float32), axis=1, keepdims=True
        )
        probability_gradient = jnp.dot(grad_head, value_head.T, preferred_element_type=jnp.float32)
        score_gradient = (attn_prob * (probability_gradient - row_delta)).astype(jnp.bfloat16)
        qgrad_head = (
            logit_scale * jnp.dot(score_gradient, key_head, preferred_element_type=jnp.float32)
        ).astype(jnp.bfloat16)
        key_partial = logit_scale * jnp.dot(
            score_gradient.T, query_head, preferred_element_type=jnp.float32
        )
        value_partial = jnp.dot(
            probability_halfwidth.T, grad_head, preferred_element_type=jnp.float32
        )
        return (attn_head, qgrad_head, key_partial, value_partial)

    attn_all, qgrad_all, key_all, value_all = lax.map(
        per_head, (query_stack, key_stack, value_stack, grad_stack)
    )
    attention_output = (
        attn_all.reshape(kv_heads, QUERIES_PER_KEY, tok_rows, HEAD_SIZE)
        .transpose(2, 0, 1, 3)
        .reshape(tok_rows, kv_heads * QUERIES_PER_KEY * HEAD_SIZE)
    )
    query_gradient = (
        qgrad_all.reshape(kv_heads, QUERIES_PER_KEY, tok_rows, HEAD_SIZE)
        .transpose(2, 0, 1, 3)
        .reshape(tok_rows, kv_heads * QUERIES_PER_KEY * HEAD_SIZE)
    )
    key_terms = key_all.transpose(1, 0, 2).reshape(key_span, kv_heads * HEAD_SIZE)
    value_terms = value_all.transpose(1, 0, 2).reshape(key_span, kv_heads * HEAD_SIZE)

    def take_slot(terms, slot_index):
        return terms[slot_index * tok_rows : (slot_index + 1) * tok_rows]

    key_sum = take_slot(key_terms, reach_blocks)
    value_sum = take_slot(value_terms, reach_blocks)
    for distance in range(1, reach_blocks + 1):
        received = passed_along(
            (
                take_slot(key_terms, reach_blocks - distance),
                take_slot(value_terms, reach_blocks - distance),
            ),
            "seq",
            -distance,
        )
        key_sum = key_sum + received[0]
        value_sum = value_sum + received[1]
    grad_key = key_sum.astype(jnp.bfloat16)
    grad_value = value_sum.astype(jnp.bfloat16)
    input_terms = jnp.dot(query_gradient, query_weight.T, preferred_element_type=jnp.float32)
    input_terms = input_terms + jnp.dot(grad_key, key_matrix.T, preferred_element_type=jnp.float32)
    input_terms = input_terms + jnp.dot(
        grad_value, value_matrix.T, preferred_element_type=jnp.float32
    )
    grad_input = lax.psum_scatter(input_terms, "head", scatter_dimension=1, tiled=True).astype(
        jnp.bfloat16
    )
    value_cols = grad_value.shape[1]
    input_cols = normed_input.T
    cot_cols = out_cotangent.T
    gathered = lax.psum_scatter(
        jnp.concatenate(
            [
                jnp.dot(input_cols, grad_value, preferred_element_type=jnp.float32),
                jnp.dot(cot_cols, attention_output, preferred_element_type=jnp.float32),
            ],
            axis=1,
        ),
        "seq",
        scatter_dimension=0,
        tiled=True,
    )
    grad_wvalue = gathered[:, :value_cols]
    grad_woutput = gathered[:, value_cols:].T
    return (grad_input, grad_wvalue, grad_woutput)


def solution(mesh):
    placed = (
        P("seq", None),
        P("seq", "head"),
        P("seq", "head"),
        P("seq", "head"),
        P(None, "head"),
        P(None, "head"),
        P(None, "head"),
        P("head", None),
        P("seq", None),
    )
    return jax.shard_map(
        local,
        mesh=mesh,
        in_specs=placed,
        out_specs=(P("seq", "head"), P("seq", "head"), P("head", "seq")),
        check_vma=False,
    )
```

```python
import functools

import jax
import jax.numpy as jnp
from jax import lax
from jax.experimental import pallas as pl
from jax.experimental.pallas import tpu as pltpu
from jax.sharding import PartitionSpec as P

HEAD_SIZE = 128
WINDOW_LENGTH = 4096
QUERIES_PER_KEY = 2


logit_scale = 1.0 / 12.0
log2_scale = 1.4426950408889634 / 12.0
excluded = -1e30


def passed_along(value, axis, steps):
    count = lax.axis_size(axis)
    leading, last = (max(0, -steps), min(count, count - steps))
    return lax.ppermute(value, axis, [(source, source + steps) for source in range(leading, last)])


NT = (((1,), (1,)), ((), ()))


def dot_nt(left, right):
    return lax.dot_general(left, right, NT, preferred_element_type=jnp.float32)


def dot_nn(left, right):
    return jnp.dot(left, right, preferred_element_type=jnp.float32)


def at(place, size):
    return pl.ds(pl.multiple_of(place * size, size), size)


def out_grad_kernel(
    cot_hbm, weight_hbm, q_hbm, k_hbm, v_hbm, same_ref, other_ref, cot_ref, weight_ref, sem
):
    core = lax.axis_index("seq") % 2
    cut = weight_ref.shape[0] // 2
    cot_copy = pltpu.make_async_copy(cot_hbm, cot_ref, sem.at[0])
    cot_copy.start()
    halves = ((other_ref, 1 - core), (same_ref, core))
    weight_copies = []
    for place, (_, half) in enumerate(halves):
        weight_copies.append(
            pltpu.make_async_copy(
                weight_hbm.at[at(half, cut)], weight_ref.at[at(place, cut)], sem.at[1 + place]
            )
        )
        weight_copies[-1].start()
    plain_copies = []
    for place, (target, half) in enumerate(halves):
        first = 0
        for which, source in enumerate((q_hbm, k_hbm, v_hbm)):
            cols = source.shape[1] // 2
            plain_copies.append(
                pltpu.make_async_copy(
                    source.at[:, at(half, cols)],
                    target.at[:, pl.ds(first, cols)],
                    sem.at[3 + 3 * place + which],
                )
            )
            plain_copies[-1].start()
            first += cols
    cot_copy.wait()
    for place, (target, _) in enumerate(halves):
        weight_copies[place].wait()
        grads_t = dot_nt(weight_ref[place * cut : (place + 1) * cut], cot_ref[...])
        for h in range(cut // HEAD_SIZE):
            target[:, first + h * HEAD_SIZE : first + (h + 1) * HEAD_SIZE] = grads_t[
                h * HEAD_SIZE : (h + 1) * HEAD_SIZE
            ].astype(jnp.bfloat16)
    for copy in plain_copies:
        copy.wait()


def turn_kernel(parts, normed_hbm, cot_hbm, _, __, turned_ref, done_ref, normed_ref, cot_ref, sem):
    cut = normed_ref.shape[1] // parts
    done_ref[...] = jnp.zeros_like(done_ref)
    copies = []
    for which, (source, target) in enumerate(((normed_hbm, normed_ref), (cot_hbm, cot_ref))):
        copies.append(pltpu.make_async_copy(source, target, sem.at[which]))
        copies[-1].start()
    for which, ref in enumerate((normed_ref, cot_ref)):
        copies[which].wait()
        turned = ref[...].astype(jnp.float32).T.astype(jnp.bfloat16)
        for part in range(parts):
            turned_ref[part, which] = turned[part * cut : (part + 1) * cut]


def attention_kernel(blocks, *refs):
    attention_body(refs[:blocks], *refs[blocks + 1 :])


def attention_body(
    block_refs,
    dx_own_ref,
    dx_far_ref,
    attn_ref,
    dv_ref,
    gathered_ref,
    score_even_ref,
    score_odd_ref,
    prob_ref,
    grad_t_ref,
    delta_ref,
    query_ref,
    value_t_ref,
    key_t_ref,
    dq_t_ref,
    dk_ref,
    sem,
):
    me = lax.axis_index("seq")
    core, chip = me % 2, me // 2
    rows = dx_own_ref.shape[0]
    arrivals = []
    for apart, source in enumerate(block_refs):
        arrivals.append(
            pltpu.make_async_copy(source, gathered_ref.at[at(me ^ apart, rows)], sem.at[apart])
        )
        arrivals[-1].start()
    for copy in arrivals:
        copy.wait()
    tokens = gathered_ref.shape[0]
    size = 2 * rows
    steps = tokens // size
    wide = QUERIES_PER_KEY * size
    heads = QUERIES_PER_KEY
    key_cols = slice(heads * HEAD_SIZE, (heads + 1) * HEAD_SIZE)
    value_cols = slice((heads + 1) * HEAD_SIZE, (heads + 2) * HEAD_SIZE)
    grad_base = (heads + 2) * HEAD_SIZE
    value_t_ref[...] = gathered_ref[:, value_cols].T
    key_t_ref[...] = gathered_ref[:, key_cols].T
    key_place = lax.broadcasted_iota(jnp.int32, (size, wide), 0)
    query_place = lax.broadcasted_iota(jnp.int32, (size, wide), 1) % size
    allowed = key_place <= query_place

    for step in range(steps):
        span = (step + 1) * size
        own = slice(step * size, span)
        lanes = slice(step * wide, (step + 1) * wide)
        score_ref = score_odd_ref if step % 2 else score_even_ref
        queries = jnp.concatenate(
            [gathered_ref[own, h * HEAD_SIZE : (h + 1) * HEAD_SIZE] for h in range(heads)], axis=0
        )
        query_ref[lanes] = queries
        top = None
        for piece in range(step + 1):
            part = slice(piece * size, (piece + 1) * size)
            scores = dot_nt(gathered_ref[part, key_cols], queries)
            if piece == step:
                scores = jnp.where(allowed, scores, excluded)
            score_ref[part] = scores
            largest = jnp.max(scores.reshape(size // 8, 8, wide), axis=0)
            top = largest if top is None else jnp.maximum(top, largest)
        top = jnp.max(top, axis=0, keepdims=True)
        total = None
        for piece in range(step + 1):
            part = slice(piece * size, (piece + 1) * size)
            weights = jnp.exp2((score_ref[part] - top) * log2_scale)
            prob_ref[part, lanes] = weights.astype(jnp.bfloat16)
            summed = jnp.sum(weights.reshape(size // 8, 8, wide), axis=0)
            total = summed if total is None else total + summed
        inverse = 1.0 / jnp.sum(total, axis=0, keepdims=True)
        attn = dot_nn(value_t_ref[:, :span], prob_ref[:span, lanes]) * inverse
        for h in range(heads):
            attn_ref[h * HEAD_SIZE : (h + 1) * HEAD_SIZE, own] = attn[
                :, h * size : (h + 1) * size
            ].astype(jnp.bfloat16)
        grads_t = jnp.concatenate(
            [
                gathered_ref[
                    block * rows : (block + 1) * rows,
                    grad_base + h * HEAD_SIZE : grad_base + (h + 1) * HEAD_SIZE,
                ]
                for h in range(heads)
                for block in (2 * step, 2 * step + 1)
            ],
            axis=1,
        )
        grads_t = (grads_t.astype(jnp.float32) * inverse).astype(jnp.bfloat16)
        grad_t_ref[:, lanes] = grads_t
        delta_ref[:, lanes] = jnp.sum(grads_t.astype(jnp.float32) * attn, axis=0, keepdims=True)

    for step in range(steps):
        own = slice(step * size, (step + 1) * size)
        dv_ref[own] = dot_nt(prob_ref[own, step * wide :], grad_t_ref[:, step * wide :]).astype(
            jnp.bfloat16
        )

    dq_t_ref[...] = jnp.zeros_like(dq_t_ref)
    dk_ref[...] = jnp.zeros_like(dk_ref)
    for step in range(steps):
        key_step = jnp.minimum(chip, step)
        query_step = jnp.maximum(chip, step)
        dprob = dot_nn(
            gathered_ref[at(key_step, size), value_cols], grad_t_ref[:, at(query_step, wide)]
        )
        dscore = (
            prob_ref[at(key_step, size), at(query_step, wide)].astype(jnp.float32)
            * (dprob - delta_ref[:, at(query_step, wide)])
        ).astype(jnp.bfloat16)

        @pl.when(step <= chip)
        def _():
            dq_t_ref[...] += dot_nn(key_t_ref[:, at(key_step, size)], dscore)

        @pl.when(step >= chip)
        def _():
            dk_ref[...] += dot_nn(dscore, query_ref[at(query_step, wide)])

    for target, half in ((dx_far_ref, 1 - core), (dx_own_ref, core)):
        for h in range(heads):
            target[:, h * HEAD_SIZE : (h + 1) * HEAD_SIZE] = (
                (logit_scale * dq_t_ref[:, at(2 * h + half, rows)])
                .T.astype(jnp.bfloat16)
            )
        target[:, key_cols] = (logit_scale * dk_ref[at(half, rows)]).astype(jnp.bfloat16)
        target[:, value_cols] = dv_ref[at(2 * chip + half, rows)]


def input_terms_kernel(
    apart_groups, own_ref, far_ref, wq_ref, wk_ref, wv_ref, *refs
):
    terms, dx_ref = refs[:-1], refs[-1]
    core = lax.axis_index("seq") % 2
    group = lax.axis_index("head")
    q_cols = wq_ref.shape[1] // 2
    kv_cols = wk_ref.shape[1] // 2
    for source, half in ((own_ref, core), (far_ref, 1 - core)):
        dx_ref[:, at(half, q_cols)] = source[:, :q_cols]
        dx_ref[:, pl.ds(pl.multiple_of(2 * q_cols + half * kv_cols, kv_cols), kv_cols)] = source[
            :, q_cols : q_cols + kv_cols
        ]
        dx_ref[
            :, pl.ds(pl.multiple_of(2 * q_cols + (2 + half) * kv_cols, kv_cols), kv_cols)
        ] = source[:, q_cols + kv_cols :]
    for apart, target in zip(apart_groups, terms):
        cut = target.shape[0]
        place = at(group ^ apart, cut)
        target[...] = (
            dot_nt(wq_ref[place], dx_ref[:, : 2 * q_cols])
            + dot_nt(wk_ref[place], dx_ref[:, 2 * q_cols : 2 * q_cols + 2 * kv_cols])
            + dot_nt(wv_ref[place], dx_ref[:, 2 * q_cols + 2 * kv_cols :])
        ).astype(target.dtype)


def weight_grad_kernel(
    turned_ref, attn_ref, far_attn_ref, dv_ref, far_dv_ref, wvalue_ref, woutput_ref, done_ref, joined_ref
):
    done_ref[...] = jnp.zeros_like(done_ref)
    core = lax.axis_index("seq") % 2
    parts = turned_ref.shape[0]
    rows = turned_ref.shape[3]
    for part in range(parts):
        joined_ref[:, :, part * rows : (part + 1) * rows] = turned_ref[part]
    for half, attn, dv in ((core, attn_ref, dv_ref), (1 - core, far_attn_ref, far_dv_ref)):
        wvalue_ref[:, at(half, dv.shape[1])] = dot_nn(joined_ref[0], dv[...])
        woutput_ref[:, at(half, attn.shape[0])] = dot_nt(joined_ref[1], attn[...])


def sum_kernel(_, own_ref, *refs):
    total = own_ref[...]
    for arrived_ref in refs[:-1]:
        total = total + arrived_ref[...].astype(jnp.float32)
    refs[-1][...] = total.astype(jnp.bfloat16)


def kernel_call(body, outs, operands, in_vmem=(), scratch=(), flops=0, moved=0, room=32):
    vmem = pl.BlockSpec(memory_space=pltpu.VMEM)
    hbm = pl.BlockSpec(memory_space=pltpu.HBM)
    return pl.pallas_call(
        body,
        out_shape=outs,
        in_specs=[vmem if place in in_vmem else hbm for place in range(len(operands))],
        out_specs=jax.tree.map(lambda _: vmem, outs),
        scratch_shapes=list(scratch),
        compiler_params=pltpu.CompilerParams(vmem_limit_bytes=room * 1024 * 1024),
        cost_estimate=pl.CostEstimate(flops=flops, bytes_accessed=moved, transcendentals=0),
    )(*operands)


def swapped(value, axis, apart):
    count = lax.axis_size(axis)
    return lax.ppermute(value, axis, [(place, place ^ apart) for place in range(count)])


def gathered_plan(
    normed_input,
    stored_queries,
    stored_keys,
    stored_values,
    query_weight,
    key_matrix,
    value_matrix,
    output_weight,
    out_cotangent,
):
    bf16, f32 = jnp.bfloat16, jnp.float32
    rows, model = normed_input.shape
    blocks = lax.axis_size("seq")
    groups = lax.axis_size("head")
    tokens = rows * blocks
    q_cols = stored_queries.shape[1] // 2
    kv_cols = HEAD_SIZE
    wide = 2 * QUERIES_PER_KEY * rows
    packed_cols = 2 * q_cols + 2 * kv_cols
    shape = jax.ShapeDtypeStruct
    same, other = kernel_call(
        out_grad_kernel,
        (shape((rows, packed_cols), bf16),) * 2,
        (out_cotangent, output_weight, stored_queries, stored_keys, stored_values),
        scratch=(
            pltpu.VMEM(out_cotangent.shape, bf16),
            pltpu.VMEM(output_weight.shape, bf16),
            pltpu.SemaphoreType.DMA((9,)),
        ),
        flops=4 * rows * model * q_cols,
        moved=2 * model * (rows + 2 * q_cols),
        room=63,
    )
    held = {0: same}
    for apart in range(blocks - 1, 0, -1):
        held[apart] = swapped(other if apart % 2 else same, "seq", apart)
    turned, turn_done = kernel_call(
        functools.partial(turn_kernel, blocks),
        (shape((blocks, 2, model // blocks, rows), bf16), shape((8, HEAD_SIZE), f32)),
        (normed_input, out_cotangent, held[1], held[2]),
        scratch=(
            pltpu.VMEM(normed_input.shape, bf16),
            pltpu.VMEM(out_cotangent.shape, bf16),
            pltpu.SemaphoreType.DMA((2,)),
        ),
        moved=8 * rows * model,
    )
    turned = lax.all_to_all(turned, "seq", 0, 0)
    dx_own, dx_far, attn, dv = kernel_call(
        functools.partial(attention_kernel, blocks),
        (
            shape((rows, q_cols + 2 * kv_cols), bf16),
            shape((rows, q_cols + 2 * kv_cols), bf16),
            shape((q_cols, tokens), bf16),
            shape((tokens, kv_cols), bf16),
        ),
        [held[apart] for apart in range(blocks)] + [turn_done],
        scratch=(
            pltpu.VMEM((tokens, packed_cols), bf16),
            pltpu.VMEM((tokens, wide), f32),
            pltpu.VMEM((tokens, wide), f32),
            pltpu.VMEM((tokens, tokens * QUERIES_PER_KEY), bf16),
            pltpu.VMEM((HEAD_SIZE, tokens * QUERIES_PER_KEY), bf16),
            pltpu.VMEM((1, tokens * QUERIES_PER_KEY), f32),
            pltpu.VMEM((tokens * QUERIES_PER_KEY, HEAD_SIZE), bf16),
            pltpu.VMEM((HEAD_SIZE, tokens), bf16),
            pltpu.VMEM((HEAD_SIZE, tokens), bf16),
            pltpu.VMEM((HEAD_SIZE, wide), f32),
            pltpu.VMEM((2 * rows, HEAD_SIZE), f32),
            pltpu.SemaphoreType.DMA((blocks,)),
        ),
        flops=8 * tokens * tokens * q_cols,
        moved=2 * tokens * packed_cols,
    )
    dx_got = swapped(dx_far, "seq", 1)
    aparts = tuple(range(groups - 1, -1, -1))
    terms = kernel_call(
        functools.partial(input_terms_kernel, aparts),
        tuple(shape((model // groups, rows), bf16 if apart else f32) for apart in aparts),
        (dx_own, dx_got, query_weight, key_matrix, value_matrix),
        in_vmem=range(5),
        scratch=(pltpu.VMEM((rows, 2 * (q_cols + 2 * kv_cols)), bf16),),
        flops=4 * rows * model * (q_cols + 2 * kv_cols),
        moved=4 * model * (q_cols + 2 * kv_cols),
    )
    arrived = [swapped(term, "head", apart) for apart, term in zip(aparts[:-1], terms[:-1])]
    grad_wvalue, grad_woutput, weights_done = kernel_call(
        weight_grad_kernel,
        (
            shape((model // blocks, 2 * kv_cols), f32),
            shape((model // blocks, 2 * q_cols), f32),
            shape((8, HEAD_SIZE), f32),
        ),
        (turned, attn, swapped(attn, "seq", 1), dv, swapped(dv, "seq", 1)),
        in_vmem=range(5),
        scratch=(pltpu.VMEM((2, model // blocks, tokens), bf16),),
        flops=4 * tokens * (model // blocks) * (q_cols + kv_cols),
        moved=4 * (model // blocks) * (tokens + 2 * q_cols + 2 * kv_cols),
    )
    grad_input = kernel_call(
        sum_kernel,
        shape((model // groups, rows), bf16),
        (weights_done, terms[-1], *arrived),
        in_vmem=range(1, groups + 1),
        moved=4 * groups * (model // groups) * rows,
    )
    return (grad_input.T, grad_wvalue, grad_woutput.T)


def power_of_two(count):
    return count & (count - 1) == 0


def local(normed_input, stored_queries, stored_keys, *others):
    blocks, groups = lax.axis_size("seq"), lax.axis_size("head")
    whole_window = normed_input.shape[0] * blocks <= WINDOW_LENGTH
    two_heads = stored_keys.shape[1] == 2 * HEAD_SIZE
    paired = blocks > 1 and power_of_two(blocks) and power_of_two(groups)
    plan = gathered_plan if whole_window and two_heads and paired else windowed_plan
    return plan(normed_input, stored_queries, stored_keys, *others)


def windowed_plan(
    normed_input,
    stored_queries,
    stored_keys,
    stored_values,
    query_weight,
    key_matrix,
    value_matrix,
    output_weight,
    out_cotangent,
):
    tok_rows = normed_input.shape[0]
    blocks_seq = lax.axis_size("seq")
    seq_place = lax.axis_index("seq")
    reach_blocks = min(WINDOW_LENGTH // tok_rows, blocks_seq - 1)
    kv_heads = stored_keys.shape[1] // HEAD_SIZE
    output_gradient = jnp.dot(
        out_cotangent, output_weight.T, preferred_element_type=jnp.float32
    ).astype(jnp.bfloat16)
    pieces = [(stored_keys, stored_values)]
    current = (stored_keys, stored_values)
    for relay_step in range(reach_blocks):
        current = passed_along((current[0], current[1]), "seq", 1)
        pieces = [current] + pieces
    key_window = jnp.concatenate([piece[0] for piece in pieces], axis=0)
    value_window = jnp.concatenate([piece[1] for piece in pieces], axis=0)
    key_span = key_window.shape[0]
    query_pos = seq_place * tok_rows + jnp.arange(tok_rows, dtype=jnp.int32)
    key_pos = (seq_place - reach_blocks) * tok_rows + jnp.arange(key_span, dtype=jnp.int32)
    pos_gap = query_pos[:, None] - key_pos[None, :]
    allowed = (pos_gap >= 0) & (pos_gap < WINDOW_LENGTH) & (key_pos >= 0)[None, :]
    allowed_rows = jnp.tile(allowed, (QUERIES_PER_KEY, 1))
    query_stack = (
        stored_queries.reshape(tok_rows, kv_heads, QUERIES_PER_KEY, HEAD_SIZE)
        .transpose(1, 2, 0, 3)
        .reshape(kv_heads, QUERIES_PER_KEY * tok_rows, HEAD_SIZE)
    )
    grad_stack = (
        output_gradient.reshape(tok_rows, kv_heads, QUERIES_PER_KEY, HEAD_SIZE)
        .transpose(1, 2, 0, 3)
        .reshape(kv_heads, QUERIES_PER_KEY * tok_rows, HEAD_SIZE)
    )
    key_stack = key_window.reshape(key_span, kv_heads, HEAD_SIZE).transpose(1, 0, 2)
    value_stack = value_window.reshape(key_span, kv_heads, HEAD_SIZE).transpose(1, 0, 2)

    def per_head(head_items):
        query_head, key_head, value_head, grad_head = head_items
        attention_logits = logit_scale * jnp.dot(
            query_head, key_head.T, preferred_element_type=jnp.float32
        )
        masked = jnp.where(allowed_rows, attention_logits, -jnp.inf)
        row_top = jnp.max(masked, axis=1, keepdims=True)
        exp_scores = jnp.exp(masked - row_top)
        attn_prob = exp_scores / jnp.sum(exp_scores, axis=1, keepdims=True)
        probability_halfwidth = attn_prob.astype(jnp.bfloat16)
        attn_head = jnp.dot(
            probability_halfwidth, value_head, preferred_element_type=jnp.float32
        ).astype(jnp.bfloat16)
        row_delta = jnp.sum(
            grad_head.astype(jnp.float32) * attn_head.astype(jnp.float32), axis=1, keepdims=True
        )
        probability_gradient = jnp.dot(grad_head, value_head.T, preferred_element_type=jnp.float32)
        score_gradient = (attn_prob * (probability_gradient - row_delta)).astype(jnp.bfloat16)
        qgrad_head = (
            logit_scale * jnp.dot(score_gradient, key_head, preferred_element_type=jnp.float32)
        ).astype(jnp.bfloat16)
        key_partial = logit_scale * jnp.dot(
            score_gradient.T, query_head, preferred_element_type=jnp.float32
        )
        value_partial = jnp.dot(
            probability_halfwidth.T, grad_head, preferred_element_type=jnp.float32
        )
        return (attn_head, qgrad_head, key_partial, value_partial)

    attn_all, qgrad_all, key_all, value_all = lax.map(
        per_head, (query_stack, key_stack, value_stack, grad_stack)
    )
    attention_output = (
        attn_all.reshape(kv_heads, QUERIES_PER_KEY, tok_rows, HEAD_SIZE)
        .transpose(2, 0, 1, 3)
        .reshape(tok_rows, kv_heads * QUERIES_PER_KEY * HEAD_SIZE)
    )
    query_gradient = (
        qgrad_all.reshape(kv_heads, QUERIES_PER_KEY, tok_rows, HEAD_SIZE)
        .transpose(2, 0, 1, 3)
        .reshape(tok_rows, kv_heads * QUERIES_PER_KEY * HEAD_SIZE)
    )
    key_terms = key_all.transpose(1, 0, 2).reshape(key_span, kv_heads * HEAD_SIZE)
    value_terms = value_all.transpose(1, 0, 2).reshape(key_span, kv_heads * HEAD_SIZE)

    def take_slot(terms, slot_index):
        return terms[slot_index * tok_rows : (slot_index + 1) * tok_rows]

    key_sum = take_slot(key_terms, reach_blocks)
    value_sum = take_slot(value_terms, reach_blocks)
    for distance in range(1, reach_blocks + 1):
        received = passed_along(
            (
                take_slot(key_terms, reach_blocks - distance),
                take_slot(value_terms, reach_blocks - distance),
            ),
            "seq",
            -distance,
        )
        key_sum = key_sum + received[0]
        value_sum = value_sum + received[1]
    grad_key = key_sum.astype(jnp.bfloat16)
    grad_value = value_sum.astype(jnp.bfloat16)
    input_terms = jnp.dot(query_gradient, query_weight.T, preferred_element_type=jnp.float32)
    input_terms = input_terms + jnp.dot(grad_key, key_matrix.T, preferred_element_type=jnp.float32)
    input_terms = input_terms + jnp.dot(
        grad_value, value_matrix.T, preferred_element_type=jnp.float32
    )
    grad_input = lax.psum_scatter(input_terms, "head", scatter_dimension=1, tiled=True).astype(
        jnp.bfloat16
    )
    value_cols = grad_value.shape[1]
    input_cols = normed_input.T
    cot_cols = out_cotangent.T
    gathered = lax.psum_scatter(
        jnp.concatenate(
            [
                jnp.dot(input_cols, grad_value, preferred_element_type=jnp.float32),
                jnp.dot(cot_cols, attention_output, preferred_element_type=jnp.float32),
            ],
            axis=1,
        ),
        "seq",
        scatter_dimension=0,
        tiled=True,
    )
    grad_wvalue = gathered[:, :value_cols]
    grad_woutput = gathered[:, value_cols:].T
    return (grad_input, grad_wvalue, grad_woutput)


def solution(mesh):
    placed = (
        P("seq", None),
        P("seq", "head"),
        P("seq", "head"),
        P("seq", "head"),
        P(None, "head"),
        P(None, "head"),
        P(None, "head"),
        P("head", None),
        P("seq", None),
    )
    return jax.shard_map(
        local,
        mesh=mesh,
        in_specs=placed,
        out_specs=(P("seq", "head"), P("seq", "head"), P("head", "seq")),
        check_vma=False,
    )
```

```python
import functools

import jax
import jax.numpy as jnp
from jax import lax
from jax.experimental import pallas as pl
from jax.experimental.pallas import tpu as pltpu
from jax.sharding import PartitionSpec as P

HEAD_SIZE = 128
WINDOW_LENGTH = 4096
QUERIES_PER_KEY = 2


logit_scale = 1.0 / 12.0
log2_scale = 1.4426950408889634 / 12.0
excluded = -1e30


def passed_along(value, axis, steps):
    count = lax.axis_size(axis)
    leading, last = (max(0, -steps), min(count, count - steps))
    return lax.ppermute(value, axis, [(source, source + steps) for source in range(leading, last)])


NT = (((1,), (1,)), ((), ()))


def dot_nt(left, right):
    return lax.dot_general(left, right, NT, preferred_element_type=jnp.float32)


def dot_nn(left, right):
    return jnp.dot(left, right, preferred_element_type=jnp.float32)


def at(place, size):
    return pl.ds(pl.multiple_of(place * size, size), size)


def out_grad_kernel(
    cot_hbm, weight_hbm, q_hbm, k_hbm, v_hbm, sent_ref, done_ref, cot_ref, weight_ref, half_ref, sem
):
    done_ref[...] = jnp.zeros_like(done_ref)
    cut = weight_ref.shape[0] // 2
    cot_copy = pltpu.make_async_copy(cot_hbm, cot_ref, sem.at[0])
    cot_copy.start()
    weight_copies = []
    for half in range(2):
        part = pl.ds(half * cut, cut)
        weight_copies.append(
            pltpu.make_async_copy(weight_hbm.at[part], weight_ref.at[part], sem.at[1 + half])
        )
        weight_copies[-1].start()
    plain_copies = []
    for half in range(2):
        first = 0
        for which, source in enumerate((q_hbm, k_hbm, v_hbm)):
            cols = source.shape[1] // 2
            plain_copies.append(
                pltpu.make_async_copy(
                    source.at[:, pl.ds(half * cols, cols)],
                    half_ref.at[half, :, pl.ds(first, cols)],
                    sem.at[3 + 3 * half + which],
                )
            )
            plain_copies[-1].start()
            first += cols
    cot_copy.wait()
    for half in range(2):
        weight_copies[half].wait()
        grads_t = dot_nt(weight_ref[half * cut : (half + 1) * cut], cot_ref[...])
        for h in range(cut // HEAD_SIZE):
            half_ref[half, :, first + h * HEAD_SIZE : first + (h + 1) * HEAD_SIZE] = grads_t[
                h * HEAD_SIZE : (h + 1) * HEAD_SIZE
            ].astype(jnp.bfloat16)
    for copy in plain_copies:
        copy.wait()
    for target in range(sent_ref.shape[0]):
        sent_ref[target] = half_ref[target % 2]


def turn_kernel(parts, normed_hbm, cot_hbm, _, turned_ref, done_ref, normed_ref, cot_ref, sem):
    cut = normed_ref.shape[1] // parts
    done_ref[...] = jnp.zeros_like(done_ref)
    copies = []
    for which, (source, target) in enumerate(((normed_hbm, normed_ref), (cot_hbm, cot_ref))):
        copies.append(pltpu.make_async_copy(source, target, sem.at[which]))
        copies[-1].start()
    for which, ref in enumerate((normed_ref, cot_ref)):
        copies[which].wait()
        turned = ref[...].astype(jnp.float32).T.astype(jnp.bfloat16)
        for part in range(parts):
            turned_ref[part, which] = turned[part * cut : (part + 1) * cut]


def attention_kernel(
    gathered_ref,
    _,
    dx_own_ref,
    dx_far_ref,
    attn_ref,
    dv_ref,
    score_even_ref,
    score_odd_ref,
    prob_ref,
    grad_t_ref,
    delta_ref,
    query_ref,
    value_t_ref,
    key_t_ref,
    dq_t_ref,
    dk_ref,
):
    me = lax.axis_index("seq")
    core, chip = me % 2, me // 2
    rows = dx_own_ref.shape[0]
    tokens = gathered_ref.shape[0]
    size = 2 * rows
    steps = tokens // size
    wide = QUERIES_PER_KEY * size
    heads = QUERIES_PER_KEY
    key_cols = slice(heads * HEAD_SIZE, (heads + 1) * HEAD_SIZE)
    value_cols = slice((heads + 1) * HEAD_SIZE, (heads + 2) * HEAD_SIZE)
    grad_base = (heads + 2) * HEAD_SIZE
    value_t_ref[...] = gathered_ref[:, value_cols].T
    key_t_ref[...] = gathered_ref[:, key_cols].T
    key_place = lax.broadcasted_iota(jnp.int32, (size, wide), 0)
    query_place = lax.broadcasted_iota(jnp.int32, (size, wide), 1) % size
    allowed = key_place <= query_place

    for step in range(steps):
        span = (step + 1) * size
        own = slice(step * size, span)
        lanes = slice(step * wide, (step + 1) * wide)
        score_ref = score_odd_ref if step % 2 else score_even_ref
        queries = jnp.concatenate(
            [gathered_ref[own, h * HEAD_SIZE : (h + 1) * HEAD_SIZE] for h in range(heads)], axis=0
        )
        query_ref[lanes] = queries
        top = None
        for piece in range(step + 1):
            part = slice(piece * size, (piece + 1) * size)
            scores = dot_nt(gathered_ref[part, key_cols], queries)
            if piece == step:
                scores = jnp.where(allowed, scores, excluded)
            score_ref[part] = scores
            largest = jnp.max(scores.reshape(size // 8, 8, wide), axis=0)
            top = largest if top is None else jnp.maximum(top, largest)
        top = jnp.max(top, axis=0, keepdims=True)
        total = None
        for piece in range(step + 1):
            part = slice(piece * size, (piece + 1) * size)
            weights = jnp.exp2((score_ref[part] - top) * log2_scale)
            prob_ref[part, lanes] = weights.astype(jnp.bfloat16)
            summed = jnp.sum(weights.reshape(size // 8, 8, wide), axis=0)
            total = summed if total is None else total + summed
        inverse = 1.0 / jnp.sum(total, axis=0, keepdims=True)
        attn = dot_nn(value_t_ref[:, :span], prob_ref[:span, lanes]) * inverse
        for h in range(heads):
            attn_ref[h * HEAD_SIZE : (h + 1) * HEAD_SIZE, own] = attn[
                :, h * size : (h + 1) * size
            ].astype(jnp.bfloat16)
        grads_t = jnp.concatenate(
            [
                gathered_ref[
                    block * rows : (block + 1) * rows,
                    grad_base + h * HEAD_SIZE : grad_base + (h + 1) * HEAD_SIZE,
                ]
                for h in range(heads)
                for block in (2 * step, 2 * step + 1)
            ],
            axis=1,
        )
        grads_t = (grads_t.astype(jnp.float32) * inverse).astype(jnp.bfloat16)
        grad_t_ref[:, lanes] = grads_t
        delta_ref[:, lanes] = jnp.sum(grads_t.astype(jnp.float32) * attn, axis=0, keepdims=True)

    for step in range(steps):
        own = slice(step * size, (step + 1) * size)
        dv_ref[own] = dot_nt(prob_ref[own, step * wide :], grad_t_ref[:, step * wide :]).astype(
            jnp.bfloat16
        )

    dq_t_ref[...] = jnp.zeros_like(dq_t_ref)
    dk_ref[...] = jnp.zeros_like(dk_ref)
    for step in range(steps):
        key_step = jnp.minimum(chip, step)
        query_step = jnp.maximum(chip, step)
        dprob = dot_nn(
            gathered_ref[at(key_step, size), value_cols], grad_t_ref[:, at(query_step, wide)]
        )
        dscore = (
            prob_ref[at(key_step, size), at(query_step, wide)].astype(jnp.float32)
            * (dprob - delta_ref[:, at(query_step, wide)])
        ).astype(jnp.bfloat16)

        @pl.when(step <= chip)
        def _():
            dq_t_ref[...] += dot_nn(key_t_ref[:, at(key_step, size)], dscore)

        @pl.when(step >= chip)
        def _():
            dk_ref[...] += dot_nn(dscore, query_ref[at(query_step, wide)])

    for target, half in ((dx_far_ref, 1 - core), (dx_own_ref, core)):
        for h in range(heads):
            target[:, h * HEAD_SIZE : (h + 1) * HEAD_SIZE] = (
                (logit_scale * dq_t_ref[:, at(2 * h + half, rows)])
                .T.astype(jnp.bfloat16)
            )
        target[:, key_cols] = (logit_scale * dk_ref[at(half, rows)]).astype(jnp.bfloat16)
        target[:, value_cols] = dv_ref[at(2 * chip + half, rows)]


def input_terms_kernel(
    apart_groups, own_ref, far_ref, wq_ref, wk_ref, wv_ref, *refs
):
    terms, dx_ref = refs[:-1], refs[-1]
    core = lax.axis_index("seq") % 2
    group = lax.axis_index("head")
    q_cols = wq_ref.shape[1] // 2
    kv_cols = wk_ref.shape[1] // 2
    for source, half in ((own_ref, core), (far_ref, 1 - core)):
        dx_ref[:, at(half, q_cols)] = source[:, :q_cols]
        dx_ref[:, pl.ds(pl.multiple_of(2 * q_cols + half * kv_cols, kv_cols), kv_cols)] = source[
            :, q_cols : q_cols + kv_cols
        ]
        dx_ref[
            :, pl.ds(pl.multiple_of(2 * q_cols + (2 + half) * kv_cols, kv_cols), kv_cols)
        ] = source[:, q_cols + kv_cols :]
    for apart, target in zip(apart_groups, terms):
        cut = target.shape[0]
        place = at(group ^ apart, cut)
        target[...] = (
            dot_nt(wq_ref[place], dx_ref[:, : 2 * q_cols])
            + dot_nt(wk_ref[place], dx_ref[:, 2 * q_cols : 2 * q_cols + 2 * kv_cols])
            + dot_nt(wv_ref[place], dx_ref[:, 2 * q_cols + 2 * kv_cols :])
        ).astype(target.dtype)


def weight_grad_kernel(
    turned_ref, attn_ref, far_attn_ref, dv_ref, far_dv_ref, wvalue_ref, woutput_ref, done_ref, joined_ref
):
    done_ref[...] = jnp.zeros_like(done_ref)
    core = lax.axis_index("seq") % 2
    parts = turned_ref.shape[0]
    rows = turned_ref.shape[3]
    for part in range(parts):
        joined_ref[:, :, part * rows : (part + 1) * rows] = turned_ref[part]
    for half, attn, dv in ((core, attn_ref, dv_ref), (1 - core, far_attn_ref, far_dv_ref)):
        wvalue_ref[:, at(half, dv.shape[1])] = dot_nn(joined_ref[0], dv[...])
        woutput_ref[:, at(half, attn.shape[0])] = dot_nt(joined_ref[1], attn[...])


def sum_kernel(_, own_ref, *refs):
    total = own_ref[...]
    for arrived_ref in refs[:-1]:
        total = total + arrived_ref[...].astype(jnp.float32)
    refs[-1][...] = total.astype(jnp.bfloat16)


def kernel_call(body, outs, operands, in_vmem=(), scratch=(), flops=0, moved=0, room=32):
    vmem = pl.BlockSpec(memory_space=pltpu.VMEM)
    hbm = pl.BlockSpec(memory_space=pltpu.HBM)
    return pl.pallas_call(
        body,
        out_shape=outs,
        in_specs=[vmem if place in in_vmem else hbm for place in range(len(operands))],
        out_specs=jax.tree.map(lambda _: vmem, outs),
        scratch_shapes=list(scratch),
        compiler_params=pltpu.CompilerParams(vmem_limit_bytes=room * 1024 * 1024),
        cost_estimate=pl.CostEstimate(flops=flops, bytes_accessed=moved, transcendentals=0),
    )(*operands)


def swapped(value, axis, apart):
    count = lax.axis_size(axis)
    return lax.ppermute(value, axis, [(place, place ^ apart) for place in range(count)])


def gathered_plan(
    normed_input,
    stored_queries,
    stored_keys,
    stored_values,
    query_weight,
    key_matrix,
    value_matrix,
    output_weight,
    out_cotangent,
):
    bf16, f32 = jnp.bfloat16, jnp.float32
    rows, model = normed_input.shape
    blocks = lax.axis_size("seq")
    groups = lax.axis_size("head")
    tokens = rows * blocks
    q_cols = stored_queries.shape[1] // 2
    kv_cols = HEAD_SIZE
    wide = 2 * QUERIES_PER_KEY * rows
    packed_cols = 2 * q_cols + 2 * kv_cols
    shape = jax.ShapeDtypeStruct
    sent, sent_done = kernel_call(
        out_grad_kernel,
        (shape((blocks, rows, packed_cols), bf16), shape((8, HEAD_SIZE), f32)),
        (out_cotangent, output_weight, stored_queries, stored_keys, stored_values),
        scratch=(
            pltpu.VMEM(out_cotangent.shape, bf16),
            pltpu.VMEM(output_weight.shape, bf16),
            pltpu.VMEM((2, rows, packed_cols), bf16),
            pltpu.SemaphoreType.DMA((9,)),
        ),
        flops=4 * rows * model * q_cols,
        moved=2 * model * (rows + 2 * q_cols),
        room=63,
    )
    gathered = lax.all_to_all(sent, "seq", 0, 0).reshape(tokens, packed_cols)
    turned, turn_done = kernel_call(
        functools.partial(turn_kernel, blocks),
        (shape((blocks, 2, model // blocks, rows), bf16), shape((8, HEAD_SIZE), f32)),
        (normed_input, out_cotangent, sent_done),
        scratch=(
            pltpu.VMEM(normed_input.shape, bf16),
            pltpu.VMEM(out_cotangent.shape, bf16),
            pltpu.SemaphoreType.DMA((2,)),
        ),
        moved=8 * rows * model,
    )
    turned = lax.all_to_all(turned, "seq", 0, 0)
    dx_own, dx_far, attn, dv = kernel_call(
        attention_kernel,
        (
            shape((rows, q_cols + 2 * kv_cols), bf16),
            shape((rows, q_cols + 2 * kv_cols), bf16),
            shape((q_cols, tokens), bf16),
            shape((tokens, kv_cols), bf16),
        ),
        (gathered, turn_done),
        in_vmem=(0,),
        scratch=(
            pltpu.VMEM((tokens, wide), f32),
            pltpu.VMEM((tokens, wide), f32),
            pltpu.VMEM((tokens, tokens * QUERIES_PER_KEY), bf16),
            pltpu.VMEM((HEAD_SIZE, tokens * QUERIES_PER_KEY), bf16),
            pltpu.VMEM((1, tokens * QUERIES_PER_KEY), f32),
            pltpu.VMEM((tokens * QUERIES_PER_KEY, HEAD_SIZE), bf16),
            pltpu.VMEM((HEAD_SIZE, tokens), bf16),
            pltpu.VMEM((HEAD_SIZE, tokens), bf16),
            pltpu.VMEM((HEAD_SIZE, wide), f32),
            pltpu.VMEM((2 * rows, HEAD_SIZE), f32),
        ),
        flops=8 * tokens * tokens * q_cols,
        moved=2 * tokens * packed_cols,
    )
    dx_got = swapped(dx_far, "seq", 1)
    aparts = tuple(range(groups - 1, -1, -1))
    terms = kernel_call(
        functools.partial(input_terms_kernel, aparts),
        tuple(shape((model // groups, rows), bf16 if apart else f32) for apart in aparts),
        (dx_own, dx_got, query_weight, key_matrix, value_matrix),
        in_vmem=range(5),
        scratch=(pltpu.VMEM((rows, 2 * (q_cols + 2 * kv_cols)), bf16),),
        flops=4 * rows * model * (q_cols + 2 * kv_cols),
        moved=4 * model * (q_cols + 2 * kv_cols),
    )
    arrived = [swapped(term, "head", apart) for apart, term in zip(aparts[:-1], terms[:-1])]
    grad_wvalue, grad_woutput, weights_done = kernel_call(
        weight_grad_kernel,
        (
            shape((model // blocks, 2 * kv_cols), f32),
            shape((model // blocks, 2 * q_cols), f32),
            shape((8, HEAD_SIZE), f32),
        ),
        (turned, attn, swapped(attn, "seq", 1), dv, swapped(dv, "seq", 1)),
        in_vmem=range(5),
        scratch=(pltpu.VMEM((2, model // blocks, tokens), bf16),),
        flops=4 * tokens * (model // blocks) * (q_cols + kv_cols),
        moved=4 * (model // blocks) * (tokens + 2 * q_cols + 2 * kv_cols),
    )
    grad_input = kernel_call(
        sum_kernel,
        shape((model // groups, rows), bf16),
        (weights_done, terms[-1], *arrived),
        in_vmem=range(1, groups + 1),
        moved=4 * groups * (model // groups) * rows,
    )
    return (grad_input.T, grad_wvalue, grad_woutput.T)


def power_of_two(count):
    return count & (count - 1) == 0


def local(normed_input, stored_queries, stored_keys, *others):
    blocks, groups = lax.axis_size("seq"), lax.axis_size("head")
    whole_window = normed_input.shape[0] * blocks <= WINDOW_LENGTH
    two_heads = stored_keys.shape[1] == 2 * HEAD_SIZE
    paired = blocks > 1 and power_of_two(blocks) and power_of_two(groups)
    plan = gathered_plan if whole_window and two_heads and paired else windowed_plan
    return plan(normed_input, stored_queries, stored_keys, *others)


def windowed_plan(
    normed_input,
    stored_queries,
    stored_keys,
    stored_values,
    query_weight,
    key_matrix,
    value_matrix,
    output_weight,
    out_cotangent,
):
    tok_rows = normed_input.shape[0]
    blocks_seq = lax.axis_size("seq")
    seq_place = lax.axis_index("seq")
    reach_blocks = min(WINDOW_LENGTH // tok_rows, blocks_seq - 1)
    kv_heads = stored_keys.shape[1] // HEAD_SIZE
    output_gradient = jnp.dot(
        out_cotangent, output_weight.T, preferred_element_type=jnp.float32
    ).astype(jnp.bfloat16)
    pieces = [(stored_keys, stored_values)]
    current = (stored_keys, stored_values)
    for relay_step in range(reach_blocks):
        current = passed_along((current[0], current[1]), "seq", 1)
        pieces = [current] + pieces
    key_window = jnp.concatenate([piece[0] for piece in pieces], axis=0)
    value_window = jnp.concatenate([piece[1] for piece in pieces], axis=0)
    key_span = key_window.shape[0]
    query_pos = seq_place * tok_rows + jnp.arange(tok_rows, dtype=jnp.int32)
    key_pos = (seq_place - reach_blocks) * tok_rows + jnp.arange(key_span, dtype=jnp.int32)
    pos_gap = query_pos[:, None] - key_pos[None, :]
    allowed = (pos_gap >= 0) & (pos_gap < WINDOW_LENGTH) & (key_pos >= 0)[None, :]
    allowed_rows = jnp.tile(allowed, (QUERIES_PER_KEY, 1))
    query_stack = (
        stored_queries.reshape(tok_rows, kv_heads, QUERIES_PER_KEY, HEAD_SIZE)
        .transpose(1, 2, 0, 3)
        .reshape(kv_heads, QUERIES_PER_KEY * tok_rows, HEAD_SIZE)
    )
    grad_stack = (
        output_gradient.reshape(tok_rows, kv_heads, QUERIES_PER_KEY, HEAD_SIZE)
        .transpose(1, 2, 0, 3)
        .reshape(kv_heads, QUERIES_PER_KEY * tok_rows, HEAD_SIZE)
    )
    key_stack = key_window.reshape(key_span, kv_heads, HEAD_SIZE).transpose(1, 0, 2)
    value_stack = value_window.reshape(key_span, kv_heads, HEAD_SIZE).transpose(1, 0, 2)

    def per_head(head_items):
        query_head, key_head, value_head, grad_head = head_items
        attention_logits = logit_scale * jnp.dot(
            query_head, key_head.T, preferred_element_type=jnp.float32
        )
        masked = jnp.where(allowed_rows, attention_logits, -jnp.inf)
        row_top = jnp.max(masked, axis=1, keepdims=True)
        exp_scores = jnp.exp(masked - row_top)
        attn_prob = exp_scores / jnp.sum(exp_scores, axis=1, keepdims=True)
        probability_halfwidth = attn_prob.astype(jnp.bfloat16)
        attn_head = jnp.dot(
            probability_halfwidth, value_head, preferred_element_type=jnp.float32
        ).astype(jnp.bfloat16)
        row_delta = jnp.sum(
            grad_head.astype(jnp.float32) * attn_head.astype(jnp.float32), axis=1, keepdims=True
        )
        probability_gradient = jnp.dot(grad_head, value_head.T, preferred_element_type=jnp.float32)
        score_gradient = (attn_prob * (probability_gradient - row_delta)).astype(jnp.bfloat16)
        qgrad_head = (
            logit_scale * jnp.dot(score_gradient, key_head, preferred_element_type=jnp.float32)
        ).astype(jnp.bfloat16)
        key_partial = logit_scale * jnp.dot(
            score_gradient.T, query_head, preferred_element_type=jnp.float32
        )
        value_partial = jnp.dot(
            probability_halfwidth.T, grad_head, preferred_element_type=jnp.float32
        )
        return (attn_head, qgrad_head, key_partial, value_partial)

    attn_all, qgrad_all, key_all, value_all = lax.map(
        per_head, (query_stack, key_stack, value_stack, grad_stack)
    )
    attention_output = (
        attn_all.reshape(kv_heads, QUERIES_PER_KEY, tok_rows, HEAD_SIZE)
        .transpose(2, 0, 1, 3)
        .reshape(tok_rows, kv_heads * QUERIES_PER_KEY * HEAD_SIZE)
    )
    query_gradient = (
        qgrad_all.reshape(kv_heads, QUERIES_PER_KEY, tok_rows, HEAD_SIZE)
        .transpose(2, 0, 1, 3)
        .reshape(tok_rows, kv_heads * QUERIES_PER_KEY * HEAD_SIZE)
    )
    key_terms = key_all.transpose(1, 0, 2).reshape(key_span, kv_heads * HEAD_SIZE)
    value_terms = value_all.transpose(1, 0, 2).reshape(key_span, kv_heads * HEAD_SIZE)

    def take_slot(terms, slot_index):
        return terms[slot_index * tok_rows : (slot_index + 1) * tok_rows]

    key_sum = take_slot(key_terms, reach_blocks)
    value_sum = take_slot(value_terms, reach_blocks)
    for distance in range(1, reach_blocks + 1):
        received = passed_along(
            (
                take_slot(key_terms, reach_blocks - distance),
                take_slot(value_terms, reach_blocks - distance),
            ),
            "seq",
            -distance,
        )
        key_sum = key_sum + received[0]
        value_sum = value_sum + received[1]
    grad_key = key_sum.astype(jnp.bfloat16)
    grad_value = value_sum.astype(jnp.bfloat16)
    input_terms = jnp.dot(query_gradient, query_weight.T, preferred_element_type=jnp.float32)
    input_terms = input_terms + jnp.dot(grad_key, key_matrix.T, preferred_element_type=jnp.float32)
    input_terms = input_terms + jnp.dot(
        grad_value, value_matrix.T, preferred_element_type=jnp.float32
    )
    grad_input = lax.psum_scatter(input_terms, "head", scatter_dimension=1, tiled=True).astype(
        jnp.bfloat16
    )
    value_cols = grad_value.shape[1]
    input_cols = normed_input.T
    cot_cols = out_cotangent.T
    gathered = lax.psum_scatter(
        jnp.concatenate(
            [
                jnp.dot(input_cols, grad_value, preferred_element_type=jnp.float32),
                jnp.dot(cot_cols, attention_output, preferred_element_type=jnp.float32),
            ],
            axis=1,
        ),
        "seq",
        scatter_dimension=0,
        tiled=True,
    )
    grad_wvalue = gathered[:, :value_cols]
    grad_woutput = gathered[:, value_cols:].T
    return (grad_input, grad_wvalue, grad_woutput)


def solution(mesh):
    placed = (
        P("seq", None),
        P("seq", "head"),
        P("seq", "head"),
        P("seq", "head"),
        P(None, "head"),
        P(None, "head"),
        P(None, "head"),
        P("head", None),
        P("seq", None),
    )
    return jax.shard_map(
        local,
        mesh=mesh,
        in_specs=placed,
        out_specs=(P("seq", "head"), P("seq", "head"), P("head", "seq")),
        check_vma=False,
    )
```

```python
import functools

import jax
import jax.numpy as jnp
from jax import lax
from jax.experimental import pallas as pl
from jax.experimental.pallas import tpu as pltpu
from jax.sharding import PartitionSpec as P

HEAD_SIZE = 128
WINDOW_LENGTH = 4096
QUERIES_PER_KEY = 2


logit_scale = 1.0 / 12.0
log2_scale = 1.4426950408889634 / 12.0
excluded = -1e30


def passed_along(value, axis, steps):
    count = lax.axis_size(axis)
    leading, last = (max(0, -steps), min(count, count - steps))
    return lax.ppermute(value, axis, [(source, source + steps) for source in range(leading, last)])


NT = (((1,), (1,)), ((), ()))


def dot_nt(left, right):
    return lax.dot_general(left, right, NT, preferred_element_type=jnp.float32)


def dot_nn(left, right):
    return jnp.dot(left, right, preferred_element_type=jnp.float32)


def at(place, size):
    return pl.ds(pl.multiple_of(place * size, size), size)


def pack_kernel(q_hbm, k_hbm, v_hbm, sent_hbm, done_ref, sem):
    done_ref[...] = jnp.zeros_like(done_ref)
    copies = []
    for target in range(sent_hbm.shape[0]):
        first = 0
        for which, source in enumerate((q_hbm, k_hbm, v_hbm)):
            cols = source.shape[1] // 2
            copies.append(
                pltpu.make_async_copy(
                    source.at[:, pl.ds(target % 2 * cols, cols)],
                    sent_hbm.at[target, :, pl.ds(first, cols)],
                    sem.at[3 * target + which],
                )
            )
            copies[-1].start()
            first += cols
    for copy in copies:
        copy.wait()


def out_grad_kernel(
    cot_hbm, weight_hbm, _, same_ref, other_ref, cot_ref, weight_ref, sem
):
    core = lax.axis_index("seq") % 2
    cut = weight_ref.shape[0] // 2
    cot_copy = pltpu.make_async_copy(cot_hbm, cot_ref, sem.at[0])
    cot_copy.start()
    halves = ((other_ref, 1 - core), (same_ref, core))
    weight_copies = []
    for place, (_, half) in enumerate(halves):
        weight_copies.append(
            pltpu.make_async_copy(
                weight_hbm.at[at(half, cut)], weight_ref.at[at(place, cut)], sem.at[1 + place]
            )
        )
        weight_copies[-1].start()
    cot_copy.wait()
    for place, (target, _) in enumerate(halves):
        weight_copies[place].wait()
        target[...] = dot_nt(
            weight_ref[place * cut : (place + 1) * cut], cot_ref[...]
        ).astype(jnp.bfloat16)


def turn_kernel(parts, normed_hbm, cot_hbm, _, turned_ref, done_ref, normed_ref, cot_ref, sem):
    cut = normed_ref.shape[1] // parts
    done_ref[...] = jnp.zeros_like(done_ref)
    copies = []
    for which, (source, target) in enumerate(((normed_hbm, normed_ref), (cot_hbm, cot_ref))):
        copies.append(pltpu.make_async_copy(source, target, sem.at[which]))
        copies[-1].start()
    for which, ref in enumerate((normed_ref, cot_ref)):
        copies[which].wait()
        turned = ref[...].astype(jnp.float32).T.astype(jnp.bfloat16)
        for part in range(parts):
            turned_ref[part, which] = turned[part * cut : (part + 1) * cut]


def probability_kernel(
    gathered_ref, prob_ref, inverse_ref, attn_ref, done_ref, score_even_ref, score_odd_ref, value_t_ref
):
    done_ref[...] = jnp.zeros_like(done_ref)
    tokens = gathered_ref.shape[0]
    heads = QUERIES_PER_KEY
    wide = score_even_ref.shape[1]
    size = wide // heads
    key_cols = slice(heads * HEAD_SIZE, (heads + 1) * HEAD_SIZE)
    value_cols = slice((heads + 1) * HEAD_SIZE, (heads + 2) * HEAD_SIZE)
    value_t_ref[...] = gathered_ref[:, value_cols].T
    key_place = lax.broadcasted_iota(jnp.int32, (size, wide), 0)
    query_place = lax.broadcasted_iota(jnp.int32, (size, wide), 1) % size
    allowed = key_place <= query_place
    for step in range(tokens // size):
        span = (step + 1) * size
        own = slice(step * size, span)
        lanes = slice(step * wide, (step + 1) * wide)
        score_ref = score_odd_ref if step % 2 else score_even_ref
        queries = jnp.concatenate(
            [gathered_ref[own, h * HEAD_SIZE : (h + 1) * HEAD_SIZE] for h in range(heads)], axis=0
        )
        top = None
        for piece in range(step + 1):
            part = slice(piece * size, (piece + 1) * size)
            scores = dot_nt(gathered_ref[part, key_cols], queries)
            if piece == step:
                scores = jnp.where(allowed, scores, excluded)
            score_ref[part] = scores
            largest = jnp.max(scores.reshape(size // 8, 8, wide), axis=0)
            top = largest if top is None else jnp.maximum(top, largest)
        top = jnp.max(top, axis=0, keepdims=True)
        total = None
        for piece in range(step + 1):
            part = slice(piece * size, (piece + 1) * size)
            weights = jnp.exp2((score_ref[part] - top) * log2_scale)
            prob_ref[part, lanes] = weights.astype(jnp.bfloat16)
            summed = jnp.sum(weights.reshape(size // 8, 8, wide), axis=0)
            total = summed if total is None else total + summed
        inverse = 1.0 / jnp.sum(total, axis=0, keepdims=True)
        inverse_ref[:, lanes] = inverse
        attn = dot_nn(value_t_ref[:, :span], prob_ref[:span, lanes]) * inverse
        for h in range(heads):
            attn_ref[h * HEAD_SIZE : (h + 1) * HEAD_SIZE, own] = attn[
                :, h * size : (h + 1) * size
            ].astype(jnp.bfloat16)


def gradient_kernel(
    gathered_ref,
    prob_ref,
    inverse_ref,
    attn_ref,
    _,
    *refs,
):
    blocks = len(refs) - 9
    og_refs = refs[:blocks]
    (
        dx_own_ref,
        dx_far_ref,
        grad_t_ref,
        og_ref,
        delta_ref,
        dq_t_ref,
        dk_ref,
        dv_ref,
        sem,
    ) = refs[blocks:]
    me = lax.axis_index("seq")
    core, chip = me % 2, me // 2
    rows = dx_own_ref.shape[0]
    arrivals = []
    for apart, source in enumerate(og_refs):
        arrivals.append(pltpu.make_async_copy(source, og_ref.at[me ^ apart], sem.at[apart]))
        arrivals[-1].start()
    dq_t_ref[...] = jnp.zeros_like(dq_t_ref)
    dk_ref[...] = jnp.zeros_like(dk_ref)
    dv_ref[...] = jnp.zeros_like(dv_ref)
    for copy in arrivals:
        copy.wait()
    tokens = gathered_ref.shape[0]
    heads = QUERIES_PER_KEY
    size = 2 * rows
    wide = heads * size
    steps = tokens // size
    key_cols = slice(heads * HEAD_SIZE, (heads + 1) * HEAD_SIZE)
    value_cols = slice((heads + 1) * HEAD_SIZE, (heads + 2) * HEAD_SIZE)
    for step in range(steps):
        lanes = slice(step * wide, (step + 1) * wide)
        grads_t = jnp.concatenate(
            [
                og_ref[block, h * HEAD_SIZE : (h + 1) * HEAD_SIZE]
                for h in range(heads)
                for block in (2 * step, 2 * step + 1)
            ],
            axis=1,
        )
        grads_t = (grads_t.astype(jnp.float32) * inverse_ref[:, lanes]).astype(jnp.bfloat16)
        grad_t_ref[:, lanes] = grads_t
        attn = jnp.concatenate(
            [
                attn_ref[h * HEAD_SIZE : (h + 1) * HEAD_SIZE, step * size : (step + 1) * size]
                for h in range(heads)
            ],
            axis=1,
        )
        delta_ref[:, lanes] = jnp.sum(
            grads_t.astype(jnp.float32) * attn.astype(jnp.float32), axis=0, keepdims=True
        )
    for step in range(steps):
        key_rows = at(jnp.minimum(chip, step), size)
        query_step = jnp.maximum(chip, step)
        lanes = at(query_step, wide)
        prob = prob_ref[key_rows, lanes]
        dprob = dot_nn(gathered_ref[key_rows, value_cols], grad_t_ref[:, lanes])
        dscore = (prob.astype(jnp.float32) * (dprob - delta_ref[:, lanes])).astype(jnp.bfloat16)

        @pl.when(step <= chip)
        def _():
            dq_t_ref[...] += dot_nn(gathered_ref[key_rows, key_cols].T, dscore)

        @pl.when(step >= chip)
        def _():
            queries = jnp.concatenate(
                [
                    gathered_ref[at(query_step, size), h * HEAD_SIZE : (h + 1) * HEAD_SIZE]
                    for h in range(heads)
                ],
                axis=0,
            )
            dk_ref[...] += dot_nn(dscore, queries)
            dv_ref[...] += dot_nt(prob, grad_t_ref[:, lanes])

    for target, half in ((dx_far_ref, 1 - core), (dx_own_ref, core)):
        for h in range(heads):
            target[:, h * HEAD_SIZE : (h + 1) * HEAD_SIZE] = (
                logit_scale * dq_t_ref[:, at(2 * h + half, rows)]
            ).T.astype(jnp.bfloat16)
        target[:, key_cols] = (logit_scale * dk_ref[at(half, rows)]).astype(jnp.bfloat16)
        target[:, value_cols] = dv_ref[at(half, rows)].astype(jnp.bfloat16)


def value_grad_kernel(size, prob_ref, grad_t_ref, dv_ref):
    steps = prob_ref.shape[0] // size
    wide = grad_t_ref.shape[1] // steps
    for step in range(steps):
        own = slice(step * size, (step + 1) * size)
        dv_ref[own] = dot_nt(prob_ref[own, step * wide :], grad_t_ref[:, step * wide :]).astype(
            jnp.bfloat16
        )


def input_terms_kernel(
    apart_groups, own_ref, far_ref, wq_ref, wk_ref, wv_ref, *refs
):
    terms, dx_ref = refs[:-1], refs[-1]
    core = lax.axis_index("seq") % 2
    group = lax.axis_index("head")
    q_cols = wq_ref.shape[1] // 2
    kv_cols = wk_ref.shape[1] // 2
    for source, half in ((own_ref, core), (far_ref, 1 - core)):
        dx_ref[:, at(half, q_cols)] = source[:, :q_cols]
        dx_ref[:, pl.ds(pl.multiple_of(2 * q_cols + half * kv_cols, kv_cols), kv_cols)] = source[
            :, q_cols : q_cols + kv_cols
        ]
        dx_ref[
            :, pl.ds(pl.multiple_of(2 * q_cols + (2 + half) * kv_cols, kv_cols), kv_cols)
        ] = source[:, q_cols + kv_cols :]
    for apart, target in zip(apart_groups, terms):
        cut = target.shape[0]
        place = at(group ^ apart, cut)
        target[...] = (
            dot_nt(wq_ref[place], dx_ref[:, : 2 * q_cols])
            + dot_nt(wk_ref[place], dx_ref[:, 2 * q_cols : 2 * q_cols + 2 * kv_cols])
            + dot_nt(wv_ref[place], dx_ref[:, 2 * q_cols + 2 * kv_cols :])
        ).astype(target.dtype)


def weight_grad_kernel(
    turned_ref, attn_ref, far_attn_ref, dv_ref, far_dv_ref, wvalue_ref, woutput_ref, done_ref, joined_ref
):
    done_ref[...] = jnp.zeros_like(done_ref)
    core = lax.axis_index("seq") % 2
    parts = turned_ref.shape[0]
    rows = turned_ref.shape[3]
    for part in range(parts):
        joined_ref[:, :, part * rows : (part + 1) * rows] = turned_ref[part]
    for half, attn, dv in ((core, attn_ref, dv_ref), (1 - core, far_attn_ref, far_dv_ref)):
        wvalue_ref[:, at(half, dv.shape[1])] = dot_nn(joined_ref[0], dv[...])
        woutput_ref[:, at(half, attn.shape[0])] = dot_nt(joined_ref[1], attn[...])


def sum_kernel(_, own_ref, *refs):
    total = own_ref[...]
    for arrived_ref in refs[:-1]:
        total = total + arrived_ref[...].astype(jnp.float32)
    refs[-1][...] = total.astype(jnp.bfloat16)


def kernel_call(
    body, outs, operands, in_vmem=(), scratch=(), flops=0, moved=0, room=16, out_hbm=()
):
    vmem = pl.BlockSpec(memory_space=pltpu.VMEM)
    hbm = pl.BlockSpec(memory_space=pltpu.HBM)
    return pl.pallas_call(
        body,
        out_shape=outs,
        in_specs=[vmem if place in in_vmem else hbm for place in range(len(operands))],
        out_specs=tuple(hbm if place in out_hbm else vmem for place in range(len(outs))),
        scratch_shapes=list(scratch),
        compiler_params=pltpu.CompilerParams(vmem_limit_bytes=room * 1024 * 1024),
        cost_estimate=pl.CostEstimate(flops=flops, bytes_accessed=moved, transcendentals=0),
    )(*operands)


def swapped(value, axis, apart):
    count = lax.axis_size(axis)
    return lax.ppermute(value, axis, [(place, place ^ apart) for place in range(count)])


def gathered_plan(
    normed_input,
    stored_queries,
    stored_keys,
    stored_values,
    query_weight,
    key_matrix,
    value_matrix,
    output_weight,
    out_cotangent,
):
    bf16, f32 = jnp.bfloat16, jnp.float32
    rows, model = normed_input.shape
    blocks = lax.axis_size("seq")
    groups = lax.axis_size("head")
    tokens = rows * blocks
    q_cols = stored_queries.shape[1] // 2
    kv_cols = HEAD_SIZE
    wide = 2 * QUERIES_PER_KEY * rows
    packed_cols = q_cols + 2 * kv_cols
    shape = jax.ShapeDtypeStruct
    sent, sent_done = kernel_call(
        pack_kernel,
        (shape((blocks, rows, packed_cols), bf16), shape((8, HEAD_SIZE), f32)),
        (stored_queries, stored_keys, stored_values),
        scratch=(pltpu.SemaphoreType.DMA((3 * blocks,)),),
        moved=4 * blocks * rows * packed_cols,
        room=63,
        out_hbm=(0,),
    )
    gathered = lax.all_to_all(sent, "seq", 0, 0).reshape(tokens, packed_cols)
    same, other = kernel_call(
        out_grad_kernel,
        (shape((q_cols, rows), bf16),) * 2,
        (out_cotangent, output_weight, sent_done),
        scratch=(
            pltpu.VMEM(out_cotangent.shape, bf16),
            pltpu.VMEM(output_weight.shape, bf16),
            pltpu.SemaphoreType.DMA((3,)),
        ),
        flops=4 * rows * model * q_cols,
        moved=2 * model * (rows + 2 * q_cols),
        room=63,
    )
    held = [same] + [
        swapped(other if apart % 2 else same, "seq", apart) for apart in range(1, blocks)
    ]
    prob, inverse, attn, prob_done = kernel_call(
        probability_kernel,
        (
            shape((tokens, tokens * QUERIES_PER_KEY), bf16),
            shape((1, tokens * QUERIES_PER_KEY), f32),
            shape((q_cols, tokens), bf16),
            shape((8, HEAD_SIZE), f32),
        ),
        (gathered,),
        in_vmem=(0,),
        scratch=(
            pltpu.VMEM((tokens, wide), f32),
            pltpu.VMEM((tokens, wide), f32),
            pltpu.VMEM((HEAD_SIZE, tokens), bf16),
        ),
        flops=3 * tokens * tokens * q_cols,
        moved=2 * tokens * (packed_cols + q_cols + tokens * QUERIES_PER_KEY),
    )
    turned, turn_done = kernel_call(
        functools.partial(turn_kernel, blocks),
        (shape((blocks, 2, model // blocks, rows), bf16), shape((8, HEAD_SIZE), f32)),
        (normed_input, out_cotangent, prob_done),
        scratch=(
            pltpu.VMEM(normed_input.shape, bf16),
            pltpu.VMEM(out_cotangent.shape, bf16),
            pltpu.SemaphoreType.DMA((2,)),
        ),
        moved=8 * rows * model,
    )
    turned = lax.all_to_all(turned, "seq", 0, 0)
    dx_own, dx_far, grad_t = kernel_call(
        gradient_kernel,
        (
            shape((rows, q_cols + 2 * kv_cols), bf16),
            shape((rows, q_cols + 2 * kv_cols), bf16),
            shape((HEAD_SIZE, tokens * QUERIES_PER_KEY), bf16),
        ),
        (gathered, prob, inverse, attn, turn_done, *held),
        in_vmem=range(4),
        scratch=(
            pltpu.VMEM((blocks, q_cols, rows), bf16),
            pltpu.VMEM((1, tokens * QUERIES_PER_KEY), f32),
            pltpu.VMEM((HEAD_SIZE, wide), f32),
            pltpu.VMEM((2 * rows, HEAD_SIZE), f32),
            pltpu.VMEM((2 * rows, HEAD_SIZE), f32),
            pltpu.SemaphoreType.DMA((blocks,)),
        ),
        flops=3 * tokens * tokens * q_cols,
        moved=2 * tokens * (packed_cols + q_cols + tokens * QUERIES_PER_KEY),
    )
    (dv,) = kernel_call(
        functools.partial(value_grad_kernel, 2 * rows),
        (shape((tokens, kv_cols), bf16),),
        (prob, grad_t),
        in_vmem=range(2),
        flops=tokens * tokens * q_cols,
        moved=2 * tokens * tokens * QUERIES_PER_KEY,
    )
    dx_got = swapped(dx_far, "seq", 1)
    terms = {}
    aparts = tuple(range(groups - 1, -1, -1))
    for chosen in (aparts[: groups // 2], aparts[groups // 2 :]):
        made = kernel_call(
            functools.partial(input_terms_kernel, chosen),
            tuple(shape((model // groups, rows), bf16 if apart else f32) for apart in chosen),
            (dx_own, dx_got, query_weight, key_matrix, value_matrix),
            in_vmem=range(5),
            scratch=(pltpu.VMEM((rows, 2 * (q_cols + 2 * kv_cols)), bf16),),
            flops=2 * rows * model * (q_cols + 2 * kv_cols),
            moved=2 * model * (q_cols + 2 * kv_cols),
        )
        terms.update(zip(chosen, made))
    arrived = [swapped(terms[apart], "head", apart) for apart in aparts[:-1]]
    grad_wvalue, grad_woutput, weights_done = kernel_call(
        weight_grad_kernel,
        (
            shape((model // blocks, 2 * kv_cols), f32),
            shape((model // blocks, 2 * q_cols), f32),
            shape((8, HEAD_SIZE), f32),
        ),
        (turned, attn, swapped(attn, "seq", 1), dv, swapped(dv, "seq", 1)),
        in_vmem=range(5),
        scratch=(pltpu.VMEM((2, model // blocks, tokens), bf16),),
        flops=4 * tokens * (model // blocks) * (q_cols + kv_cols),
        moved=4 * (model // blocks) * (tokens + 2 * q_cols + 2 * kv_cols),
    )
    (grad_input,) = kernel_call(
        sum_kernel,
        (shape((model // groups, rows), bf16),),
        (weights_done, terms[0], *arrived),
        in_vmem=range(1, groups + 1),
        moved=4 * groups * (model // groups) * rows,
    )
    return (grad_input.T, grad_wvalue, grad_woutput.T)


def power_of_two(count):
    return count & (count - 1) == 0


def local(normed_input, stored_queries, stored_keys, *others):
    blocks, groups = lax.axis_size("seq"), lax.axis_size("head")
    whole_window = normed_input.shape[0] * blocks <= WINDOW_LENGTH
    two_heads = stored_keys.shape[1] == 2 * HEAD_SIZE
    paired = blocks > 1 and power_of_two(blocks) and power_of_two(groups)
    plan = gathered_plan if whole_window and two_heads and paired else windowed_plan
    return plan(normed_input, stored_queries, stored_keys, *others)


def windowed_plan(
    normed_input,
    stored_queries,
    stored_keys,
    stored_values,
    query_weight,
    key_matrix,
    value_matrix,
    output_weight,
    out_cotangent,
):
    tok_rows = normed_input.shape[0]
    blocks_seq = lax.axis_size("seq")
    seq_place = lax.axis_index("seq")
    reach_blocks = min(WINDOW_LENGTH // tok_rows, blocks_seq - 1)
    kv_heads = stored_keys.shape[1] // HEAD_SIZE
    output_gradient = jnp.dot(
        out_cotangent, output_weight.T, preferred_element_type=jnp.float32
    ).astype(jnp.bfloat16)
    pieces = [(stored_keys, stored_values)]
    current = (stored_keys, stored_values)
    for relay_step in range(reach_blocks):
        current = passed_along((current[0], current[1]), "seq", 1)
        pieces = [current] + pieces
    key_window = jnp.concatenate([piece[0] for piece in pieces], axis=0)
    value_window = jnp.concatenate([piece[1] for piece in pieces], axis=0)
    key_span = key_window.shape[0]
    query_pos = seq_place * tok_rows + jnp.arange(tok_rows, dtype=jnp.int32)
    key_pos = (seq_place - reach_blocks) * tok_rows + jnp.arange(key_span, dtype=jnp.int32)
    pos_gap = query_pos[:, None] - key_pos[None, :]
    allowed = (pos_gap >= 0) & (pos_gap < WINDOW_LENGTH) & (key_pos >= 0)[None, :]
    allowed_rows = jnp.tile(allowed, (QUERIES_PER_KEY, 1))
    query_stack = (
        stored_queries.reshape(tok_rows, kv_heads, QUERIES_PER_KEY, HEAD_SIZE)
        .transpose(1, 2, 0, 3)
        .reshape(kv_heads, QUERIES_PER_KEY * tok_rows, HEAD_SIZE)
    )
    grad_stack = (
        output_gradient.reshape(tok_rows, kv_heads, QUERIES_PER_KEY, HEAD_SIZE)
        .transpose(1, 2, 0, 3)
        .reshape(kv_heads, QUERIES_PER_KEY * tok_rows, HEAD_SIZE)
    )
    key_stack = key_window.reshape(key_span, kv_heads, HEAD_SIZE).transpose(1, 0, 2)
    value_stack = value_window.reshape(key_span, kv_heads, HEAD_SIZE).transpose(1, 0, 2)

    def per_head(head_items):
        query_head, key_head, value_head, grad_head = head_items
        attention_logits = logit_scale * jnp.dot(
            query_head, key_head.T, preferred_element_type=jnp.float32
        )
        masked = jnp.where(allowed_rows, attention_logits, -jnp.inf)
        row_top = jnp.max(masked, axis=1, keepdims=True)
        exp_scores = jnp.exp(masked - row_top)
        attn_prob = exp_scores / jnp.sum(exp_scores, axis=1, keepdims=True)
        probability_halfwidth = attn_prob.astype(jnp.bfloat16)
        attn_head = jnp.dot(
            probability_halfwidth, value_head, preferred_element_type=jnp.float32
        ).astype(jnp.bfloat16)
        row_delta = jnp.sum(
            grad_head.astype(jnp.float32) * attn_head.astype(jnp.float32), axis=1, keepdims=True
        )
        probability_gradient = jnp.dot(grad_head, value_head.T, preferred_element_type=jnp.float32)
        score_gradient = (attn_prob * (probability_gradient - row_delta)).astype(jnp.bfloat16)
        qgrad_head = (
            logit_scale * jnp.dot(score_gradient, key_head, preferred_element_type=jnp.float32)
        ).astype(jnp.bfloat16)
        key_partial = logit_scale * jnp.dot(
            score_gradient.T, query_head, preferred_element_type=jnp.float32
        )
        value_partial = jnp.dot(
            probability_halfwidth.T, grad_head, preferred_element_type=jnp.float32
        )
        return (attn_head, qgrad_head, key_partial, value_partial)

    attn_all, qgrad_all, key_all, value_all = lax.map(
        per_head, (query_stack, key_stack, value_stack, grad_stack)
    )
    attention_output = (
        attn_all.reshape(kv_heads, QUERIES_PER_KEY, tok_rows, HEAD_SIZE)
        .transpose(2, 0, 1, 3)
        .reshape(tok_rows, kv_heads * QUERIES_PER_KEY * HEAD_SIZE)
    )
    query_gradient = (
        qgrad_all.reshape(kv_heads, QUERIES_PER_KEY, tok_rows, HEAD_SIZE)
        .transpose(2, 0, 1, 3)
        .reshape(tok_rows, kv_heads * QUERIES_PER_KEY * HEAD_SIZE)
    )
    key_terms = key_all.transpose(1, 0, 2).reshape(key_span, kv_heads * HEAD_SIZE)
    value_terms = value_all.transpose(1, 0, 2).reshape(key_span, kv_heads * HEAD_SIZE)

    def take_slot(terms, slot_index):
        return terms[slot_index * tok_rows : (slot_index + 1) * tok_rows]

    key_sum = take_slot(key_terms, reach_blocks)
    value_sum = take_slot(value_terms, reach_blocks)
    for distance in range(1, reach_blocks + 1):
        received = passed_along(
            (
                take_slot(key_terms, reach_blocks - distance),
                take_slot(value_terms, reach_blocks - distance),
            ),
            "seq",
            -distance,
        )
        key_sum = key_sum + received[0]
        value_sum = value_sum + received[1]
    grad_key = key_sum.astype(jnp.bfloat16)
    grad_value = value_sum.astype(jnp.bfloat16)
    input_terms = jnp.dot(query_gradient, query_weight.T, preferred_element_type=jnp.float32)
    input_terms = input_terms + jnp.dot(grad_key, key_matrix.T, preferred_element_type=jnp.float32)
    input_terms = input_terms + jnp.dot(
        grad_value, value_matrix.T, preferred_element_type=jnp.float32
    )
    grad_input = lax.psum_scatter(input_terms, "head", scatter_dimension=1, tiled=True).astype(
        jnp.bfloat16
    )
    value_cols = grad_value.shape[1]
    input_cols = normed_input.T
    cot_cols = out_cotangent.T
    gathered = lax.psum_scatter(
        jnp.concatenate(
            [
                jnp.dot(input_cols, grad_value, preferred_element_type=jnp.float32),
                jnp.dot(cot_cols, attention_output, preferred_element_type=jnp.float32),
            ],
            axis=1,
        ),
        "seq",
        scatter_dimension=0,
        tiled=True,
    )
    grad_wvalue = gathered[:, :value_cols]
    grad_woutput = gathered[:, value_cols:].T
    return (grad_input, grad_wvalue, grad_woutput)


def solution(mesh):
    placed = (
        P("seq", None),
        P("seq", "head"),
        P("seq", "head"),
        P("seq", "head"),
        P(None, "head"),
        P(None, "head"),
        P(None, "head"),
        P("head", None),
        P("seq", None),
    )
    return jax.shard_map(
        local,
        mesh=mesh,
        in_specs=placed,
        out_specs=(P("seq", "head"), P("seq", "head"), P("head", "seq")),
        check_vma=False,
    )
```

```python
import functools

import jax
import jax.numpy as jnp
from jax import lax
from jax.experimental import pallas as pl
from jax.experimental.pallas import tpu as pltpu
from jax.sharding import PartitionSpec as P

HEAD_SIZE = 128
WINDOW_LENGTH = 4096
QUERIES_PER_KEY = 2


logit_scale = 1.0 / 12.0
log2_scale = 1.4426950408889634 / 12.0
excluded = -1e30


def passed_along(value, axis, steps):
    count = lax.axis_size(axis)
    leading, last = (max(0, -steps), min(count, count - steps))
    return lax.ppermute(value, axis, [(source, source + steps) for source in range(leading, last)])


NT = (((1,), (1,)), ((), ()))


def dot_nt(left, right):
    return lax.dot_general(left, right, NT, preferred_element_type=jnp.float32)


def dot_nn(left, right):
    return jnp.dot(left, right, preferred_element_type=jnp.float32)


def at(place, size):
    return pl.ds(pl.multiple_of(place * size, size), size)


def out_grad_kernel(
    cot_hbm, weight_hbm, q_hbm, k_hbm, v_hbm, same_ref, other_ref, cot_ref, weight_ref, sem
):
    core = lax.axis_index("seq") % 2
    cut = weight_ref.shape[0] // 2
    cot_copy = pltpu.make_async_copy(cot_hbm, cot_ref, sem.at[0])
    cot_copy.start()
    halves = ((other_ref, 1 - core), (same_ref, core))
    weight_copies = []
    for place, (_, half) in enumerate(halves):
        weight_copies.append(
            pltpu.make_async_copy(
                weight_hbm.at[at(half, cut)], weight_ref.at[at(place, cut)], sem.at[1 + place]
            )
        )
        weight_copies[-1].start()
    plain_copies = []
    for place, (target, half) in enumerate(halves):
        first = 0
        for which, source in enumerate((q_hbm, k_hbm, v_hbm)):
            cols = source.shape[1] // 2
            plain_copies.append(
                pltpu.make_async_copy(
                    source.at[:, at(half, cols)],
                    target.at[:, pl.ds(first, cols)],
                    sem.at[3 + 3 * place + which],
                )
            )
            plain_copies[-1].start()
            first += cols
    cot_copy.wait()
    for place, (target, _) in enumerate(halves):
        weight_copies[place].wait()
        grads_t = dot_nt(weight_ref[place * cut : (place + 1) * cut], cot_ref[...])
        for h in range(cut // HEAD_SIZE):
            target[:, first + h * HEAD_SIZE : first + (h + 1) * HEAD_SIZE] = grads_t[
                h * HEAD_SIZE : (h + 1) * HEAD_SIZE
            ].astype(jnp.bfloat16)
    for copy in plain_copies:
        copy.wait()


def turn_kernel(parts, normed_hbm, cot_hbm, _, __, turned_ref, done_ref, normed_ref, cot_ref, sem):
    cut = normed_ref.shape[1] // parts
    done_ref[...] = jnp.zeros_like(done_ref)
    copies = []
    for which, (source, target) in enumerate(((normed_hbm, normed_ref), (cot_hbm, cot_ref))):
        copies.append(pltpu.make_async_copy(source, target, sem.at[which]))
        copies[-1].start()
    for which, ref in enumerate((normed_ref, cot_ref)):
        copies[which].wait()
        turned = ref[...].astype(jnp.float32).T.astype(jnp.bfloat16)
        for part in range(parts):
            turned_ref[part, which] = turned[part * cut : (part + 1) * cut]


def attention_kernel(blocks, *refs):
    attention_body(refs[:blocks], *refs[blocks:])


def attention_body(
    block_refs,
    _,
    dx_own_ref,
    dx_far_ref,
    attn_ref,
    dv_ref,
    gathered_ref,
    score_even_ref,
    score_odd_ref,
    prob_ref,
    grad_t_ref,
    delta_ref,
    query_ref,
    value_t_ref,
    key_t_ref,
    dq_t_ref,
    dk_ref,
    sem,
):
    me = lax.axis_index("seq")
    core, chip = me % 2, me // 2
    rows = dx_own_ref.shape[0]
    for apart, source in enumerate(block_refs):
        place = me ^ apart
        pltpu.make_async_copy(source, gathered_ref.at[at(place, rows)], sem.at[place]).start()
    tokens = gathered_ref.shape[0]
    size = 2 * rows
    steps = tokens // size
    wide = QUERIES_PER_KEY * size
    heads = QUERIES_PER_KEY
    key_cols = slice(heads * HEAD_SIZE, (heads + 1) * HEAD_SIZE)
    value_cols = slice((heads + 1) * HEAD_SIZE, (heads + 2) * HEAD_SIZE)
    grad_base = (heads + 2) * HEAD_SIZE
    key_place = lax.broadcasted_iota(jnp.int32, (size, wide), 0)
    query_place = lax.broadcasted_iota(jnp.int32, (size, wide), 1) % size
    allowed = key_place <= query_place

    for step in range(steps):
        span = (step + 1) * size
        own = slice(step * size, span)
        lanes = slice(step * wide, (step + 1) * wide)
        score_ref = score_odd_ref if step % 2 else score_even_ref
        for block in (2 * step, 2 * step + 1):
            pltpu.make_async_copy(
                block_refs[0], gathered_ref.at[pl.ds(block * rows, rows)], sem.at[block]
            ).wait()
        value_t_ref[:, own] = gathered_ref[own, value_cols].T
        key_t_ref[:, own] = gathered_ref[own, key_cols].T
        queries = jnp.concatenate(
            [gathered_ref[own, h * HEAD_SIZE : (h + 1) * HEAD_SIZE] for h in range(heads)], axis=0
        )
        query_ref[lanes] = queries
        top = None
        for piece in range(step + 1):
            part = slice(piece * size, (piece + 1) * size)
            scores = dot_nt(gathered_ref[part, key_cols], queries)
            if piece == step:
                scores = jnp.where(allowed, scores, excluded)
            score_ref[part] = scores
            largest = jnp.max(scores.reshape(size // 8, 8, wide), axis=0)
            top = largest if top is None else jnp.maximum(top, largest)
        top = jnp.max(top, axis=0, keepdims=True)
        total = None
        for piece in range(step + 1):
            part = slice(piece * size, (piece + 1) * size)
            weights = jnp.exp2((score_ref[part] - top) * log2_scale)
            prob_ref[part, lanes] = weights.astype(jnp.bfloat16)
            summed = jnp.sum(weights.reshape(size // 8, 8, wide), axis=0)
            total = summed if total is None else total + summed
        inverse = 1.0 / jnp.sum(total, axis=0, keepdims=True)
        attn = dot_nn(value_t_ref[:, :span], prob_ref[:span, lanes]) * inverse
        for h in range(heads):
            attn_ref[h * HEAD_SIZE : (h + 1) * HEAD_SIZE, own] = attn[
                :, h * size : (h + 1) * size
            ].astype(jnp.bfloat16)
        grads_t = jnp.concatenate(
            [
                gathered_ref[
                    block * rows : (block + 1) * rows,
                    grad_base + h * HEAD_SIZE : grad_base + (h + 1) * HEAD_SIZE,
                ]
                for h in range(heads)
                for block in (2 * step, 2 * step + 1)
            ],
            axis=1,
        )
        grads_t = (grads_t.astype(jnp.float32) * inverse).astype(jnp.bfloat16)
        grad_t_ref[:, lanes] = grads_t
        delta_ref[:, lanes] = jnp.sum(grads_t.astype(jnp.float32) * attn, axis=0, keepdims=True)

    for step in range(steps):
        own = slice(step * size, (step + 1) * size)
        dv_ref[own] = dot_nt(prob_ref[own, step * wide :], grad_t_ref[:, step * wide :]).astype(
            jnp.bfloat16
        )

    dq_t_ref[...] = jnp.zeros_like(dq_t_ref)
    dk_ref[...] = jnp.zeros_like(dk_ref)
    for step in range(steps):
        key_step = jnp.minimum(chip, step)
        query_step = jnp.maximum(chip, step)
        dprob = dot_nn(
            gathered_ref[at(key_step, size), value_cols], grad_t_ref[:, at(query_step, wide)]
        )
        dscore = (
            prob_ref[at(key_step, size), at(query_step, wide)].astype(jnp.float32)
            * (dprob - delta_ref[:, at(query_step, wide)])
        ).astype(jnp.bfloat16)

        @pl.when(step <= chip)
        def _():
            dq_t_ref[...] += dot_nn(key_t_ref[:, at(key_step, size)], dscore)

        @pl.when(step >= chip)
        def _():
            dk_ref[...] += dot_nn(dscore, query_ref[at(query_step, wide)])

    for target, half in ((dx_far_ref, 1 - core), (dx_own_ref, core)):
        for h in range(heads):
            target[:, h * HEAD_SIZE : (h + 1) * HEAD_SIZE] = (
                (logit_scale * dq_t_ref[:, at(2 * h + half, rows)])
                .T.astype(jnp.bfloat16)
            )
        target[:, key_cols] = (logit_scale * dk_ref[at(half, rows)]).astype(jnp.bfloat16)
        target[:, value_cols] = dv_ref[at(2 * chip + half, rows)]


def input_terms_kernel(
    apart_groups, own_ref, far_ref, wq_ref, wk_ref, wv_ref, *refs
):
    terms, dx_ref = refs[:-1], refs[-1]
    core = lax.axis_index("seq") % 2
    group = lax.axis_index("head")
    q_cols = wq_ref.shape[1] // 2
    kv_cols = wk_ref.shape[1] // 2
    for source, half in ((own_ref, core), (far_ref, 1 - core)):
        dx_ref[:, at(half, q_cols)] = source[:, :q_cols]
        dx_ref[:, pl.ds(pl.multiple_of(2 * q_cols + half * kv_cols, kv_cols), kv_cols)] = source[
            :, q_cols : q_cols + kv_cols
        ]
        dx_ref[
            :, pl.ds(pl.multiple_of(2 * q_cols + (2 + half) * kv_cols, kv_cols), kv_cols)
        ] = source[:, q_cols + kv_cols :]
    for apart, target in zip(apart_groups, terms):
        cut = target.shape[0]
        place = at(group ^ apart, cut)
        target[...] = (
            dot_nt(wq_ref[place], dx_ref[:, : 2 * q_cols])
            + dot_nt(wk_ref[place], dx_ref[:, 2 * q_cols : 2 * q_cols + 2 * kv_cols])
            + dot_nt(wv_ref[place], dx_ref[:, 2 * q_cols + 2 * kv_cols :])
        ).astype(target.dtype)


def weight_grad_kernel(
    turned_ref, attn_ref, far_attn_ref, dv_ref, far_dv_ref, wvalue_ref, woutput_ref, done_ref, joined_ref
):
    done_ref[...] = jnp.zeros_like(done_ref)
    core = lax.axis_index("seq") % 2
    parts = turned_ref.shape[0]
    rows = turned_ref.shape[3]
    for part in range(parts):
        joined_ref[:, :, part * rows : (part + 1) * rows] = turned_ref[part]
    for half, attn, dv in ((core, attn_ref, dv_ref), (1 - core, far_attn_ref, far_dv_ref)):
        wvalue_ref[:, at(half, dv.shape[1])] = dot_nn(joined_ref[0], dv[...])
        woutput_ref[:, at(half, attn.shape[0])] = dot_nt(joined_ref[1], attn[...])


def sum_kernel(_, own_ref, *refs):
    total = own_ref[...]
    for arrived_ref in refs[:-1]:
        total = total + arrived_ref[...].astype(jnp.float32)
    refs[-1][...] = total.astype(jnp.bfloat16)


def kernel_call(body, outs, operands, in_vmem=(), scratch=(), flops=0, moved=0, room=16):
    vmem = pl.BlockSpec(memory_space=pltpu.VMEM)
    hbm = pl.BlockSpec(memory_space=pltpu.HBM)
    return pl.pallas_call(
        body,
        out_shape=outs,
        in_specs=[vmem if place in in_vmem else hbm for place in range(len(operands))],
        out_specs=jax.tree.map(lambda _: vmem, outs),
        scratch_shapes=list(scratch),
        compiler_params=pltpu.CompilerParams(vmem_limit_bytes=room * 1024 * 1024),
        cost_estimate=pl.CostEstimate(flops=flops, bytes_accessed=moved, transcendentals=0),
    )(*operands)


def swapped(value, axis, apart):
    count = lax.axis_size(axis)
    return lax.ppermute(value, axis, [(place, place ^ apart) for place in range(count)])


def gathered_plan(
    normed_input,
    stored_queries,
    stored_keys,
    stored_values,
    query_weight,
    key_matrix,
    value_matrix,
    output_weight,
    out_cotangent,
):
    bf16, f32 = jnp.bfloat16, jnp.float32
    rows, model = normed_input.shape
    blocks = lax.axis_size("seq")
    groups = lax.axis_size("head")
    tokens = rows * blocks
    q_cols = stored_queries.shape[1] // 2
    kv_cols = HEAD_SIZE
    wide = 2 * QUERIES_PER_KEY * rows
    packed_cols = 2 * q_cols + 2 * kv_cols
    shape = jax.ShapeDtypeStruct
    same, other = kernel_call(
        out_grad_kernel,
        (shape((rows, packed_cols), bf16),) * 2,
        (out_cotangent, output_weight, stored_queries, stored_keys, stored_values),
        scratch=(
            pltpu.VMEM(out_cotangent.shape, bf16),
            pltpu.VMEM(output_weight.shape, bf16),
            pltpu.SemaphoreType.DMA((9,)),
        ),
        flops=4 * rows * model * q_cols,
        moved=2 * model * (rows + 2 * q_cols),
        room=63,
    )
    held = {0: same}
    for apart in range(2, blocks):
        lowest, highest = 2, 1 << (apart.bit_length() - 1)
        while not apart & lowest:
            lowest *= 2
        through = lowest if apart % 2 else highest
        if lowest == highest:
            held[apart] = swapped(other if apart % 2 else same, "seq", apart)
        else:
            held[apart] = swapped(held[apart ^ through], "seq", through)
    held[1] = swapped(other, "seq", 1)
    turned, turn_done = kernel_call(
        functools.partial(turn_kernel, blocks),
        (shape((blocks, 2, model // blocks, rows), bf16), shape((8, HEAD_SIZE), f32)),
        (normed_input, out_cotangent, held[3], held[4]),
        scratch=(
            pltpu.VMEM(normed_input.shape, bf16),
            pltpu.VMEM(out_cotangent.shape, bf16),
            pltpu.SemaphoreType.DMA((2,)),
        ),
        moved=8 * rows * model,
    )
    turned = lax.all_to_all(turned, "seq", 0, 0)
    dx_own, dx_far, attn, dv = kernel_call(
        functools.partial(attention_kernel, blocks),
        (
            shape((rows, q_cols + 2 * kv_cols), bf16),
            shape((rows, q_cols + 2 * kv_cols), bf16),
            shape((q_cols, tokens), bf16),
            shape((tokens, kv_cols), bf16),
        ),
        [held[apart] for apart in range(blocks)] + [turn_done],
        scratch=(
            pltpu.VMEM((tokens, packed_cols), bf16),
            pltpu.VMEM((tokens, wide), f32),
            pltpu.VMEM((tokens, wide), f32),
            pltpu.VMEM((tokens, tokens * QUERIES_PER_KEY), bf16),
            pltpu.VMEM((HEAD_SIZE, tokens * QUERIES_PER_KEY), bf16),
            pltpu.VMEM((1, tokens * QUERIES_PER_KEY), f32),
            pltpu.VMEM((tokens * QUERIES_PER_KEY, HEAD_SIZE), bf16),
            pltpu.VMEM((HEAD_SIZE, tokens), bf16),
            pltpu.VMEM((HEAD_SIZE, tokens), bf16),
            pltpu.VMEM((HEAD_SIZE, wide), f32),
            pltpu.VMEM((2 * rows, HEAD_SIZE), f32),
            pltpu.SemaphoreType.DMA((blocks,)),
        ),
        flops=8 * tokens * tokens * q_cols,
        moved=2 * tokens * packed_cols,
    )
    dx_got = swapped(dx_far, "seq", 1)
    aparts = tuple(range(groups - 1, -1, -1))
    terms = {}
    for chosen in (aparts[: groups // 2], aparts[groups // 2 :]):
        made = kernel_call(
            functools.partial(input_terms_kernel, chosen),
            tuple(shape((model // groups, rows), bf16 if apart else f32) for apart in chosen),
            (dx_own, dx_got, query_weight, key_matrix, value_matrix),
            in_vmem=range(5),
            scratch=(pltpu.VMEM((rows, 2 * (q_cols + 2 * kv_cols)), bf16),),
            flops=2 * rows * model * (q_cols + 2 * kv_cols),
            moved=2 * model * (q_cols + 2 * kv_cols),
        )
        terms.update(zip(chosen, made))
    arrived = [swapped(terms[apart], "head", apart) for apart in aparts[:-1]]
    grad_wvalue, grad_woutput, weights_done = kernel_call(
        weight_grad_kernel,
        (
            shape((model // blocks, 2 * kv_cols), f32),
            shape((model // blocks, 2 * q_cols), f32),
            shape((8, HEAD_SIZE), f32),
        ),
        (turned, attn, swapped(attn, "seq", 1), dv, swapped(dv, "seq", 1)),
        in_vmem=range(5),
        scratch=(pltpu.VMEM((2, model // blocks, tokens), bf16),),
        flops=4 * tokens * (model // blocks) * (q_cols + kv_cols),
        moved=4 * (model // blocks) * (tokens + 2 * q_cols + 2 * kv_cols),
    )
    grad_input = kernel_call(
        sum_kernel,
        shape((model // groups, rows), bf16),
        (weights_done, terms[0], *arrived),
        in_vmem=range(1, groups + 1),
        moved=4 * groups * (model // groups) * rows,
    )
    return (grad_input.T, grad_wvalue, grad_woutput.T)


def power_of_two(count):
    return count & (count - 1) == 0


def local(normed_input, stored_queries, stored_keys, *others):
    blocks, groups = lax.axis_size("seq"), lax.axis_size("head")
    whole_window = normed_input.shape[0] * blocks <= WINDOW_LENGTH
    two_heads = stored_keys.shape[1] == 2 * HEAD_SIZE
    paired = blocks > 1 and power_of_two(blocks) and power_of_two(groups)
    plan = gathered_plan if whole_window and two_heads and paired else windowed_plan
    return plan(normed_input, stored_queries, stored_keys, *others)


def windowed_plan(
    normed_input,
    stored_queries,
    stored_keys,
    stored_values,
    query_weight,
    key_matrix,
    value_matrix,
    output_weight,
    out_cotangent,
):
    tok_rows = normed_input.shape[0]
    blocks_seq = lax.axis_size("seq")
    seq_place = lax.axis_index("seq")
    reach_blocks = min(WINDOW_LENGTH // tok_rows, blocks_seq - 1)
    kv_heads = stored_keys.shape[1] // HEAD_SIZE
    output_gradient = jnp.dot(
        out_cotangent, output_weight.T, preferred_element_type=jnp.float32
    ).astype(jnp.bfloat16)
    pieces = [(stored_keys, stored_values)]
    current = (stored_keys, stored_values)
    for relay_step in range(reach_blocks):
        current = passed_along((current[0], current[1]), "seq", 1)
        pieces = [current] + pieces
    key_window = jnp.concatenate([piece[0] for piece in pieces], axis=0)
    value_window = jnp.concatenate([piece[1] for piece in pieces], axis=0)
    key_span = key_window.shape[0]
    query_pos = seq_place * tok_rows + jnp.arange(tok_rows, dtype=jnp.int32)
    key_pos = (seq_place - reach_blocks) * tok_rows + jnp.arange(key_span, dtype=jnp.int32)
    pos_gap = query_pos[:, None] - key_pos[None, :]
    allowed = (pos_gap >= 0) & (pos_gap < WINDOW_LENGTH) & (key_pos >= 0)[None, :]
    allowed_rows = jnp.tile(allowed, (QUERIES_PER_KEY, 1))
    query_stack = (
        stored_queries.reshape(tok_rows, kv_heads, QUERIES_PER_KEY, HEAD_SIZE)
        .transpose(1, 2, 0, 3)
        .reshape(kv_heads, QUERIES_PER_KEY * tok_rows, HEAD_SIZE)
    )
    grad_stack = (
        output_gradient.reshape(tok_rows, kv_heads, QUERIES_PER_KEY, HEAD_SIZE)
        .transpose(1, 2, 0, 3)
        .reshape(kv_heads, QUERIES_PER_KEY * tok_rows, HEAD_SIZE)
    )
    key_stack = key_window.reshape(key_span, kv_heads, HEAD_SIZE).transpose(1, 0, 2)
    value_stack = value_window.reshape(key_span, kv_heads, HEAD_SIZE).transpose(1, 0, 2)

    def per_head(head_items):
        query_head, key_head, value_head, grad_head = head_items
        attention_logits = logit_scale * jnp.dot(
            query_head, key_head.T, preferred_element_type=jnp.float32
        )
        masked = jnp.where(allowed_rows, attention_logits, -jnp.inf)
        row_top = jnp.max(masked, axis=1, keepdims=True)
        exp_scores = jnp.exp(masked - row_top)
        attn_prob = exp_scores / jnp.sum(exp_scores, axis=1, keepdims=True)
        probability_halfwidth = attn_prob.astype(jnp.bfloat16)
        attn_head = jnp.dot(
            probability_halfwidth, value_head, preferred_element_type=jnp.float32
        ).astype(jnp.bfloat16)
        row_delta = jnp.sum(
            grad_head.astype(jnp.float32) * attn_head.astype(jnp.float32), axis=1, keepdims=True
        )
        probability_gradient = jnp.dot(grad_head, value_head.T, preferred_element_type=jnp.float32)
        score_gradient = (attn_prob * (probability_gradient - row_delta)).astype(jnp.bfloat16)
        qgrad_head = (
            logit_scale * jnp.dot(score_gradient, key_head, preferred_element_type=jnp.float32)
        ).astype(jnp.bfloat16)
        key_partial = logit_scale * jnp.dot(
            score_gradient.T, query_head, preferred_element_type=jnp.float32
        )
        value_partial = jnp.dot(
            probability_halfwidth.T, grad_head, preferred_element_type=jnp.float32
        )
        return (attn_head, qgrad_head, key_partial, value_partial)

    attn_all, qgrad_all, key_all, value_all = lax.map(
        per_head, (query_stack, key_stack, value_stack, grad_stack)
    )
    attention_output = (
        attn_all.reshape(kv_heads, QUERIES_PER_KEY, tok_rows, HEAD_SIZE)
        .transpose(2, 0, 1, 3)
        .reshape(tok_rows, kv_heads * QUERIES_PER_KEY * HEAD_SIZE)
    )
    query_gradient = (
        qgrad_all.reshape(kv_heads, QUERIES_PER_KEY, tok_rows, HEAD_SIZE)
        .transpose(2, 0, 1, 3)
        .reshape(tok_rows, kv_heads * QUERIES_PER_KEY * HEAD_SIZE)
    )
    key_terms = key_all.transpose(1, 0, 2).reshape(key_span, kv_heads * HEAD_SIZE)
    value_terms = value_all.transpose(1, 0, 2).reshape(key_span, kv_heads * HEAD_SIZE)

    def take_slot(terms, slot_index):
        return terms[slot_index * tok_rows : (slot_index + 1) * tok_rows]

    key_sum = take_slot(key_terms, reach_blocks)
    value_sum = take_slot(value_terms, reach_blocks)
    for distance in range(1, reach_blocks + 1):
        received = passed_along(
            (
                take_slot(key_terms, reach_blocks - distance),
                take_slot(value_terms, reach_blocks - distance),
            ),
            "seq",
            -distance,
        )
        key_sum = key_sum + received[0]
        value_sum = value_sum + received[1]
    grad_key = key_sum.astype(jnp.bfloat16)
    grad_value = value_sum.astype(jnp.bfloat16)
    input_terms = jnp.dot(query_gradient, query_weight.T, preferred_element_type=jnp.float32)
    input_terms = input_terms + jnp.dot(grad_key, key_matrix.T, preferred_element_type=jnp.float32)
    input_terms = input_terms + jnp.dot(
        grad_value, value_matrix.T, preferred_element_type=jnp.float32
    )
    grad_input = lax.psum_scatter(input_terms, "head", scatter_dimension=1, tiled=True).astype(
        jnp.bfloat16
    )
    value_cols = grad_value.shape[1]
    input_cols = normed_input.T
    cot_cols = out_cotangent.T
    gathered = lax.psum_scatter(
        jnp.concatenate(
            [
                jnp.dot(input_cols, grad_value, preferred_element_type=jnp.float32),
                jnp.dot(cot_cols, attention_output, preferred_element_type=jnp.float32),
            ],
            axis=1,
        ),
        "seq",
        scatter_dimension=0,
        tiled=True,
    )
    grad_wvalue = gathered[:, :value_cols]
    grad_woutput = gathered[:, value_cols:].T
    return (grad_input, grad_wvalue, grad_woutput)


def solution(mesh):
    placed = (
        P("seq", None),
        P("seq", "head"),
        P("seq", "head"),
        P("seq", "head"),
        P(None, "head"),
        P(None, "head"),
        P(None, "head"),
        P("head", None),
        P("seq", None),
    )
    return jax.shard_map(
        local,
        mesh=mesh,
        in_specs=placed,
        out_specs=(P("seq", "head"), P("seq", "head"), P("head", "seq")),
        check_vma=False,
    )
```

```python
import functools

import jax
import jax.numpy as jnp
from jax import lax
from jax.experimental import pallas as pl
from jax.experimental.pallas import tpu as pltpu
from jax.sharding import PartitionSpec as P

HEAD_SIZE = 128
WINDOW_LENGTH = 4096
QUERIES_PER_KEY = 2


logit_scale = 1.0 / 12.0
log2_scale = 1.4426950408889634 / 12.0
excluded = -1e30


def passed_along(value, axis, steps):
    count = lax.axis_size(axis)
    leading, last = (max(0, -steps), min(count, count - steps))
    return lax.ppermute(value, axis, [(source, source + steps) for source in range(leading, last)])


NT = (((1,), (1,)), ((), ()))


def dot_nt(left, right):
    return lax.dot_general(left, right, NT, preferred_element_type=jnp.float32)


def dot_nn(left, right):
    return jnp.dot(left, right, preferred_element_type=jnp.float32)


def at(place, size):
    return pl.ds(pl.multiple_of(place * size, size), size)


def out_grad_kernel(
    cot_hbm, weight_hbm, q_hbm, k_hbm, v_hbm, same_ref, other_ref, cot_ref, weight_ref, sem
):
    core = lax.axis_index("seq") % 2
    cut = weight_ref.shape[0] // 2
    cot_copy = pltpu.make_async_copy(cot_hbm, cot_ref, sem.at[0])
    cot_copy.start()
    halves = ((other_ref, 1 - core), (same_ref, core))
    weight_copies = []
    for place, (_, half) in enumerate(halves):
        weight_copies.append(
            pltpu.make_async_copy(
                weight_hbm.at[at(half, cut)], weight_ref.at[at(place, cut)], sem.at[1 + place]
            )
        )
        weight_copies[-1].start()
    plain_copies = []
    for place, (target, half) in enumerate(halves):
        first = 0
        for which, source in enumerate((q_hbm, k_hbm, v_hbm)):
            cols = source.shape[1] // 2
            plain_copies.append(
                pltpu.make_async_copy(
                    source.at[:, at(half, cols)],
                    target.at[:, pl.ds(first, cols)],
                    sem.at[3 + 3 * place + which],
                )
            )
            plain_copies[-1].start()
            first += cols
    cot_copy.wait()
    for place, (target, _) in enumerate(halves):
        weight_copies[place].wait()
        grads_t = dot_nt(weight_ref[place * cut : (place + 1) * cut], cot_ref[...])
        for h in range(cut // HEAD_SIZE):
            target[:, first + h * HEAD_SIZE : first + (h + 1) * HEAD_SIZE] = grads_t[
                h * HEAD_SIZE : (h + 1) * HEAD_SIZE
            ].astype(jnp.bfloat16)
    for copy in plain_copies:
        copy.wait()


def turn_kernel(parts, normed_hbm, cot_hbm, _, __, turned_ref, done_ref, normed_ref, cot_ref, sem):
    cut = normed_ref.shape[1] // parts
    done_ref[...] = jnp.zeros_like(done_ref)
    copies = []
    for which, (source, target) in enumerate(((normed_hbm, normed_ref), (cot_hbm, cot_ref))):
        copies.append(pltpu.make_async_copy(source, target, sem.at[which]))
        copies[-1].start()
    for which, ref in enumerate((normed_ref, cot_ref)):
        copies[which].wait()
        turned = ref[...].astype(jnp.float32).T.astype(jnp.bfloat16)
        for part in range(parts):
            turned_ref[part, which] = turned[part * cut : (part + 1) * cut]


def attention_kernel(blocks, *refs):
    attention_body(refs[:blocks], *refs[blocks:])


def attention_body(
    block_refs,
    _,
    dx_own_ref,
    dx_far_ref,
    attn_ref,
    dv_ref,
    gathered_ref,
    score_even_ref,
    score_odd_ref,
    prob_ref,
    grad_t_ref,
    delta_ref,
    query_ref,
    value_t_ref,
    key_t_ref,
    dq_t_ref,
    dk_ref,
):
    me = lax.axis_index("seq")
    core, chip = me % 2, me // 2
    rows = dx_own_ref.shape[0]
    for apart, source in enumerate(block_refs):
        gathered_ref[at(me ^ apart, rows)] = source[...]
    tokens = gathered_ref.shape[0]
    size = 2 * rows
    steps = tokens // size
    wide = QUERIES_PER_KEY * size
    heads = QUERIES_PER_KEY
    key_cols = slice(heads * HEAD_SIZE, (heads + 1) * HEAD_SIZE)
    value_cols = slice((heads + 1) * HEAD_SIZE, (heads + 2) * HEAD_SIZE)
    grad_base = (heads + 2) * HEAD_SIZE
    value_t_ref[...] = gathered_ref[:, value_cols].T
    key_t_ref[...] = gathered_ref[:, key_cols].T
    key_place = lax.broadcasted_iota(jnp.int32, (size, wide), 0)
    query_place = lax.broadcasted_iota(jnp.int32, (size, wide), 1) % size
    allowed = key_place <= query_place

    for step in range(steps):
        span = (step + 1) * size
        own = slice(step * size, span)
        lanes = slice(step * wide, (step + 1) * wide)
        score_ref = score_odd_ref if step % 2 else score_even_ref
        queries = jnp.concatenate(
            [gathered_ref[own, h * HEAD_SIZE : (h + 1) * HEAD_SIZE] for h in range(heads)], axis=0
        )
        query_ref[lanes] = queries
        top = None
        for piece in range(step + 1):
            part = slice(piece * size, (piece + 1) * size)
            scores = dot_nt(gathered_ref[part, key_cols], queries)
            if piece == step:
                scores = jnp.where(allowed, scores, excluded)
            score_ref[part] = scores
            largest = jnp.max(scores.reshape(size // 8, 8, wide), axis=0)
            top = largest if top is None else jnp.maximum(top, largest)
        top = jnp.max(top, axis=0, keepdims=True)
        total = None
        for piece in range(step + 1):
            part = slice(piece * size, (piece + 1) * size)
            weights = jnp.exp2((score_ref[part] - top) * log2_scale)
            prob_ref[part, lanes] = weights.astype(jnp.bfloat16)
            summed = jnp.sum(weights.reshape(size // 8, 8, wide), axis=0)
            total = summed if total is None else total + summed
        inverse = 1.0 / jnp.sum(total, axis=0, keepdims=True)
        attn = dot_nn(value_t_ref[:, :span], prob_ref[:span, lanes]) * inverse
        for h in range(heads):
            attn_ref[h * HEAD_SIZE : (h + 1) * HEAD_SIZE, own] = attn[
                :, h * size : (h + 1) * size
            ].astype(jnp.bfloat16)
        grads_t = jnp.concatenate(
            [
                gathered_ref[
                    block * rows : (block + 1) * rows,
                    grad_base + h * HEAD_SIZE : grad_base + (h + 1) * HEAD_SIZE,
                ]
                for h in range(heads)
                for block in (2 * step, 2 * step + 1)
            ],
            axis=1,
        )
        grads_t = (grads_t.astype(jnp.float32) * inverse).astype(jnp.bfloat16)
        grad_t_ref[:, lanes] = grads_t
        delta_ref[:, lanes] = jnp.sum(grads_t.astype(jnp.float32) * attn, axis=0, keepdims=True)

    for step in range(steps):
        own = slice(step * size, (step + 1) * size)
        dv_ref[own] = dot_nt(prob_ref[own, step * wide :], grad_t_ref[:, step * wide :]).astype(
            jnp.bfloat16
        )

    dq_t_ref[...] = jnp.zeros_like(dq_t_ref)
    dk_ref[...] = jnp.zeros_like(dk_ref)
    for step in range(steps):
        key_step = jnp.minimum(chip, step)
        query_step = jnp.maximum(chip, step)
        dprob = dot_nn(
            gathered_ref[at(key_step, size), value_cols], grad_t_ref[:, at(query_step, wide)]
        )
        dscore = (
            prob_ref[at(key_step, size), at(query_step, wide)].astype(jnp.float32)
            * (dprob - delta_ref[:, at(query_step, wide)])
        ).astype(jnp.bfloat16)

        @pl.when(step <= chip)
        def _():
            dq_t_ref[...] += dot_nn(key_t_ref[:, at(key_step, size)], dscore)

        @pl.when(step >= chip)
        def _():
            dk_ref[...] += dot_nn(dscore, query_ref[at(query_step, wide)])

    for target, half in ((dx_far_ref, 1 - core), (dx_own_ref, core)):
        for h in range(heads):
            target[:, h * HEAD_SIZE : (h + 1) * HEAD_SIZE] = (
                (logit_scale * dq_t_ref[:, at(2 * h + half, rows)])
                .T.astype(jnp.bfloat16)
            )
        target[:, key_cols] = (logit_scale * dk_ref[at(half, rows)]).astype(jnp.bfloat16)
        target[:, value_cols] = dv_ref[at(2 * chip + half, rows)]


def input_terms_kernel(
    apart_groups, own_ref, far_ref, wq_ref, wk_ref, wv_ref, *refs
):
    terms, dx_ref = refs[:-1], refs[-1]
    core = lax.axis_index("seq") % 2
    group = lax.axis_index("head")
    q_cols = wq_ref.shape[1] // 2
    kv_cols = wk_ref.shape[1] // 2
    for source, half in ((own_ref, core), (far_ref, 1 - core)):
        dx_ref[:, at(half, q_cols)] = source[:, :q_cols]
        dx_ref[:, pl.ds(pl.multiple_of(2 * q_cols + half * kv_cols, kv_cols), kv_cols)] = source[
            :, q_cols : q_cols + kv_cols
        ]
        dx_ref[
            :, pl.ds(pl.multiple_of(2 * q_cols + (2 + half) * kv_cols, kv_cols), kv_cols)
        ] = source[:, q_cols + kv_cols :]
    for apart, target in zip(apart_groups, terms):
        cut = target.shape[0]
        place = at(group ^ apart, cut)
        target[...] = (
            dot_nt(wq_ref[place], dx_ref[:, : 2 * q_cols])
            + dot_nt(wk_ref[place], dx_ref[:, 2 * q_cols : 2 * q_cols + 2 * kv_cols])
            + dot_nt(wv_ref[place], dx_ref[:, 2 * q_cols + 2 * kv_cols :])
        ).astype(target.dtype)


def weight_grad_kernel(
    turned_ref, attn_ref, far_attn_ref, dv_ref, far_dv_ref, wvalue_ref, woutput_ref, done_ref, joined_ref
):
    done_ref[...] = jnp.zeros_like(done_ref)
    core = lax.axis_index("seq") % 2
    parts = turned_ref.shape[0]
    rows = turned_ref.shape[3]
    for part in range(parts):
        joined_ref[:, :, part * rows : (part + 1) * rows] = turned_ref[part]
    for half, attn, dv in ((core, attn_ref, dv_ref), (1 - core, far_attn_ref, far_dv_ref)):
        wvalue_ref[:, at(half, dv.shape[1])] = dot_nn(joined_ref[0], dv[...])
        woutput_ref[:, at(half, attn.shape[0])] = dot_nt(joined_ref[1], attn[...])


def sum_kernel(_, own_ref, *refs):
    total = own_ref[...]
    for arrived_ref in refs[:-1]:
        total = total + arrived_ref[...].astype(jnp.float32)
    refs[-1][...] = total.astype(jnp.bfloat16)


def kernel_call(body, outs, operands, in_vmem=(), scratch=(), flops=0, moved=0, room=16):
    vmem = pl.BlockSpec(memory_space=pltpu.VMEM)
    hbm = pl.BlockSpec(memory_space=pltpu.HBM)
    return pl.pallas_call(
        body,
        out_shape=outs,
        in_specs=[vmem if place in in_vmem else hbm for place in range(len(operands))],
        out_specs=jax.tree.map(lambda _: vmem, outs),
        scratch_shapes=list(scratch),
        compiler_params=pltpu.CompilerParams(vmem_limit_bytes=room * 1024 * 1024),
        cost_estimate=pl.CostEstimate(flops=flops, bytes_accessed=moved, transcendentals=0),
    )(*operands)


def swapped(value, axis, apart):
    count = lax.axis_size(axis)
    return lax.ppermute(value, axis, [(place, place ^ apart) for place in range(count)])


def gathered_plan(
    normed_input,
    stored_queries,
    stored_keys,
    stored_values,
    query_weight,
    key_matrix,
    value_matrix,
    output_weight,
    out_cotangent,
):
    bf16, f32 = jnp.bfloat16, jnp.float32
    rows, model = normed_input.shape
    blocks = lax.axis_size("seq")
    groups = lax.axis_size("head")
    tokens = rows * blocks
    q_cols = stored_queries.shape[1] // 2
    kv_cols = HEAD_SIZE
    wide = 2 * QUERIES_PER_KEY * rows
    packed_cols = 2 * q_cols + 2 * kv_cols
    shape = jax.ShapeDtypeStruct
    same, other = kernel_call(
        out_grad_kernel,
        (shape((rows, packed_cols), bf16),) * 2,
        (out_cotangent, output_weight, stored_queries, stored_keys, stored_values),
        scratch=(
            pltpu.VMEM(out_cotangent.shape, bf16),
            pltpu.VMEM(output_weight.shape, bf16),
            pltpu.SemaphoreType.DMA((9,)),
        ),
        flops=4 * rows * model * q_cols,
        moved=2 * model * (rows + 2 * q_cols),
        room=63,
    )
    held = {0: same}
    for apart in range(2, blocks):
        lowest, highest = 2, 1 << (apart.bit_length() - 1)
        while not apart & lowest:
            lowest *= 2
        through = lowest if apart % 2 else highest
        if lowest == highest:
            held[apart] = swapped(other if apart % 2 else same, "seq", apart)
        else:
            held[apart] = swapped(held[apart ^ through], "seq", through)
    held[1] = swapped(other, "seq", 1)
    turned, turn_done = kernel_call(
        functools.partial(turn_kernel, blocks),
        (shape((blocks, 2, model // blocks, rows), bf16), shape((8, HEAD_SIZE), f32)),
        (normed_input, out_cotangent, held[2], held[blocks // 2 + 1]),
        scratch=(
            pltpu.VMEM(normed_input.shape, bf16),
            pltpu.VMEM(out_cotangent.shape, bf16),
            pltpu.SemaphoreType.DMA((2,)),
        ),
        moved=256 * rows * model,
    )
    turned = lax.all_to_all(turned, "seq", 0, 0)
    dx_own, dx_far, attn, dv = kernel_call(
        functools.partial(attention_kernel, blocks),
        (
            shape((rows, q_cols + 2 * kv_cols), bf16),
            shape((rows, q_cols + 2 * kv_cols), bf16),
            shape((q_cols, tokens), bf16),
            shape((tokens, kv_cols), bf16),
        ),
        [held[apart] for apart in range(blocks)] + [turn_done],
        in_vmem=range(blocks),
        scratch=(
            pltpu.VMEM((tokens, packed_cols), bf16),
            pltpu.VMEM((tokens, wide), f32),
            pltpu.VMEM((tokens, wide), f32),
            pltpu.VMEM((tokens, tokens * QUERIES_PER_KEY), bf16),
            pltpu.VMEM((HEAD_SIZE, tokens * QUERIES_PER_KEY), bf16),
            pltpu.VMEM((1, tokens * QUERIES_PER_KEY), f32),
            pltpu.VMEM((tokens * QUERIES_PER_KEY, HEAD_SIZE), bf16),
            pltpu.VMEM((HEAD_SIZE, tokens), bf16),
            pltpu.VMEM((HEAD_SIZE, tokens), bf16),
            pltpu.VMEM((HEAD_SIZE, wide), f32),
            pltpu.VMEM((2 * rows, HEAD_SIZE), f32),
        ),
        flops=8 * tokens * tokens * q_cols,
        moved=2 * tokens * packed_cols,
    )
    dx_got = swapped(dx_far, "seq", 1)
    aparts = tuple(range(groups - 1, -1, -1))
    terms = {}
    for chosen in (aparts[: groups // 2], aparts[groups // 2 :]):
        made = kernel_call(
            functools.partial(input_terms_kernel, chosen),
            tuple(shape((model // groups, rows), bf16 if apart else f32) for apart in chosen),
            (dx_own, dx_got, query_weight, key_matrix, value_matrix),
            in_vmem=range(5),
            scratch=(pltpu.VMEM((rows, 2 * (q_cols + 2 * kv_cols)), bf16),),
            flops=2 * rows * model * (q_cols + 2 * kv_cols),
            moved=2 * model * (q_cols + 2 * kv_cols),
            room=4,
        )
        terms.update(zip(chosen, made))
    arrived = [swapped(terms[apart], "head", apart) for apart in aparts[:-1]]
    grad_wvalue, grad_woutput, weights_done = kernel_call(
        weight_grad_kernel,
        (
            shape((model // blocks, 2 * kv_cols), f32),
            shape((model // blocks, 2 * q_cols), f32),
            shape((8, HEAD_SIZE), f32),
        ),
        (turned, attn, swapped(attn, "seq", 1), dv, swapped(dv, "seq", 1)),
        in_vmem=range(5),
        scratch=(pltpu.VMEM((2, model // blocks, tokens), bf16),),
        flops=4 * tokens * (model // blocks) * (q_cols + kv_cols),
        moved=4 * (model // blocks) * (tokens + 2 * q_cols + 2 * kv_cols),
    )
    grad_input = kernel_call(
        sum_kernel,
        shape((model // groups, rows), bf16),
        (weights_done, terms[0], *arrived),
        in_vmem=range(1, groups + 1),
        moved=4 * groups * (model // groups) * rows,
    )
    return (grad_input.T, grad_wvalue, grad_woutput.T)


def power_of_two(count):
    return count & (count - 1) == 0


def local(normed_input, stored_queries, stored_keys, *others):
    blocks, groups = lax.axis_size("seq"), lax.axis_size("head")
    whole_window = normed_input.shape[0] * blocks <= WINDOW_LENGTH
    two_heads = stored_keys.shape[1] == 2 * HEAD_SIZE
    paired = blocks > 1 and power_of_two(blocks) and power_of_two(groups)
    plan = gathered_plan if whole_window and two_heads and paired else windowed_plan
    return plan(normed_input, stored_queries, stored_keys, *others)


def windowed_plan(
    normed_input,
    stored_queries,
    stored_keys,
    stored_values,
    query_weight,
    key_matrix,
    value_matrix,
    output_weight,
    out_cotangent,
):
    tok_rows = normed_input.shape[0]
    blocks_seq = lax.axis_size("seq")
    seq_place = lax.axis_index("seq")
    reach_blocks = min(WINDOW_LENGTH // tok_rows, blocks_seq - 1)
    kv_heads = stored_keys.shape[1] // HEAD_SIZE
    output_gradient = jnp.dot(
        out_cotangent, output_weight.T, preferred_element_type=jnp.float32
    ).astype(jnp.bfloat16)
    pieces = [(stored_keys, stored_values)]
    current = (stored_keys, stored_values)
    for relay_step in range(reach_blocks):
        current = passed_along((current[0], current[1]), "seq", 1)
        pieces = [current] + pieces
    key_window = jnp.concatenate([piece[0] for piece in pieces], axis=0)
    value_window = jnp.concatenate([piece[1] for piece in pieces], axis=0)
    key_span = key_window.shape[0]
    query_pos = seq_place * tok_rows + jnp.arange(tok_rows, dtype=jnp.int32)
    key_pos = (seq_place - reach_blocks) * tok_rows + jnp.arange(key_span, dtype=jnp.int32)
    pos_gap = query_pos[:, None] - key_pos[None, :]
    allowed = (pos_gap >= 0) & (pos_gap < WINDOW_LENGTH) & (key_pos >= 0)[None, :]
    allowed_rows = jnp.tile(allowed, (QUERIES_PER_KEY, 1))
    query_stack = (
        stored_queries.reshape(tok_rows, kv_heads, QUERIES_PER_KEY, HEAD_SIZE)
        .transpose(1, 2, 0, 3)
        .reshape(kv_heads, QUERIES_PER_KEY * tok_rows, HEAD_SIZE)
    )
    grad_stack = (
        output_gradient.reshape(tok_rows, kv_heads, QUERIES_PER_KEY, HEAD_SIZE)
        .transpose(1, 2, 0, 3)
        .reshape(kv_heads, QUERIES_PER_KEY * tok_rows, HEAD_SIZE)
    )
    key_stack = key_window.reshape(key_span, kv_heads, HEAD_SIZE).transpose(1, 0, 2)
    value_stack = value_window.reshape(key_span, kv_heads, HEAD_SIZE).transpose(1, 0, 2)

    def per_head(head_items):
        query_head, key_head, value_head, grad_head = head_items
        attention_logits = logit_scale * jnp.dot(
            query_head, key_head.T, preferred_element_type=jnp.float32
        )
        masked = jnp.where(allowed_rows, attention_logits, -jnp.inf)
        row_top = jnp.max(masked, axis=1, keepdims=True)
        exp_scores = jnp.exp(masked - row_top)
        attn_prob = exp_scores / jnp.sum(exp_scores, axis=1, keepdims=True)
        probability_halfwidth = attn_prob.astype(jnp.bfloat16)
        attn_head = jnp.dot(
            probability_halfwidth, value_head, preferred_element_type=jnp.float32
        ).astype(jnp.bfloat16)
        row_delta = jnp.sum(
            grad_head.astype(jnp.float32) * attn_head.astype(jnp.float32), axis=1, keepdims=True
        )
        probability_gradient = jnp.dot(grad_head, value_head.T, preferred_element_type=jnp.float32)
        score_gradient = (attn_prob * (probability_gradient - row_delta)).astype(jnp.bfloat16)
        qgrad_head = (
            logit_scale * jnp.dot(score_gradient, key_head, preferred_element_type=jnp.float32)
        ).astype(jnp.bfloat16)
        key_partial = logit_scale * jnp.dot(
            score_gradient.T, query_head, preferred_element_type=jnp.float32
        )
        value_partial = jnp.dot(
            probability_halfwidth.T, grad_head, preferred_element_type=jnp.float32
        )
        return (attn_head, qgrad_head, key_partial, value_partial)

    attn_all, qgrad_all, key_all, value_all = lax.map(
        per_head, (query_stack, key_stack, value_stack, grad_stack)
    )
    attention_output = (
        attn_all.reshape(kv_heads, QUERIES_PER_KEY, tok_rows, HEAD_SIZE)
        .transpose(2, 0, 1, 3)
        .reshape(tok_rows, kv_heads * QUERIES_PER_KEY * HEAD_SIZE)
    )
    query_gradient = (
        qgrad_all.reshape(kv_heads, QUERIES_PER_KEY, tok_rows, HEAD_SIZE)
        .transpose(2, 0, 1, 3)
        .reshape(tok_rows, kv_heads * QUERIES_PER_KEY * HEAD_SIZE)
    )
    key_terms = key_all.transpose(1, 0, 2).reshape(key_span, kv_heads * HEAD_SIZE)
    value_terms = value_all.transpose(1, 0, 2).reshape(key_span, kv_heads * HEAD_SIZE)

    def take_slot(terms, slot_index):
        return terms[slot_index * tok_rows : (slot_index + 1) * tok_rows]

    key_sum = take_slot(key_terms, reach_blocks)
    value_sum = take_slot(value_terms, reach_blocks)
    for distance in range(1, reach_blocks + 1):
        received = passed_along(
            (
                take_slot(key_terms, reach_blocks - distance),
                take_slot(value_terms, reach_blocks - distance),
            ),
            "seq",
            -distance,
        )
        key_sum = key_sum + received[0]
        value_sum = value_sum + received[1]
    grad_key = key_sum.astype(jnp.bfloat16)
    grad_value = value_sum.astype(jnp.bfloat16)
    input_terms = jnp.dot(query_gradient, query_weight.T, preferred_element_type=jnp.float32)
    input_terms = input_terms + jnp.dot(grad_key, key_matrix.T, preferred_element_type=jnp.float32)
    input_terms = input_terms + jnp.dot(
        grad_value, value_matrix.T, preferred_element_type=jnp.float32
    )
    grad_input = lax.psum_scatter(input_terms, "head", scatter_dimension=1, tiled=True).astype(
        jnp.bfloat16
    )
    value_cols = grad_value.shape[1]
    input_cols = normed_input.T
    cot_cols = out_cotangent.T
    gathered = lax.psum_scatter(
        jnp.concatenate(
            [
                jnp.dot(input_cols, grad_value, preferred_element_type=jnp.float32),
                jnp.dot(cot_cols, attention_output, preferred_element_type=jnp.float32),
            ],
            axis=1,
        ),
        "seq",
        scatter_dimension=0,
        tiled=True,
    )
    grad_wvalue = gathered[:, :value_cols]
    grad_woutput = gathered[:, value_cols:].T
    return (grad_input, grad_wvalue, grad_woutput)


def solution(mesh):
    placed = (
        P("seq", None),
        P("seq", "head"),
        P("seq", "head"),
        P("seq", "head"),
        P(None, "head"),
        P(None, "head"),
        P(None, "head"),
        P("head", None),
        P("seq", None),
    )
    return jax.shard_map(
        local,
        mesh=mesh,
        in_specs=placed,
        out_specs=(P("seq", "head"), P("seq", "head"), P("head", "seq")),
        check_vma=False,
    )
```

```python
import functools

import jax
import jax.numpy as jnp
from jax import lax
from jax.experimental import pallas as pl
from jax.experimental.pallas import tpu as pltpu
from jax.sharding import PartitionSpec as P

HEAD_SIZE = 128
WINDOW_LENGTH = 4096
QUERIES_PER_KEY = 2


logit_scale = 1.0 / 12.0
log2_scale = 1.4426950408889634 / 12.0
excluded = -1e30


def passed_along(value, axis, steps):
    count = lax.axis_size(axis)
    leading, last = (max(0, -steps), min(count, count - steps))
    return lax.ppermute(value, axis, [(source, source + steps) for source in range(leading, last)])


NT = (((1,), (1,)), ((), ()))


def dot_nt(left, right):
    return lax.dot_general(left, right, NT, preferred_element_type=jnp.float32)


def dot_nn(left, right):
    return jnp.dot(left, right, preferred_element_type=jnp.float32)


def at(place, size):
    return pl.ds(pl.multiple_of(place * size, size), size)


def out_grad_kernel(
    cot_hbm, weight_hbm, q_hbm, k_hbm, v_hbm, same_ref, other_ref, cot_ref, weight_ref, sem
):
    core = lax.axis_index("seq") % 2
    cut = weight_ref.shape[0] // 2
    cot_copy = pltpu.make_async_copy(cot_hbm, cot_ref, sem.at[0])
    cot_copy.start()
    halves = ((other_ref, 1 - core), (same_ref, core))
    weight_copies = []
    for place, (_, half) in enumerate(halves):
        weight_copies.append(
            pltpu.make_async_copy(
                weight_hbm.at[at(half, cut)], weight_ref.at[at(place, cut)], sem.at[1 + place]
            )
        )
        weight_copies[-1].start()
    plain_copies = []
    for place, (target, half) in enumerate(halves):
        first = 0
        for which, source in enumerate((q_hbm, k_hbm, v_hbm)):
            cols = source.shape[1] // 2
            plain_copies.append(
                pltpu.make_async_copy(
                    source.at[:, at(half, cols)],
                    target.at[:, pl.ds(first, cols)],
                    sem.at[3 + 3 * place + which],
                )
            )
            plain_copies[-1].start()
            first += cols
    cot_copy.wait()
    for place, (target, _) in enumerate(halves):
        weight_copies[place].wait()
        grads_t = dot_nt(weight_ref[place * cut : (place + 1) * cut], cot_ref[...])
        for h in range(cut // HEAD_SIZE):
            target[:, first + h * HEAD_SIZE : first + (h + 1) * HEAD_SIZE] = grads_t[
                h * HEAD_SIZE : (h + 1) * HEAD_SIZE
            ].astype(jnp.bfloat16)
    for copy in plain_copies:
        copy.wait()


def turn_kernel(normed_hbm, cot_hbm, _, __, *refs):
    turned_refs, (done_ref, normed_ref, cot_ref, turned_ref, sem) = refs[:-5], refs[-5:]
    me = lax.axis_index("seq")
    done_ref[...] = jnp.zeros_like(done_ref)
    cut = turned_refs[0].shape[1]
    copies = []
    for which, (source, target) in enumerate(((normed_hbm, normed_ref), (cot_hbm, cot_ref))):
        copies.append(pltpu.make_async_copy(source, target, sem.at[which]))
        copies[-1].start()
    for which, ref in enumerate((normed_ref, cot_ref)):
        copies[which].wait()
        turned_ref[which] = ref[...].astype(jnp.float32).T.astype(jnp.bfloat16)
        for apart, target in enumerate(turned_refs):
            target[which] = turned_ref[which, at(me ^ apart, cut)]


def attention_kernel(blocks, *refs):
    attention_body(refs[:blocks], *refs[blocks:])


def attention_body(
    block_refs,
    _,
    dx_own_ref,
    dx_far_ref,
    attn_ref,
    dv_ref,
    gathered_ref,
    score_even_ref,
    score_odd_ref,
    prob_ref,
    grad_t_ref,
    delta_ref,
    query_ref,
    value_t_ref,
    key_t_ref,
    dq_t_ref,
    dk_ref,
):
    me = lax.axis_index("seq")
    core, chip = me % 2, me // 2
    rows = dx_own_ref.shape[0]
    for apart, source in enumerate(block_refs):
        gathered_ref[at(me ^ apart, rows)] = source[...]
    tokens = gathered_ref.shape[0]
    size = 2 * rows
    steps = tokens // size
    wide = QUERIES_PER_KEY * size
    heads = QUERIES_PER_KEY
    key_cols = slice(heads * HEAD_SIZE, (heads + 1) * HEAD_SIZE)
    value_cols = slice((heads + 1) * HEAD_SIZE, (heads + 2) * HEAD_SIZE)
    grad_base = (heads + 2) * HEAD_SIZE
    value_t_ref[...] = gathered_ref[:, value_cols].T
    key_t_ref[...] = gathered_ref[:, key_cols].T
    key_place = lax.broadcasted_iota(jnp.int32, (size, wide), 0)
    query_place = lax.broadcasted_iota(jnp.int32, (size, wide), 1) % size
    allowed = key_place <= query_place

    for step in range(steps):
        span = (step + 1) * size
        own = slice(step * size, span)
        lanes = slice(step * wide, (step + 1) * wide)
        score_ref = score_odd_ref if step % 2 else score_even_ref
        queries = jnp.concatenate(
            [gathered_ref[own, h * HEAD_SIZE : (h + 1) * HEAD_SIZE] for h in range(heads)], axis=0
        )
        query_ref[lanes] = queries
        top = None
        for piece in range(step + 1):
            part = slice(piece * size, (piece + 1) * size)
            scores = dot_nt(gathered_ref[part, key_cols], queries)
            if piece == step:
                scores = jnp.where(allowed, scores, excluded)
            score_ref[part] = scores
            largest = jnp.max(scores.reshape(size // 8, 8, wide), axis=0)
            top = largest if top is None else jnp.maximum(top, largest)
        top = jnp.max(top, axis=0, keepdims=True)
        total = None
        for piece in range(step + 1):
            part = slice(piece * size, (piece + 1) * size)
            weights = jnp.exp2((score_ref[part] - top) * log2_scale)
            prob_ref[part, lanes] = weights.astype(jnp.bfloat16)
            summed = jnp.sum(weights.reshape(size // 8, 8, wide), axis=0)
            total = summed if total is None else total + summed
        inverse = 1.0 / jnp.sum(total, axis=0, keepdims=True)
        attn = dot_nn(value_t_ref[:, :span], prob_ref[:span, lanes]) * inverse
        for h in range(heads):
            attn_ref[h * HEAD_SIZE : (h + 1) * HEAD_SIZE, own] = attn[
                :, h * size : (h + 1) * size
            ].astype(jnp.bfloat16)
        grads_t = jnp.concatenate(
            [
                gathered_ref[
                    block * rows : (block + 1) * rows,
                    grad_base + h * HEAD_SIZE : grad_base + (h + 1) * HEAD_SIZE,
                ]
                for h in range(heads)
                for block in (2 * step, 2 * step + 1)
            ],
            axis=1,
        )
        grads_t = (grads_t.astype(jnp.float32) * inverse).astype(jnp.bfloat16)
        grad_t_ref[:, lanes] = grads_t
        delta_ref[:, lanes] = jnp.sum(grads_t.astype(jnp.float32) * attn, axis=0, keepdims=True)

    for step in range(steps):
        own = slice(step * size, (step + 1) * size)
        dv_ref[own] = dot_nt(prob_ref[own, step * wide :], grad_t_ref[:, step * wide :]).astype(
            jnp.bfloat16
        )

    dq_t_ref[...] = jnp.zeros_like(dq_t_ref)
    dk_ref[...] = jnp.zeros_like(dk_ref)
    for step in range(steps):
        key_step = jnp.minimum(chip, step)
        query_step = jnp.maximum(chip, step)
        dprob = dot_nn(
            gathered_ref[at(key_step, size), value_cols], grad_t_ref[:, at(query_step, wide)]
        )
        dscore = (
            prob_ref[at(key_step, size), at(query_step, wide)].astype(jnp.float32)
            * (dprob - delta_ref[:, at(query_step, wide)])
        ).astype(jnp.bfloat16)

        @pl.when(step <= chip)
        def _():
            dq_t_ref[...] += dot_nn(key_t_ref[:, at(key_step, size)], dscore)

        @pl.when(step >= chip)
        def _():
            dk_ref[...] += dot_nn(dscore, query_ref[at(query_step, wide)])

    for target, half in ((dx_far_ref, 1 - core), (dx_own_ref, core)):
        for h in range(heads):
            target[:, h * HEAD_SIZE : (h + 1) * HEAD_SIZE] = (
                (logit_scale * dq_t_ref[:, at(2 * h + half, rows)])
                .T.astype(jnp.bfloat16)
            )
        target[:, key_cols] = (logit_scale * dk_ref[at(half, rows)]).astype(jnp.bfloat16)
        target[:, value_cols] = dv_ref[at(2 * chip + half, rows)]


def input_terms_kernel(
    apart_groups, own_ref, far_ref, wq_ref, wk_ref, wv_ref, *refs
):
    terms, dx_ref = refs[:-1], refs[-1]
    core = lax.axis_index("seq") % 2
    group = lax.axis_index("head")
    q_cols = wq_ref.shape[1] // 2
    kv_cols = wk_ref.shape[1] // 2
    for source, half in ((own_ref, core), (far_ref, 1 - core)):
        dx_ref[:, at(half, q_cols)] = source[:, :q_cols]
        dx_ref[:, pl.ds(pl.multiple_of(2 * q_cols + half * kv_cols, kv_cols), kv_cols)] = source[
            :, q_cols : q_cols + kv_cols
        ]
        dx_ref[
            :, pl.ds(pl.multiple_of(2 * q_cols + (2 + half) * kv_cols, kv_cols), kv_cols)
        ] = source[:, q_cols + kv_cols :]
    for apart, target in zip(apart_groups, terms):
        cut = target.shape[0]
        place = at(group ^ apart, cut)
        target[...] = (
            dot_nt(wq_ref[place], dx_ref[:, : 2 * q_cols])
            + dot_nt(wk_ref[place], dx_ref[:, 2 * q_cols : 2 * q_cols + 2 * kv_cols])
            + dot_nt(wv_ref[place], dx_ref[:, 2 * q_cols + 2 * kv_cols :])
        ).astype(target.dtype)


def weight_grad_kernel(
    attn_ref, far_attn_ref, dv_ref, far_dv_ref, *refs
):
    column_refs, (wvalue_ref, woutput_ref, done_ref, joined_ref) = refs[:-4], refs[-4:]
    done_ref[...] = jnp.zeros_like(done_ref)
    me = lax.axis_index("seq")
    core = me % 2
    for apart, ref in enumerate(column_refs):
        joined_ref[:, :, at(me ^ apart, ref.shape[2])] = ref[...]
    for half, attn, dv in ((core, attn_ref, dv_ref), (1 - core, far_attn_ref, far_dv_ref)):
        wvalue_ref[:, at(half, dv.shape[1])] = dot_nn(joined_ref[0], dv[...])
        woutput_ref[:, at(half, attn.shape[0])] = dot_nt(joined_ref[1], attn[...])


def sum_kernel(_, own_ref, *refs):
    total = own_ref[...]
    for arrived_ref in refs[:-1]:
        total = total + arrived_ref[...].astype(jnp.float32)
    refs[-1][...] = total.astype(jnp.bfloat16)


def kernel_call(body, outs, operands, in_vmem=(), scratch=(), flops=0, moved=0, room=16):
    vmem = pl.BlockSpec(memory_space=pltpu.VMEM)
    hbm = pl.BlockSpec(memory_space=pltpu.HBM)
    return pl.pallas_call(
        body,
        out_shape=outs,
        in_specs=[vmem if place in in_vmem else hbm for place in range(len(operands))],
        out_specs=jax.tree.map(lambda _: vmem, outs),
        scratch_shapes=list(scratch),
        compiler_params=pltpu.CompilerParams(vmem_limit_bytes=room * 1024 * 1024),
        cost_estimate=pl.CostEstimate(flops=flops, bytes_accessed=moved, transcendentals=0),
    )(*operands)


def swapped(value, axis, apart):
    count = lax.axis_size(axis)
    return lax.ppermute(value, axis, [(place, place ^ apart) for place in range(count)])


def gathered_plan(
    normed_input,
    stored_queries,
    stored_keys,
    stored_values,
    query_weight,
    key_matrix,
    value_matrix,
    output_weight,
    out_cotangent,
):
    bf16, f32 = jnp.bfloat16, jnp.float32
    rows, model = normed_input.shape
    blocks = lax.axis_size("seq")
    groups = lax.axis_size("head")
    tokens = rows * blocks
    q_cols = stored_queries.shape[1] // 2
    kv_cols = HEAD_SIZE
    wide = 2 * QUERIES_PER_KEY * rows
    packed_cols = 2 * q_cols + 2 * kv_cols
    shape = jax.ShapeDtypeStruct
    same, other = kernel_call(
        out_grad_kernel,
        (shape((rows, packed_cols), bf16),) * 2,
        (out_cotangent, output_weight, stored_queries, stored_keys, stored_values),
        scratch=(
            pltpu.VMEM(out_cotangent.shape, bf16),
            pltpu.VMEM(output_weight.shape, bf16),
            pltpu.SemaphoreType.DMA((9,)),
        ),
        flops=4 * rows * model * q_cols,
        moved=2 * model * (rows + 2 * q_cols),
        room=63,
    )
    held = {0: same}
    for apart in range(2, blocks):
        lowest, highest = 2, 1 << (apart.bit_length() - 1)
        while not apart & lowest:
            lowest *= 2
        through = lowest if apart % 2 else highest
        if lowest == highest:
            held[apart] = swapped(other if apart % 2 else same, "seq", apart)
        else:
            held[apart] = swapped(held[apart ^ through], "seq", through)
    held[1] = swapped(other, "seq", 1)
    *turned, turn_done = kernel_call(
        turn_kernel,
        (shape((2, model // blocks, rows), bf16),) * blocks + (shape((8, HEAD_SIZE), f32),),
        (normed_input, out_cotangent, held[2], held[blocks // 2 + 1]),
        scratch=(
            pltpu.VMEM(normed_input.shape, bf16),
            pltpu.VMEM(out_cotangent.shape, bf16),
            pltpu.VMEM((2, model, rows), bf16),
            pltpu.SemaphoreType.DMA((2,)),
        ),
        moved=8 * rows * model,
    )
    columns = [turned[0]] + [
        swapped(turned[apart], "seq", apart) for apart in range(1, blocks)
    ]
    dx_own, dx_far, attn, dv = kernel_call(
        functools.partial(attention_kernel, blocks),
        (
            shape((rows, q_cols + 2 * kv_cols), bf16),
            shape((rows, q_cols + 2 * kv_cols), bf16),
            shape((q_cols, tokens), bf16),
            shape((tokens, kv_cols), bf16),
        ),
        [held[apart] for apart in range(blocks)] + [turn_done],
        in_vmem=range(blocks),
        scratch=(
            pltpu.VMEM((tokens, packed_cols), bf16),
            pltpu.VMEM((tokens, wide), f32),
            pltpu.VMEM((tokens, wide), f32),
            pltpu.VMEM((tokens, tokens * QUERIES_PER_KEY), bf16),
            pltpu.VMEM((HEAD_SIZE, tokens * QUERIES_PER_KEY), bf16),
            pltpu.VMEM((1, tokens * QUERIES_PER_KEY), f32),
            pltpu.VMEM((tokens * QUERIES_PER_KEY, HEAD_SIZE), bf16),
            pltpu.VMEM((HEAD_SIZE, tokens), bf16),
            pltpu.VMEM((HEAD_SIZE, tokens), bf16),
            pltpu.VMEM((HEAD_SIZE, wide), f32),
            pltpu.VMEM((2 * rows, HEAD_SIZE), f32),
        ),
        flops=8 * tokens * tokens * q_cols,
        moved=2 * tokens * packed_cols,
    )
    dx_got = swapped(dx_far, "seq", 1)
    aparts = tuple(range(groups - 1, -1, -1))
    terms = {}
    for chosen in (aparts[: groups // 2], aparts[groups // 2 :]):
        made = kernel_call(
            functools.partial(input_terms_kernel, chosen),
            tuple(shape((model // groups, rows), bf16 if apart else f32) for apart in chosen),
            (dx_own, dx_got, query_weight, key_matrix, value_matrix),
            in_vmem=range(5),
            scratch=(pltpu.VMEM((rows, 2 * (q_cols + 2 * kv_cols)), bf16),),
            flops=2 * rows * model * (q_cols + 2 * kv_cols),
            moved=2 * model * (q_cols + 2 * kv_cols),
            room=4,
        )
        terms.update(zip(chosen, made))
    arrived = [swapped(terms[apart], "head", apart) for apart in aparts[:-1]]
    grad_wvalue, grad_woutput, weights_done = kernel_call(
        weight_grad_kernel,
        (
            shape((model // blocks, 2 * kv_cols), f32),
            shape((model // blocks, 2 * q_cols), f32),
            shape((8, HEAD_SIZE), f32),
        ),
        (attn, swapped(attn, "seq", 1), dv, swapped(dv, "seq", 1), *columns),
        in_vmem=range(4 + blocks),
        scratch=(pltpu.VMEM((2, model // blocks, tokens), bf16),),
        flops=4 * tokens * (model // blocks) * (q_cols + kv_cols),
        moved=4 * (model // blocks) * (tokens + 2 * q_cols + 2 * kv_cols),
    )
    grad_input = kernel_call(
        sum_kernel,
        shape((model // groups, rows), bf16),
        (weights_done, terms[0], *arrived),
        in_vmem=range(1, groups + 1),
        moved=4 * groups * (model // groups) * rows,
    )
    return (grad_input.T, grad_wvalue, grad_woutput.T)


def power_of_two(count):
    return count & (count - 1) == 0


def local(normed_input, stored_queries, stored_keys, *others):
    blocks, groups = lax.axis_size("seq"), lax.axis_size("head")
    whole_window = normed_input.shape[0] * blocks <= WINDOW_LENGTH
    two_heads = stored_keys.shape[1] == 2 * HEAD_SIZE
    paired = blocks > 1 and power_of_two(blocks) and power_of_two(groups)
    plan = gathered_plan if whole_window and two_heads and paired else windowed_plan
    return plan(normed_input, stored_queries, stored_keys, *others)


def windowed_plan(
    normed_input,
    stored_queries,
    stored_keys,
    stored_values,
    query_weight,
    key_matrix,
    value_matrix,
    output_weight,
    out_cotangent,
):
    tok_rows = normed_input.shape[0]
    blocks_seq = lax.axis_size("seq")
    seq_place = lax.axis_index("seq")
    reach_blocks = min(WINDOW_LENGTH // tok_rows, blocks_seq - 1)
    kv_heads = stored_keys.shape[1] // HEAD_SIZE
    output_gradient = jnp.dot(
        out_cotangent, output_weight.T, preferred_element_type=jnp.float32
    ).astype(jnp.bfloat16)
    pieces = [(stored_keys, stored_values)]
    current = (stored_keys, stored_values)
    for relay_step in range(reach_blocks):
        current = passed_along((current[0], current[1]), "seq", 1)
        pieces = [current] + pieces
    key_window = jnp.concatenate([piece[0] for piece in pieces], axis=0)
    value_window = jnp.concatenate([piece[1] for piece in pieces], axis=0)
    key_span = key_window.shape[0]
    query_pos = seq_place * tok_rows + jnp.arange(tok_rows, dtype=jnp.int32)
    key_pos = (seq_place - reach_blocks) * tok_rows + jnp.arange(key_span, dtype=jnp.int32)
    pos_gap = query_pos[:, None] - key_pos[None, :]
    allowed = (pos_gap >= 0) & (pos_gap < WINDOW_LENGTH) & (key_pos >= 0)[None, :]
    allowed_rows = jnp.tile(allowed, (QUERIES_PER_KEY, 1))
    query_stack = (
        stored_queries.reshape(tok_rows, kv_heads, QUERIES_PER_KEY, HEAD_SIZE)
        .transpose(1, 2, 0, 3)
        .reshape(kv_heads, QUERIES_PER_KEY * tok_rows, HEAD_SIZE)
    )
    grad_stack = (
        output_gradient.reshape(tok_rows, kv_heads, QUERIES_PER_KEY, HEAD_SIZE)
        .transpose(1, 2, 0, 3)
        .reshape(kv_heads, QUERIES_PER_KEY * tok_rows, HEAD_SIZE)
    )
    key_stack = key_window.reshape(key_span, kv_heads, HEAD_SIZE).transpose(1, 0, 2)
    value_stack = value_window.reshape(key_span, kv_heads, HEAD_SIZE).transpose(1, 0, 2)

    def per_head(head_items):
        query_head, key_head, value_head, grad_head = head_items
        attention_logits = logit_scale * jnp.dot(
            query_head, key_head.T, preferred_element_type=jnp.float32
        )
        masked = jnp.where(allowed_rows, attention_logits, -jnp.inf)
        row_top = jnp.max(masked, axis=1, keepdims=True)
        exp_scores = jnp.exp(masked - row_top)
        attn_prob = exp_scores / jnp.sum(exp_scores, axis=1, keepdims=True)
        probability_halfwidth = attn_prob.astype(jnp.bfloat16)
        attn_head = jnp.dot(
            probability_halfwidth, value_head, preferred_element_type=jnp.float32
        ).astype(jnp.bfloat16)
        row_delta = jnp.sum(
            grad_head.astype(jnp.float32) * attn_head.astype(jnp.float32), axis=1, keepdims=True
        )
        probability_gradient = jnp.dot(grad_head, value_head.T, preferred_element_type=jnp.float32)
        score_gradient = (attn_prob * (probability_gradient - row_delta)).astype(jnp.bfloat16)
        qgrad_head = (
            logit_scale * jnp.dot(score_gradient, key_head, preferred_element_type=jnp.float32)
        ).astype(jnp.bfloat16)
        key_partial = logit_scale * jnp.dot(
            score_gradient.T, query_head, preferred_element_type=jnp.float32
        )
        value_partial = jnp.dot(
            probability_halfwidth.T, grad_head, preferred_element_type=jnp.float32
        )
        return (attn_head, qgrad_head, key_partial, value_partial)

    attn_all, qgrad_all, key_all, value_all = lax.map(
        per_head, (query_stack, key_stack, value_stack, grad_stack)
    )
    attention_output = (
        attn_all.reshape(kv_heads, QUERIES_PER_KEY, tok_rows, HEAD_SIZE)
        .transpose(2, 0, 1, 3)
        .reshape(tok_rows, kv_heads * QUERIES_PER_KEY * HEAD_SIZE)
    )
    query_gradient = (
        qgrad_all.reshape(kv_heads, QUERIES_PER_KEY, tok_rows, HEAD_SIZE)
        .transpose(2, 0, 1, 3)
        .reshape(tok_rows, kv_heads * QUERIES_PER_KEY * HEAD_SIZE)
    )
    key_terms = key_all.transpose(1, 0, 2).reshape(key_span, kv_heads * HEAD_SIZE)
    value_terms = value_all.transpose(1, 0, 2).reshape(key_span, kv_heads * HEAD_SIZE)

    def take_slot(terms, slot_index):
        return terms[slot_index * tok_rows : (slot_index + 1) * tok_rows]

    key_sum = take_slot(key_terms, reach_blocks)
    value_sum = take_slot(value_terms, reach_blocks)
    for distance in range(1, reach_blocks + 1):
        received = passed_along(
            (
                take_slot(key_terms, reach_blocks - distance),
                take_slot(value_terms, reach_blocks - distance),
            ),
            "seq",
            -distance,
        )
        key_sum = key_sum + received[0]
        value_sum = value_sum + received[1]
    grad_key = key_sum.astype(jnp.bfloat16)
    grad_value = value_sum.astype(jnp.bfloat16)
    input_terms = jnp.dot(query_gradient, query_weight.T, preferred_element_type=jnp.float32)
    input_terms = input_terms + jnp.dot(grad_key, key_matrix.T, preferred_element_type=jnp.float32)
    input_terms = input_terms + jnp.dot(
        grad_value, value_matrix.T, preferred_element_type=jnp.float32
    )
    grad_input = lax.psum_scatter(input_terms, "head", scatter_dimension=1, tiled=True).astype(
        jnp.bfloat16
    )
    value_cols = grad_value.shape[1]
    input_cols = normed_input.T
    cot_cols = out_cotangent.T
    gathered = lax.psum_scatter(
        jnp.concatenate(
            [
                jnp.dot(input_cols, grad_value, preferred_element_type=jnp.float32),
                jnp.dot(cot_cols, attention_output, preferred_element_type=jnp.float32),
            ],
            axis=1,
        ),
        "seq",
        scatter_dimension=0,
        tiled=True,
    )
    grad_wvalue = gathered[:, :value_cols]
    grad_woutput = gathered[:, value_cols:].T
    return (grad_input, grad_wvalue, grad_woutput)


def solution(mesh):
    placed = (
        P("seq", None),
        P("seq", "head"),
        P("seq", "head"),
        P("seq", "head"),
        P(None, "head"),
        P(None, "head"),
        P(None, "head"),
        P("head", None),
        P("seq", None),
    )
    return jax.shard_map(
        local,
        mesh=mesh,
        in_specs=placed,
        out_specs=(P("seq", "head"), P("seq", "head"), P("head", "seq")),
        check_vma=False,
    )
```

```python
import functools

import jax
import jax.numpy as jnp
from jax import lax
from jax.experimental import pallas as pl
from jax.experimental.pallas import tpu as pltpu
from jax.sharding import PartitionSpec as P

HEAD_SIZE = 128
WINDOW_LENGTH = 4096
QUERIES_PER_KEY = 2


logit_scale = 1.0 / 12.0
log2_scale = 1.4426950408889634 / 12.0
excluded = -1e30


def passed_along(value, axis, steps):
    count = lax.axis_size(axis)
    leading, last = (max(0, -steps), min(count, count - steps))
    return lax.ppermute(value, axis, [(source, source + steps) for source in range(leading, last)])


NT = (((1,), (1,)), ((), ()))


def dot_nt(left, right):
    return lax.dot_general(left, right, NT, preferred_element_type=jnp.float32)


def dot_nn(left, right):
    return jnp.dot(left, right, preferred_element_type=jnp.float32)


def at(place, size):
    return pl.ds(pl.multiple_of(place * size, size), size)


def out_grad_kernel(
    cot_hbm, weight_hbm, q_hbm, k_hbm, v_hbm, same_ref, other_ref, cot_ref, weight_ref, sem
):
    core = lax.axis_index("seq") % 2
    cut = weight_ref.shape[0] // 2
    cot_copy = pltpu.make_async_copy(cot_hbm, cot_ref, sem.at[0])
    cot_copy.start()
    halves = ((other_ref, 1 - core), (same_ref, core))
    weight_copies = []
    for place, (_, half) in enumerate(halves):
        weight_copies.append(
            pltpu.make_async_copy(
                weight_hbm.at[at(half, cut)], weight_ref.at[at(place, cut)], sem.at[1 + place]
            )
        )
        weight_copies[-1].start()
    plain_copies = []
    for place, (target, half) in enumerate(halves):
        first = 0
        for which, source in enumerate((q_hbm, k_hbm, v_hbm)):
            cols = source.shape[1] // 2
            plain_copies.append(
                pltpu.make_async_copy(
                    source.at[:, at(half, cols)],
                    target.at[:, pl.ds(first, cols)],
                    sem.at[3 + 3 * place + which],
                )
            )
            plain_copies[-1].start()
            first += cols
    cot_copy.wait()
    for place, (target, _) in enumerate(halves):
        weight_copies[place].wait()
        grads_t = dot_nt(weight_ref[place * cut : (place + 1) * cut], cot_ref[...])
        for h in range(cut // HEAD_SIZE):
            target[:, first + h * HEAD_SIZE : first + (h + 1) * HEAD_SIZE] = grads_t[
                h * HEAD_SIZE : (h + 1) * HEAD_SIZE
            ].astype(jnp.bfloat16)
    for copy in plain_copies:
        copy.wait()


def turn_kernel(
    parts, normed_hbm, cot_hbm, block_hbm, _, turned_ref, own_ref, normed_ref, cot_ref, sem
):
    cut = normed_ref.shape[1] // parts
    copies = []
    for which, (source, target) in enumerate(
        ((normed_hbm, normed_ref), (cot_hbm, cot_ref), (block_hbm, own_ref))
    ):
        copies.append(pltpu.make_async_copy(source, target, sem.at[which]))
        copies[-1].start()
    for which, ref in enumerate((normed_ref, cot_ref)):
        copies[which].wait()
        turned = ref[...].astype(jnp.float32).T.astype(jnp.bfloat16)
        for part in range(parts):
            turned_ref[part, which] = turned[part * cut : (part + 1) * cut]
    copies[2].wait()


def attention_kernel(blocks, *refs):
    attention_body(refs[:blocks], *refs[blocks:])


def attention_body(
    block_refs,
    _,
    dx_own_ref,
    dx_far_ref,
    parts_ref,
    __,
    gathered_ref,
    score_even_ref,
    score_odd_ref,
    prob_ref,
    grad_t_ref,
    delta_ref,
    query_ref,
    value_t_ref,
    key_t_ref,
    dq_t_ref,
    dk_ref,
):
    me = lax.axis_index("seq")
    core, chip = me % 2, me // 2
    rows = dx_own_ref.shape[0]
    for apart, source in enumerate(block_refs):
        gathered_ref[at(me ^ apart, rows)] = source[...]
    tokens = gathered_ref.shape[0]
    size = 2 * rows
    steps = tokens // size
    wide = QUERIES_PER_KEY * size
    heads = QUERIES_PER_KEY
    key_cols = slice(heads * HEAD_SIZE, (heads + 1) * HEAD_SIZE)
    value_cols = slice((heads + 1) * HEAD_SIZE, (heads + 2) * HEAD_SIZE)
    grad_base = (heads + 2) * HEAD_SIZE
    value_t_ref[...] = gathered_ref[:, value_cols].T
    key_t_ref[...] = gathered_ref[:, key_cols].T
    key_place = lax.broadcasted_iota(jnp.int32, (size, wide), 0)
    query_place = lax.broadcasted_iota(jnp.int32, (size, wide), 1) % size
    allowed = key_place <= query_place

    for step in range(steps):
        span = (step + 1) * size
        own = slice(step * size, span)
        lanes = slice(step * wide, (step + 1) * wide)
        score_ref = score_odd_ref if step % 2 else score_even_ref
        queries = jnp.concatenate(
            [gathered_ref[own, h * HEAD_SIZE : (h + 1) * HEAD_SIZE] for h in range(heads)], axis=0
        )
        query_ref[lanes] = queries
        top = None
        for piece in range(step + 1):
            part = slice(piece * size, (piece + 1) * size)
            scores = dot_nt(gathered_ref[part, key_cols], queries)
            if piece == step:
                scores = jnp.where(allowed, scores, excluded)
            score_ref[part] = scores
            largest = jnp.max(scores.reshape(size // 8, 8, wide), axis=0)
            top = largest if top is None else jnp.maximum(top, largest)
        top = jnp.max(top, axis=0, keepdims=True)
        total = None
        for piece in range(step + 1):
            part = slice(piece * size, (piece + 1) * size)
            weights = jnp.exp2((score_ref[part] - top) * log2_scale)
            prob_ref[part, lanes] = weights.astype(jnp.bfloat16)
            summed = jnp.sum(weights.reshape(size // 8, 8, wide), axis=0)
            total = summed if total is None else total + summed
        inverse = 1.0 / jnp.sum(total, axis=0, keepdims=True)
        attn = dot_nn(value_t_ref[:, :span], prob_ref[:span, lanes]) * inverse
        for h in range(heads):
            parts_ref[h * HEAD_SIZE : (h + 1) * HEAD_SIZE, own] = attn[
                :, h * size : (h + 1) * size
            ].astype(jnp.bfloat16)
        grads_t = jnp.concatenate(
            [
                gathered_ref[
                    block * rows : (block + 1) * rows,
                    grad_base + h * HEAD_SIZE : grad_base + (h + 1) * HEAD_SIZE,
                ]
                for h in range(heads)
                for block in (2 * step, 2 * step + 1)
            ],
            axis=1,
        )
        grads_t = (grads_t.astype(jnp.float32) * inverse).astype(jnp.bfloat16)
        grad_t_ref[:, lanes] = grads_t
        delta_ref[:, lanes] = jnp.sum(grads_t.astype(jnp.float32) * attn, axis=0, keepdims=True)

    for step in range(steps):
        own = slice(step * size, (step + 1) * size)
        parts_ref[heads * HEAD_SIZE :, own] = dot_nt(
            grad_t_ref[:, step * wide :], prob_ref[own, step * wide :]
        ).astype(jnp.bfloat16)

    dq_t_ref[...] = jnp.zeros_like(dq_t_ref)
    dk_ref[...] = jnp.zeros_like(dk_ref)
    for step in range(steps):
        key_step = jnp.minimum(chip, step)
        query_step = jnp.maximum(chip, step)
        dprob = dot_nn(
            gathered_ref[at(key_step, size), value_cols], grad_t_ref[:, at(query_step, wide)]
        )
        dscore = (
            prob_ref[at(key_step, size), at(query_step, wide)].astype(jnp.float32)
            * (dprob - delta_ref[:, at(query_step, wide)])
        ).astype(jnp.bfloat16)

        @pl.when(step <= chip)
        def _():
            dq_t_ref[...] += dot_nn(key_t_ref[:, at(key_step, size)], dscore)

        @pl.when(step >= chip)
        def _():
            dk_ref[...] += dot_nn(dscore, query_ref[at(query_step, wide)])

    for target, half in ((dx_far_ref, 1 - core), (dx_own_ref, core)):
        for h in range(heads):
            target[:, h * HEAD_SIZE : (h + 1) * HEAD_SIZE] = (
                (logit_scale * dq_t_ref[:, at(2 * h + half, rows)])
                .T.astype(jnp.bfloat16)
            )
        target[:, key_cols] = (logit_scale * dk_ref[at(half, rows)]).astype(jnp.bfloat16)
        target[:, value_cols] = parts_ref[heads * HEAD_SIZE :, at(2 * chip + half, rows)].T


def input_terms_kernel(
    apart_groups, own_ref, far_ref, wq_ref, wk_ref, wv_ref, *refs
):
    terms, dx_ref = refs[:-1], refs[-1]
    core = lax.axis_index("seq") % 2
    group = lax.axis_index("head")
    q_cols = wq_ref.shape[1] // 2
    kv_cols = wk_ref.shape[1] // 2
    for source, half in ((own_ref, core), (far_ref, 1 - core)):
        dx_ref[:, at(half, q_cols)] = source[:, :q_cols]
        dx_ref[:, pl.ds(pl.multiple_of(2 * q_cols + half * kv_cols, kv_cols), kv_cols)] = source[
            :, q_cols : q_cols + kv_cols
        ]
        dx_ref[
            :, pl.ds(pl.multiple_of(2 * q_cols + (2 + half) * kv_cols, kv_cols), kv_cols)
        ] = source[:, q_cols + kv_cols :]
    for apart, target in zip(apart_groups, terms):
        cut = target.shape[0]
        place = at(group ^ apart, cut)
        target[...] = (
            dot_nt(wq_ref[place], dx_ref[:, : 2 * q_cols])
            + dot_nt(wk_ref[place], dx_ref[:, 2 * q_cols : 2 * q_cols + 2 * kv_cols])
            + dot_nt(wv_ref[place], dx_ref[:, 2 * q_cols + 2 * kv_cols :])
        ).astype(target.dtype)


def weight_grad_kernel(
    turned_ref, own_ref, far_ref, wvalue_ref, woutput_ref, done_ref, joined_ref
):
    done_ref[...] = jnp.zeros_like(done_ref)
    core = lax.axis_index("seq") % 2
    parts = turned_ref.shape[0]
    rows = turned_ref.shape[3]
    for part in range(parts):
        joined_ref[:, :, part * rows : (part + 1) * rows] = turned_ref[part]
    kv_cols = wvalue_ref.shape[1] // 2
    q_cols = woutput_ref.shape[1] // 2
    for half, ref in ((core, own_ref), (1 - core, far_ref)):
        woutput_ref[:, at(half, q_cols)] = dot_nt(joined_ref[1], ref[:q_cols])
        wvalue_ref[:, at(half, kv_cols)] = dot_nt(joined_ref[0], ref[q_cols:])


def sum_kernel(_, own_ref, *refs):
    total = own_ref[...]
    for arrived_ref in refs[:-1]:
        total = total + arrived_ref[...].astype(jnp.float32)
    refs[-1][...] = total.astype(jnp.bfloat16)


def kernel_call(
    body, outs, operands, in_vmem=(), scratch=(), flops=0, moved=0, room=16,
    out_hbm=(), aliases={},
):
    vmem = pl.BlockSpec(memory_space=pltpu.VMEM)
    hbm = pl.BlockSpec(memory_space=pltpu.HBM)
    return pl.pallas_call(
        body,
        out_shape=outs,
        in_specs=[vmem if place in in_vmem else hbm for place in range(len(operands))],
        out_specs=tuple(hbm if place in out_hbm else vmem for place in range(len(outs))),
        input_output_aliases=aliases,
        scratch_shapes=list(scratch),
        compiler_params=pltpu.CompilerParams(vmem_limit_bytes=room * 1024 * 1024),
        cost_estimate=pl.CostEstimate(flops=flops, bytes_accessed=moved, transcendentals=0),
    )(*operands)


def swapped(value, axis, apart):
    count = lax.axis_size(axis)
    return lax.ppermute(value, axis, [(place, place ^ apart) for place in range(count)])


def gathered_plan(
    normed_input,
    stored_queries,
    stored_keys,
    stored_values,
    query_weight,
    key_matrix,
    value_matrix,
    output_weight,
    out_cotangent,
):
    bf16, f32 = jnp.bfloat16, jnp.float32
    rows, model = normed_input.shape
    blocks = lax.axis_size("seq")
    groups = lax.axis_size("head")
    tokens = rows * blocks
    q_cols = stored_queries.shape[1] // 2
    kv_cols = HEAD_SIZE
    wide = 2 * QUERIES_PER_KEY * rows
    packed_cols = 2 * q_cols + 2 * kv_cols
    shape = jax.ShapeDtypeStruct
    same, other = kernel_call(
        out_grad_kernel,
        (shape((rows, packed_cols), bf16),) * 2,
        (out_cotangent, output_weight, stored_queries, stored_keys, stored_values),
        scratch=(
            pltpu.VMEM(out_cotangent.shape, bf16),
            pltpu.VMEM(output_weight.shape, bf16),
            pltpu.SemaphoreType.DMA((9,)),
        ),
        flops=4 * rows * model * q_cols,
        moved=2 * model * (rows + 2 * q_cols),
        room=63,
    )
    held = {0: same}
    for apart in range(2, blocks):
        lowest, highest = 2, 1 << (apart.bit_length() - 1)
        while not apart & lowest:
            lowest *= 2
        through = lowest if apart % 2 else highest
        if lowest == highest:
            held[apart] = swapped(other if apart % 2 else same, "seq", apart)
        else:
            held[apart] = swapped(held[apart ^ through], "seq", through)
    held[1] = swapped(other, "seq", 1)
    turned, own_block = kernel_call(
        functools.partial(turn_kernel, blocks),
        (shape((blocks, 2, model // blocks, rows), bf16), shape((rows, packed_cols), bf16)),
        (normed_input, out_cotangent, same, held[2]),
        scratch=(
            pltpu.VMEM(normed_input.shape, bf16),
            pltpu.VMEM(out_cotangent.shape, bf16),
            pltpu.SemaphoreType.DMA((3,)),
        ),
        moved=8 * rows * model,
    )
    held[0] = own_block
    dx_own, dx_far, grad_parts, turned = kernel_call(
        functools.partial(attention_kernel, blocks),
        (
            shape((rows, q_cols + 2 * kv_cols), bf16),
            shape((rows, q_cols + 2 * kv_cols), bf16),
            shape((q_cols + kv_cols, tokens), bf16),
            shape(turned.shape, bf16),
        ),
        [held[apart] for apart in range(blocks)] + [turned],
        in_vmem=range(blocks),
        out_hbm=(3,),
        aliases={blocks: 3},
        scratch=(
            pltpu.VMEM((tokens, packed_cols), bf16),
            pltpu.VMEM((tokens, wide), f32),
            pltpu.VMEM((tokens, wide), f32),
            pltpu.VMEM((tokens, tokens * QUERIES_PER_KEY), bf16),
            pltpu.VMEM((HEAD_SIZE, tokens * QUERIES_PER_KEY), bf16),
            pltpu.VMEM((1, tokens * QUERIES_PER_KEY), f32),
            pltpu.VMEM((tokens * QUERIES_PER_KEY, HEAD_SIZE), bf16),
            pltpu.VMEM((HEAD_SIZE, tokens), bf16),
            pltpu.VMEM((HEAD_SIZE, tokens), bf16),
            pltpu.VMEM((HEAD_SIZE, wide), f32),
            pltpu.VMEM((2 * rows, HEAD_SIZE), f32),
        ),
        flops=8 * tokens * tokens * q_cols,
        moved=2 * tokens * packed_cols,
    )
    dx_got = swapped(dx_far, "seq", 1)
    turned = lax.all_to_all(turned, "seq", 0, 0)
    aparts = tuple(range(groups - 1, -1, -1))
    terms = {}
    for chosen in (aparts[: groups // 2], aparts[groups // 2 :]):
        made = kernel_call(
            functools.partial(input_terms_kernel, chosen),
            tuple(shape((model // groups, rows), bf16 if apart else f32) for apart in chosen),
            (dx_own, dx_got, query_weight, key_matrix, value_matrix),
            in_vmem=range(5),
            scratch=(pltpu.VMEM((rows, 2 * (q_cols + 2 * kv_cols)), bf16),),
            flops=2 * rows * model * (q_cols + 2 * kv_cols),
            moved=2 * model * (q_cols + 2 * kv_cols),
            room=4,
        )
        terms.update(zip(chosen, made))
    arrived = [swapped(terms[apart], "head", apart) for apart in aparts[:-1]]
    grad_wvalue, grad_woutput, weights_done = kernel_call(
        weight_grad_kernel,
        (
            shape((model // blocks, 2 * kv_cols), f32),
            shape((model // blocks, 2 * q_cols), f32),
            shape((8, HEAD_SIZE), f32),
        ),
        (turned, grad_parts, swapped(grad_parts, "seq", 1)),
        in_vmem=range(3),
        scratch=(pltpu.VMEM((2, model // blocks, tokens), bf16),),
        flops=4 * tokens * (model // blocks) * (q_cols + kv_cols),
        moved=4 * (model // blocks) * (tokens + 2 * q_cols + 2 * kv_cols),
    )
    (grad_input,) = kernel_call(
        sum_kernel,
        (shape((model // groups, rows), bf16),),
        (weights_done, terms[0], *arrived),
        in_vmem=range(1, groups + 1),
        moved=4 * groups * (model // groups) * rows,
    )
    return (grad_input.T, grad_wvalue, grad_woutput.T)


def power_of_two(count):
    return count & (count - 1) == 0


def local(normed_input, stored_queries, stored_keys, *others):
    blocks, groups = lax.axis_size("seq"), lax.axis_size("head")
    whole_window = normed_input.shape[0] * blocks <= WINDOW_LENGTH
    two_heads = stored_keys.shape[1] == 2 * HEAD_SIZE
    paired = blocks > 1 and power_of_two(blocks) and power_of_two(groups)
    plan = gathered_plan if whole_window and two_heads and paired else windowed_plan
    return plan(normed_input, stored_queries, stored_keys, *others)


def windowed_plan(
    normed_input,
    stored_queries,
    stored_keys,
    stored_values,
    query_weight,
    key_matrix,
    value_matrix,
    output_weight,
    out_cotangent,
):
    tok_rows = normed_input.shape[0]
    blocks_seq = lax.axis_size("seq")
    seq_place = lax.axis_index("seq")
    reach_blocks = min(WINDOW_LENGTH // tok_rows, blocks_seq - 1)
    kv_heads = stored_keys.shape[1] // HEAD_SIZE
    output_gradient = jnp.dot(
        out_cotangent, output_weight.T, preferred_element_type=jnp.float32
    ).astype(jnp.bfloat16)
    pieces = [(stored_keys, stored_values)]
    current = (stored_keys, stored_values)
    for relay_step in range(reach_blocks):
        current = passed_along((current[0], current[1]), "seq", 1)
        pieces = [current] + pieces
    key_window = jnp.concatenate([piece[0] for piece in pieces], axis=0)
    value_window = jnp.concatenate([piece[1] for piece in pieces], axis=0)
    key_span = key_window.shape[0]
    query_pos = seq_place * tok_rows + jnp.arange(tok_rows, dtype=jnp.int32)
    key_pos = (seq_place - reach_blocks) * tok_rows + jnp.arange(key_span, dtype=jnp.int32)
    pos_gap = query_pos[:, None] - key_pos[None, :]
    allowed = (pos_gap >= 0) & (pos_gap < WINDOW_LENGTH) & (key_pos >= 0)[None, :]
    allowed_rows = jnp.tile(allowed, (QUERIES_PER_KEY, 1))
    query_stack = (
        stored_queries.reshape(tok_rows, kv_heads, QUERIES_PER_KEY, HEAD_SIZE)
        .transpose(1, 2, 0, 3)
        .reshape(kv_heads, QUERIES_PER_KEY * tok_rows, HEAD_SIZE)
    )
    grad_stack = (
        output_gradient.reshape(tok_rows, kv_heads, QUERIES_PER_KEY, HEAD_SIZE)
        .transpose(1, 2, 0, 3)
        .reshape(kv_heads, QUERIES_PER_KEY * tok_rows, HEAD_SIZE)
    )
    key_stack = key_window.reshape(key_span, kv_heads, HEAD_SIZE).transpose(1, 0, 2)
    value_stack = value_window.reshape(key_span, kv_heads, HEAD_SIZE).transpose(1, 0, 2)

    def per_head(head_items):
        query_head, key_head, value_head, grad_head = head_items
        attention_logits = logit_scale * jnp.dot(
            query_head, key_head.T, preferred_element_type=jnp.float32
        )
        masked = jnp.where(allowed_rows, attention_logits, -jnp.inf)
        row_top = jnp.max(masked, axis=1, keepdims=True)
        exp_scores = jnp.exp(masked - row_top)
        attn_prob = exp_scores / jnp.sum(exp_scores, axis=1, keepdims=True)
        probability_halfwidth = attn_prob.astype(jnp.bfloat16)
        attn_head = jnp.dot(
            probability_halfwidth, value_head, preferred_element_type=jnp.float32
        ).astype(jnp.bfloat16)
        row_delta = jnp.sum(
            grad_head.astype(jnp.float32) * attn_head.astype(jnp.float32), axis=1, keepdims=True
        )
        probability_gradient = jnp.dot(grad_head, value_head.T, preferred_element_type=jnp.float32)
        score_gradient = (attn_prob * (probability_gradient - row_delta)).astype(jnp.bfloat16)
        qgrad_head = (
            logit_scale * jnp.dot(score_gradient, key_head, preferred_element_type=jnp.float32)
        ).astype(jnp.bfloat16)
        key_partial = logit_scale * jnp.dot(
            score_gradient.T, query_head, preferred_element_type=jnp.float32
        )
        value_partial = jnp.dot(
            probability_halfwidth.T, grad_head, preferred_element_type=jnp.float32
        )
        return (attn_head, qgrad_head, key_partial, value_partial)

    attn_all, qgrad_all, key_all, value_all = lax.map(
        per_head, (query_stack, key_stack, value_stack, grad_stack)
    )
    attention_output = (
        attn_all.reshape(kv_heads, QUERIES_PER_KEY, tok_rows, HEAD_SIZE)
        .transpose(2, 0, 1, 3)
        .reshape(tok_rows, kv_heads * QUERIES_PER_KEY * HEAD_SIZE)
    )
    query_gradient = (
        qgrad_all.reshape(kv_heads, QUERIES_PER_KEY, tok_rows, HEAD_SIZE)
        .transpose(2, 0, 1, 3)
        .reshape(tok_rows, kv_heads * QUERIES_PER_KEY * HEAD_SIZE)
    )
    key_terms = key_all.transpose(1, 0, 2).reshape(key_span, kv_heads * HEAD_SIZE)
    value_terms = value_all.transpose(1, 0, 2).reshape(key_span, kv_heads * HEAD_SIZE)

    def take_slot(terms, slot_index):
        return terms[slot_index * tok_rows : (slot_index + 1) * tok_rows]

    key_sum = take_slot(key_terms, reach_blocks)
    value_sum = take_slot(value_terms, reach_blocks)
    for distance in range(1, reach_blocks + 1):
        received = passed_along(
            (
                take_slot(key_terms, reach_blocks - distance),
                take_slot(value_terms, reach_blocks - distance),
            ),
            "seq",
            -distance,
        )
        key_sum = key_sum + received[0]
        value_sum = value_sum + received[1]
    grad_key = key_sum.astype(jnp.bfloat16)
    grad_value = value_sum.astype(jnp.bfloat16)
    input_terms = jnp.dot(query_gradient, query_weight.T, preferred_element_type=jnp.float32)
    input_terms = input_terms + jnp.dot(grad_key, key_matrix.T, preferred_element_type=jnp.float32)
    input_terms = input_terms + jnp.dot(
        grad_value, value_matrix.T, preferred_element_type=jnp.float32
    )
    grad_input = lax.psum_scatter(input_terms, "head", scatter_dimension=1, tiled=True).astype(
        jnp.bfloat16
    )
    value_cols = grad_value.shape[1]
    input_cols = normed_input.T
    cot_cols = out_cotangent.T
    gathered = lax.psum_scatter(
        jnp.concatenate(
            [
                jnp.dot(input_cols, grad_value, preferred_element_type=jnp.float32),
                jnp.dot(cot_cols, attention_output, preferred_element_type=jnp.float32),
            ],
            axis=1,
        ),
        "seq",
        scatter_dimension=0,
        tiled=True,
    )
    grad_wvalue = gathered[:, :value_cols]
    grad_woutput = gathered[:, value_cols:].T
    return (grad_input, grad_wvalue, grad_woutput)


def solution(mesh):
    placed = (
        P("seq", None),
        P("seq", "head"),
        P("seq", "head"),
        P("seq", "head"),
        P(None, "head"),
        P(None, "head"),
        P(None, "head"),
        P("head", None),
        P("seq", None),
    )
    return jax.shard_map(
        local,
        mesh=mesh,
        in_specs=placed,
        out_specs=(P("seq", "head"), P("seq", "head"), P("head", "seq")),
        check_vma=False,
    )
```

```python
import functools

import jax
import jax.numpy as jnp
from jax import lax
from jax.experimental import pallas as pl
from jax.experimental.pallas import tpu as pltpu
from jax.sharding import PartitionSpec as P

HEAD_SIZE = 128
WINDOW_LENGTH = 4096
QUERIES_PER_KEY = 2


logit_scale = 1.0 / 12.0
log2_scale = 1.4426950408889634 / 12.0
excluded = -1e30


def passed_along(value, axis, steps):
    count = lax.axis_size(axis)
    leading, last = (max(0, -steps), min(count, count - steps))
    return lax.ppermute(value, axis, [(source, source + steps) for source in range(leading, last)])


NT = (((1,), (1,)), ((), ()))


def dot_nt(left, right):
    return lax.dot_general(left, right, NT, preferred_element_type=jnp.float32)


def dot_nn(left, right):
    return jnp.dot(left, right, preferred_element_type=jnp.float32)


def at(place, size):
    return pl.ds(pl.multiple_of(place * size, size), size)


def out_grad_kernel(
    cot_hbm, weight_hbm, q_hbm, k_hbm, v_hbm, same_ref, other_ref, cot_ref, weight_ref, sem
):
    core = lax.axis_index("seq") % 2
    cut = weight_ref.shape[0] // 2
    cot_copy = pltpu.make_async_copy(cot_hbm, cot_ref, sem.at[0])
    cot_copy.start()
    halves = ((other_ref, 1 - core), (same_ref, core))
    weight_copies = []
    for place, (_, half) in enumerate(halves):
        weight_copies.append(
            pltpu.make_async_copy(
                weight_hbm.at[at(half, cut)], weight_ref.at[at(place, cut)], sem.at[1 + place]
            )
        )
        weight_copies[-1].start()
    plain_copies = []
    for place, (target, half) in enumerate(halves):
        first = 0
        for which, source in enumerate((q_hbm, k_hbm, v_hbm)):
            cols = source.shape[1] // 2
            plain_copies.append(
                pltpu.make_async_copy(
                    source.at[:, at(half, cols)],
                    target.at[:, pl.ds(first, cols)],
                    sem.at[3 + 3 * place + which],
                )
            )
            plain_copies[-1].start()
            first += cols
    cot_copy.wait()
    for place, (target, _) in enumerate(halves):
        weight_copies[place].wait()
        grads_t = dot_nt(weight_ref[place * cut : (place + 1) * cut], cot_ref[...])
        for h in range(cut // HEAD_SIZE):
            target[:, first + h * HEAD_SIZE : first + (h + 1) * HEAD_SIZE] = grads_t[
                h * HEAD_SIZE : (h + 1) * HEAD_SIZE
            ].astype(jnp.bfloat16)
    for copy in plain_copies:
        copy.wait()


def turn_kernel(
    normed_hbm, cot_hbm, _, keep_ref, give_ref, normed_ref, cot_ref, turned_ref, sem
):
    me = lax.axis_index("seq")
    cut = keep_ref.shape[2]
    copies = []
    for which, (source, target) in enumerate(((normed_hbm, normed_ref), (cot_hbm, cot_ref))):
        copies.append(pltpu.make_async_copy(source, target, sem.at[which]))
        copies[-1].start()
    for which, ref in enumerate((normed_ref, cot_ref)):
        copies[which].wait()
        turned_ref[which] = ref[...].astype(jnp.float32).T.astype(jnp.bfloat16)
        for chip in range(keep_ref.shape[0]):
            keep_ref[chip, which] = turned_ref[which, at(me ^ (2 * chip), cut)]
            give_ref[chip, which] = turned_ref[which, at(me ^ (2 * chip + 1), cut)]


def join_kernel(keep_ref, got_ref, block_ref, *joined_refs):
    joined_refs, own_ref = joined_refs[:-1], joined_refs[-1]
    own_ref[...] = block_ref[...]
    for chip, ref in enumerate(joined_refs):
        ref[0] = keep_ref[chip]
        ref[1] = got_ref[chip]


def attention_kernel(blocks, *refs):
    attention_body(refs[:blocks], *refs[blocks:])


def attention_body(
    block_refs,
    dx_own_ref,
    dx_far_ref,
    parts_ref,
    gathered_ref,
    score_even_ref,
    score_odd_ref,
    prob_ref,
    grad_t_ref,
    delta_ref,
    query_ref,
    value_t_ref,
    key_t_ref,
    dq_t_ref,
    dk_ref,
):
    me = lax.axis_index("seq")
    core, chip = me % 2, me // 2
    rows = dx_own_ref.shape[0]
    for apart, source in enumerate(block_refs):
        gathered_ref[at(me ^ apart, rows)] = source[...]
    tokens = gathered_ref.shape[0]
    size = 2 * rows
    steps = tokens // size
    wide = QUERIES_PER_KEY * size
    heads = QUERIES_PER_KEY
    key_cols = slice(heads * HEAD_SIZE, (heads + 1) * HEAD_SIZE)
    value_cols = slice((heads + 1) * HEAD_SIZE, (heads + 2) * HEAD_SIZE)
    grad_base = (heads + 2) * HEAD_SIZE
    value_t_ref[...] = gathered_ref[:, value_cols].T
    key_t_ref[...] = gathered_ref[:, key_cols].T
    key_place = lax.broadcasted_iota(jnp.int32, (size, wide), 0)
    query_place = lax.broadcasted_iota(jnp.int32, (size, wide), 1) % size
    allowed = key_place <= query_place

    for step in range(steps):
        span = (step + 1) * size
        own = slice(step * size, span)
        lanes = slice(step * wide, (step + 1) * wide)
        score_ref = score_odd_ref if step % 2 else score_even_ref
        queries = jnp.concatenate(
            [gathered_ref[own, h * HEAD_SIZE : (h + 1) * HEAD_SIZE] for h in range(heads)], axis=0
        )
        query_ref[lanes] = queries
        top = None
        for piece in range(step + 1):
            part = slice(piece * size, (piece + 1) * size)
            scores = dot_nt(gathered_ref[part, key_cols], queries)
            if piece == step:
                scores = jnp.where(allowed, scores, excluded)
            score_ref[part] = scores
            largest = jnp.max(scores.reshape(size // 8, 8, wide), axis=0)
            top = largest if top is None else jnp.maximum(top, largest)
        top = jnp.max(top, axis=0, keepdims=True)
        total = None
        for piece in range(step + 1):
            part = slice(piece * size, (piece + 1) * size)
            weights = jnp.exp2((score_ref[part] - top) * log2_scale)
            prob_ref[part, lanes] = weights.astype(jnp.bfloat16)
            summed = jnp.sum(weights.reshape(size // 8, 8, wide), axis=0)
            total = summed if total is None else total + summed
        inverse = 1.0 / jnp.sum(total, axis=0, keepdims=True)
        attn = dot_nn(value_t_ref[:, :span], prob_ref[:span, lanes]) * inverse
        for h in range(heads):
            parts_ref[h * HEAD_SIZE : (h + 1) * HEAD_SIZE, own] = attn[
                :, h * size : (h + 1) * size
            ].astype(jnp.bfloat16)
        grads_t = jnp.concatenate(
            [
                gathered_ref[
                    block * rows : (block + 1) * rows,
                    grad_base + h * HEAD_SIZE : grad_base + (h + 1) * HEAD_SIZE,
                ]
                for h in range(heads)
                for block in (2 * step, 2 * step + 1)
            ],
            axis=1,
        )
        grads_t = (grads_t.astype(jnp.float32) * inverse).astype(jnp.bfloat16)
        grad_t_ref[:, lanes] = grads_t
        delta_ref[:, lanes] = jnp.sum(grads_t.astype(jnp.float32) * attn, axis=0, keepdims=True)

    for step in range(steps):
        own = slice(step * size, (step + 1) * size)
        parts_ref[heads * HEAD_SIZE :, own] = dot_nt(
            grad_t_ref[:, step * wide :], prob_ref[own, step * wide :]
        ).astype(jnp.bfloat16)

    dq_t_ref[...] = jnp.zeros_like(dq_t_ref)
    dk_ref[...] = jnp.zeros_like(dk_ref)
    for step in range(steps):
        key_step = jnp.minimum(chip, step)
        query_step = jnp.maximum(chip, step)
        dprob = dot_nn(
            gathered_ref[at(key_step, size), value_cols], grad_t_ref[:, at(query_step, wide)]
        )
        dscore = (
            prob_ref[at(key_step, size), at(query_step, wide)].astype(jnp.float32)
            * (dprob - delta_ref[:, at(query_step, wide)])
        ).astype(jnp.bfloat16)

        @pl.when(step <= chip)
        def _():
            dq_t_ref[...] += dot_nn(key_t_ref[:, at(key_step, size)], dscore)

        @pl.when(step >= chip)
        def _():
            dk_ref[...] += dot_nn(dscore, query_ref[at(query_step, wide)])

    for target, half in ((dx_far_ref, 1 - core), (dx_own_ref, core)):
        for h in range(heads):
            target[:, h * HEAD_SIZE : (h + 1) * HEAD_SIZE] = (
                (logit_scale * dq_t_ref[:, at(2 * h + half, rows)])
                .T.astype(jnp.bfloat16)
            )
        target[:, key_cols] = (logit_scale * dk_ref[at(half, rows)]).astype(jnp.bfloat16)
        target[:, value_cols] = parts_ref[heads * HEAD_SIZE :, at(2 * chip + half, rows)].T


def input_terms_kernel(
    apart_groups, own_ref, far_ref, wq_ref, wk_ref, wv_ref, *refs
):
    terms, dx_ref = refs[:-1], refs[-1]
    core = lax.axis_index("seq") % 2
    group = lax.axis_index("head")
    q_cols = wq_ref.shape[1] // 2
    kv_cols = wk_ref.shape[1] // 2
    for source, half in ((own_ref, core), (far_ref, 1 - core)):
        dx_ref[:, at(half, q_cols)] = source[:, :q_cols]
        dx_ref[:, pl.ds(pl.multiple_of(2 * q_cols + half * kv_cols, kv_cols), kv_cols)] = source[
            :, q_cols : q_cols + kv_cols
        ]
        dx_ref[
            :, pl.ds(pl.multiple_of(2 * q_cols + (2 + half) * kv_cols, kv_cols), kv_cols)
        ] = source[:, q_cols + kv_cols :]
    for apart, target in zip(apart_groups, terms):
        cut = target.shape[0]
        place = at(group ^ apart, cut)
        target[...] = (
            dot_nt(wq_ref[place], dx_ref[:, : 2 * q_cols])
            + dot_nt(wk_ref[place], dx_ref[:, 2 * q_cols : 2 * q_cols + 2 * kv_cols])
            + dot_nt(wv_ref[place], dx_ref[:, 2 * q_cols + 2 * kv_cols :])
        ).astype(target.dtype)


def weight_grad_kernel(own_ref, far_ref, *refs):
    column_refs, (wvalue_ref, woutput_ref, done_ref, joined_ref) = refs[:-4], refs[-4:]
    done_ref[...] = jnp.zeros_like(done_ref)
    me = lax.axis_index("seq")
    core = me % 2
    for chip, ref in enumerate(column_refs):
        for far in range(2):
            joined_ref[:, :, at(me ^ (2 * chip + far), ref.shape[3])] = ref[far]
    kv_cols = wvalue_ref.shape[1] // 2
    q_cols = woutput_ref.shape[1] // 2
    for half, ref in ((core, own_ref), (1 - core, far_ref)):
        woutput_ref[:, at(half, q_cols)] = dot_nt(joined_ref[1], ref[:q_cols])
        wvalue_ref[:, at(half, kv_cols)] = dot_nt(joined_ref[0], ref[q_cols:])


def sum_kernel(_, own_ref, *refs):
    total = own_ref[...]
    for arrived_ref in refs[:-1]:
        total = total + arrived_ref[...].astype(jnp.float32)
    refs[-1][...] = total.astype(jnp.bfloat16)


def kernel_call(
    body, outs, operands, in_vmem=(), scratch=(), flops=0, moved=0, room=16
):
    vmem = pl.BlockSpec(memory_space=pltpu.VMEM)
    hbm = pl.BlockSpec(memory_space=pltpu.HBM)
    return pl.pallas_call(
        body,
        out_shape=outs,
        in_specs=[vmem if place in in_vmem else hbm for place in range(len(operands))],
        out_specs=(vmem,) * len(outs),
        scratch_shapes=list(scratch),
        compiler_params=pltpu.CompilerParams(vmem_limit_bytes=room * 1024 * 1024),
        cost_estimate=pl.CostEstimate(flops=flops, bytes_accessed=moved, transcendentals=0),
    )(*operands)


def swapped(value, axis, apart):
    count = lax.axis_size(axis)
    return lax.ppermute(value, axis, [(place, place ^ apart) for place in range(count)])


def gathered_plan(
    normed_input,
    stored_queries,
    stored_keys,
    stored_values,
    query_weight,
    key_matrix,
    value_matrix,
    output_weight,
    out_cotangent,
):
    bf16, f32 = jnp.bfloat16, jnp.float32
    rows, model = normed_input.shape
    blocks = lax.axis_size("seq")
    groups = lax.axis_size("head")
    tokens = rows * blocks
    q_cols = stored_queries.shape[1] // 2
    kv_cols = HEAD_SIZE
    wide = 2 * QUERIES_PER_KEY * rows
    packed_cols = 2 * q_cols + 2 * kv_cols
    shape = jax.ShapeDtypeStruct
    same, other = kernel_call(
        out_grad_kernel,
        (shape((rows, packed_cols), bf16),) * 2,
        (out_cotangent, output_weight, stored_queries, stored_keys, stored_values),
        scratch=(
            pltpu.VMEM(out_cotangent.shape, bf16),
            pltpu.VMEM(output_weight.shape, bf16),
            pltpu.SemaphoreType.DMA((9,)),
        ),
        flops=4 * rows * model * q_cols,
        moved=2 * model * (rows + 2 * q_cols),
        room=63,
    )
    held = {0: same}
    for apart in range(2, blocks):
        lowest, highest = 2, 1 << (apart.bit_length() - 1)
        while not apart & lowest:
            lowest *= 2
        through = lowest if apart % 2 else highest
        if lowest == highest:
            held[apart] = swapped(other if apart % 2 else same, "seq", apart)
        else:
            held[apart] = swapped(held[apart ^ through], "seq", through)
    held[1] = swapped(other, "seq", 1)
    cut = model // blocks
    keep, give = kernel_call(
        turn_kernel,
        (
            shape((blocks // 2, 2, cut, rows), bf16),
            shape((blocks // 2, 2, cut, rows), bf16),
        ),
        (normed_input, out_cotangent, held[2]),
        scratch=(
            pltpu.VMEM(normed_input.shape, bf16),
            pltpu.VMEM(out_cotangent.shape, bf16),
            pltpu.VMEM((2, model, rows), bf16),
            pltpu.SemaphoreType.DMA((2,)),
        ),
        moved=8 * rows * model,
        room=8,
    )
    *columns, held[0] = kernel_call(
        join_kernel,
        (shape((2, 2, cut, rows), bf16),) * (blocks // 2) + (shape(same.shape, bf16),),
        (keep, swapped(give, "seq", 1), same),
        in_vmem=range(3),
        moved=8 * rows * model,
        room=4,
    )
    columns = [columns[0]] + [
        swapped(columns[chip], "seq", 2 * chip) for chip in range(1, blocks // 2)
    ]
    dx_own, dx_far, grad_parts = kernel_call(
        functools.partial(attention_kernel, blocks),
        (
            shape((rows, q_cols + 2 * kv_cols), bf16),
            shape((rows, q_cols + 2 * kv_cols), bf16),
            shape((q_cols + kv_cols, tokens), bf16),
        ),
        [held[apart] for apart in range(blocks)],
        in_vmem=range(blocks),
        scratch=(
            pltpu.VMEM((tokens, packed_cols), bf16),
            pltpu.VMEM((tokens, wide), f32),
            pltpu.VMEM((tokens, wide), f32),
            pltpu.VMEM((tokens, tokens * QUERIES_PER_KEY), bf16),
            pltpu.VMEM((HEAD_SIZE, tokens * QUERIES_PER_KEY), bf16),
            pltpu.VMEM((1, tokens * QUERIES_PER_KEY), f32),
            pltpu.VMEM((tokens * QUERIES_PER_KEY, HEAD_SIZE), bf16),
            pltpu.VMEM((HEAD_SIZE, tokens), bf16),
            pltpu.VMEM((HEAD_SIZE, tokens), bf16),
            pltpu.VMEM((HEAD_SIZE, wide), f32),
            pltpu.VMEM((2 * rows, HEAD_SIZE), f32),
        ),
        flops=8 * tokens * tokens * q_cols,
        moved=2 * tokens * packed_cols,
    )
    dx_got = swapped(dx_far, "seq", 1)
    aparts = tuple(range(groups - 1, -1, -1))
    terms = {}
    for chosen in (aparts[: groups // 2], aparts[groups // 2 :]):
        made = kernel_call(
            functools.partial(input_terms_kernel, chosen),
            tuple(shape((model // groups, rows), bf16 if apart else f32) for apart in chosen),
            (dx_own, dx_got, query_weight, key_matrix, value_matrix),
            in_vmem=range(5),
            scratch=(pltpu.VMEM((rows, 2 * (q_cols + 2 * kv_cols)), bf16),),
            flops=2 * rows * model * (q_cols + 2 * kv_cols),
            moved=2 * model * (q_cols + 2 * kv_cols),
            room=4,
        )
        terms.update(zip(chosen, made))
    arrived = [swapped(terms[apart], "head", apart) for apart in aparts[:-1]]
    grad_wvalue, grad_woutput, weights_done = kernel_call(
        weight_grad_kernel,
        (
            shape((model // blocks, 2 * kv_cols), f32),
            shape((model // blocks, 2 * q_cols), f32),
            shape((8, HEAD_SIZE), f32),
        ),
        (grad_parts, swapped(grad_parts, "seq", 1), *columns),
        in_vmem=range(2 + blocks // 2),
        scratch=(pltpu.VMEM((2, model // blocks, tokens), bf16),),
        room=8,
        flops=4 * tokens * (model // blocks) * (q_cols + kv_cols),
        moved=4 * (model // blocks) * (tokens + 2 * q_cols + 2 * kv_cols),
    )
    (grad_input,) = kernel_call(
        sum_kernel,
        (shape((model // groups, rows), bf16),),
        (weights_done, terms[0], *arrived),
        in_vmem=range(1, groups + 1),
        moved=4 * groups * (model // groups) * rows,
    )
    return (grad_input.T, grad_wvalue, grad_woutput.T)


def power_of_two(count):
    return count & (count - 1) == 0


def local(normed_input, stored_queries, stored_keys, *others):
    blocks, groups = lax.axis_size("seq"), lax.axis_size("head")
    whole_window = normed_input.shape[0] * blocks <= WINDOW_LENGTH
    two_heads = stored_keys.shape[1] == 2 * HEAD_SIZE
    paired = blocks > 1 and power_of_two(blocks) and power_of_two(groups)
    plan = gathered_plan if whole_window and two_heads and paired else windowed_plan
    return plan(normed_input, stored_queries, stored_keys, *others)


def windowed_plan(
    normed_input,
    stored_queries,
    stored_keys,
    stored_values,
    query_weight,
    key_matrix,
    value_matrix,
    output_weight,
    out_cotangent,
):
    tok_rows = normed_input.shape[0]
    blocks_seq = lax.axis_size("seq")
    seq_place = lax.axis_index("seq")
    reach_blocks = min(WINDOW_LENGTH // tok_rows, blocks_seq - 1)
    kv_heads = stored_keys.shape[1] // HEAD_SIZE
    output_gradient = jnp.dot(
        out_cotangent, output_weight.T, preferred_element_type=jnp.float32
    ).astype(jnp.bfloat16)
    pieces = [(stored_keys, stored_values)]
    current = (stored_keys, stored_values)
    for relay_step in range(reach_blocks):
        current = passed_along((current[0], current[1]), "seq", 1)
        pieces = [current] + pieces
    key_window = jnp.concatenate([piece[0] for piece in pieces], axis=0)
    value_window = jnp.concatenate([piece[1] for piece in pieces], axis=0)
    key_span = key_window.shape[0]
    query_pos = seq_place * tok_rows + jnp.arange(tok_rows, dtype=jnp.int32)
    key_pos = (seq_place - reach_blocks) * tok_rows + jnp.arange(key_span, dtype=jnp.int32)
    pos_gap = query_pos[:, None] - key_pos[None, :]
    allowed = (pos_gap >= 0) & (pos_gap < WINDOW_LENGTH) & (key_pos >= 0)[None, :]
    allowed_rows = jnp.tile(allowed, (QUERIES_PER_KEY, 1))
    query_stack = (
        stored_queries.reshape(tok_rows, kv_heads, QUERIES_PER_KEY, HEAD_SIZE)
        .transpose(1, 2, 0, 3)
        .reshape(kv_heads, QUERIES_PER_KEY * tok_rows, HEAD_SIZE)
    )
    grad_stack = (
        output_gradient.reshape(tok_rows, kv_heads, QUERIES_PER_KEY, HEAD_SIZE)
        .transpose(1, 2, 0, 3)
        .reshape(kv_heads, QUERIES_PER_KEY * tok_rows, HEAD_SIZE)
    )
    key_stack = key_window.reshape(key_span, kv_heads, HEAD_SIZE).transpose(1, 0, 2)
    value_stack = value_window.reshape(key_span, kv_heads, HEAD_SIZE).transpose(1, 0, 2)

    def per_head(head_items):
        query_head, key_head, value_head, grad_head = head_items
        attention_logits = logit_scale * jnp.dot(
            query_head, key_head.T, preferred_element_type=jnp.float32
        )
        masked = jnp.where(allowed_rows, attention_logits, -jnp.inf)
        row_top = jnp.max(masked, axis=1, keepdims=True)
        exp_scores = jnp.exp(masked - row_top)
        attn_prob = exp_scores / jnp.sum(exp_scores, axis=1, keepdims=True)
        probability_halfwidth = attn_prob.astype(jnp.bfloat16)
        attn_head = jnp.dot(
            probability_halfwidth, value_head, preferred_element_type=jnp.float32
        ).astype(jnp.bfloat16)
        row_delta = jnp.sum(
            grad_head.astype(jnp.float32) * attn_head.astype(jnp.float32), axis=1, keepdims=True
        )
        probability_gradient = jnp.dot(grad_head, value_head.T, preferred_element_type=jnp.float32)
        score_gradient = (attn_prob * (probability_gradient - row_delta)).astype(jnp.bfloat16)
        qgrad_head = (
            logit_scale * jnp.dot(score_gradient, key_head, preferred_element_type=jnp.float32)
        ).astype(jnp.bfloat16)
        key_partial = logit_scale * jnp.dot(
            score_gradient.T, query_head, preferred_element_type=jnp.float32
        )
        value_partial = jnp.dot(
            probability_halfwidth.T, grad_head, preferred_element_type=jnp.float32
        )
        return (attn_head, qgrad_head, key_partial, value_partial)

    attn_all, qgrad_all, key_all, value_all = lax.map(
        per_head, (query_stack, key_stack, value_stack, grad_stack)
    )
    attention_output = (
        attn_all.reshape(kv_heads, QUERIES_PER_KEY, tok_rows, HEAD_SIZE)
        .transpose(2, 0, 1, 3)
        .reshape(tok_rows, kv_heads * QUERIES_PER_KEY * HEAD_SIZE)
    )
    query_gradient = (
        qgrad_all.reshape(kv_heads, QUERIES_PER_KEY, tok_rows, HEAD_SIZE)
        .transpose(2, 0, 1, 3)
        .reshape(tok_rows, kv_heads * QUERIES_PER_KEY * HEAD_SIZE)
    )
    key_terms = key_all.transpose(1, 0, 2).reshape(key_span, kv_heads * HEAD_SIZE)
    value_terms = value_all.transpose(1, 0, 2).reshape(key_span, kv_heads * HEAD_SIZE)

    def take_slot(terms, slot_index):
        return terms[slot_index * tok_rows : (slot_index + 1) * tok_rows]

    key_sum = take_slot(key_terms, reach_blocks)
    value_sum = take_slot(value_terms, reach_blocks)
    for distance in range(1, reach_blocks + 1):
        received = passed_along(
            (
                take_slot(key_terms, reach_blocks - distance),
                take_slot(value_terms, reach_blocks - distance),
            ),
            "seq",
            -distance,
        )
        key_sum = key_sum + received[0]
        value_sum = value_sum + received[1]
    grad_key = key_sum.astype(jnp.bfloat16)
    grad_value = value_sum.astype(jnp.bfloat16)
    input_terms = jnp.dot(query_gradient, query_weight.T, preferred_element_type=jnp.float32)
    input_terms = input_terms + jnp.dot(grad_key, key_matrix.T, preferred_element_type=jnp.float32)
    input_terms = input_terms + jnp.dot(
        grad_value, value_matrix.T, preferred_element_type=jnp.float32
    )
    grad_input = lax.psum_scatter(input_terms, "head", scatter_dimension=1, tiled=True).astype(
        jnp.bfloat16
    )
    value_cols = grad_value.shape[1]
    input_cols = normed_input.T
    cot_cols = out_cotangent.T
    gathered = lax.psum_scatter(
        jnp.concatenate(
            [
                jnp.dot(input_cols, grad_value, preferred_element_type=jnp.float32),
                jnp.dot(cot_cols, attention_output, preferred_element_type=jnp.float32),
            ],
            axis=1,
        ),
        "seq",
        scatter_dimension=0,
        tiled=True,
    )
    grad_wvalue = gathered[:, :value_cols]
    grad_woutput = gathered[:, value_cols:].T
    return (grad_input, grad_wvalue, grad_woutput)


def solution(mesh):
    placed = (
        P("seq", None),
        P("seq", "head"),
        P("seq", "head"),
        P("seq", "head"),
        P(None, "head"),
        P(None, "head"),
        P(None, "head"),
        P("head", None),
        P("seq", None),
    )
    return jax.shard_map(
        local,
        mesh=mesh,
        in_specs=placed,
        out_specs=(P("seq", "head"), P("seq", "head"), P("head", "seq")),
        check_vma=False,
    )
```

```python
import functools

import jax
import jax.numpy as jnp
from jax import lax
from jax.experimental import pallas as pl
from jax.experimental.pallas import tpu as pltpu
from jax.sharding import PartitionSpec as P

HEAD_SIZE = 128
WINDOW_LENGTH = 4096
QUERIES_PER_KEY = 2


logit_scale = 1.0 / 12.0
log2_scale = 1.4426950408889634 / 12.0
excluded = -1e30


def passed_along(value, axis, steps):
    count = lax.axis_size(axis)
    leading, last = (max(0, -steps), min(count, count - steps))
    return lax.ppermute(value, axis, [(source, source + steps) for source in range(leading, last)])


NT = (((1,), (1,)), ((), ()))


def dot_nt(left, right):
    return lax.dot_general(left, right, NT, preferred_element_type=jnp.float32)


def dot_nn(left, right):
    return jnp.dot(left, right, preferred_element_type=jnp.float32)


def at(place, size):
    return pl.ds(pl.multiple_of(place * size, size), size)


def out_grad_kernel(
    cot_hbm, weight_hbm, q_hbm, k_hbm, v_hbm, same_ref, other_ref, cot_ref, weight_ref, sem
):
    core = lax.axis_index("seq") % 2
    cot_copy = pltpu.make_async_copy(cot_hbm, cot_ref, sem.at[0])
    cot_copy.start()
    heads = weight_ref.shape[0] // HEAD_SIZE
    halves = ((other_ref, 1 - core), (same_ref, core))
    weight_copies = []
    for head in range(heads):
        half = halves[2 * head // heads][1]
        source = half * (heads // 2) + head % (heads // 2)
        weight_copies.append(
            pltpu.make_async_copy(
                weight_hbm.at[at(source, HEAD_SIZE)],
                weight_ref.at[pl.ds(head * HEAD_SIZE, HEAD_SIZE)],
                sem.at[7 + head],
            )
        )
        weight_copies[-1].start()
    plain_copies = []
    for place, (target, half) in enumerate(halves):
        first = 0
        for which, source in enumerate((q_hbm, k_hbm, v_hbm)):
            cols = source.shape[1] // 2
            plain_copies.append(
                pltpu.make_async_copy(
                    source.at[:, at(half, cols)],
                    target.at[:, pl.ds(first, cols)],
                    sem.at[1 + 3 * place + which],
                )
            )
            plain_copies[-1].start()
            first += cols
    cot_copy.wait()
    for head, copy in enumerate(weight_copies):
        copy.wait()
        place = first + head % (heads // 2) * HEAD_SIZE
        halves[2 * head // heads][0][:, place : place + HEAD_SIZE] = dot_nt(
            weight_ref[head * HEAD_SIZE : (head + 1) * HEAD_SIZE], cot_ref[...]
        ).astype(jnp.bfloat16)
    for copy in plain_copies:
        copy.wait()


def turn_kernel(
    normed_hbm, cot_hbm, block_hbm, _, __, keep_ref, give_ref, own_ref, normed_ref, cot_ref, turned_ref, sem
):
    me = lax.axis_index("seq")
    cut = keep_ref.shape[2]
    copies = []
    for which, (source, target) in enumerate(
        ((normed_hbm, normed_ref), (cot_hbm, cot_ref), (block_hbm, own_ref))
    ):
        copies.append(pltpu.make_async_copy(source, target, sem.at[which]))
        copies[-1].start()
    for which, ref in enumerate((normed_ref, cot_ref)):
        copies[which].wait()
        turned_ref[which] = ref[...].astype(jnp.float32).T.astype(jnp.bfloat16)
        for chip in range(keep_ref.shape[0]):
            keep_ref[chip, which] = turned_ref[which, at(me ^ (2 * chip), cut)]
            give_ref[chip, which] = turned_ref[which, at(me ^ (2 * chip + 1), cut)]
    copies[2].wait()


def join_kernel(keep_ref, got_ref, *joined_refs):
    for chip, ref in enumerate(joined_refs):
        ref[0] = keep_ref[chip]
        ref[1] = got_ref[chip]


def attention_kernel(blocks, *refs):
    attention_body(refs[:blocks], *refs[blocks:])


def attention_body(
    block_refs,
    dx_own_ref,
    dx_far_ref,
    parts_ref,
    gathered_ref,
    score_even_ref,
    score_odd_ref,
    prob_ref,
    grad_t_ref,
    delta_ref,
    query_ref,
    value_t_ref,
    key_t_ref,
    dq_t_ref,
    dk_ref,
):
    me = lax.axis_index("seq")
    core, chip = me % 2, me // 2
    rows = dx_own_ref.shape[0]
    for apart, source in enumerate(block_refs):
        gathered_ref[at(me ^ apart, rows)] = source[...]
    tokens = gathered_ref.shape[0]
    size = 2 * rows
    steps = tokens // size
    wide = QUERIES_PER_KEY * size
    heads = QUERIES_PER_KEY
    key_cols = slice(heads * HEAD_SIZE, (heads + 1) * HEAD_SIZE)
    value_cols = slice((heads + 1) * HEAD_SIZE, (heads + 2) * HEAD_SIZE)
    grad_base = (heads + 2) * HEAD_SIZE
    value_t_ref[...] = gathered_ref[:, value_cols].T
    key_t_ref[...] = gathered_ref[:, key_cols].T
    key_place = lax.broadcasted_iota(jnp.int32, (size, wide), 0)
    query_place = lax.broadcasted_iota(jnp.int32, (size, wide), 1) % size
    allowed = key_place <= query_place

    for step in range(steps):
        span = (step + 1) * size
        own = slice(step * size, span)
        lanes = slice(step * wide, (step + 1) * wide)
        score_ref = score_odd_ref if step % 2 else score_even_ref
        queries = jnp.concatenate(
            [gathered_ref[own, h * HEAD_SIZE : (h + 1) * HEAD_SIZE] for h in range(heads)], axis=0
        )
        query_ref[lanes] = queries
        top = None
        for piece in range(step + 1):
            part = slice(piece * size, (piece + 1) * size)
            scores = dot_nt(gathered_ref[part, key_cols], queries)
            if piece == step:
                scores = jnp.where(allowed, scores, excluded)
            score_ref[part] = scores
            largest = jnp.max(scores.reshape(size // 8, 8, wide), axis=0)
            top = largest if top is None else jnp.maximum(top, largest)
        top = jnp.max(top, axis=0, keepdims=True)
        total = None
        for piece in range(step + 1):
            part = slice(piece * size, (piece + 1) * size)
            weights = jnp.exp2((score_ref[part] - top) * log2_scale)
            prob_ref[part, lanes] = weights.astype(jnp.bfloat16)
            summed = jnp.sum(weights.reshape(size // 8, 8, wide), axis=0)
            total = summed if total is None else total + summed
        inverse = 1.0 / jnp.sum(total, axis=0, keepdims=True)
        attn = dot_nn(value_t_ref[:, :span], prob_ref[:span, lanes]) * inverse
        for h in range(heads):
            parts_ref[h * HEAD_SIZE : (h + 1) * HEAD_SIZE, own] = attn[
                :, h * size : (h + 1) * size
            ].astype(jnp.bfloat16)
        grads_t = jnp.concatenate(
            [
                gathered_ref[
                    block * rows : (block + 1) * rows,
                    grad_base + h * HEAD_SIZE : grad_base + (h + 1) * HEAD_SIZE,
                ]
                for h in range(heads)
                for block in (2 * step, 2 * step + 1)
            ],
            axis=1,
        )
        grads_t = (grads_t.astype(jnp.float32) * inverse).astype(jnp.bfloat16)
        grad_t_ref[:, lanes] = grads_t
        delta_ref[:, lanes] = jnp.sum(grads_t.astype(jnp.float32) * attn, axis=0, keepdims=True)

    for step in range(steps):
        own = slice(step * size, (step + 1) * size)
        parts_ref[heads * HEAD_SIZE :, own] = dot_nt(
            grad_t_ref[:, step * wide :], prob_ref[own, step * wide :]
        ).astype(jnp.bfloat16)

    dq_t_ref[...] = jnp.zeros_like(dq_t_ref)
    dk_ref[...] = jnp.zeros_like(dk_ref)
    for step in range(steps):
        key_step = jnp.minimum(chip, step)
        query_step = jnp.maximum(chip, step)
        dprob = dot_nn(
            gathered_ref[at(key_step, size), value_cols], grad_t_ref[:, at(query_step, wide)]
        )
        dscore = (
            prob_ref[at(key_step, size), at(query_step, wide)].astype(jnp.float32)
            * (dprob - delta_ref[:, at(query_step, wide)])
        ).astype(jnp.bfloat16)

        @pl.when(step <= chip)
        def _():
            dq_t_ref[...] += dot_nn(key_t_ref[:, at(key_step, size)], dscore)

        @pl.when(step >= chip)
        def _():
            dk_ref[...] += dot_nn(dscore, query_ref[at(query_step, wide)])

    for target, half in ((dx_far_ref, 1 - core), (dx_own_ref, core)):
        for h in range(heads):
            target[:, h * HEAD_SIZE : (h + 1) * HEAD_SIZE] = (
                (logit_scale * dq_t_ref[:, at(2 * h + half, rows)])
                .T.astype(jnp.bfloat16)
            )
        target[:, key_cols] = (logit_scale * dk_ref[at(half, rows)]).astype(jnp.bfloat16)
        target[:, value_cols] = parts_ref[heads * HEAD_SIZE :, at(2 * chip + half, rows)].T


def input_terms_kernel(
    apart_groups, own_ref, far_ref, wq_ref, wk_ref, wv_ref, *refs
):
    terms, dx_ref = refs[:-1], refs[-1]
    core = lax.axis_index("seq") % 2
    group = lax.axis_index("head")
    q_cols = wq_ref.shape[1] // 2
    kv_cols = wk_ref.shape[1] // 2
    for source, half in ((own_ref, core), (far_ref, 1 - core)):
        dx_ref[:, at(half, q_cols)] = source[:, :q_cols]
        dx_ref[:, pl.ds(pl.multiple_of(2 * q_cols + half * kv_cols, kv_cols), kv_cols)] = source[
            :, q_cols : q_cols + kv_cols
        ]
        dx_ref[
            :, pl.ds(pl.multiple_of(2 * q_cols + (2 + half) * kv_cols, kv_cols), kv_cols)
        ] = source[:, q_cols + kv_cols :]
    for apart, target in zip(apart_groups, terms):
        cut = target.shape[0]
        place = at(group ^ apart, cut)
        target[...] = (
            dot_nt(wq_ref[place], dx_ref[:, : 2 * q_cols])
            + dot_nt(wk_ref[place], dx_ref[:, 2 * q_cols : 2 * q_cols + 2 * kv_cols])
            + dot_nt(wv_ref[place], dx_ref[:, 2 * q_cols + 2 * kv_cols :])
        ).astype(target.dtype)


def weight_grad_kernel(own_ref, far_ref, *refs):
    column_refs, (wvalue_ref, woutput_ref, done_ref, joined_ref) = refs[:-4], refs[-4:]
    done_ref[...] = jnp.zeros_like(done_ref)
    me = lax.axis_index("seq")
    core = me % 2
    for chip, ref in enumerate(column_refs):
        for far in range(2):
            joined_ref[:, :, at(me ^ (2 * chip + far), ref.shape[3])] = ref[far]
    kv_cols = wvalue_ref.shape[1] // 2
    q_cols = woutput_ref.shape[1] // 2
    for half, ref in ((core, own_ref), (1 - core, far_ref)):
        woutput_ref[:, at(half, q_cols)] = dot_nt(joined_ref[1], ref[:q_cols])
        wvalue_ref[:, at(half, kv_cols)] = dot_nt(joined_ref[0], ref[q_cols:])


def add_kernel(own_ref, arrived_ref, sum_ref):
    total = own_ref[...].astype(jnp.float32) + arrived_ref[...].astype(jnp.float32)
    sum_ref[...] = total.astype(jnp.bfloat16)


def sum_kernel(_, own_ref, *refs):
    total = own_ref[...]
    for arrived_ref in refs[:-1]:
        total = total + arrived_ref[...].astype(jnp.float32)
    refs[-1][...] = total.astype(jnp.bfloat16)


def kernel_call(
    body, outs, operands, in_vmem=(), scratch=(), flops=0, moved=0, room=16
):
    vmem = pl.BlockSpec(memory_space=pltpu.VMEM)
    hbm = pl.BlockSpec(memory_space=pltpu.HBM)
    return pl.pallas_call(
        body,
        out_shape=outs,
        in_specs=[vmem if place in in_vmem else hbm for place in range(len(operands))],
        out_specs=(vmem,) * len(outs),
        scratch_shapes=list(scratch),
        compiler_params=pltpu.CompilerParams(vmem_limit_bytes=room * 1024 * 1024),
        cost_estimate=pl.CostEstimate(flops=flops, bytes_accessed=moved, transcendentals=0),
    )(*operands)


def swapped(value, axis, apart):
    count = lax.axis_size(axis)
    return lax.ppermute(value, axis, [(place, place ^ apart) for place in range(count)])


def gathered_plan(
    normed_input,
    stored_queries,
    stored_keys,
    stored_values,
    query_weight,
    key_matrix,
    value_matrix,
    output_weight,
    out_cotangent,
):
    bf16, f32 = jnp.bfloat16, jnp.float32
    rows, model = normed_input.shape
    blocks = lax.axis_size("seq")
    groups = lax.axis_size("head")
    tokens = rows * blocks
    q_cols = stored_queries.shape[1] // 2
    kv_cols = HEAD_SIZE
    wide = 2 * QUERIES_PER_KEY * rows
    packed_cols = 2 * q_cols + 2 * kv_cols
    shape = jax.ShapeDtypeStruct
    same, other = kernel_call(
        out_grad_kernel,
        (shape((rows, packed_cols), bf16),) * 2,
        (out_cotangent, output_weight, stored_queries, stored_keys, stored_values),
        scratch=(
            pltpu.VMEM(out_cotangent.shape, bf16),
            pltpu.VMEM(output_weight.shape, bf16),
            pltpu.SemaphoreType.DMA((7 + 2 * q_cols // HEAD_SIZE,)),
        ),
        flops=4 * rows * model * q_cols,
        moved=2 * model * (rows + 2 * q_cols),
        room=63,
    )
    held = {0: same}
    for apart in range(2, blocks):
        lowest, highest = 2, 1 << (apart.bit_length() - 1)
        while not apart & lowest:
            lowest *= 2
        through = lowest if apart % 2 else highest
        if lowest == highest:
            held[apart] = swapped(other if apart % 2 else same, "seq", apart)
        else:
            held[apart] = swapped(held[apart ^ through], "seq", through)
    held[1] = swapped(other, "seq", 1)
    cut = model // blocks
    keep, give, held[0] = kernel_call(
        turn_kernel,
        (
            shape((blocks // 2, 2, cut, rows), bf16),
            shape((blocks // 2, 2, cut, rows), bf16),
            shape(same.shape, bf16),
        ),
        (normed_input, out_cotangent, same, held[2], held[blocks // 2 + 1]),
        scratch=(
            pltpu.VMEM(normed_input.shape, bf16),
            pltpu.VMEM(out_cotangent.shape, bf16),
            pltpu.VMEM((2, model, rows), bf16),
            pltpu.SemaphoreType.DMA((3,)),
        ),
        moved=8 * rows * model,
        room=8,
    )
    columns = kernel_call(
        join_kernel,
        (shape((2, 2, cut, rows), bf16),) * (blocks // 2),
        (keep, swapped(give, "seq", 1)),
        in_vmem=range(2),
        moved=8 * rows * model,
        room=4,
    )
    columns = [columns[0]] + [
        swapped(columns[chip], "seq", 2 * chip) for chip in range(1, blocks // 2)
    ]
    dx_own, dx_far, grad_parts = kernel_call(
        functools.partial(attention_kernel, blocks),
        (
            shape((rows, q_cols + 2 * kv_cols), bf16),
            shape((rows, q_cols + 2 * kv_cols), bf16),
            shape((q_cols + kv_cols, tokens), bf16),
        ),
        [held[apart] for apart in range(blocks)],
        in_vmem=range(blocks),
        scratch=(
            pltpu.VMEM((tokens, packed_cols), bf16),
            pltpu.VMEM((tokens, wide), f32),
            pltpu.VMEM((tokens, wide), f32),
            pltpu.VMEM((tokens, tokens * QUERIES_PER_KEY), bf16),
            pltpu.VMEM((HEAD_SIZE, tokens * QUERIES_PER_KEY), bf16),
            pltpu.VMEM((1, tokens * QUERIES_PER_KEY), f32),
            pltpu.VMEM((tokens * QUERIES_PER_KEY, HEAD_SIZE), bf16),
            pltpu.VMEM((HEAD_SIZE, tokens), bf16),
            pltpu.VMEM((HEAD_SIZE, tokens), bf16),
            pltpu.VMEM((HEAD_SIZE, wide), f32),
            pltpu.VMEM((2 * rows, HEAD_SIZE), f32),
        ),
        flops=8 * tokens * tokens * q_cols,
        moved=2 * tokens * packed_cols,
    )
    dx_got = swapped(dx_far, "seq", 1)
    terms = {}
    for chosen in ((groups - 1,), tuple(range(groups - 2, -1, -1))):
        made = kernel_call(
            functools.partial(input_terms_kernel, chosen),
            tuple(shape((model // groups, rows), f32 if not apart else bf16) for apart in chosen),
            (dx_own, dx_got, query_weight, key_matrix, value_matrix),
            in_vmem=range(5),
            scratch=(pltpu.VMEM((rows, 2 * (q_cols + 2 * kv_cols)), bf16),),
            flops=2 * len(chosen) * rows * (model // groups) * 2 * (q_cols + 2 * kv_cols),
            moved=2 * len(chosen) * (model // groups) * 2 * (q_cols + 2 * kv_cols),
            room=4,
        )
        terms.update(zip(chosen, made))
    (pair_sum,) = kernel_call(
        add_kernel,
        (shape(terms[2].shape, bf16),),
        (terms[2], swapped(terms[3], "head", 1)),
        in_vmem=range(2),
        moved=6 * rows * (model // groups),
        room=4,
    )
    arrived = [swapped(terms[1], "head", 1), swapped(pair_sum, "head", 2)]
    grad_wvalue, grad_woutput, weights_done = kernel_call(
        weight_grad_kernel,
        (
            shape((model // blocks, 2 * kv_cols), f32),
            shape((model // blocks, 2 * q_cols), f32),
            shape((8, HEAD_SIZE), f32),
        ),
        (grad_parts, swapped(grad_parts, "seq", 1), *columns),
        in_vmem=range(2 + blocks // 2),
        scratch=(pltpu.VMEM((2, model // blocks, tokens), bf16),),
        room=8,
        flops=4 * tokens * (model // blocks) * (q_cols + kv_cols),
        moved=4 * (model // blocks) * (tokens + 2 * q_cols + 2 * kv_cols),
    )
    (grad_input,) = kernel_call(
        sum_kernel,
        (shape((model // groups, rows), bf16),),
        (weights_done, terms[0], *arrived),
        in_vmem=range(1, 4),
        moved=4 * groups * (model // groups) * rows,
    )
    return (grad_input.T, grad_wvalue, grad_woutput.T)


def power_of_two(count):
    return count & (count - 1) == 0


def local(normed_input, stored_queries, stored_keys, *others):
    blocks, groups = lax.axis_size("seq"), lax.axis_size("head")
    whole_window = normed_input.shape[0] * blocks <= WINDOW_LENGTH
    two_heads = stored_keys.shape[1] == 2 * HEAD_SIZE
    paired = blocks >= 4 and power_of_two(blocks) and groups == 4
    plan = gathered_plan if whole_window and two_heads and paired else windowed_plan
    return plan(normed_input, stored_queries, stored_keys, *others)


def windowed_plan(
    normed_input,
    stored_queries,
    stored_keys,
    stored_values,
    query_weight,
    key_matrix,
    value_matrix,
    output_weight,
    out_cotangent,
):
    tok_rows = normed_input.shape[0]
    blocks_seq = lax.axis_size("seq")
    seq_place = lax.axis_index("seq")
    reach_blocks = min(WINDOW_LENGTH // tok_rows, blocks_seq - 1)
    kv_heads = stored_keys.shape[1] // HEAD_SIZE
    output_gradient = jnp.dot(
        out_cotangent, output_weight.T, preferred_element_type=jnp.float32
    ).astype(jnp.bfloat16)
    pieces = [(stored_keys, stored_values)]
    current = (stored_keys, stored_values)
    for relay_step in range(reach_blocks):
        current = passed_along((current[0], current[1]), "seq", 1)
        pieces = [current] + pieces
    key_window = jnp.concatenate([piece[0] for piece in pieces], axis=0)
    value_window = jnp.concatenate([piece[1] for piece in pieces], axis=0)
    key_span = key_window.shape[0]
    query_pos = seq_place * tok_rows + jnp.arange(tok_rows, dtype=jnp.int32)
    key_pos = (seq_place - reach_blocks) * tok_rows + jnp.arange(key_span, dtype=jnp.int32)
    pos_gap = query_pos[:, None] - key_pos[None, :]
    allowed = (pos_gap >= 0) & (pos_gap < WINDOW_LENGTH) & (key_pos >= 0)[None, :]
    allowed_rows = jnp.tile(allowed, (QUERIES_PER_KEY, 1))
    query_stack = (
        stored_queries.reshape(tok_rows, kv_heads, QUERIES_PER_KEY, HEAD_SIZE)
        .transpose(1, 2, 0, 3)
        .reshape(kv_heads, QUERIES_PER_KEY * tok_rows, HEAD_SIZE)
    )
    grad_stack = (
        output_gradient.reshape(tok_rows, kv_heads, QUERIES_PER_KEY, HEAD_SIZE)
        .transpose(1, 2, 0, 3)
        .reshape(kv_heads, QUERIES_PER_KEY * tok_rows, HEAD_SIZE)
    )
    key_stack = key_window.reshape(key_span, kv_heads, HEAD_SIZE).transpose(1, 0, 2)
    value_stack = value_window.reshape(key_span, kv_heads, HEAD_SIZE).transpose(1, 0, 2)

    def per_head(head_items):
        query_head, key_head, value_head, grad_head = head_items
        attention_logits = logit_scale * jnp.dot(
            query_head, key_head.T, preferred_element_type=jnp.float32
        )
        masked = jnp.where(allowed_rows, attention_logits, -jnp.inf)
        row_top = jnp.max(masked, axis=1, keepdims=True)
        exp_scores = jnp.exp(masked - row_top)
        attn_prob = exp_scores / jnp.sum(exp_scores, axis=1, keepdims=True)
        probability_halfwidth = attn_prob.astype(jnp.bfloat16)
        attn_head = jnp.dot(
            probability_halfwidth, value_head, preferred_element_type=jnp.float32
        ).astype(jnp.bfloat16)
        row_delta = jnp.sum(
            grad_head.astype(jnp.float32) * attn_head.astype(jnp.float32), axis=1, keepdims=True
        )
        probability_gradient = jnp.dot(grad_head, value_head.T, preferred_element_type=jnp.float32)
        score_gradient = (attn_prob * (probability_gradient - row_delta)).astype(jnp.bfloat16)
        qgrad_head = (
            logit_scale * jnp.dot(score_gradient, key_head, preferred_element_type=jnp.float32)
        ).astype(jnp.bfloat16)
        key_partial = logit_scale * jnp.dot(
            score_gradient.T, query_head, preferred_element_type=jnp.float32
        )
        value_partial = jnp.dot(
            probability_halfwidth.T, grad_head, preferred_element_type=jnp.float32
        )
        return (attn_head, qgrad_head, key_partial, value_partial)

    attn_all, qgrad_all, key_all, value_all = lax.map(
        per_head, (query_stack, key_stack, value_stack, grad_stack)
    )
    attention_output = (
        attn_all.reshape(kv_heads, QUERIES_PER_KEY, tok_rows, HEAD_SIZE)
        .transpose(2, 0, 1, 3)
        .reshape(tok_rows, kv_heads * QUERIES_PER_KEY * HEAD_SIZE)
    )
    query_gradient = (
        qgrad_all.reshape(kv_heads, QUERIES_PER_KEY, tok_rows, HEAD_SIZE)
        .transpose(2, 0, 1, 3)
        .reshape(tok_rows, kv_heads * QUERIES_PER_KEY * HEAD_SIZE)
    )
    key_terms = key_all.transpose(1, 0, 2).reshape(key_span, kv_heads * HEAD_SIZE)
    value_terms = value_all.transpose(1, 0, 2).reshape(key_span, kv_heads * HEAD_SIZE)

    def take_slot(terms, slot_index):
        return terms[slot_index * tok_rows : (slot_index + 1) * tok_rows]

    key_sum = take_slot(key_terms, reach_blocks)
    value_sum = take_slot(value_terms, reach_blocks)
    for distance in range(1, reach_blocks + 1):
        received = passed_along(
            (
                take_slot(key_terms, reach_blocks - distance),
                take_slot(value_terms, reach_blocks - distance),
            ),
            "seq",
            -distance,
        )
        key_sum = key_sum + received[0]
        value_sum = value_sum + received[1]
    grad_key = key_sum.astype(jnp.bfloat16)
    grad_value = value_sum.astype(jnp.bfloat16)
    input_terms = jnp.dot(query_gradient, query_weight.T, preferred_element_type=jnp.float32)
    input_terms = input_terms + jnp.dot(grad_key, key_matrix.T, preferred_element_type=jnp.float32)
    input_terms = input_terms + jnp.dot(
        grad_value, value_matrix.T, preferred_element_type=jnp.float32
    )
    grad_input = lax.psum_scatter(input_terms, "head", scatter_dimension=1, tiled=True).astype(
        jnp.bfloat16
    )
    value_cols = grad_value.shape[1]
    input_cols = normed_input.T
    cot_cols = out_cotangent.T
    gathered = lax.psum_scatter(
        jnp.concatenate(
            [
                jnp.dot(input_cols, grad_value, preferred_element_type=jnp.float32),
                jnp.dot(cot_cols, attention_output, preferred_element_type=jnp.float32),
            ],
            axis=1,
        ),
        "seq",
        scatter_dimension=0,
        tiled=True,
    )
    grad_wvalue = gathered[:, :value_cols]
    grad_woutput = gathered[:, value_cols:].T
    return (grad_input, grad_wvalue, grad_woutput)


def solution(mesh):
    placed = (
        P("seq", None),
        P("seq", "head"),
        P("seq", "head"),
        P("seq", "head"),
        P(None, "head"),
        P(None, "head"),
        P(None, "head"),
        P("head", None),
        P("seq", None),
    )
    return jax.shard_map(
        local,
        mesh=mesh,
        in_specs=placed,
        out_specs=(P("seq", "head"), P("seq", "head"), P("head", "seq")),
        check_vma=False,
    )
```

```python
import functools

import jax
import jax.numpy as jnp
from jax import lax
from jax.experimental import pallas as pl
from jax.experimental.pallas import tpu as pltpu
from jax.sharding import PartitionSpec as P

HEAD_SIZE = 128
WINDOW_LENGTH = 4096
QUERIES_PER_KEY = 2


logit_scale = 1.0 / 12.0
log2_scale = 1.4426950408889634 / 12.0
excluded = -1e30


def passed_along(value, axis, steps):
    count = lax.axis_size(axis)
    leading, last = (max(0, -steps), min(count, count - steps))
    return lax.ppermute(value, axis, [(source, source + steps) for source in range(leading, last)])


NT = (((1,), (1,)), ((), ()))


def dot_nt(left, right):
    return lax.dot_general(left, right, NT, preferred_element_type=jnp.float32)


def dot_nn(left, right):
    return jnp.dot(left, right, preferred_element_type=jnp.float32)


def at(place, size):
    return pl.ds(pl.multiple_of(place * size, size), size)


def out_grad_kernel(
    cot_hbm, weight_hbm, q_hbm, k_hbm, v_hbm, same_ref, other_ref, cot_ref, weight_ref, sem
):
    core = lax.axis_index("seq") % 2
    halves = ((other_ref, 1 - core), (same_ref, core))
    rows = weight_ref.shape[0] // 2
    pieces = (sem.shape[0] - 6) // 3
    cut = weight_ref.shape[1] // pieces
    model_copies = []
    for piece in range(pieces):
        part = pl.ds(piece * cut, cut)
        model_copies.append(
            [
                pltpu.make_async_copy(
                    cot_hbm.at[:, part], cot_ref.at[:, part], sem.at[6 + 3 * piece]
                )
            ]
        )
        for place, (_, half) in enumerate(halves):
            model_copies[-1].append(
                pltpu.make_async_copy(
                    weight_hbm.at[at(half, rows), part],
                    weight_ref.at[pl.ds(place * rows, rows), part],
                    sem.at[7 + 3 * piece + place],
                )
            )
        for copy in model_copies[-1]:
            copy.start()
    plain_copies = []
    for place, (target, half) in enumerate(halves):
        first = 0
        for which, source in enumerate((q_hbm, k_hbm, v_hbm)):
            cols = source.shape[1] // 2
            plain_copies.append(
                pltpu.make_async_copy(
                    source.at[:, at(half, cols)],
                    target.at[:, pl.ds(first, cols)],
                    sem.at[3 * place + which],
                )
            )
            plain_copies[-1].start()
            first += cols
    total = None
    for piece in range(pieces):
        for copy in model_copies[piece]:
            copy.wait()
        part = slice(piece * cut, (piece + 1) * cut)
        product = dot_nt(weight_ref[:, part], cot_ref[:, part])
        total = product if total is None else total + product
    for place, (target, _) in enumerate(halves):
        for head in range(rows // HEAD_SIZE):
            row = place * rows + head * HEAD_SIZE
            target[:, first + head * HEAD_SIZE : first + (head + 1) * HEAD_SIZE] = total[
                row : row + HEAD_SIZE
            ].astype(jnp.bfloat16)
    for copy in plain_copies:
        copy.wait()


def turn_kernel(
    normed_hbm, cot_hbm, block_hbm, _, __, keep_ref, give_ref, own_ref, normed_ref, cot_ref, turned_ref, sem
):
    me = lax.axis_index("seq")
    cut = keep_ref.shape[2]
    copies = []
    for which, (source, target) in enumerate(
        ((normed_hbm, normed_ref), (cot_hbm, cot_ref), (block_hbm, own_ref))
    ):
        copies.append(pltpu.make_async_copy(source, target, sem.at[which]))
        copies[-1].start()
    for which, ref in enumerate((normed_ref, cot_ref)):
        copies[which].wait()
        turned_ref[which] = ref[...].astype(jnp.float32).T.astype(jnp.bfloat16)
        for chip in range(keep_ref.shape[0]):
            keep_ref[chip, which] = turned_ref[which, at(me ^ (2 * chip), cut)]
            give_ref[chip, which] = turned_ref[which, at(me ^ (2 * chip + 1), cut)]
    copies[2].wait()


def join_kernel(keep_ref, got_ref, *joined_refs):
    for chip, ref in enumerate(joined_refs):
        ref[0] = keep_ref[chip]
        ref[1] = got_ref[chip]


def attention_kernel(blocks, *refs):
    attention_body(refs[:blocks], *refs[blocks:])


def attention_body(
    block_refs,
    dx_own_ref,
    dx_far_ref,
    parts_ref,
    gathered_ref,
    score_even_ref,
    score_odd_ref,
    prob_ref,
    grad_t_ref,
    delta_ref,
    query_ref,
    value_t_ref,
    key_t_ref,
    dq_t_ref,
    dk_ref,
):
    me = lax.axis_index("seq")
    core, chip = me % 2, me // 2
    rows = dx_own_ref.shape[0]
    for apart, source in enumerate(block_refs):
        gathered_ref[at(me ^ apart, rows)] = source[...]
    tokens = gathered_ref.shape[0]
    size = 2 * rows
    steps = tokens // size
    wide = QUERIES_PER_KEY * size
    heads = QUERIES_PER_KEY
    key_cols = slice(heads * HEAD_SIZE, (heads + 1) * HEAD_SIZE)
    value_cols = slice((heads + 1) * HEAD_SIZE, (heads + 2) * HEAD_SIZE)
    grad_base = (heads + 2) * HEAD_SIZE
    value_t_ref[...] = gathered_ref[:, value_cols].T
    key_t_ref[...] = gathered_ref[:, key_cols].T
    key_place = lax.broadcasted_iota(jnp.int32, (size, wide), 0)
    query_place = lax.broadcasted_iota(jnp.int32, (size, wide), 1) % size
    allowed = key_place <= query_place

    for step in range(steps):
        span = (step + 1) * size
        own = slice(step * size, span)
        lanes = slice(step * wide, (step + 1) * wide)
        score_ref = score_odd_ref if step % 2 else score_even_ref
        queries = jnp.concatenate(
            [gathered_ref[own, h * HEAD_SIZE : (h + 1) * HEAD_SIZE] for h in range(heads)], axis=0
        )
        query_ref[lanes] = queries
        top = None
        for piece in range(step + 1):
            part = slice(piece * size, (piece + 1) * size)
            scores = dot_nt(gathered_ref[part, key_cols], queries)
            if piece == step:
                scores = jnp.where(allowed, scores, excluded)
            score_ref[part] = scores
            largest = jnp.max(scores.reshape(size // 8, 8, wide), axis=0)
            top = largest if top is None else jnp.maximum(top, largest)
        top = jnp.max(top, axis=0, keepdims=True)
        total = None
        for piece in range(step + 1):
            part = slice(piece * size, (piece + 1) * size)
            weights = jnp.exp2((score_ref[part] - top) * log2_scale)
            prob_ref[part, lanes] = weights.astype(jnp.bfloat16)
            summed = jnp.sum(weights.reshape(size // 8, 8, wide), axis=0)
            total = summed if total is None else total + summed
        inverse = 1.0 / jnp.sum(total, axis=0, keepdims=True)
        attn = dot_nn(value_t_ref[:, :span], prob_ref[:span, lanes]) * inverse
        for h in range(heads):
            parts_ref[h * HEAD_SIZE : (h + 1) * HEAD_SIZE, own] = attn[
                :, h * size : (h + 1) * size
            ].astype(jnp.bfloat16)
        grads_t = jnp.concatenate(
            [
                gathered_ref[
                    block * rows : (block + 1) * rows,
                    grad_base + h * HEAD_SIZE : grad_base + (h + 1) * HEAD_SIZE,
                ]
                for h in range(heads)
                for block in (2 * step, 2 * step + 1)
            ],
            axis=1,
        )
        grads_t = (grads_t.astype(jnp.float32) * inverse).astype(jnp.bfloat16)
        grad_t_ref[:, lanes] = grads_t
        delta_ref[:, lanes] = jnp.sum(grads_t.astype(jnp.float32) * attn, axis=0, keepdims=True)

    for step in range(steps):
        own = slice(step * size, (step + 1) * size)
        parts_ref[heads * HEAD_SIZE :, own] = dot_nt(
            grad_t_ref[:, step * wide :], prob_ref[own, step * wide :]
        ).astype(jnp.bfloat16)

    dq_t_ref[...] = jnp.zeros_like(dq_t_ref)
    dk_ref[...] = jnp.zeros_like(dk_ref)
    for step in range(steps):
        key_step = jnp.minimum(chip, step)
        query_step = jnp.maximum(chip, step)
        dprob = dot_nn(
            gathered_ref[at(key_step, size), value_cols], grad_t_ref[:, at(query_step, wide)]
        )
        dscore = (
            prob_ref[at(key_step, size), at(query_step, wide)].astype(jnp.float32)
            * (dprob - delta_ref[:, at(query_step, wide)])
        ).astype(jnp.bfloat16)

        @pl.when(step <= chip)
        def _():
            dq_t_ref[...] += dot_nn(key_t_ref[:, at(key_step, size)], dscore)

        @pl.when(step >= chip)
        def _():
            dk_ref[...] += dot_nn(dscore, query_ref[at(query_step, wide)])

    for target, half in ((dx_far_ref, 1 - core), (dx_own_ref, core)):
        for h in range(heads):
            target[:, h * HEAD_SIZE : (h + 1) * HEAD_SIZE] = (
                (logit_scale * dq_t_ref[:, at(2 * h + half, rows)])
                .T.astype(jnp.bfloat16)
            )
        target[:, key_cols] = (logit_scale * dk_ref[at(half, rows)]).astype(jnp.bfloat16)
        target[:, value_cols] = parts_ref[heads * HEAD_SIZE :, at(2 * chip + half, rows)].T


def input_terms_kernel(apart_groups, own_ref, far_ref, wq_ref, wk_ref, wv_ref, *refs):
    terms, dx_ref = refs[-1 - len(apart_groups) : -1], refs[-1]
    core = lax.axis_index("seq") % 2
    group = lax.axis_index("head")
    q_cols = wq_ref.shape[1] // 2
    kv_cols = wk_ref.shape[1] // 2
    for source, half in ((own_ref, core), (far_ref, 1 - core)):
        dx_ref[:, at(half, q_cols)] = source[:, :q_cols]
        dx_ref[:, pl.ds(pl.multiple_of(2 * q_cols + half * kv_cols, kv_cols), kv_cols)] = source[
            :, q_cols : q_cols + kv_cols
        ]
        dx_ref[
            :, pl.ds(pl.multiple_of(2 * q_cols + (2 + half) * kv_cols, kv_cols), kv_cols)
        ] = source[:, q_cols + kv_cols :]
    for apart, target in zip(apart_groups, terms):
        cut = target.shape[0]
        place = at(group ^ apart, cut)
        target[...] = (
            dot_nt(wq_ref[place], dx_ref[:, : 2 * q_cols])
            + dot_nt(wk_ref[place], dx_ref[:, 2 * q_cols : 2 * q_cols + 2 * kv_cols])
            + dot_nt(wv_ref[place], dx_ref[:, 2 * q_cols + 2 * kv_cols :])
        ).astype(target.dtype)


def weight_grad_kernel(own_ref, far_ref, *refs):
    column_refs, (wvalue_ref, woutput_ref, done_ref, joined_ref) = refs[:-4], refs[-4:]
    done_ref[...] = jnp.zeros_like(done_ref)
    me = lax.axis_index("seq")
    core = me % 2
    for chip, ref in enumerate(column_refs):
        for far in range(2):
            joined_ref[:, :, at(me ^ (2 * chip + far), ref.shape[3])] = ref[far]
    kv_cols = wvalue_ref.shape[1] // 2
    q_cols = woutput_ref.shape[1] // 2
    for half, ref in ((core, own_ref), (1 - core, far_ref)):
        woutput_ref[:, at(half, q_cols)] = dot_nt(joined_ref[1], ref[:q_cols])
        wvalue_ref[:, at(half, kv_cols)] = dot_nt(joined_ref[0], ref[q_cols:])


def add_kernel(own_ref, arrived_ref, sum_ref):
    total = own_ref[...].astype(jnp.float32) + arrived_ref[...].astype(jnp.float32)
    sum_ref[...] = total.astype(jnp.bfloat16)


def sum_kernel(_, own_ref, *refs):
    total = own_ref[...]
    for arrived_ref in refs[:-1]:
        total = total + arrived_ref[...].astype(jnp.float32)
    refs[-1][...] = total.astype(jnp.bfloat16)


def kernel_call(
    body, outs, operands, in_vmem=(), scratch=(), flops=0, moved=0, room=16
):
    vmem = pl.BlockSpec(memory_space=pltpu.VMEM)
    hbm = pl.BlockSpec(memory_space=pltpu.HBM)
    return pl.pallas_call(
        body,
        out_shape=outs,
        in_specs=[vmem if place in in_vmem else hbm for place in range(len(operands))],
        out_specs=(vmem,) * len(outs),
        scratch_shapes=list(scratch),
        compiler_params=pltpu.CompilerParams(vmem_limit_bytes=room * 1024 * 1024),
        cost_estimate=pl.CostEstimate(flops=flops, bytes_accessed=moved, transcendentals=0),
    )(*operands)


def swapped(value, axis, apart):
    count = lax.axis_size(axis)
    return lax.ppermute(value, axis, [(place, place ^ apart) for place in range(count)])


def gathered_plan(
    normed_input,
    stored_queries,
    stored_keys,
    stored_values,
    query_weight,
    key_matrix,
    value_matrix,
    output_weight,
    out_cotangent,
):
    bf16, f32 = jnp.bfloat16, jnp.float32
    rows, model = normed_input.shape
    blocks = lax.axis_size("seq")
    groups = lax.axis_size("head")
    tokens = rows * blocks
    q_cols = stored_queries.shape[1] // 2
    kv_cols = HEAD_SIZE
    wide = 2 * QUERIES_PER_KEY * rows
    packed_cols = 2 * q_cols + 2 * kv_cols
    pieces = 3 if model % (6 * HEAD_SIZE) == 0 else 1
    shape = jax.ShapeDtypeStruct
    same, other = kernel_call(
        out_grad_kernel,
        (shape((rows, packed_cols), bf16),) * 2,
        (out_cotangent, output_weight, stored_queries, stored_keys, stored_values),
        scratch=(
            pltpu.VMEM(out_cotangent.shape, bf16),
            pltpu.VMEM(output_weight.shape, bf16),
            pltpu.SemaphoreType.DMA((6 + 3 * pieces,)),
        ),
        flops=4 * rows * model * q_cols,
        moved=2 * model * (rows + 2 * q_cols),
        room=63,
    )
    held = {0: same}
    for apart in range(2, blocks):
        lowest, highest = 2, 1 << (apart.bit_length() - 1)
        while not apart & lowest:
            lowest *= 2
        through = lowest if apart % 2 else highest
        if lowest == highest:
            held[apart] = swapped(other if apart % 2 else same, "seq", apart)
        else:
            held[apart] = swapped(held[apart ^ through], "seq", through)
    held[1] = swapped(other, "seq", 1)
    cut = model // blocks
    keep, give, held[0] = kernel_call(
        turn_kernel,
        (
            shape((blocks // 2, 2, cut, rows), bf16),
            shape((blocks // 2, 2, cut, rows), bf16),
            shape(same.shape, bf16),
        ),
        (normed_input, out_cotangent, same, held[2], held[blocks // 2 + 1]),
        scratch=(
            pltpu.VMEM(normed_input.shape, bf16),
            pltpu.VMEM(out_cotangent.shape, bf16),
            pltpu.VMEM((2, model, rows), bf16),
            pltpu.SemaphoreType.DMA((3,)),
        ),
        moved=8 * rows * model,
        room=8,
    )
    columns = kernel_call(
        join_kernel,
        (shape((2, 2, cut, rows), bf16),) * (blocks // 2),
        (keep, swapped(give, "seq", 1)),
        in_vmem=range(2),
        moved=8 * rows * model,
        room=4,
    )
    columns = [columns[0]] + [
        swapped(columns[chip], "seq", 2 * chip) for chip in range(1, blocks // 2)
    ]
    dx_own, dx_far, grad_parts = kernel_call(
        functools.partial(attention_kernel, blocks),
        (
            shape((rows, q_cols + 2 * kv_cols), bf16),
            shape((rows, q_cols + 2 * kv_cols), bf16),
            shape((q_cols + kv_cols, tokens), bf16),
        ),
        [held[apart] for apart in range(blocks)],
        in_vmem=range(blocks),
        scratch=(
            pltpu.VMEM((tokens, packed_cols), bf16),
            pltpu.VMEM((tokens, wide), f32),
            pltpu.VMEM((tokens, wide), f32),
            pltpu.VMEM((tokens, tokens * QUERIES_PER_KEY), bf16),
            pltpu.VMEM((HEAD_SIZE, tokens * QUERIES_PER_KEY), bf16),
            pltpu.VMEM((1, tokens * QUERIES_PER_KEY), f32),
            pltpu.VMEM((tokens * QUERIES_PER_KEY, HEAD_SIZE), bf16),
            pltpu.VMEM((HEAD_SIZE, tokens), bf16),
            pltpu.VMEM((HEAD_SIZE, tokens), bf16),
            pltpu.VMEM((HEAD_SIZE, wide), f32),
            pltpu.VMEM((2 * rows, HEAD_SIZE), f32),
        ),
        moved=2 * tokens * packed_cols,
    )
    dx_got = swapped(dx_far, "seq", 1)
    terms = {}
    for chosen, waited in (((3,), []), ((2, 1, 0), [columns[1], columns[blocks // 4]])):
        made = kernel_call(
            functools.partial(input_terms_kernel, chosen),
            tuple(shape((model // groups, rows), f32 if not apart else bf16) for apart in chosen),
            (dx_own, dx_got, query_weight, key_matrix, value_matrix, *waited),
            in_vmem=range(5),
            scratch=(pltpu.VMEM((rows, 2 * (q_cols + 2 * kv_cols)), bf16),),
            flops=2 * len(chosen) * rows * (model // groups) * 2 * (q_cols + 2 * kv_cols),
            moved=2 * len(chosen) * (model // groups) * 2 * (q_cols + 2 * kv_cols),
            room=4,
        )
        terms.update(zip(chosen, made))
    (pair_sum,) = kernel_call(
        add_kernel,
        (shape(terms[2].shape, bf16),),
        (terms[2], swapped(terms[3], "head", 1)),
        in_vmem=range(2),
        moved=6 * rows * (model // groups),
        room=4,
    )
    arrived = [swapped(terms[1], "head", 1), swapped(pair_sum, "head", 2)]
    grad_wvalue, grad_woutput, weights_done = kernel_call(
        weight_grad_kernel,
        (
            shape((model // blocks, 2 * kv_cols), f32),
            shape((model // blocks, 2 * q_cols), f32),
            shape((8, HEAD_SIZE), f32),
        ),
        (grad_parts, swapped(grad_parts, "seq", 1), *columns),
        in_vmem=range(2 + blocks // 2),
        scratch=(pltpu.VMEM((2, model // blocks, tokens), bf16),),
        room=8,
        flops=4 * tokens * (model // blocks) * (q_cols + kv_cols),
        moved=4 * (model // blocks) * (tokens + 2 * q_cols + 2 * kv_cols),
    )
    (grad_input,) = kernel_call(
        sum_kernel,
        (shape((model // groups, rows), bf16),),
        (weights_done, terms[0], *arrived),
        in_vmem=range(1, 4),
        moved=4 * groups * (model // groups) * rows,
    )
    return (grad_input.T, grad_wvalue, grad_woutput.T)


def power_of_two(count):
    return count & (count - 1) == 0


def local(normed_input, stored_queries, stored_keys, *others):
    blocks, groups = lax.axis_size("seq"), lax.axis_size("head")
    whole_window = normed_input.shape[0] * blocks <= WINDOW_LENGTH
    two_heads = stored_keys.shape[1] == 2 * HEAD_SIZE
    paired = blocks >= 4 and power_of_two(blocks) and groups == 4
    plan = gathered_plan if whole_window and two_heads and paired else windowed_plan
    return plan(normed_input, stored_queries, stored_keys, *others)


def windowed_plan(
    normed_input,
    stored_queries,
    stored_keys,
    stored_values,
    query_weight,
    key_matrix,
    value_matrix,
    output_weight,
    out_cotangent,
):
    tok_rows = normed_input.shape[0]
    blocks_seq = lax.axis_size("seq")
    seq_place = lax.axis_index("seq")
    reach_blocks = min(WINDOW_LENGTH // tok_rows, blocks_seq - 1)
    kv_heads = stored_keys.shape[1] // HEAD_SIZE
    output_gradient = jnp.dot(
        out_cotangent, output_weight.T, preferred_element_type=jnp.float32
    ).astype(jnp.bfloat16)
    pieces = [(stored_keys, stored_values)]
    current = (stored_keys, stored_values)
    for relay_step in range(reach_blocks):
        current = passed_along((current[0], current[1]), "seq", 1)
        pieces = [current] + pieces
    key_window = jnp.concatenate([piece[0] for piece in pieces], axis=0)
    value_window = jnp.concatenate([piece[1] for piece in pieces], axis=0)
    key_span = key_window.shape[0]
    query_pos = seq_place * tok_rows + jnp.arange(tok_rows, dtype=jnp.int32)
    key_pos = (seq_place - reach_blocks) * tok_rows + jnp.arange(key_span, dtype=jnp.int32)
    pos_gap = query_pos[:, None] - key_pos[None, :]
    allowed = (pos_gap >= 0) & (pos_gap < WINDOW_LENGTH) & (key_pos >= 0)[None, :]
    allowed_rows = jnp.tile(allowed, (QUERIES_PER_KEY, 1))
    query_stack = (
        stored_queries.reshape(tok_rows, kv_heads, QUERIES_PER_KEY, HEAD_SIZE)
        .transpose(1, 2, 0, 3)
        .reshape(kv_heads, QUERIES_PER_KEY * tok_rows, HEAD_SIZE)
    )
    grad_stack = (
        output_gradient.reshape(tok_rows, kv_heads, QUERIES_PER_KEY, HEAD_SIZE)
        .transpose(1, 2, 0, 3)
        .reshape(kv_heads, QUERIES_PER_KEY * tok_rows, HEAD_SIZE)
    )
    key_stack = key_window.reshape(key_span, kv_heads, HEAD_SIZE).transpose(1, 0, 2)
    value_stack = value_window.reshape(key_span, kv_heads, HEAD_SIZE).transpose(1, 0, 2)

    def per_head(head_items):
        query_head, key_head, value_head, grad_head = head_items
        attention_logits = logit_scale * jnp.dot(
            query_head, key_head.T, preferred_element_type=jnp.float32
        )
        masked = jnp.where(allowed_rows, attention_logits, -jnp.inf)
        row_top = jnp.max(masked, axis=1, keepdims=True)
        exp_scores = jnp.exp(masked - row_top)
        attn_prob = exp_scores / jnp.sum(exp_scores, axis=1, keepdims=True)
        probability_halfwidth = attn_prob.astype(jnp.bfloat16)
        attn_head = jnp.dot(
            probability_halfwidth, value_head, preferred_element_type=jnp.float32
        ).astype(jnp.bfloat16)
        row_delta = jnp.sum(
            grad_head.astype(jnp.float32) * attn_head.astype(jnp.float32), axis=1, keepdims=True
        )
        probability_gradient = jnp.dot(grad_head, value_head.T, preferred_element_type=jnp.float32)
        score_gradient = (attn_prob * (probability_gradient - row_delta)).astype(jnp.bfloat16)
        qgrad_head = (
            logit_scale * jnp.dot(score_gradient, key_head, preferred_element_type=jnp.float32)
        ).astype(jnp.bfloat16)
        key_partial = logit_scale * jnp.dot(
            score_gradient.T, query_head, preferred_element_type=jnp.float32
        )
        value_partial = jnp.dot(
            probability_halfwidth.T, grad_head, preferred_element_type=jnp.float32
        )
        return (attn_head, qgrad_head, key_partial, value_partial)

    attn_all, qgrad_all, key_all, value_all = lax.map(
        per_head, (query_stack, key_stack, value_stack, grad_stack)
    )
    attention_output = (
        attn_all.reshape(kv_heads, QUERIES_PER_KEY, tok_rows, HEAD_SIZE)
        .transpose(2, 0, 1, 3)
        .reshape(tok_rows, kv_heads * QUERIES_PER_KEY * HEAD_SIZE)
    )
    query_gradient = (
        qgrad_all.reshape(kv_heads, QUERIES_PER_KEY, tok_rows, HEAD_SIZE)
        .transpose(2, 0, 1, 3)
        .reshape(tok_rows, kv_heads * QUERIES_PER_KEY * HEAD_SIZE)
    )
    key_terms = key_all.transpose(1, 0, 2).reshape(key_span, kv_heads * HEAD_SIZE)
    value_terms = value_all.transpose(1, 0, 2).reshape(key_span, kv_heads * HEAD_SIZE)

    def take_slot(terms, slot_index):
        return terms[slot_index * tok_rows : (slot_index + 1) * tok_rows]

    key_sum = take_slot(key_terms, reach_blocks)
    value_sum = take_slot(value_terms, reach_blocks)
    for distance in range(1, reach_blocks + 1):
        received = passed_along(
            (
                take_slot(key_terms, reach_blocks - distance),
                take_slot(value_terms, reach_blocks - distance),
            ),
            "seq",
            -distance,
        )
        key_sum = key_sum + received[0]
        value_sum = value_sum + received[1]
    grad_key = key_sum.astype(jnp.bfloat16)
    grad_value = value_sum.astype(jnp.bfloat16)
    input_terms = jnp.dot(query_gradient, query_weight.T, preferred_element_type=jnp.float32)
    input_terms = input_terms + jnp.dot(grad_key, key_matrix.T, preferred_element_type=jnp.float32)
    input_terms = input_terms + jnp.dot(
        grad_value, value_matrix.T, preferred_element_type=jnp.float32
    )
    grad_input = lax.psum_scatter(input_terms, "head", scatter_dimension=1, tiled=True).astype(
        jnp.bfloat16
    )
    value_cols = grad_value.shape[1]
    input_cols = normed_input.T
    cot_cols = out_cotangent.T
    gathered = lax.psum_scatter(
        jnp.concatenate(
            [
                jnp.dot(input_cols, grad_value, preferred_element_type=jnp.float32),
                jnp.dot(cot_cols, attention_output, preferred_element_type=jnp.float32),
            ],
            axis=1,
        ),
        "seq",
        scatter_dimension=0,
        tiled=True,
    )
    grad_wvalue = gathered[:, :value_cols]
    grad_woutput = gathered[:, value_cols:].T
    return (grad_input, grad_wvalue, grad_woutput)


def solution(mesh):
    placed = (
        P("seq", None),
        P("seq", "head"),
        P("seq", "head"),
        P("seq", "head"),
        P(None, "head"),
        P(None, "head"),
        P(None, "head"),
        P("head", None),
        P("seq", None),
    )
    return jax.shard_map(
        local,
        mesh=mesh,
        in_specs=placed,
        out_specs=(P("seq", "head"), P("seq", "head"), P("head", "seq")),
        check_vma=False,
    )
```

```python
import functools

import jax
import jax.numpy as jnp
from jax import lax
from jax.experimental import pallas as pl
from jax.experimental.pallas import tpu as pltpu
from jax.sharding import PartitionSpec as P

HEAD_SIZE = 128
WINDOW_LENGTH = 4096
QUERIES_PER_KEY = 2


logit_scale = 1.0 / 12.0
log2_scale = 1.4426950408889634 / 12.0
excluded = -1e30


def passed_along(value, axis, steps):
    count = lax.axis_size(axis)
    leading, last = (max(0, -steps), min(count, count - steps))
    return lax.ppermute(value, axis, [(source, source + steps) for source in range(leading, last)])


NT = (((1,), (1,)), ((), ()))


def dot_nt(left, right):
    return lax.dot_general(left, right, NT, preferred_element_type=jnp.float32)


def dot_nn(left, right):
    return jnp.dot(left, right, preferred_element_type=jnp.float32)


def at(place, size):
    return pl.ds(pl.multiple_of(place * size, size), size)


def out_grad_kernel(
    cot_hbm, weight_hbm, q_hbm, k_hbm, v_hbm, same_ref, other_ref, cot_ref, weight_ref, sem
):
    core = lax.axis_index("seq") % 2
    halves = ((other_ref, 1 - core), (same_ref, core))
    rows = weight_ref.shape[0] // 2
    pieces = (sem.shape[0] - 6) // 3
    cut = weight_ref.shape[1] // pieces
    model_copies = []
    for piece in range(pieces):
        part = pl.ds(piece * cut, cut)
        model_copies.append(
            [
                pltpu.make_async_copy(
                    cot_hbm.at[:, part], cot_ref.at[:, part], sem.at[6 + 3 * piece]
                )
            ]
        )
        for place, (_, half) in enumerate(halves):
            model_copies[-1].append(
                pltpu.make_async_copy(
                    weight_hbm.at[at(half, rows), part],
                    weight_ref.at[pl.ds(place * rows, rows), part],
                    sem.at[7 + 3 * piece + place],
                )
            )
        for copy in model_copies[-1]:
            copy.start()
    plain_copies = []
    for place, (target, half) in enumerate(halves):
        first = 0
        for which, source in enumerate((q_hbm, k_hbm, v_hbm)):
            cols = source.shape[1] // 2
            plain_copies.append(
                pltpu.make_async_copy(
                    source.at[:, at(half, cols)],
                    target.at[:, pl.ds(first, cols)],
                    sem.at[3 * place + which],
                )
            )
            plain_copies[-1].start()
            first += cols
    total = None
    for piece in range(pieces):
        for copy in model_copies[piece]:
            copy.wait()
        part = slice(piece * cut, (piece + 1) * cut)
        product = dot_nt(weight_ref[:, part], cot_ref[:, part])
        total = product if total is None else total + product
    for place, (target, _) in enumerate(halves):
        for head in range(rows // HEAD_SIZE):
            row = place * rows + head * HEAD_SIZE
            target[:, first + head * HEAD_SIZE : first + (head + 1) * HEAD_SIZE] = total[
                row : row + HEAD_SIZE
            ].astype(jnp.bfloat16)
    for copy in plain_copies:
        copy.wait()


def turn_kernel(normed_hbm, cot_hbm, block_hbm, _, __, *refs):
    *column_refs, own_ref, normed_ref, cot_ref, turned_ref, sem = refs
    me = lax.axis_index("seq")
    cut = column_refs[0].shape[2]
    copies = []
    for which, (source, target) in enumerate(
        ((normed_hbm, normed_ref), (cot_hbm, cot_ref), (block_hbm, own_ref))
    ):
        copies.append(pltpu.make_async_copy(source, target, sem.at[which]))
        copies[-1].start()
    for which, ref in enumerate((normed_ref, cot_ref)):
        copies[which].wait()
        turned_ref[which] = ref[...].astype(jnp.float32).T.astype(jnp.bfloat16)
        for chip, target in enumerate(column_refs):
            for far in range(2):
                target[far, which] = turned_ref[which, at(me ^ (2 * chip + far), cut)]
    copies[2].wait()


def pass_on_kernel(_, *refs):
    *column_refs, give_ref = refs
    for chip, ref in enumerate(column_refs):
        give_ref[chip] = ref[1]


def attention_kernel(blocks, *refs):
    attention_body(refs[:blocks], *refs[blocks:])


def attention_body(
    block_refs,
    dx_own_ref,
    dx_far_ref,
    parts_ref,
    gathered_ref,
    score_even_ref,
    score_odd_ref,
    prob_ref,
    grad_t_ref,
    delta_ref,
    query_ref,
    value_t_ref,
    key_t_ref,
    dq_t_ref,
    dk_ref,
):
    me = lax.axis_index("seq")
    core, chip = me % 2, me // 2
    rows = dx_own_ref.shape[0]
    for apart, source in enumerate(block_refs):
        gathered_ref[at(me ^ apart, rows)] = source[...]
    tokens = gathered_ref.shape[0]
    size = 2 * rows
    steps = tokens // size
    wide = QUERIES_PER_KEY * size
    heads = QUERIES_PER_KEY
    key_cols = slice(heads * HEAD_SIZE, (heads + 1) * HEAD_SIZE)
    value_cols = slice((heads + 1) * HEAD_SIZE, (heads + 2) * HEAD_SIZE)
    grad_base = (heads + 2) * HEAD_SIZE
    value_t_ref[...] = gathered_ref[:, value_cols].T
    key_t_ref[...] = gathered_ref[:, key_cols].T
    key_place = lax.broadcasted_iota(jnp.int32, (size, wide), 0)
    query_place = lax.broadcasted_iota(jnp.int32, (size, wide), 1) % size
    allowed = key_place <= query_place

    for step in range(steps):
        span = (step + 1) * size
        own = slice(step * size, span)
        lanes = slice(step * wide, (step + 1) * wide)
        score_ref = score_odd_ref if step % 2 else score_even_ref
        queries = jnp.concatenate(
            [gathered_ref[own, h * HEAD_SIZE : (h + 1) * HEAD_SIZE] for h in range(heads)], axis=0
        )
        query_ref[lanes] = queries
        top = None
        for piece in range(step + 1):
            part = slice(piece * size, (piece + 1) * size)
            scores = dot_nt(gathered_ref[part, key_cols], queries)
            if piece == step:
                scores = jnp.where(allowed, scores, excluded)
            score_ref[part] = scores
            largest = jnp.max(scores.reshape(size // 8, 8, wide), axis=0)
            top = largest if top is None else jnp.maximum(top, largest)
        top = jnp.max(top, axis=0, keepdims=True)
        total = None
        for piece in range(step + 1):
            part = slice(piece * size, (piece + 1) * size)
            weights = jnp.exp2((score_ref[part] - top) * log2_scale)
            prob_ref[part, lanes] = weights.astype(jnp.bfloat16)
            summed = jnp.sum(weights.reshape(size // 8, 8, wide), axis=0)
            total = summed if total is None else total + summed
        inverse = 1.0 / jnp.sum(total, axis=0, keepdims=True)
        attn = dot_nn(value_t_ref[:, :span], prob_ref[:span, lanes]) * inverse
        for h in range(heads):
            parts_ref[h * HEAD_SIZE : (h + 1) * HEAD_SIZE, own] = attn[
                :, h * size : (h + 1) * size
            ].astype(jnp.bfloat16)
        grads_t = jnp.concatenate(
            [
                gathered_ref[
                    block * rows : (block + 1) * rows,
                    grad_base + h * HEAD_SIZE : grad_base + (h + 1) * HEAD_SIZE,
                ]
                for h in range(heads)
                for block in (2 * step, 2 * step + 1)
            ],
            axis=1,
        )
        grads_t = (grads_t.astype(jnp.float32) * inverse).astype(jnp.bfloat16)
        grad_t_ref[:, lanes] = grads_t
        delta_ref[:, lanes] = jnp.sum(grads_t.astype(jnp.float32) * attn, axis=0, keepdims=True)

    for step in range(steps):
        own = slice(step * size, (step + 1) * size)
        parts_ref[heads * HEAD_SIZE :, own] = dot_nt(
            grad_t_ref[:, step * wide :], prob_ref[own, step * wide :]
        ).astype(jnp.bfloat16)

    dq_t_ref[...] = jnp.zeros_like(dq_t_ref)
    dk_ref[...] = jnp.zeros_like(dk_ref)
    for step in range(steps):
        key_step = jnp.minimum(chip, step)
        query_step = jnp.maximum(chip, step)
        dprob = dot_nn(
            gathered_ref[at(key_step, size), value_cols], grad_t_ref[:, at(query_step, wide)]
        )
        dscore = (
            prob_ref[at(key_step, size), at(query_step, wide)].astype(jnp.float32)
            * (dprob - delta_ref[:, at(query_step, wide)])
        ).astype(jnp.bfloat16)

        @pl.when(step <= chip)
        def _():
            dq_t_ref[...] += dot_nn(key_t_ref[:, at(key_step, size)], dscore)

        @pl.when(step >= chip)
        def _():
            dk_ref[...] += dot_nn(dscore, query_ref[at(query_step, wide)])

    for target, half in ((dx_far_ref, 1 - core), (dx_own_ref, core)):
        for h in range(heads):
            target[:, h * HEAD_SIZE : (h + 1) * HEAD_SIZE] = (
                (logit_scale * dq_t_ref[:, at(2 * h + half, rows)])
                .T.astype(jnp.bfloat16)
            )
        target[:, key_cols] = (logit_scale * dk_ref[at(half, rows)]).astype(jnp.bfloat16)
        target[:, value_cols] = parts_ref[heads * HEAD_SIZE :, at(2 * chip + half, rows)].T


def input_terms_kernel(apart_groups, own_ref, far_ref, wq_ref, wk_ref, wv_ref, *refs):
    terms, dx_ref = refs[-1 - len(apart_groups) : -1], refs[-1]
    core = lax.axis_index("seq") % 2
    group = lax.axis_index("head")
    q_cols = wq_ref.shape[1] // 2
    kv_cols = wk_ref.shape[1] // 2
    for source, half in ((own_ref, core), (far_ref, 1 - core)):
        dx_ref[:, at(half, q_cols)] = source[:, :q_cols]
        dx_ref[:, pl.ds(pl.multiple_of(2 * q_cols + half * kv_cols, kv_cols), kv_cols)] = source[
            :, q_cols : q_cols + kv_cols
        ]
        dx_ref[
            :, pl.ds(pl.multiple_of(2 * q_cols + (2 + half) * kv_cols, kv_cols), kv_cols)
        ] = source[:, q_cols + kv_cols :]
    for apart, target in zip(apart_groups, terms):
        cut = target.shape[0]
        place = at(group ^ apart, cut)
        target[...] = (
            dot_nt(wq_ref[place], dx_ref[:, : 2 * q_cols])
            + dot_nt(wk_ref[place], dx_ref[:, 2 * q_cols : 2 * q_cols + 2 * kv_cols])
            + dot_nt(wv_ref[place], dx_ref[:, 2 * q_cols + 2 * kv_cols :])
        ).astype(target.dtype)


def weight_grad_kernel(own_ref, far_ref, *refs):
    column_refs, (wvalue_ref, woutput_ref, done_ref, joined_ref) = refs[:-4], refs[-4:]
    done_ref[...] = jnp.zeros_like(done_ref)
    me = lax.axis_index("seq")
    core = me % 2
    *column_refs, got_ref = column_refs
    for chip, ref in enumerate(column_refs):
        joined_ref[:, :, at(me ^ (2 * chip), ref.shape[3])] = ref[0]
        joined_ref[:, :, at(me ^ (2 * chip + 1), ref.shape[3])] = got_ref[chip]
    kv_cols = wvalue_ref.shape[1] // 2
    q_cols = woutput_ref.shape[1] // 2
    for half, ref in ((core, own_ref), (1 - core, far_ref)):
        woutput_ref[:, at(half, q_cols)] = dot_nt(joined_ref[1], ref[:q_cols])
        wvalue_ref[:, at(half, kv_cols)] = dot_nt(joined_ref[0], ref[q_cols:])


def add_kernel(own_ref, arrived_ref, sum_ref):
    total = own_ref[...].astype(jnp.float32) + arrived_ref[...].astype(jnp.float32)
    sum_ref[...] = total.astype(jnp.bfloat16)


def sum_kernel(_, own_ref, *refs):
    total = own_ref[...]
    for arrived_ref in refs[:-1]:
        total = total + arrived_ref[...].astype(jnp.float32)
    refs[-1][...] = total.astype(jnp.bfloat16)


def kernel_call(
    body, outs, operands, in_vmem=(), scratch=(), flops=0, moved=0, room=16
):
    vmem = pl.BlockSpec(memory_space=pltpu.VMEM)
    hbm = pl.BlockSpec(memory_space=pltpu.HBM)
    return pl.pallas_call(
        body,
        out_shape=outs,
        in_specs=[vmem if place in in_vmem else hbm for place in range(len(operands))],
        out_specs=(vmem,) * len(outs),
        scratch_shapes=list(scratch),
        compiler_params=pltpu.CompilerParams(vmem_limit_bytes=room * 1024 * 1024),
        cost_estimate=pl.CostEstimate(flops=flops, bytes_accessed=moved, transcendentals=0),
    )(*operands)


def swapped(value, axis, apart):
    count = lax.axis_size(axis)
    return lax.ppermute(value, axis, [(place, place ^ apart) for place in range(count)])


def gathered_plan(
    normed_input,
    stored_queries,
    stored_keys,
    stored_values,
    query_weight,
    key_matrix,
    value_matrix,
    output_weight,
    out_cotangent,
):
    bf16, f32 = jnp.bfloat16, jnp.float32
    rows, model = normed_input.shape
    blocks = lax.axis_size("seq")
    groups = lax.axis_size("head")
    tokens = rows * blocks
    q_cols = stored_queries.shape[1] // 2
    kv_cols = HEAD_SIZE
    wide = 2 * QUERIES_PER_KEY * rows
    packed_cols = 2 * q_cols + 2 * kv_cols
    pieces = 3 if model % (6 * HEAD_SIZE) == 0 else 1
    shape = jax.ShapeDtypeStruct
    same, other = kernel_call(
        out_grad_kernel,
        (shape((rows, packed_cols), bf16),) * 2,
        (out_cotangent, output_weight, stored_queries, stored_keys, stored_values),
        scratch=(
            pltpu.VMEM(out_cotangent.shape, bf16),
            pltpu.VMEM(output_weight.shape, bf16),
            pltpu.SemaphoreType.DMA((6 + 3 * pieces,)),
        ),
        flops=4 * rows * model * q_cols,
        moved=2 * model * (rows + 2 * q_cols),
        room=63,
    )
    held = {0: same}
    for apart in range(2, blocks):
        lowest, highest = 2, 1 << (apart.bit_length() - 1)
        while not apart & lowest:
            lowest *= 2
        through = lowest if apart % 2 else highest
        if lowest == highest:
            held[apart] = swapped(other if apart % 2 else same, "seq", apart)
        else:
            held[apart] = swapped(held[apart ^ through], "seq", through)
    held[1] = swapped(other, "seq", 1)
    cut = model // blocks
    *columns, held[0] = kernel_call(
        turn_kernel,
        (shape((2, 2, cut, rows), bf16),) * (blocks // 2) + (shape(same.shape, bf16),),
        (normed_input, out_cotangent, same, held[2], held[blocks // 2 + 1]),
        scratch=(
            pltpu.VMEM(normed_input.shape, bf16),
            pltpu.VMEM(out_cotangent.shape, bf16),
            pltpu.VMEM((2, model, rows), bf16),
            pltpu.SemaphoreType.DMA((3,)),
        ),
        moved=8 * rows * model,
        room=8,
    )
    columns = [columns[0]] + [
        swapped(columns[chip], "seq", 2 * chip) for chip in range(1, blocks // 2)
    ]
    dx_own, dx_far, grad_parts = kernel_call(
        functools.partial(attention_kernel, blocks),
        (
            shape((rows, q_cols + 2 * kv_cols), bf16),
            shape((rows, q_cols + 2 * kv_cols), bf16),
            shape((q_cols + kv_cols, tokens), bf16),
        ),
        [held[apart] for apart in range(blocks)],
        in_vmem=range(blocks),
        scratch=(
            pltpu.VMEM((tokens, packed_cols), bf16),
            pltpu.VMEM((tokens, wide), f32),
            pltpu.VMEM((tokens, wide), f32),
            pltpu.VMEM((tokens, tokens * QUERIES_PER_KEY), bf16),
            pltpu.VMEM((HEAD_SIZE, tokens * QUERIES_PER_KEY), bf16),
            pltpu.VMEM((1, tokens * QUERIES_PER_KEY), f32),
            pltpu.VMEM((tokens * QUERIES_PER_KEY, HEAD_SIZE), bf16),
            pltpu.VMEM((HEAD_SIZE, tokens), bf16),
            pltpu.VMEM((HEAD_SIZE, tokens), bf16),
            pltpu.VMEM((HEAD_SIZE, wide), f32),
            pltpu.VMEM((2 * rows, HEAD_SIZE), f32),
        ),
    )
    dx_got = swapped(dx_far, "seq", 1)
    terms = {}
    for chosen in ((3,), (2, 1, 0)):
        made = kernel_call(
            functools.partial(input_terms_kernel, chosen),
            tuple(shape((model // groups, rows), f32 if not apart else bf16) for apart in chosen),
            (dx_own, dx_got, query_weight, key_matrix, value_matrix),
            in_vmem=range(5),
            scratch=(pltpu.VMEM((rows, 2 * (q_cols + 2 * kv_cols)), bf16),),
            flops=2 * len(chosen) * rows * (model // groups) * 2 * (q_cols + 2 * kv_cols),
            moved=2 * len(chosen) * (model // groups) * 2 * (q_cols + 2 * kv_cols),
            room=4,
        )
        terms.update(zip(chosen, made))
    (pair_sum,) = kernel_call(
        add_kernel,
        (shape(terms[2].shape, bf16),),
        (terms[2], swapped(terms[3], "head", 1)),
        in_vmem=range(2),
        moved=6 * rows * (model // groups),
        room=4,
    )
    (give,) = kernel_call(
        pass_on_kernel,
        (shape((blocks // 2, 2, cut, rows), bf16),),
        (pair_sum, *columns),
        in_vmem=range(1, 1 + blocks // 2),
        moved=8 * cut * rows * blocks // 2,
        room=4,
    )
    arrived = [swapped(terms[1], "head", 1), swapped(pair_sum, "head", 2)]
    grad_wvalue, grad_woutput, weights_done = kernel_call(
        weight_grad_kernel,
        (
            shape((model // blocks, 2 * kv_cols), f32),
            shape((model // blocks, 2 * q_cols), f32),
            shape((8, HEAD_SIZE), f32),
        ),
        (grad_parts, swapped(grad_parts, "seq", 1), *columns, swapped(give, "seq", 1)),
        in_vmem=range(3 + blocks // 2),
        scratch=(pltpu.VMEM((2, model // blocks, tokens), bf16),),
        room=8,
        flops=4 * tokens * (model // blocks) * (q_cols + kv_cols),
        moved=4 * (model // blocks) * (tokens + 2 * q_cols + 2 * kv_cols),
    )
    (grad_input,) = kernel_call(
        sum_kernel,
        (shape((model // groups, rows), bf16),),
        (weights_done, terms[0], *arrived),
        in_vmem=range(1, 4),
        moved=4 * groups * (model // groups) * rows,
    )
    return (grad_input.T, grad_wvalue, grad_woutput.T)


def power_of_two(count):
    return count & (count - 1) == 0


def local(normed_input, stored_queries, stored_keys, *others):
    blocks, groups = lax.axis_size("seq"), lax.axis_size("head")
    whole_window = normed_input.shape[0] * blocks <= WINDOW_LENGTH
    two_heads = stored_keys.shape[1] == 2 * HEAD_SIZE
    paired = blocks >= 4 and power_of_two(blocks) and groups == 4
    plan = gathered_plan if whole_window and two_heads and paired else windowed_plan
    return plan(normed_input, stored_queries, stored_keys, *others)


def windowed_plan(
    normed_input,
    stored_queries,
    stored_keys,
    stored_values,
    query_weight,
    key_matrix,
    value_matrix,
    output_weight,
    out_cotangent,
):
    tok_rows = normed_input.shape[0]
    blocks_seq = lax.axis_size("seq")
    seq_place = lax.axis_index("seq")
    reach_blocks = min(WINDOW_LENGTH // tok_rows, blocks_seq - 1)
    kv_heads = stored_keys.shape[1] // HEAD_SIZE
    output_gradient = jnp.dot(
        out_cotangent, output_weight.T, preferred_element_type=jnp.float32
    ).astype(jnp.bfloat16)
    pieces = [(stored_keys, stored_values)]
    current = (stored_keys, stored_values)
    for relay_step in range(reach_blocks):
        current = passed_along((current[0], current[1]), "seq", 1)
        pieces = [current] + pieces
    key_window = jnp.concatenate([piece[0] for piece in pieces], axis=0)
    value_window = jnp.concatenate([piece[1] for piece in pieces], axis=0)
    key_span = key_window.shape[0]
    query_pos = seq_place * tok_rows + jnp.arange(tok_rows, dtype=jnp.int32)
    key_pos = (seq_place - reach_blocks) * tok_rows + jnp.arange(key_span, dtype=jnp.int32)
    pos_gap = query_pos[:, None] - key_pos[None, :]
    allowed = (pos_gap >= 0) & (pos_gap < WINDOW_LENGTH) & (key_pos >= 0)[None, :]
    allowed_rows = jnp.tile(allowed, (QUERIES_PER_KEY, 1))
    query_stack = (
        stored_queries.reshape(tok_rows, kv_heads, QUERIES_PER_KEY, HEAD_SIZE)
        .transpose(1, 2, 0, 3)
        .reshape(kv_heads, QUERIES_PER_KEY * tok_rows, HEAD_SIZE)
    )
    grad_stack = (
        output_gradient.reshape(tok_rows, kv_heads, QUERIES_PER_KEY, HEAD_SIZE)
        .transpose(1, 2, 0, 3)
        .reshape(kv_heads, QUERIES_PER_KEY * tok_rows, HEAD_SIZE)
    )
    key_stack = key_window.reshape(key_span, kv_heads, HEAD_SIZE).transpose(1, 0, 2)
    value_stack = value_window.reshape(key_span, kv_heads, HEAD_SIZE).transpose(1, 0, 2)

    def per_head(head_items):
        query_head, key_head, value_head, grad_head = head_items
        attention_logits = logit_scale * jnp.dot(
            query_head, key_head.T, preferred_element_type=jnp.float32
        )
        masked = jnp.where(allowed_rows, attention_logits, -jnp.inf)
        row_top = jnp.max(masked, axis=1, keepdims=True)
        exp_scores = jnp.exp(masked - row_top)
        attn_prob = exp_scores / jnp.sum(exp_scores, axis=1, keepdims=True)
        probability_halfwidth = attn_prob.astype(jnp.bfloat16)
        attn_head = jnp.dot(
            probability_halfwidth, value_head, preferred_element_type=jnp.float32
        ).astype(jnp.bfloat16)
        row_delta = jnp.sum(
            grad_head.astype(jnp.float32) * attn_head.astype(jnp.float32), axis=1, keepdims=True
        )
        probability_gradient = jnp.dot(grad_head, value_head.T, preferred_element_type=jnp.float32)
        score_gradient = (attn_prob * (probability_gradient - row_delta)).astype(jnp.bfloat16)
        qgrad_head = (
            logit_scale * jnp.dot(score_gradient, key_head, preferred_element_type=jnp.float32)
        ).astype(jnp.bfloat16)
        key_partial = logit_scale * jnp.dot(
            score_gradient.T, query_head, preferred_element_type=jnp.float32
        )
        value_partial = jnp.dot(
            probability_halfwidth.T, grad_head, preferred_element_type=jnp.float32
        )
        return (attn_head, qgrad_head, key_partial, value_partial)

    attn_all, qgrad_all, key_all, value_all = lax.map(
        per_head, (query_stack, key_stack, value_stack, grad_stack)
    )
    attention_output = (
        attn_all.reshape(kv_heads, QUERIES_PER_KEY, tok_rows, HEAD_SIZE)
        .transpose(2, 0, 1, 3)
        .reshape(tok_rows, kv_heads * QUERIES_PER_KEY * HEAD_SIZE)
    )
    query_gradient = (
        qgrad_all.reshape(kv_heads, QUERIES_PER_KEY, tok_rows, HEAD_SIZE)
        .transpose(2, 0, 1, 3)
        .reshape(tok_rows, kv_heads * QUERIES_PER_KEY * HEAD_SIZE)
    )
    key_terms = key_all.transpose(1, 0, 2).reshape(key_span, kv_heads * HEAD_SIZE)
    value_terms = value_all.transpose(1, 0, 2).reshape(key_span, kv_heads * HEAD_SIZE)

    def take_slot(terms, slot_index):
        return terms[slot_index * tok_rows : (slot_index + 1) * tok_rows]

    key_sum = take_slot(key_terms, reach_blocks)
    value_sum = take_slot(value_terms, reach_blocks)
    for distance in range(1, reach_blocks + 1):
        received = passed_along(
            (
                take_slot(key_terms, reach_blocks - distance),
                take_slot(value_terms, reach_blocks - distance),
            ),
            "seq",
            -distance,
        )
        key_sum = key_sum + received[0]
        value_sum = value_sum + received[1]
    grad_key = key_sum.astype(jnp.bfloat16)
    grad_value = value_sum.astype(jnp.bfloat16)
    input_terms = jnp.dot(query_gradient, query_weight.T, preferred_element_type=jnp.float32)
    input_terms = input_terms + jnp.dot(grad_key, key_matrix.T, preferred_element_type=jnp.float32)
    input_terms = input_terms + jnp.dot(
        grad_value, value_matrix.T, preferred_element_type=jnp.float32
    )
    grad_input = lax.psum_scatter(input_terms, "head", scatter_dimension=1, tiled=True).astype(
        jnp.bfloat16
    )
    value_cols = grad_value.shape[1]
    input_cols = normed_input.T
    cot_cols = out_cotangent.T
    gathered = lax.psum_scatter(
        jnp.concatenate(
            [
                jnp.dot(input_cols, grad_value, preferred_element_type=jnp.float32),
                jnp.dot(cot_cols, attention_output, preferred_element_type=jnp.float32),
            ],
            axis=1,
        ),
        "seq",
        scatter_dimension=0,
        tiled=True,
    )
    grad_wvalue = gathered[:, :value_cols]
    grad_woutput = gathered[:, value_cols:].T
    return (grad_input, grad_wvalue, grad_woutput)


def solution(mesh):
    placed = (
        P("seq", None),
        P("seq", "head"),
        P("seq", "head"),
        P("seq", "head"),
        P(None, "head"),
        P(None, "head"),
        P(None, "head"),
        P("head", None),
        P("seq", None),
    )
    return jax.shard_map(
        local,
        mesh=mesh,
        in_specs=placed,
        out_specs=(P("seq", "head"), P("seq", "head"), P("head", "seq")),
        check_vma=False,
    )
```

```python
import functools

import jax
import jax.numpy as jnp
from jax import lax
from jax.experimental import pallas as pl
from jax.experimental.pallas import tpu as pltpu
from jax.sharding import PartitionSpec as P

HEAD_SIZE = 128
WINDOW_LENGTH = 4096
QUERIES_PER_KEY = 2


logit_scale = 1.0 / 12.0
log2_scale = 1.4426950408889634 / 12.0
excluded = -1e30


def passed_along(value, axis, steps):
    count = lax.axis_size(axis)
    leading, last = (max(0, -steps), min(count, count - steps))
    return lax.ppermute(value, axis, [(source, source + steps) for source in range(leading, last)])


NT = (((1,), (1,)), ((), ()))


def dot_nt(left, right):
    return lax.dot_general(left, right, NT, preferred_element_type=jnp.float32)


def dot_nn(left, right):
    return jnp.dot(left, right, preferred_element_type=jnp.float32)


def at(place, size):
    return pl.ds(pl.multiple_of(place * size, size), size)


def out_grad_kernel(
    cot_hbm, weight_hbm, q_hbm, k_hbm, v_hbm, same_ref, other_ref, cot_ref, weight_ref, sem
):
    core = lax.axis_index("seq") % 2
    halves = ((other_ref, 1 - core), (same_ref, core))
    rows = weight_ref.shape[0] // 2
    pieces = (sem.shape[0] - 6) // 3
    cut = weight_ref.shape[1] // pieces
    model_copies = []
    for piece in range(pieces):
        part = pl.ds(piece * cut, cut)
        model_copies.append(
            [
                pltpu.make_async_copy(
                    cot_hbm.at[:, part], cot_ref.at[:, part], sem.at[6 + 3 * piece]
                )
            ]
        )
        for place, (_, half) in enumerate(halves):
            model_copies[-1].append(
                pltpu.make_async_copy(
                    weight_hbm.at[at(half, rows), part],
                    weight_ref.at[pl.ds(place * rows, rows), part],
                    sem.at[7 + 3 * piece + place],
                )
            )
        for copy in model_copies[-1]:
            copy.start()
    plain_copies = []
    for place, (target, half) in enumerate(halves):
        first = 0
        for which, source in enumerate((q_hbm, k_hbm, v_hbm)):
            cols = source.shape[1] // 2
            plain_copies.append(
                pltpu.make_async_copy(
                    source.at[:, at(half, cols)],
                    target.at[:, pl.ds(first, cols)],
                    sem.at[3 * place + which],
                )
            )
            plain_copies[-1].start()
            first += cols
    total = None
    for piece in range(pieces):
        for copy in model_copies[piece]:
            copy.wait()
        part = slice(piece * cut, (piece + 1) * cut)
        product = dot_nt(weight_ref[:, part], cot_ref[:, part])
        total = product if total is None else total + product
    for place, (target, _) in enumerate(halves):
        for head in range(rows // HEAD_SIZE):
            row = place * rows + head * HEAD_SIZE
            target[:, first + head * HEAD_SIZE : first + (head + 1) * HEAD_SIZE] = total[
                row : row + HEAD_SIZE
            ].astype(jnp.bfloat16)
    for copy in plain_copies:
        copy.wait()


def turn_kernel(normed_hbm, cot_hbm, block_hbm, _, __, *refs):
    *column_refs, own_ref, normed_ref, cot_ref, turned_ref, sem = refs
    me = lax.axis_index("seq")
    cut = column_refs[0].shape[2]
    copies = []
    for which, (source, target) in enumerate(
        ((normed_hbm, normed_ref), (cot_hbm, cot_ref), (block_hbm, own_ref))
    ):
        copies.append(pltpu.make_async_copy(source, target, sem.at[which]))
        copies[-1].start()
    for which, ref in enumerate((normed_ref, cot_ref)):
        copies[which].wait()
        turned_ref[which] = ref[...].astype(jnp.float32).T.astype(jnp.bfloat16)
        for chip, target in enumerate(column_refs):
            for far in range(2):
                target[far, which] = turned_ref[which, at(me ^ (2 * chip + far), cut)]
    copies[2].wait()


def pass_on_kernel(_, *refs):
    *column_refs, give_ref = refs
    for chip, ref in enumerate(column_refs):
        give_ref[chip] = ref[1]


def attention_kernel(blocks, *refs):
    attention_body(refs[:blocks], *refs[blocks:])


def attention_body(
    block_refs,
    wq_hbm,
    wk_hbm,
    wv_hbm,
    dx_own_ref,
    dx_far_ref,
    parts_ref,
    wq_ref,
    wk_ref,
    wv_ref,
    gathered_ref,
    score_even_ref,
    score_odd_ref,
    prob_ref,
    grad_t_ref,
    delta_ref,
    query_ref,
    value_t_ref,
    key_t_ref,
    dq_t_ref,
    dk_ref,
    sem,
):
    copies = [
        pltpu.make_async_copy(source, target, sem.at[place])
        for place, (source, target) in enumerate(
            ((wq_hbm, wq_ref), (wk_hbm, wk_ref), (wv_hbm, wv_ref))
        )
    ]
    for copy in copies:
        copy.start()
    me = lax.axis_index("seq")
    core, chip = me % 2, me // 2
    rows = dx_own_ref.shape[0]
    for apart, source in enumerate(block_refs):
        gathered_ref[at(me ^ apart, rows)] = source[...]
    tokens = gathered_ref.shape[0]
    size = 2 * rows
    steps = tokens // size
    wide = QUERIES_PER_KEY * size
    heads = QUERIES_PER_KEY
    key_cols = slice(heads * HEAD_SIZE, (heads + 1) * HEAD_SIZE)
    value_cols = slice((heads + 1) * HEAD_SIZE, (heads + 2) * HEAD_SIZE)
    grad_base = (heads + 2) * HEAD_SIZE
    value_t_ref[...] = gathered_ref[:, value_cols].T
    key_t_ref[...] = gathered_ref[:, key_cols].T
    key_place = lax.broadcasted_iota(jnp.int32, (size, wide), 0)
    query_place = lax.broadcasted_iota(jnp.int32, (size, wide), 1) % size
    allowed = key_place <= query_place

    for step in range(steps):
        span = (step + 1) * size
        own = slice(step * size, span)
        lanes = slice(step * wide, (step + 1) * wide)
        score_ref = score_odd_ref if step % 2 else score_even_ref
        queries = jnp.concatenate(
            [gathered_ref[own, h * HEAD_SIZE : (h + 1) * HEAD_SIZE] for h in range(heads)], axis=0
        )
        query_ref[lanes] = queries
        top = None
        for piece in range(step + 1):
            part = slice(piece * size, (piece + 1) * size)
            scores = dot_nt(gathered_ref[part, key_cols], queries)
            if piece == step:
                scores = jnp.where(allowed, scores, excluded)
            score_ref[part] = scores
            largest = jnp.max(scores.reshape(size // 8, 8, wide), axis=0)
            top = largest if top is None else jnp.maximum(top, largest)
        top = jnp.max(top, axis=0, keepdims=True)
        total = None
        for piece in range(step + 1):
            part = slice(piece * size, (piece + 1) * size)
            weights = jnp.exp2((score_ref[part] - top) * log2_scale)
            prob_ref[part, lanes] = weights.astype(jnp.bfloat16)
            summed = jnp.sum(weights.reshape(size // 8, 8, wide), axis=0)
            total = summed if total is None else total + summed
        inverse = 1.0 / jnp.sum(total, axis=0, keepdims=True)
        attn = dot_nn(value_t_ref[:, :span], prob_ref[:span, lanes]) * inverse
        for h in range(heads):
            parts_ref[h * HEAD_SIZE : (h + 1) * HEAD_SIZE, own] = attn[
                :, h * size : (h + 1) * size
            ].astype(jnp.bfloat16)
        grads_t = jnp.concatenate(
            [
                gathered_ref[
                    block * rows : (block + 1) * rows,
                    grad_base + h * HEAD_SIZE : grad_base + (h + 1) * HEAD_SIZE,
                ]
                for h in range(heads)
                for block in (2 * step, 2 * step + 1)
            ],
            axis=1,
        )
        grads_t = (grads_t.astype(jnp.float32) * inverse).astype(jnp.bfloat16)
        grad_t_ref[:, lanes] = grads_t
        delta_ref[:, lanes] = jnp.sum(grads_t.astype(jnp.float32) * attn, axis=0, keepdims=True)

    for step in range(steps):
        own = slice(step * size, (step + 1) * size)
        parts_ref[heads * HEAD_SIZE :, own] = dot_nt(
            grad_t_ref[:, step * wide :], prob_ref[own, step * wide :]
        ).astype(jnp.bfloat16)

    dq_t_ref[...] = jnp.zeros_like(dq_t_ref)
    dk_ref[...] = jnp.zeros_like(dk_ref)
    for step in range(steps):
        key_step = jnp.minimum(chip, step)
        query_step = jnp.maximum(chip, step)
        dprob = dot_nn(
            gathered_ref[at(key_step, size), value_cols], grad_t_ref[:, at(query_step, wide)]
        )
        dscore = (
            prob_ref[at(key_step, size), at(query_step, wide)].astype(jnp.float32)
            * (dprob - delta_ref[:, at(query_step, wide)])
        ).astype(jnp.bfloat16)

        @pl.when(step <= chip)
        def _():
            dq_t_ref[...] += dot_nn(key_t_ref[:, at(key_step, size)], dscore)

        @pl.when(step >= chip)
        def _():
            dk_ref[...] += dot_nn(dscore, query_ref[at(query_step, wide)])

    for target, half in ((dx_far_ref, 1 - core), (dx_own_ref, core)):
        for h in range(heads):
            target[:, h * HEAD_SIZE : (h + 1) * HEAD_SIZE] = (
                (logit_scale * dq_t_ref[:, at(2 * h + half, rows)])
                .T.astype(jnp.bfloat16)
            )
        target[:, key_cols] = (logit_scale * dk_ref[at(half, rows)]).astype(jnp.bfloat16)
        target[:, value_cols] = parts_ref[heads * HEAD_SIZE :, at(2 * chip + half, rows)].T
    for copy in copies:
        copy.wait()


def input_terms_kernel(apart_groups, own_ref, far_ref, wq_ref, wk_ref, wv_ref, *refs):
    terms, dx_ref = refs[-1 - len(apart_groups) : -1], refs[-1]
    core = lax.axis_index("seq") % 2
    group = lax.axis_index("head")
    q_cols = wq_ref.shape[1] // 2
    kv_cols = wk_ref.shape[1] // 2
    for source, half in ((own_ref, core), (far_ref, 1 - core)):
        dx_ref[:, at(half, q_cols)] = source[:, :q_cols]
        dx_ref[:, pl.ds(pl.multiple_of(2 * q_cols + half * kv_cols, kv_cols), kv_cols)] = source[
            :, q_cols : q_cols + kv_cols
        ]
        dx_ref[
            :, pl.ds(pl.multiple_of(2 * q_cols + (2 + half) * kv_cols, kv_cols), kv_cols)
        ] = source[:, q_cols + kv_cols :]
    for apart, target in zip(apart_groups, terms):
        cut = target.shape[0]
        place = at(group ^ apart, cut)
        target[...] = (
            dot_nt(wq_ref[place], dx_ref[:, : 2 * q_cols])
            + dot_nt(wk_ref[place], dx_ref[:, 2 * q_cols : 2 * q_cols + 2 * kv_cols])
            + dot_nt(wv_ref[place], dx_ref[:, 2 * q_cols + 2 * kv_cols :])
        ).astype(target.dtype)


def weight_grad_kernel(own_ref, far_ref, *refs):
    column_refs, (wvalue_ref, woutput_ref, done_ref, joined_ref) = refs[:-4], refs[-4:]
    done_ref[...] = jnp.zeros_like(done_ref)
    me = lax.axis_index("seq")
    core = me % 2
    *column_refs, got_ref = column_refs
    for chip, ref in enumerate(column_refs):
        joined_ref[:, :, at(me ^ (2 * chip), ref.shape[3])] = ref[0]
        joined_ref[:, :, at(me ^ (2 * chip + 1), ref.shape[3])] = got_ref[chip]
    kv_cols = wvalue_ref.shape[1] // 2
    q_cols = woutput_ref.shape[1] // 2
    for half, ref in ((core, own_ref), (1 - core, far_ref)):
        woutput_ref[:, at(half, q_cols)] = dot_nt(joined_ref[1], ref[:q_cols])
        wvalue_ref[:, at(half, kv_cols)] = dot_nt(joined_ref[0], ref[q_cols:])


def add_kernel(own_ref, arrived_ref, sum_ref):
    total = own_ref[...].astype(jnp.float32) + arrived_ref[...].astype(jnp.float32)
    sum_ref[...] = total.astype(jnp.bfloat16)


def sum_kernel(_, own_ref, *refs):
    total = own_ref[...]
    for arrived_ref in refs[:-1]:
        total = total + arrived_ref[...].astype(jnp.float32)
    refs[-1][...] = total.astype(jnp.bfloat16)


def kernel_call(
    body, outs, operands, in_vmem=(), scratch=(), flops=0, moved=0, room=16
):
    vmem = pl.BlockSpec(memory_space=pltpu.VMEM)
    hbm = pl.BlockSpec(memory_space=pltpu.HBM)
    return pl.pallas_call(
        body,
        out_shape=outs,
        in_specs=[vmem if place in in_vmem else hbm for place in range(len(operands))],
        out_specs=(vmem,) * len(outs),
        scratch_shapes=list(scratch),
        compiler_params=pltpu.CompilerParams(vmem_limit_bytes=room * 1024 * 1024),
        cost_estimate=pl.CostEstimate(flops=flops, bytes_accessed=moved, transcendentals=0),
    )(*operands)


def swapped(value, axis, apart):
    count = lax.axis_size(axis)
    return lax.ppermute(value, axis, [(place, place ^ apart) for place in range(count)])


def gathered_plan(
    normed_input,
    stored_queries,
    stored_keys,
    stored_values,
    query_weight,
    key_matrix,
    value_matrix,
    output_weight,
    out_cotangent,
):
    bf16, f32 = jnp.bfloat16, jnp.float32
    rows, model = normed_input.shape
    blocks = lax.axis_size("seq")
    groups = lax.axis_size("head")
    tokens = rows * blocks
    q_cols = stored_queries.shape[1] // 2
    kv_cols = HEAD_SIZE
    wide = 2 * QUERIES_PER_KEY * rows
    packed_cols = 2 * q_cols + 2 * kv_cols
    pieces = 3 if model % (6 * HEAD_SIZE) == 0 else 1
    shape = jax.ShapeDtypeStruct
    same, other = kernel_call(
        out_grad_kernel,
        (shape((rows, packed_cols), bf16),) * 2,
        (out_cotangent, output_weight, stored_queries, stored_keys, stored_values),
        scratch=(
            pltpu.VMEM(out_cotangent.shape, bf16),
            pltpu.VMEM(output_weight.shape, bf16),
            pltpu.SemaphoreType.DMA((6 + 3 * pieces,)),
        ),
        flops=4 * rows * model * q_cols,
        moved=2 * model * (rows + 2 * q_cols),
        room=63,
    )
    held = {0: same}
    for apart in range(2, blocks):
        lowest, highest = 2, 1 << (apart.bit_length() - 1)
        while not apart & lowest:
            lowest *= 2
        through = lowest if apart % 2 else highest
        if lowest == highest:
            held[apart] = swapped(other if apart % 2 else same, "seq", apart)
        else:
            held[apart] = swapped(held[apart ^ through], "seq", through)
    held[1] = swapped(other, "seq", 1)
    cut = model // blocks
    *columns, held[0] = kernel_call(
        turn_kernel,
        (shape((2, 2, cut, rows), bf16),) * (blocks // 2) + (shape(same.shape, bf16),),
        (normed_input, out_cotangent, same, held[2], held[blocks // 2 + 1]),
        scratch=(
            pltpu.VMEM(normed_input.shape, bf16),
            pltpu.VMEM(out_cotangent.shape, bf16),
            pltpu.VMEM((2, model, rows), bf16),
            pltpu.SemaphoreType.DMA((3,)),
        ),
        moved=8 * rows * model,
        room=8,
    )
    columns = [columns[0]] + [
        swapped(columns[chip], "seq", 2 * chip) for chip in range(1, blocks // 2)
    ]
    weights = (query_weight, key_matrix, value_matrix)
    dx_own, dx_far, grad_parts, *weights = kernel_call(
        functools.partial(attention_kernel, blocks),
        (
            shape((rows, q_cols + 2 * kv_cols), bf16),
            shape((rows, q_cols + 2 * kv_cols), bf16),
            shape((q_cols + kv_cols, tokens), bf16),
        )
        + tuple(shape(weight.shape, bf16) for weight in weights),
        [held[apart] for apart in range(blocks)] + list(weights),
        in_vmem=range(blocks),
        scratch=(
            pltpu.VMEM((tokens, packed_cols), bf16),
            pltpu.VMEM((tokens, wide), f32),
            pltpu.VMEM((tokens, wide), f32),
            pltpu.VMEM((tokens, tokens * QUERIES_PER_KEY), bf16),
            pltpu.VMEM((HEAD_SIZE, tokens * QUERIES_PER_KEY), bf16),
            pltpu.VMEM((1, tokens * QUERIES_PER_KEY), f32),
            pltpu.VMEM((tokens * QUERIES_PER_KEY, HEAD_SIZE), bf16),
            pltpu.VMEM((HEAD_SIZE, tokens), bf16),
            pltpu.VMEM((HEAD_SIZE, tokens), bf16),
            pltpu.VMEM((HEAD_SIZE, wide), f32),
            pltpu.VMEM((2 * rows, HEAD_SIZE), f32),
            pltpu.SemaphoreType.DMA((3,)),
        ),
    )
    dx_got = swapped(dx_far, "seq", 1)
    terms = {}
    for chosen in ((3,), (2, 1, 0)):
        made = kernel_call(
            functools.partial(input_terms_kernel, chosen),
            tuple(shape((model // groups, rows), f32 if not apart else bf16) for apart in chosen),
            (dx_own, dx_got, *weights),
            in_vmem=range(5),
            scratch=(pltpu.VMEM((rows, 2 * (q_cols + 2 * kv_cols)), bf16),),
            flops=2 * len(chosen) * rows * (model // groups) * 2 * (q_cols + 2 * kv_cols),
            moved=2 * len(chosen) * (model // groups) * 2 * (q_cols + 2 * kv_cols),
            room=4,
        )
        terms.update(zip(chosen, made))
    (pair_sum,) = kernel_call(
        add_kernel,
        (shape(terms[2].shape, bf16),),
        (terms[2], swapped(terms[3], "head", 1)),
        in_vmem=range(2),
        moved=6 * rows * (model // groups),
        room=4,
    )
    (give,) = kernel_call(
        pass_on_kernel,
        (shape((blocks // 2, 2, cut, rows), bf16),),
        (pair_sum, *columns),
        in_vmem=range(1, 1 + blocks // 2),
        moved=8 * cut * rows * blocks // 2,
        room=4,
    )
    arrived = [swapped(pair_sum, "head", 2), swapped(terms[1], "head", 1)]
    grad_wvalue, grad_woutput, weights_done = kernel_call(
        weight_grad_kernel,
        (
            shape((model // blocks, 2 * kv_cols), f32),
            shape((model // blocks, 2 * q_cols), f32),
            shape((8, HEAD_SIZE), f32),
        ),
        (grad_parts, swapped(grad_parts, "seq", 1), *columns, swapped(give, "seq", 1)),
        in_vmem=range(3 + blocks // 2),
        scratch=(pltpu.VMEM((2, model // blocks, tokens), bf16),),
        room=8,
        flops=4 * tokens * (model // blocks) * (q_cols + kv_cols),
        moved=4 * (model // blocks) * (tokens + 2 * q_cols + 2 * kv_cols),
    )
    (grad_input,) = kernel_call(
        sum_kernel,
        (shape((model // groups, rows), bf16),),
        (weights_done, terms[0], *arrived),
        in_vmem=range(1, 4),
        moved=4 * groups * (model // groups) * rows,
    )
    return (grad_input.T, grad_wvalue, grad_woutput.T)


def power_of_two(count):
    return count & (count - 1) == 0


def local(normed_input, stored_queries, stored_keys, *others):
    blocks, groups = lax.axis_size("seq"), lax.axis_size("head")
    whole_window = normed_input.shape[0] * blocks <= WINDOW_LENGTH
    two_heads = stored_keys.shape[1] == 2 * HEAD_SIZE
    paired = blocks >= 4 and power_of_two(blocks) and groups == 4
    plan = gathered_plan if whole_window and two_heads and paired else windowed_plan
    return plan(normed_input, stored_queries, stored_keys, *others)


def windowed_plan(
    normed_input,
    stored_queries,
    stored_keys,
    stored_values,
    query_weight,
    key_matrix,
    value_matrix,
    output_weight,
    out_cotangent,
):
    tok_rows = normed_input.shape[0]
    blocks_seq = lax.axis_size("seq")
    seq_place = lax.axis_index("seq")
    reach_blocks = min(WINDOW_LENGTH // tok_rows, blocks_seq - 1)
    kv_heads = stored_keys.shape[1] // HEAD_SIZE
    output_gradient = jnp.dot(
        out_cotangent, output_weight.T, preferred_element_type=jnp.float32
    ).astype(jnp.bfloat16)
    pieces = [(stored_keys, stored_values)]
    current = (stored_keys, stored_values)
    for relay_step in range(reach_blocks):
        current = passed_along((current[0], current[1]), "seq", 1)
        pieces = [current] + pieces
    key_window = jnp.concatenate([piece[0] for piece in pieces], axis=0)
    value_window = jnp.concatenate([piece[1] for piece in pieces], axis=0)
    key_span = key_window.shape[0]
    query_pos = seq_place * tok_rows + jnp.arange(tok_rows, dtype=jnp.int32)
    key_pos = (seq_place - reach_blocks) * tok_rows + jnp.arange(key_span, dtype=jnp.int32)
    pos_gap = query_pos[:, None] - key_pos[None, :]
    allowed = (pos_gap >= 0) & (pos_gap < WINDOW_LENGTH) & (key_pos >= 0)[None, :]
    allowed_rows = jnp.tile(allowed, (QUERIES_PER_KEY, 1))
    query_stack = (
        stored_queries.reshape(tok_rows, kv_heads, QUERIES_PER_KEY, HEAD_SIZE)
        .transpose(1, 2, 0, 3)
        .reshape(kv_heads, QUERIES_PER_KEY * tok_rows, HEAD_SIZE)
    )
    grad_stack = (
        output_gradient.reshape(tok_rows, kv_heads, QUERIES_PER_KEY, HEAD_SIZE)
        .transpose(1, 2, 0, 3)
        .reshape(kv_heads, QUERIES_PER_KEY * tok_rows, HEAD_SIZE)
    )
    key_stack = key_window.reshape(key_span, kv_heads, HEAD_SIZE).transpose(1, 0, 2)
    value_stack = value_window.reshape(key_span, kv_heads, HEAD_SIZE).transpose(1, 0, 2)

    def per_head(head_items):
        query_head, key_head, value_head, grad_head = head_items
        attention_logits = logit_scale * jnp.dot(
            query_head, key_head.T, preferred_element_type=jnp.float32
        )
        masked = jnp.where(allowed_rows, attention_logits, -jnp.inf)
        row_top = jnp.max(masked, axis=1, keepdims=True)
        exp_scores = jnp.exp(masked - row_top)
        attn_prob = exp_scores / jnp.sum(exp_scores, axis=1, keepdims=True)
        probability_halfwidth = attn_prob.astype(jnp.bfloat16)
        attn_head = jnp.dot(
            probability_halfwidth, value_head, preferred_element_type=jnp.float32
        ).astype(jnp.bfloat16)
        row_delta = jnp.sum(
            grad_head.astype(jnp.float32) * attn_head.astype(jnp.float32), axis=1, keepdims=True
        )
        probability_gradient = jnp.dot(grad_head, value_head.T, preferred_element_type=jnp.float32)
        score_gradient = (attn_prob * (probability_gradient - row_delta)).astype(jnp.bfloat16)
        qgrad_head = (
            logit_scale * jnp.dot(score_gradient, key_head, preferred_element_type=jnp.float32)
        ).astype(jnp.bfloat16)
        key_partial = logit_scale * jnp.dot(
            score_gradient.T, query_head, preferred_element_type=jnp.float32
        )
        value_partial = jnp.dot(
            probability_halfwidth.T, grad_head, preferred_element_type=jnp.float32
        )
        return (attn_head, qgrad_head, key_partial, value_partial)

    attn_all, qgrad_all, key_all, value_all = lax.map(
        per_head, (query_stack, key_stack, value_stack, grad_stack)
    )
    attention_output = (
        attn_all.reshape(kv_heads, QUERIES_PER_KEY, tok_rows, HEAD_SIZE)
        .transpose(2, 0, 1, 3)
        .reshape(tok_rows, kv_heads * QUERIES_PER_KEY * HEAD_SIZE)
    )
    query_gradient = (
        qgrad_all.reshape(kv_heads, QUERIES_PER_KEY, tok_rows, HEAD_SIZE)
        .transpose(2, 0, 1, 3)
        .reshape(tok_rows, kv_heads * QUERIES_PER_KEY * HEAD_SIZE)
    )
    key_terms = key_all.transpose(1, 0, 2).reshape(key_span, kv_heads * HEAD_SIZE)
    value_terms = value_all.transpose(1, 0, 2).reshape(key_span, kv_heads * HEAD_SIZE)

    def take_slot(terms, slot_index):
        return terms[slot_index * tok_rows : (slot_index + 1) * tok_rows]

    key_sum = take_slot(key_terms, reach_blocks)
    value_sum = take_slot(value_terms, reach_blocks)
    for distance in range(1, reach_blocks + 1):
        received = passed_along(
            (
                take_slot(key_terms, reach_blocks - distance),
                take_slot(value_terms, reach_blocks - distance),
            ),
            "seq",
            -distance,
        )
        key_sum = key_sum + received[0]
        value_sum = value_sum + received[1]
    grad_key = key_sum.astype(jnp.bfloat16)
    grad_value = value_sum.astype(jnp.bfloat16)
    input_terms = jnp.dot(query_gradient, query_weight.T, preferred_element_type=jnp.float32)
    input_terms = input_terms + jnp.dot(grad_key, key_matrix.T, preferred_element_type=jnp.float32)
    input_terms = input_terms + jnp.dot(
        grad_value, value_matrix.T, preferred_element_type=jnp.float32
    )
    grad_input = lax.psum_scatter(input_terms, "head", scatter_dimension=1, tiled=True).astype(
        jnp.bfloat16
    )
    value_cols = grad_value.shape[1]
    input_cols = normed_input.T
    cot_cols = out_cotangent.T
    gathered = lax.psum_scatter(
        jnp.concatenate(
            [
                jnp.dot(input_cols, grad_value, preferred_element_type=jnp.float32),
                jnp.dot(cot_cols, attention_output, preferred_element_type=jnp.float32),
            ],
            axis=1,
        ),
        "seq",
        scatter_dimension=0,
        tiled=True,
    )
    grad_wvalue = gathered[:, :value_cols]
    grad_woutput = gathered[:, value_cols:].T
    return (grad_input, grad_wvalue, grad_woutput)


def solution(mesh):
    placed = (
        P("seq", None),
        P("seq", "head"),
        P("seq", "head"),
        P("seq", "head"),
        P(None, "head"),
        P(None, "head"),
        P(None, "head"),
        P("head", None),
        P("seq", None),
    )
    return jax.shard_map(
        local,
        mesh=mesh,
        in_specs=placed,
        out_specs=(P("seq", "head"), P("seq", "head"), P("head", "seq")),
        check_vma=False,
    )
```

```python
import functools

import jax
import jax.numpy as jnp
from jax import lax
from jax.experimental import pallas as pl
from jax.experimental.pallas import tpu as pltpu
from jax.sharding import PartitionSpec as P

HEAD_SIZE = 128
WINDOW_LENGTH = 4096
QUERIES_PER_KEY = 2


logit_scale = 1.0 / 12.0
log2_scale = 1.4426950408889634 / 12.0
excluded = -1e30


def passed_along(value, axis, steps):
    count = lax.axis_size(axis)
    leading, last = (max(0, -steps), min(count, count - steps))
    return lax.ppermute(value, axis, [(source, source + steps) for source in range(leading, last)])


NT = (((1,), (1,)), ((), ()))


def dot_nt(left, right):
    return lax.dot_general(left, right, NT, preferred_element_type=jnp.float32)


def dot_nn(left, right):
    return jnp.dot(left, right, preferred_element_type=jnp.float32)


def at(place, size):
    return pl.ds(pl.multiple_of(place * size, size), size)


def out_grad_kernel(
    cot_hbm, weight_hbm, q_hbm, k_hbm, v_hbm, same_ref, other_ref, cot_ref, weight_ref, sem
):
    core = lax.axis_index("seq") % 2
    halves = ((other_ref, 1 - core), (same_ref, core))
    rows = weight_ref.shape[0] // 2
    pieces = (sem.shape[0] - 6) // 3
    cut = weight_ref.shape[1] // pieces
    model_copies = []
    for piece in range(pieces):
        part = pl.ds(piece * cut, cut)
        model_copies.append(
            [
                pltpu.make_async_copy(
                    cot_hbm.at[:, part], cot_ref.at[:, part], sem.at[6 + 3 * piece]
                )
            ]
        )
        for place, (_, half) in enumerate(halves):
            model_copies[-1].append(
                pltpu.make_async_copy(
                    weight_hbm.at[at(half, rows), part],
                    weight_ref.at[pl.ds(place * rows, rows), part],
                    sem.at[7 + 3 * piece + place],
                )
            )
        for copy in model_copies[-1]:
            copy.start()
    plain_copies = []
    for place, (target, half) in enumerate(halves):
        first = 0
        for which, source in enumerate((q_hbm, k_hbm, v_hbm)):
            cols = source.shape[1] // 2
            plain_copies.append(
                pltpu.make_async_copy(
                    source.at[:, at(half, cols)],
                    target.at[:, pl.ds(first, cols)],
                    sem.at[3 * place + which],
                )
            )
            plain_copies[-1].start()
            first += cols
    total = None
    for piece in range(pieces):
        for copy in model_copies[piece]:
            copy.wait()
        part = slice(piece * cut, (piece + 1) * cut)
        product = dot_nt(weight_ref[:, part], cot_ref[:, part])
        total = product if total is None else total + product
    for place, (target, _) in enumerate(halves):
        for head in range(rows // HEAD_SIZE):
            row = place * rows + head * HEAD_SIZE
            target[:, first + head * HEAD_SIZE : first + (head + 1) * HEAD_SIZE] = total[
                row : row + HEAD_SIZE
            ].astype(jnp.bfloat16)
    for copy in plain_copies:
        copy.wait()


def turn_kernel(normed_ref, cot_ref, block_ref, _, __, *refs):
    *column_refs, own_ref, turned_ref = refs
    me = lax.axis_index("seq")
    cut = column_refs[0].shape[2]
    own_ref[...] = block_ref[...]
    for which, ref in enumerate((normed_ref, cot_ref)):
        turned_ref[which] = ref[...].astype(jnp.float32).T.astype(jnp.bfloat16)
        for chip, target in enumerate(column_refs):
            for far in range(2):
                target[far, which] = turned_ref[which, at(me ^ (2 * chip + far), cut)]


def pass_on_kernel(_, *refs):
    *column_refs, give_ref = refs
    for chip, ref in enumerate(column_refs):
        give_ref[chip] = ref[1]


def attention_kernel(blocks, *refs):
    attention_body(refs[:blocks], *refs[blocks:])


def attention_body(
    block_refs,
    dx_own_ref,
    dx_far_ref,
    parts_ref,
    gathered_ref,
    score_even_ref,
    score_odd_ref,
    prob_ref,
    grad_t_ref,
    delta_ref,
    query_ref,
    value_t_ref,
    key_t_ref,
    dq_t_ref,
    dk_ref,
):
    me = lax.axis_index("seq")
    core, chip = me % 2, me // 2
    rows = dx_own_ref.shape[0]
    for apart, source in enumerate(block_refs):
        gathered_ref[at(me ^ apart, rows)] = source[...]
    tokens = gathered_ref.shape[0]
    size = 2 * rows
    steps = tokens // size
    wide = QUERIES_PER_KEY * size
    heads = QUERIES_PER_KEY
    key_cols = slice(heads * HEAD_SIZE, (heads + 1) * HEAD_SIZE)
    value_cols = slice((heads + 1) * HEAD_SIZE, (heads + 2) * HEAD_SIZE)
    grad_base = (heads + 2) * HEAD_SIZE
    value_t_ref[...] = gathered_ref[:, value_cols].T
    key_t_ref[...] = gathered_ref[:, key_cols].T
    key_place = lax.broadcasted_iota(jnp.int32, (size, wide), 0)
    query_place = lax.broadcasted_iota(jnp.int32, (size, wide), 1) % size
    allowed = key_place <= query_place

    for step in range(steps):
        span = (step + 1) * size
        own = slice(step * size, span)
        lanes = slice(step * wide, (step + 1) * wide)
        score_ref = score_odd_ref if step % 2 else score_even_ref
        queries = jnp.concatenate(
            [gathered_ref[own, h * HEAD_SIZE : (h + 1) * HEAD_SIZE] for h in range(heads)], axis=0
        )
        query_ref[lanes] = queries
        top = None
        for piece in range(step + 1):
            part = slice(piece * size, (piece + 1) * size)
            scores = dot_nt(gathered_ref[part, key_cols], queries)
            if piece == step:
                scores = jnp.where(allowed, scores, excluded)
            score_ref[part] = scores
            largest = jnp.max(scores.reshape(size // 8, 8, wide), axis=0)
            top = largest if top is None else jnp.maximum(top, largest)
        top = jnp.max(top, axis=0, keepdims=True)
        total = None
        for piece in range(step + 1):
            part = slice(piece * size, (piece + 1) * size)
            weights = jnp.exp2((score_ref[part] - top) * log2_scale)
            prob_ref[part, lanes] = weights.astype(jnp.bfloat16)
            summed = jnp.sum(weights.reshape(size // 8, 8, wide), axis=0)
            total = summed if total is None else total + summed
        inverse = 1.0 / jnp.sum(total, axis=0, keepdims=True)
        attn = dot_nn(value_t_ref[:, :span], prob_ref[:span, lanes]) * inverse
        for h in range(heads):
            parts_ref[h * HEAD_SIZE : (h + 1) * HEAD_SIZE, own] = attn[
                :, h * size : (h + 1) * size
            ].astype(jnp.bfloat16)
        grads_t = jnp.concatenate(
            [
                gathered_ref[
                    block * rows : (block + 1) * rows,
                    grad_base + h * HEAD_SIZE : grad_base + (h + 1) * HEAD_SIZE,
                ]
                for h in range(heads)
                for block in (2 * step, 2 * step + 1)
            ],
            axis=1,
        )
        grads_t = (grads_t.astype(jnp.float32) * inverse).astype(jnp.bfloat16)
        grad_t_ref[:, lanes] = grads_t
        delta_ref[:, lanes] = jnp.sum(grads_t.astype(jnp.float32) * attn, axis=0, keepdims=True)

    for step in range(steps):
        own = slice(step * size, (step + 1) * size)
        parts_ref[heads * HEAD_SIZE :, own] = dot_nt(
            grad_t_ref[:, step * wide :], prob_ref[own, step * wide :]
        ).astype(jnp.bfloat16)

    dq_t_ref[...] = jnp.zeros_like(dq_t_ref)
    dk_ref[...] = jnp.zeros_like(dk_ref)
    for step in range(steps):
        key_step = jnp.minimum(chip, step)
        query_step = jnp.maximum(chip, step)
        dprob = dot_nn(
            gathered_ref[at(key_step, size), value_cols], grad_t_ref[:, at(query_step, wide)]
        )
        dscore = (
            prob_ref[at(key_step, size), at(query_step, wide)].astype(jnp.float32)
            * (dprob - delta_ref[:, at(query_step, wide)])
        ).astype(jnp.bfloat16)

        @pl.when(step <= chip)
        def _():
            dq_t_ref[...] += dot_nn(key_t_ref[:, at(key_step, size)], dscore)

        @pl.when(step >= chip)
        def _():
            dk_ref[...] += dot_nn(dscore, query_ref[at(query_step, wide)])

    for target, half in ((dx_far_ref, 1 - core), (dx_own_ref, core)):
        for h in range(heads):
            target[:, h * HEAD_SIZE : (h + 1) * HEAD_SIZE] = (
                (logit_scale * dq_t_ref[:, at(2 * h + half, rows)])
                .T.astype(jnp.bfloat16)
            )
        target[:, key_cols] = (logit_scale * dk_ref[at(half, rows)]).astype(jnp.bfloat16)
        target[:, value_cols] = parts_ref[heads * HEAD_SIZE :, at(2 * chip + half, rows)].T


def input_terms_kernel(apart_groups, own_ref, far_ref, wq_ref, wk_ref, wv_ref, *refs):
    terms, dx_ref = refs[-1 - len(apart_groups) : -1], refs[-1]
    core = lax.axis_index("seq") % 2
    group = lax.axis_index("head")
    q_cols = wq_ref.shape[1] // 2
    kv_cols = wk_ref.shape[1] // 2
    for source, half in ((own_ref, core), (far_ref, 1 - core)):
        dx_ref[:, at(half, q_cols)] = source[:, :q_cols]
        dx_ref[:, pl.ds(pl.multiple_of(2 * q_cols + half * kv_cols, kv_cols), kv_cols)] = source[
            :, q_cols : q_cols + kv_cols
        ]
        dx_ref[
            :, pl.ds(pl.multiple_of(2 * q_cols + (2 + half) * kv_cols, kv_cols), kv_cols)
        ] = source[:, q_cols + kv_cols :]
    for apart, target in zip(apart_groups, terms):
        cut = target.shape[0]
        place = at(group ^ apart, cut)
        target[...] = (
            dot_nt(wq_ref[place], dx_ref[:, : 2 * q_cols])
            + dot_nt(wk_ref[place], dx_ref[:, 2 * q_cols : 2 * q_cols + 2 * kv_cols])
            + dot_nt(wv_ref[place], dx_ref[:, 2 * q_cols + 2 * kv_cols :])
        ).astype(target.dtype)


def weight_grad_kernel(own_ref, far_ref, *refs):
    column_refs, (wvalue_ref, woutput_ref, done_ref, joined_ref) = refs[:-4], refs[-4:]
    done_ref[...] = jnp.zeros_like(done_ref)
    me = lax.axis_index("seq")
    core = me % 2
    *column_refs, got_ref = column_refs
    for chip, ref in enumerate(column_refs):
        joined_ref[:, :, at(me ^ (2 * chip), ref.shape[3])] = ref[0]
        joined_ref[:, :, at(me ^ (2 * chip + 1), ref.shape[3])] = got_ref[chip]
    kv_cols = wvalue_ref.shape[1] // 2
    q_cols = woutput_ref.shape[1] // 2
    for half, ref in ((core, own_ref), (1 - core, far_ref)):
        woutput_ref[:, at(half, q_cols)] = dot_nt(joined_ref[1], ref[:q_cols])
        wvalue_ref[:, at(half, kv_cols)] = dot_nt(joined_ref[0], ref[q_cols:])


def add_kernel(own_ref, arrived_ref, sum_ref):
    total = own_ref[...].astype(jnp.float32) + arrived_ref[...].astype(jnp.float32)
    sum_ref[...] = total.astype(jnp.bfloat16)


def sum_kernel(_, own_ref, *refs):
    total = own_ref[...]
    for arrived_ref in refs[:-1]:
        total = total + arrived_ref[...].astype(jnp.float32)
    refs[-1][...] = total.astype(jnp.bfloat16)


def kernel_call(
    body, outs, operands, in_vmem=(), scratch=(), flops=0, moved=0, room=16
):
    vmem = pl.BlockSpec(memory_space=pltpu.VMEM)
    hbm = pl.BlockSpec(memory_space=pltpu.HBM)
    return pl.pallas_call(
        body,
        out_shape=outs,
        in_specs=[vmem if place in in_vmem else hbm for place in range(len(operands))],
        out_specs=(vmem,) * len(outs),
        scratch_shapes=list(scratch),
        compiler_params=pltpu.CompilerParams(vmem_limit_bytes=room * 1024 * 1024),
        cost_estimate=pl.CostEstimate(flops=flops, bytes_accessed=moved, transcendentals=0),
    )(*operands)


def swapped(value, axis, apart):
    count = lax.axis_size(axis)
    return lax.ppermute(value, axis, [(place, place ^ apart) for place in range(count)])


def gathered_plan(
    normed_input,
    stored_queries,
    stored_keys,
    stored_values,
    query_weight,
    key_matrix,
    value_matrix,
    output_weight,
    out_cotangent,
):
    bf16, f32 = jnp.bfloat16, jnp.float32
    rows, model = normed_input.shape
    blocks = lax.axis_size("seq")
    groups = lax.axis_size("head")
    tokens = rows * blocks
    q_cols = stored_queries.shape[1] // 2
    kv_cols = HEAD_SIZE
    wide = 2 * QUERIES_PER_KEY * rows
    packed_cols = 2 * q_cols + 2 * kv_cols
    pieces = 3 if model % (6 * HEAD_SIZE) == 0 else 1
    shape = jax.ShapeDtypeStruct
    same, other = kernel_call(
        out_grad_kernel,
        (shape((rows, packed_cols), bf16),) * 2,
        (out_cotangent, output_weight, stored_queries, stored_keys, stored_values),
        scratch=(
            pltpu.VMEM(out_cotangent.shape, bf16),
            pltpu.VMEM(output_weight.shape, bf16),
            pltpu.SemaphoreType.DMA((6 + 3 * pieces,)),
        ),
        flops=4 * rows * model * q_cols,
        moved=2 * model * (rows + 2 * q_cols),
        room=63,
    )
    held = {0: same}
    for apart in range(2, blocks):
        lowest, highest = 2, 1 << (apart.bit_length() - 1)
        while not apart & lowest:
            lowest *= 2
        through = lowest if apart % 2 else highest
        if lowest == highest:
            held[apart] = swapped(other if apart % 2 else same, "seq", apart)
        else:
            held[apart] = swapped(held[apart ^ through], "seq", through)
    held[1] = swapped(other, "seq", 1)
    cut = model // blocks
    *columns, held[0] = kernel_call(
        turn_kernel,
        (shape((2, 2, cut, rows), bf16),) * (blocks // 2) + (shape(same.shape, bf16),),
        (normed_input, out_cotangent, same, held[2], held[blocks // 2 + 1]),
        in_vmem=range(3),
        scratch=(pltpu.VMEM((2, model, rows), bf16),),
        moved=8 * rows * model,
        room=8,
    )
    columns = [columns[0]] + [
        swapped(columns[chip], "seq", 2 * chip) for chip in range(1, blocks // 2)
    ]
    dx_own, dx_far, grad_parts = kernel_call(
        functools.partial(attention_kernel, blocks),
        (
            shape((rows, q_cols + 2 * kv_cols), bf16),
            shape((rows, q_cols + 2 * kv_cols), bf16),
            shape((q_cols + kv_cols, tokens), bf16),
        ),
        [held[apart] for apart in range(blocks)],
        in_vmem=range(blocks),
        scratch=(
            pltpu.VMEM((tokens, packed_cols), bf16),
            pltpu.VMEM((tokens, wide), f32),
            pltpu.VMEM((tokens, wide), f32),
            pltpu.VMEM((tokens, tokens * QUERIES_PER_KEY), bf16),
            pltpu.VMEM((HEAD_SIZE, tokens * QUERIES_PER_KEY), bf16),
            pltpu.VMEM((1, tokens * QUERIES_PER_KEY), f32),
            pltpu.VMEM((tokens * QUERIES_PER_KEY, HEAD_SIZE), bf16),
            pltpu.VMEM((HEAD_SIZE, tokens), bf16),
            pltpu.VMEM((HEAD_SIZE, tokens), bf16),
            pltpu.VMEM((HEAD_SIZE, wide), f32),
            pltpu.VMEM((2 * rows, HEAD_SIZE), f32),
        ),
        flops=8 * tokens * tokens * q_cols,
        moved=2 * tokens * packed_cols,
    )
    dx_got = swapped(dx_far, "seq", 1)
    def terms_of(chosen, after):
        return kernel_call(
            functools.partial(input_terms_kernel, chosen),
            tuple(shape((model // groups, rows), f32 if not apart else bf16) for apart in chosen),
            (dx_own, dx_got, query_weight, key_matrix, value_matrix, *after),
            in_vmem=range(5),
            scratch=(pltpu.VMEM((rows, 2 * (q_cols + 2 * kv_cols)), bf16),),
            room=4,
        )

    (far_term,) = terms_of((3,), ())
    pair_term, own_term = terms_of((2, 0), (far_term,))
    (pair_sum,) = kernel_call(
        add_kernel,
        (shape(pair_term.shape, bf16),),
        (pair_term, swapped(far_term, "head", 1)),
        in_vmem=range(2),
        room=4,
    )
    (near_term,) = terms_of((1,), (pair_sum,))
    (give,) = kernel_call(
        pass_on_kernel,
        (shape((blocks // 2, 2, cut, rows), bf16),),
        (pair_term, *columns),
        in_vmem=range(1, 1 + blocks // 2),
        room=4,
    )
    arrived = [swapped(pair_sum, "head", 2), swapped(near_term, "head", 1)]
    grad_wvalue, grad_woutput, weights_done = kernel_call(
        weight_grad_kernel,
        (
            shape((model // blocks, 2 * kv_cols), f32),
            shape((model // blocks, 2 * q_cols), f32),
            shape((8, HEAD_SIZE), f32),
        ),
        (grad_parts, swapped(grad_parts, "seq", 1), *columns, swapped(give, "seq", 1)),
        in_vmem=range(3 + blocks // 2),
        scratch=(pltpu.VMEM((2, model // blocks, tokens), bf16),),
        room=8,
    )
    (grad_input,) = kernel_call(
        sum_kernel,
        (shape((model // groups, rows), bf16),),
        (weights_done, own_term, *arrived),
        in_vmem=range(1, 4),
        moved=4 * groups * (model // groups) * rows,
    )
    return (grad_input.T, grad_wvalue, grad_woutput.T)


def power_of_two(count):
    return count & (count - 1) == 0


def local(normed_input, stored_queries, stored_keys, *others):
    blocks, groups = lax.axis_size("seq"), lax.axis_size("head")
    whole_window = normed_input.shape[0] * blocks <= WINDOW_LENGTH
    two_heads = stored_keys.shape[1] == 2 * HEAD_SIZE
    paired = blocks >= 4 and power_of_two(blocks) and groups == 4
    plan = gathered_plan if whole_window and two_heads and paired else windowed_plan
    return plan(normed_input, stored_queries, stored_keys, *others)


def windowed_plan(
    normed_input,
    stored_queries,
    stored_keys,
    stored_values,
    query_weight,
    key_matrix,
    value_matrix,
    output_weight,
    out_cotangent,
):
    tok_rows = normed_input.shape[0]
    blocks_seq = lax.axis_size("seq")
    seq_place = lax.axis_index("seq")
    reach_blocks = min(WINDOW_LENGTH // tok_rows, blocks_seq - 1)
    kv_heads = stored_keys.shape[1] // HEAD_SIZE
    output_gradient = jnp.dot(
        out_cotangent, output_weight.T, preferred_element_type=jnp.float32
    ).astype(jnp.bfloat16)
    pieces = [(stored_keys, stored_values)]
    current = (stored_keys, stored_values)
    for relay_step in range(reach_blocks):
        current = passed_along((current[0], current[1]), "seq", 1)
        pieces = [current] + pieces
    key_window = jnp.concatenate([piece[0] for piece in pieces], axis=0)
    value_window = jnp.concatenate([piece[1] for piece in pieces], axis=0)
    key_span = key_window.shape[0]
    query_pos = seq_place * tok_rows + jnp.arange(tok_rows, dtype=jnp.int32)
    key_pos = (seq_place - reach_blocks) * tok_rows + jnp.arange(key_span, dtype=jnp.int32)
    pos_gap = query_pos[:, None] - key_pos[None, :]
    allowed = (pos_gap >= 0) & (pos_gap < WINDOW_LENGTH) & (key_pos >= 0)[None, :]
    allowed_rows = jnp.tile(allowed, (QUERIES_PER_KEY, 1))
    query_stack = (
        stored_queries.reshape(tok_rows, kv_heads, QUERIES_PER_KEY, HEAD_SIZE)
        .transpose(1, 2, 0, 3)
        .reshape(kv_heads, QUERIES_PER_KEY * tok_rows, HEAD_SIZE)
    )
    grad_stack = (
        output_gradient.reshape(tok_rows, kv_heads, QUERIES_PER_KEY, HEAD_SIZE)
        .transpose(1, 2, 0, 3)
        .reshape(kv_heads, QUERIES_PER_KEY * tok_rows, HEAD_SIZE)
    )
    key_stack = key_window.reshape(key_span, kv_heads, HEAD_SIZE).transpose(1, 0, 2)
    value_stack = value_window.reshape(key_span, kv_heads, HEAD_SIZE).transpose(1, 0, 2)

    def per_head(head_items):
        query_head, key_head, value_head, grad_head = head_items
        attention_logits = logit_scale * jnp.dot(
            query_head, key_head.T, preferred_element_type=jnp.float32
        )
        masked = jnp.where(allowed_rows, attention_logits, -jnp.inf)
        row_top = jnp.max(masked, axis=1, keepdims=True)
        exp_scores = jnp.exp(masked - row_top)
        attn_prob = exp_scores / jnp.sum(exp_scores, axis=1, keepdims=True)
        probability_halfwidth = attn_prob.astype(jnp.bfloat16)
        attn_head = jnp.dot(
            probability_halfwidth, value_head, preferred_element_type=jnp.float32
        ).astype(jnp.bfloat16)
        row_delta = jnp.sum(
            grad_head.astype(jnp.float32) * attn_head.astype(jnp.float32), axis=1, keepdims=True
        )
        probability_gradient = jnp.dot(grad_head, value_head.T, preferred_element_type=jnp.float32)
        score_gradient = (attn_prob * (probability_gradient - row_delta)).astype(jnp.bfloat16)
        qgrad_head = (
            logit_scale * jnp.dot(score_gradient, key_head, preferred_element_type=jnp.float32)
        ).astype(jnp.bfloat16)
        key_partial = logit_scale * jnp.dot(
            score_gradient.T, query_head, preferred_element_type=jnp.float32
        )
        value_partial = jnp.dot(
            probability_halfwidth.T, grad_head, preferred_element_type=jnp.float32
        )
        return (attn_head, qgrad_head, key_partial, value_partial)

    attn_all, qgrad_all, key_all, value_all = lax.map(
        per_head, (query_stack, key_stack, value_stack, grad_stack)
    )
    attention_output = (
        attn_all.reshape(kv_heads, QUERIES_PER_KEY, tok_rows, HEAD_SIZE)
        .transpose(2, 0, 1, 3)
        .reshape(tok_rows, kv_heads * QUERIES_PER_KEY * HEAD_SIZE)
    )
    query_gradient = (
        qgrad_all.reshape(kv_heads, QUERIES_PER_KEY, tok_rows, HEAD_SIZE)
        .transpose(2, 0, 1, 3)
        .reshape(tok_rows, kv_heads * QUERIES_PER_KEY * HEAD_SIZE)
    )
    key_terms = key_all.transpose(1, 0, 2).reshape(key_span, kv_heads * HEAD_SIZE)
    value_terms = value_all.transpose(1, 0, 2).reshape(key_span, kv_heads * HEAD_SIZE)

    def take_slot(terms, slot_index):
        return terms[slot_index * tok_rows : (slot_index + 1) * tok_rows]

    key_sum = take_slot(key_terms, reach_blocks)
    value_sum = take_slot(value_terms, reach_blocks)
    for distance in range(1, reach_blocks + 1):
        received = passed_along(
            (
                take_slot(key_terms, reach_blocks - distance),
                take_slot(value_terms, reach_blocks - distance),
            ),
            "seq",
            -distance,
        )
        key_sum = key_sum + received[0]
        value_sum = value_sum + received[1]
    grad_key = key_sum.astype(jnp.bfloat16)
    grad_value = value_sum.astype(jnp.bfloat16)
    input_terms = jnp.dot(query_gradient, query_weight.T, preferred_element_type=jnp.float32)
    input_terms = input_terms + jnp.dot(grad_key, key_matrix.T, preferred_element_type=jnp.float32)
    input_terms = input_terms + jnp.dot(
        grad_value, value_matrix.T, preferred_element_type=jnp.float32
    )
    grad_input = lax.psum_scatter(input_terms, "head", scatter_dimension=1, tiled=True).astype(
        jnp.bfloat16
    )
    value_cols = grad_value.shape[1]
    input_cols = normed_input.T
    cot_cols = out_cotangent.T
    gathered = lax.psum_scatter(
        jnp.concatenate(
            [
                jnp.dot(input_cols, grad_value, preferred_element_type=jnp.float32),
                jnp.dot(cot_cols, attention_output, preferred_element_type=jnp.float32),
            ],
            axis=1,
        ),
        "seq",
        scatter_dimension=0,
        tiled=True,
    )
    grad_wvalue = gathered[:, :value_cols]
    grad_woutput = gathered[:, value_cols:].T
    return (grad_input, grad_wvalue, grad_woutput)


def solution(mesh):
    placed = (
        P("seq", None),
        P("seq", "head"),
        P("seq", "head"),
        P("seq", "head"),
        P(None, "head"),
        P(None, "head"),
        P(None, "head"),
        P("head", None),
        P("seq", None),
    )
    return jax.shard_map(
        local,
        mesh=mesh,
        in_specs=placed,
        out_specs=(P("seq", "head"), P("seq", "head"), P("head", "seq")),
        check_vma=False,
    )
```

```python
import functools

import jax
import jax.numpy as jnp
from jax import lax
from jax.experimental import pallas as pl
from jax.experimental.pallas import tpu as pltpu
from jax.sharding import PartitionSpec as P

HEAD_SIZE = 128
WINDOW_LENGTH = 4096
QUERIES_PER_KEY = 2


logit_scale = 1.0 / 12.0
log2_scale = 1.4426950408889634 / 12.0
excluded = -1e30


def passed_along(value, axis, steps):
    count = lax.axis_size(axis)
    leading, last = (max(0, -steps), min(count, count - steps))
    return lax.ppermute(value, axis, [(source, source + steps) for source in range(leading, last)])


NT = (((1,), (1,)), ((), ()))


def dot_nt(left, right):
    return lax.dot_general(left, right, NT, preferred_element_type=jnp.float32)


def dot_nn(left, right):
    return jnp.dot(left, right, preferred_element_type=jnp.float32)


def at(place, size):
    return pl.ds(pl.multiple_of(place * size, size), size)


def out_grad_kernel(
    cot_hbm, weight_hbm, q_hbm, k_hbm, v_hbm, same_ref, other_ref, cot_ref, weight_ref, sem
):
    core = lax.axis_index("seq") % 2
    halves = ((other_ref, 1 - core), (same_ref, core))
    rows = weight_ref.shape[0] // 2
    pieces = (sem.shape[0] - 6) // 3
    cut = weight_ref.shape[1] // pieces
    model_copies = []
    for piece in range(pieces):
        part = pl.ds(piece * cut, cut)
        model_copies.append(
            [
                pltpu.make_async_copy(
                    cot_hbm.at[:, part], cot_ref.at[:, part], sem.at[6 + 3 * piece]
                )
            ]
        )
        for place, (_, half) in enumerate(halves):
            model_copies[-1].append(
                pltpu.make_async_copy(
                    weight_hbm.at[at(half, rows), part],
                    weight_ref.at[pl.ds(place * rows, rows), part],
                    sem.at[7 + 3 * piece + place],
                )
            )
        for copy in model_copies[-1]:
            copy.start()
    plain_copies = []
    for place, (target, half) in enumerate(halves):
        first = 0
        for which, source in enumerate((q_hbm, k_hbm, v_hbm)):
            cols = source.shape[1] // 2
            plain_copies.append(
                pltpu.make_async_copy(
                    source.at[:, at(half, cols)],
                    target.at[:, pl.ds(first, cols)],
                    sem.at[3 * place + which],
                )
            )
            plain_copies[-1].start()
            first += cols
    total = None
    for piece in range(pieces):
        for copy in model_copies[piece]:
            copy.wait()
        part = slice(piece * cut, (piece + 1) * cut)
        product = dot_nt(weight_ref[:, part], cot_ref[:, part])
        total = product if total is None else total + product
    for place, (target, _) in enumerate(halves):
        for head in range(rows // HEAD_SIZE):
            row = place * rows + head * HEAD_SIZE
            target[:, first + head * HEAD_SIZE : first + (head + 1) * HEAD_SIZE] = total[
                row : row + HEAD_SIZE
            ].astype(jnp.bfloat16)
    for copy in plain_copies:
        copy.wait()


def turn_kernel(normed_ref, cot_ref, block_ref, _, __, *refs):
    *column_refs, own_ref, turned_ref = refs
    me = lax.axis_index("seq")
    cut = column_refs[0].shape[2]
    own_ref[...] = block_ref[...]
    for which, ref in enumerate((normed_ref, cot_ref)):
        turned_ref[which] = ref[...].astype(jnp.float32).T.astype(jnp.bfloat16)
        for chip, target in enumerate(column_refs):
            for far in range(2):
                target[far, which] = turned_ref[which, at(me ^ (2 * chip + far), cut)]


def pass_on_kernel(_, parts_ref, *refs):
    *column_refs, give_ref = refs
    cut, rows = column_refs[0].shape[2:]
    for chip, ref in enumerate(column_refs):
        for which in range(2):
            first = (2 * chip + which) * cut
            give_ref[first : first + cut] = ref[1, which]
    first = 2 * len(column_refs) * cut
    part_rows = parts_ref.shape[0]
    for block in range(parts_ref.shape[1] // rows):
        give_ref[first : first + part_rows] = parts_ref[:, block * rows : (block + 1) * rows]
        first += part_rows


def attention_kernel(blocks, *refs):
    attention_body(refs[:blocks], *refs[blocks:])


def attention_body(
    block_refs,
    dx_own_ref,
    dx_far_ref,
    parts_ref,
    gathered_ref,
    score_even_ref,
    score_odd_ref,
    prob_ref,
    grad_t_ref,
    delta_ref,
    query_ref,
    value_t_ref,
    key_t_ref,
    dq_t_ref,
    dk_ref,
):
    me = lax.axis_index("seq")
    core, chip = me % 2, me // 2
    rows = dx_own_ref.shape[0]
    for apart, source in enumerate(block_refs):
        gathered_ref[at(me ^ apart, rows)] = source[...]
    tokens = gathered_ref.shape[0]
    size = 2 * rows
    steps = tokens // size
    wide = QUERIES_PER_KEY * size
    heads = QUERIES_PER_KEY
    key_cols = slice(heads * HEAD_SIZE, (heads + 1) * HEAD_SIZE)
    value_cols = slice((heads + 1) * HEAD_SIZE, (heads + 2) * HEAD_SIZE)
    grad_base = (heads + 2) * HEAD_SIZE
    value_t_ref[...] = gathered_ref[:, value_cols].T
    key_t_ref[...] = gathered_ref[:, key_cols].T
    key_place = lax.broadcasted_iota(jnp.int32, (size, wide), 0)
    query_place = lax.broadcasted_iota(jnp.int32, (size, wide), 1) % size
    allowed = key_place <= query_place

    for step in range(steps):
        span = (step + 1) * size
        own = slice(step * size, span)
        lanes = slice(step * wide, (step + 1) * wide)
        score_ref = score_odd_ref if step % 2 else score_even_ref
        queries = jnp.concatenate(
            [gathered_ref[own, h * HEAD_SIZE : (h + 1) * HEAD_SIZE] for h in range(heads)], axis=0
        )
        query_ref[lanes] = queries
        top = None
        for piece in range(step + 1):
            part = slice(piece * size, (piece + 1) * size)
            scores = dot_nt(gathered_ref[part, key_cols], queries)
            if piece == step:
                scores = jnp.where(allowed, scores, excluded)
            score_ref[part] = scores
            largest = jnp.max(scores.reshape(size // 8, 8, wide), axis=0)
            top = largest if top is None else jnp.maximum(top, largest)
        top = jnp.max(top, axis=0, keepdims=True)
        total = None
        for piece in range(step + 1):
            part = slice(piece * size, (piece + 1) * size)
            weights = jnp.exp2((score_ref[part] - top) * log2_scale)
            prob_ref[part, lanes] = weights.astype(jnp.bfloat16)
            summed = jnp.sum(weights.reshape(size // 8, 8, wide), axis=0)
            total = summed if total is None else total + summed
        inverse = 1.0 / jnp.sum(total, axis=0, keepdims=True)
        attn = dot_nn(value_t_ref[:, :span], prob_ref[:span, lanes]) * inverse
        for h in range(heads):
            parts_ref[h * HEAD_SIZE : (h + 1) * HEAD_SIZE, own] = attn[
                :, h * size : (h + 1) * size
            ].astype(jnp.bfloat16)
        grads_t = jnp.concatenate(
            [
                gathered_ref[
                    block * rows : (block + 1) * rows,
                    grad_base + h * HEAD_SIZE : grad_base + (h + 1) * HEAD_SIZE,
                ]
                for h in range(heads)
                for block in (2 * step, 2 * step + 1)
            ],
            axis=1,
        )
        grads_t = (grads_t.astype(jnp.float32) * inverse).astype(jnp.bfloat16)
        grad_t_ref[:, lanes] = grads_t
        delta_ref[:, lanes] = jnp.sum(grads_t.astype(jnp.float32) * attn, axis=0, keepdims=True)

    for step in range(steps):
        own = slice(step * size, (step + 1) * size)
        parts_ref[heads * HEAD_SIZE :, own] = dot_nt(
            grad_t_ref[:, step * wide :], prob_ref[own, step * wide :]
        ).astype(jnp.bfloat16)

    dq_t_ref[...] = jnp.zeros_like(dq_t_ref)
    dk_ref[...] = jnp.zeros_like(dk_ref)
    for step in range(steps):
        key_step = jnp.minimum(chip, step)
        query_step = jnp.maximum(chip, step)
        dprob = dot_nn(
            gathered_ref[at(key_step, size), value_cols], grad_t_ref[:, at(query_step, wide)]
        )
        dscore = (
            prob_ref[at(key_step, size), at(query_step, wide)].astype(jnp.float32)
            * (dprob - delta_ref[:, at(query_step, wide)])
        ).astype(jnp.bfloat16)

        @pl.when(step <= chip)
        def _():
            dq_t_ref[...] += dot_nn(key_t_ref[:, at(key_step, size)], dscore)

        @pl.when(step >= chip)
        def _():
            dk_ref[...] += dot_nn(dscore, query_ref[at(query_step, wide)])

    for target, half in ((dx_far_ref, 1 - core), (dx_own_ref, core)):
        for h in range(heads):
            target[:, h * HEAD_SIZE : (h + 1) * HEAD_SIZE] = (
                (logit_scale * dq_t_ref[:, at(2 * h + half, rows)])
                .T.astype(jnp.bfloat16)
            )
        target[:, key_cols] = (logit_scale * dk_ref[at(half, rows)]).astype(jnp.bfloat16)
        target[:, value_cols] = parts_ref[heads * HEAD_SIZE :, at(2 * chip + half, rows)].T


def input_terms_kernel(apart_groups, own_ref, far_ref, wq_ref, wk_ref, wv_ref, *refs):
    terms, dx_ref = refs[-1 - len(apart_groups) : -1], refs[-1]
    core = lax.axis_index("seq") % 2
    group = lax.axis_index("head")
    q_cols = wq_ref.shape[1] // 2
    kv_cols = wk_ref.shape[1] // 2
    for source, half in ((own_ref, core), (far_ref, 1 - core)):
        dx_ref[:, at(half, q_cols)] = source[:, :q_cols]
        dx_ref[:, pl.ds(pl.multiple_of(2 * q_cols + half * kv_cols, kv_cols), kv_cols)] = source[
            :, q_cols : q_cols + kv_cols
        ]
        dx_ref[
            :, pl.ds(pl.multiple_of(2 * q_cols + (2 + half) * kv_cols, kv_cols), kv_cols)
        ] = source[:, q_cols + kv_cols :]
    for apart, target in zip(apart_groups, terms):
        cut = target.shape[0]
        place = at(group ^ apart, cut)
        target[...] = (
            dot_nt(wq_ref[place], dx_ref[:, : 2 * q_cols])
            + dot_nt(wk_ref[place], dx_ref[:, 2 * q_cols : 2 * q_cols + 2 * kv_cols])
            + dot_nt(wv_ref[place], dx_ref[:, 2 * q_cols + 2 * kv_cols :])
        ).astype(target.dtype)


def weight_grad_kernel(own_ref, got_ref, *refs):
    column_refs, refs = refs[:-5], refs[-5:]
    wvalue_ref, woutput_ref, done_ref, joined_ref, far_ref = refs
    done_ref[...] = jnp.zeros_like(done_ref)
    me = lax.axis_index("seq")
    core = me % 2
    cut, rows = column_refs[0].shape[2:]
    for chip, ref in enumerate(column_refs):
        joined_ref[:, :, at(me ^ (2 * chip), rows)] = ref[0]
        for which in range(2):
            first = (2 * chip + which) * cut
            joined_ref[which, :, at(me ^ (2 * chip + 1), rows)] = got_ref[first : first + cut]
    first = 2 * len(column_refs) * cut
    part_rows = far_ref.shape[0]
    for block in range(far_ref.shape[1] // rows):
        far_ref[:, block * rows : (block + 1) * rows] = got_ref[first : first + part_rows]
        first += part_rows
    kv_cols = wvalue_ref.shape[1] // 2
    q_cols = woutput_ref.shape[1] // 2
    for half, ref in ((core, own_ref), (1 - core, far_ref)):
        woutput_ref[:, at(half, q_cols)] = dot_nt(joined_ref[1], ref[:q_cols])
        wvalue_ref[:, at(half, kv_cols)] = dot_nt(joined_ref[0], ref[q_cols:])


def add_kernel(own_ref, arrived_ref, sum_ref):
    total = own_ref[...].astype(jnp.float32) + arrived_ref[...].astype(jnp.float32)
    sum_ref[...] = total.astype(jnp.bfloat16)


def sum_kernel(_, own_ref, *refs):
    total = own_ref[...]
    for arrived_ref in refs[:-1]:
        total = total + arrived_ref[...].astype(jnp.float32)
    refs[-1][...] = total.astype(jnp.bfloat16)


def kernel_call(
    body, outs, operands, in_vmem=(), scratch=(), flops=0, moved=0, room=16
):
    vmem = pl.BlockSpec(memory_space=pltpu.VMEM)
    hbm = pl.BlockSpec(memory_space=pltpu.HBM)
    return pl.pallas_call(
        body,
        out_shape=outs,
        in_specs=[vmem if place in in_vmem else hbm for place in range(len(operands))],
        out_specs=(vmem,) * len(outs),
        scratch_shapes=list(scratch),
        compiler_params=pltpu.CompilerParams(vmem_limit_bytes=room * 1024 * 1024),
        cost_estimate=pl.CostEstimate(flops=flops, bytes_accessed=moved, transcendentals=0),
    )(*operands)


def swapped(value, axis, apart):
    count = lax.axis_size(axis)
    return lax.ppermute(value, axis, [(place, place ^ apart) for place in range(count)])


def gathered_plan(
    normed_input,
    stored_queries,
    stored_keys,
    stored_values,
    query_weight,
    key_matrix,
    value_matrix,
    output_weight,
    out_cotangent,
):
    bf16, f32 = jnp.bfloat16, jnp.float32
    rows, model = normed_input.shape
    blocks = lax.axis_size("seq")
    groups = lax.axis_size("head")
    tokens = rows * blocks
    q_cols = stored_queries.shape[1] // 2
    kv_cols = HEAD_SIZE
    wide = 2 * QUERIES_PER_KEY * rows
    packed_cols = 2 * q_cols + 2 * kv_cols
    pieces = 3 if model % (6 * HEAD_SIZE) == 0 else 1
    shape = jax.ShapeDtypeStruct
    same, other = kernel_call(
        out_grad_kernel,
        (shape((rows, packed_cols), bf16),) * 2,
        (out_cotangent, output_weight, stored_queries, stored_keys, stored_values),
        scratch=(
            pltpu.VMEM(out_cotangent.shape, bf16),
            pltpu.VMEM(output_weight.shape, bf16),
            pltpu.SemaphoreType.DMA((6 + 3 * pieces,)),
        ),
        flops=4 * rows * model * q_cols,
        moved=2 * model * (rows + 2 * q_cols),
        room=63,
    )
    held = {0: same}
    for apart in range(2, blocks):
        lowest, highest = 2, 1 << (apart.bit_length() - 1)
        while not apart & lowest:
            lowest *= 2
        through = lowest if apart % 2 else highest
        if lowest == highest:
            held[apart] = swapped(other if apart % 2 else same, "seq", apart)
        else:
            held[apart] = swapped(held[apart ^ through], "seq", through)
    held[1] = swapped(other, "seq", 1)
    cut = model // blocks
    *columns, held[0] = kernel_call(
        turn_kernel,
        (shape((2, 2, cut, rows), bf16),) * (blocks // 2) + (shape(same.shape, bf16),),
        (normed_input, out_cotangent, same, held[2], held[blocks // 2 + 1]),
        in_vmem=range(3),
        scratch=(pltpu.VMEM((2, model, rows), bf16),),
        moved=8 * rows * model,
        room=8,
    )
    columns = [columns[0]] + [
        swapped(columns[chip], "seq", 2 * chip) for chip in range(1, blocks // 2)
    ]
    dx_own, dx_far, grad_parts = kernel_call(
        functools.partial(attention_kernel, blocks),
        (
            shape((rows, q_cols + 2 * kv_cols), bf16),
            shape((rows, q_cols + 2 * kv_cols), bf16),
            shape((q_cols + kv_cols, tokens), bf16),
        ),
        [held[apart] for apart in range(blocks)],
        in_vmem=range(blocks),
        scratch=(
            pltpu.VMEM((tokens, packed_cols), bf16),
            pltpu.VMEM((tokens, wide), f32),
            pltpu.VMEM((tokens, wide), f32),
            pltpu.VMEM((tokens, tokens * QUERIES_PER_KEY), bf16),
            pltpu.VMEM((HEAD_SIZE, tokens * QUERIES_PER_KEY), bf16),
            pltpu.VMEM((1, tokens * QUERIES_PER_KEY), f32),
            pltpu.VMEM((tokens * QUERIES_PER_KEY, HEAD_SIZE), bf16),
            pltpu.VMEM((HEAD_SIZE, tokens), bf16),
            pltpu.VMEM((HEAD_SIZE, tokens), bf16),
            pltpu.VMEM((HEAD_SIZE, wide), f32),
            pltpu.VMEM((2 * rows, HEAD_SIZE), f32),
        ),
        flops=8 * tokens * tokens * q_cols,
        moved=2 * tokens * packed_cols,
    )
    dx_got = swapped(dx_far, "seq", 1)
    def terms_of(chosen):
        return kernel_call(
            functools.partial(input_terms_kernel, chosen),
            tuple(shape((model // groups, rows), f32 if not apart else bf16) for apart in chosen),
            (dx_own, dx_got, query_weight, key_matrix, value_matrix),
            in_vmem=range(5),
            scratch=(pltpu.VMEM((rows, 2 * (q_cols + 2 * kv_cols)), bf16),),
            flops=2 * len(chosen) * rows * (model // groups) * 2 * (q_cols + 2 * kv_cols),
            moved=2 * len(chosen) * (model // groups) * 2 * (q_cols + 2 * kv_cols),
            room=4,
        )

    (far_term,) = terms_of((3,))
    pair_term, near_term, own_term = terms_of((2, 1, 0))
    (pair_sum,) = kernel_call(
        add_kernel,
        (shape(pair_term.shape, bf16),),
        (pair_term, swapped(far_term, "head", 1)),
        in_vmem=range(2),
        room=4,
    )
    part_rows = q_cols + kv_cols
    (give,) = kernel_call(
        pass_on_kernel,
        (shape((blocks * (cut + part_rows), rows), bf16),),
        (pair_sum, grad_parts, *columns),
        in_vmem=range(1, 2 + blocks // 2),
        room=4,
    )
    arrived = [swapped(pair_sum, "head", 2), swapped(near_term, "head", 1)]
    grad_wvalue, grad_woutput, weights_done = kernel_call(
        weight_grad_kernel,
        (
            shape((model // blocks, 2 * kv_cols), f32),
            shape((model // blocks, 2 * q_cols), f32),
            shape((8, HEAD_SIZE), f32),
        ),
        (grad_parts, swapped(give, "seq", 1), *columns),
        in_vmem=range(2 + blocks // 2),
        scratch=(
            pltpu.VMEM((2, model // blocks, tokens), bf16),
            pltpu.VMEM((part_rows, tokens), bf16),
        ),
        room=8,
    )
    (grad_input,) = kernel_call(
        sum_kernel,
        (shape((model // groups, rows), bf16),),
        (weights_done, own_term, *arrived),
        in_vmem=range(1, 4),
        moved=4 * groups * (model // groups) * rows,
    )
    return (grad_input.T, grad_wvalue, grad_woutput.T)


def power_of_two(count):
    return count & (count - 1) == 0


def local(normed_input, stored_queries, stored_keys, *others):
    blocks, groups = lax.axis_size("seq"), lax.axis_size("head")
    whole_window = normed_input.shape[0] * blocks <= WINDOW_LENGTH
    two_heads = stored_keys.shape[1] == 2 * HEAD_SIZE
    paired = blocks >= 4 and power_of_two(blocks) and groups == 4
    plan = gathered_plan if whole_window and two_heads and paired else windowed_plan
    return plan(normed_input, stored_queries, stored_keys, *others)


def windowed_plan(
    normed_input,
    stored_queries,
    stored_keys,
    stored_values,
    query_weight,
    key_matrix,
    value_matrix,
    output_weight,
    out_cotangent,
):
    tok_rows = normed_input.shape[0]
    blocks_seq = lax.axis_size("seq")
    seq_place = lax.axis_index("seq")
    reach_blocks = min(WINDOW_LENGTH // tok_rows, blocks_seq - 1)
    kv_heads = stored_keys.shape[1] // HEAD_SIZE
    output_gradient = jnp.dot(
        out_cotangent, output_weight.T, preferred_element_type=jnp.float32
    ).astype(jnp.bfloat16)
    pieces = [(stored_keys, stored_values)]
    current = (stored_keys, stored_values)
    for relay_step in range(reach_blocks):
        current = passed_along((current[0], current[1]), "seq", 1)
        pieces = [current] + pieces
    key_window = jnp.concatenate([piece[0] for piece in pieces], axis=0)
    value_window = jnp.concatenate([piece[1] for piece in pieces], axis=0)
    key_span = key_window.shape[0]
    query_pos = seq_place * tok_rows + jnp.arange(tok_rows, dtype=jnp.int32)
    key_pos = (seq_place - reach_blocks) * tok_rows + jnp.arange(key_span, dtype=jnp.int32)
    pos_gap = query_pos[:, None] - key_pos[None, :]
    allowed = (pos_gap >= 0) & (pos_gap < WINDOW_LENGTH) & (key_pos >= 0)[None, :]
    allowed_rows = jnp.tile(allowed, (QUERIES_PER_KEY, 1))
    query_stack = (
        stored_queries.reshape(tok_rows, kv_heads, QUERIES_PER_KEY, HEAD_SIZE)
        .transpose(1, 2, 0, 3)
        .reshape(kv_heads, QUERIES_PER_KEY * tok_rows, HEAD_SIZE)
    )
    grad_stack = (
        output_gradient.reshape(tok_rows, kv_heads, QUERIES_PER_KEY, HEAD_SIZE)
        .transpose(1, 2, 0, 3)
        .reshape(kv_heads, QUERIES_PER_KEY * tok_rows, HEAD_SIZE)
    )
    key_stack = key_window.reshape(key_span, kv_heads, HEAD_SIZE).transpose(1, 0, 2)
    value_stack = value_window.reshape(key_span, kv_heads, HEAD_SIZE).transpose(1, 0, 2)

    def per_head(head_items):
        query_head, key_head, value_head, grad_head = head_items
        attention_logits = logit_scale * jnp.dot(
            query_head, key_head.T, preferred_element_type=jnp.float32
        )
        masked = jnp.where(allowed_rows, attention_logits, -jnp.inf)
        row_top = jnp.max(masked, axis=1, keepdims=True)
        exp_scores = jnp.exp(masked - row_top)
        attn_prob = exp_scores / jnp.sum(exp_scores, axis=1, keepdims=True)
        probability_halfwidth = attn_prob.astype(jnp.bfloat16)
        attn_head = jnp.dot(
            probability_halfwidth, value_head, preferred_element_type=jnp.float32
        ).astype(jnp.bfloat16)
        row_delta = jnp.sum(
            grad_head.astype(jnp.float32) * attn_head.astype(jnp.float32), axis=1, keepdims=True
        )
        probability_gradient = jnp.dot(grad_head, value_head.T, preferred_element_type=jnp.float32)
        score_gradient = (attn_prob * (probability_gradient - row_delta)).astype(jnp.bfloat16)
        qgrad_head = (
            logit_scale * jnp.dot(score_gradient, key_head, preferred_element_type=jnp.float32)
        ).astype(jnp.bfloat16)
        key_partial = logit_scale * jnp.dot(
            score_gradient.T, query_head, preferred_element_type=jnp.float32
        )
        value_partial = jnp.dot(
            probability_halfwidth.T, grad_head, preferred_element_type=jnp.float32
        )
        return (attn_head, qgrad_head, key_partial, value_partial)

    attn_all, qgrad_all, key_all, value_all = lax.map(
        per_head, (query_stack, key_stack, value_stack, grad_stack)
    )
    attention_output = (
        attn_all.reshape(kv_heads, QUERIES_PER_KEY, tok_rows, HEAD_SIZE)
        .transpose(2, 0, 1, 3)
        .reshape(tok_rows, kv_heads * QUERIES_PER_KEY * HEAD_SIZE)
    )
    query_gradient = (
        qgrad_all.reshape(kv_heads, QUERIES_PER_KEY, tok_rows, HEAD_SIZE)
        .transpose(2, 0, 1, 3)
        .reshape(tok_rows, kv_heads * QUERIES_PER_KEY * HEAD_SIZE)
    )
    key_terms = key_all.transpose(1, 0, 2).reshape(key_span, kv_heads * HEAD_SIZE)
    value_terms = value_all.transpose(1, 0, 2).reshape(key_span, kv_heads * HEAD_SIZE)

    def take_slot(terms, slot_index):
        return terms[slot_index * tok_rows : (slot_index + 1) * tok_rows]

    key_sum = take_slot(key_terms, reach_blocks)
    value_sum = take_slot(value_terms, reach_blocks)
    for distance in range(1, reach_blocks + 1):
        received = passed_along(
            (
                take_slot(key_terms, reach_blocks - distance),
                take_slot(value_terms, reach_blocks - distance),
            ),
            "seq",
            -distance,
        )
        key_sum = key_sum + received[0]
        value_sum = value_sum + received[1]
    grad_key = key_sum.astype(jnp.bfloat16)
    grad_value = value_sum.astype(jnp.bfloat16)
    input_terms = jnp.dot(query_gradient, query_weight.T, preferred_element_type=jnp.float32)
    input_terms = input_terms + jnp.dot(grad_key, key_matrix.T, preferred_element_type=jnp.float32)
    input_terms = input_terms + jnp.dot(
        grad_value, value_matrix.T, preferred_element_type=jnp.float32
    )
    grad_input = lax.psum_scatter(input_terms, "head", scatter_dimension=1, tiled=True).astype(
        jnp.bfloat16
    )
    value_cols = grad_value.shape[1]
    input_cols = normed_input.T
    cot_cols = out_cotangent.T
    gathered = lax.psum_scatter(
        jnp.concatenate(
            [
                jnp.dot(input_cols, grad_value, preferred_element_type=jnp.float32),
                jnp.dot(cot_cols, attention_output, preferred_element_type=jnp.float32),
            ],
            axis=1,
        ),
        "seq",
        scatter_dimension=0,
        tiled=True,
    )
    grad_wvalue = gathered[:, :value_cols]
    grad_woutput = gathered[:, value_cols:].T
    return (grad_input, grad_wvalue, grad_woutput)


def solution(mesh):
    placed = (
        P("seq", None),
        P("seq", "head"),
        P("seq", "head"),
        P("seq", "head"),
        P(None, "head"),
        P(None, "head"),
        P(None, "head"),
        P("head", None),
        P("seq", None),
    )
    return jax.shard_map(
        local,
        mesh=mesh,
        in_specs=placed,
        out_specs=(P("seq", "head"), P("seq", "head"), P("head", "seq")),
        check_vma=False,
    )
```

```python
import functools

import jax
import jax.numpy as jnp
from jax import lax
from jax.experimental import pallas as pl
from jax.experimental.pallas import tpu as pltpu
from jax.sharding import PartitionSpec as P

HEAD_SIZE = 128
WINDOW_LENGTH = 4096
QUERIES_PER_KEY = 2


logit_scale = 1.0 / 12.0
log2_scale = 1.4426950408889634 / 12.0
excluded = -1e30


def passed_along(value, axis, steps):
    count = lax.axis_size(axis)
    leading, last = (max(0, -steps), min(count, count - steps))
    return lax.ppermute(value, axis, [(source, source + steps) for source in range(leading, last)])


NT = (((1,), (1,)), ((), ()))


def dot_nt(left, right):
    return lax.dot_general(left, right, NT, preferred_element_type=jnp.float32)


def dot_nn(left, right):
    return jnp.dot(left, right, preferred_element_type=jnp.float32)


def at(place, size):
    return pl.ds(pl.multiple_of(place * size, size), size)


def out_grad_kernel(
    cot_hbm, weight_hbm, q_hbm, k_hbm, v_hbm, same_ref, other_ref, cot_ref, weight_ref, sem
):
    core = lax.axis_index("seq") % 2
    halves = ((other_ref, 1 - core), (same_ref, core))
    rows = weight_ref.shape[0] // 2
    pieces = (sem.shape[0] - 6) // 3
    cut = weight_ref.shape[1] // pieces
    model_copies = []
    for piece in range(pieces):
        part = pl.ds(piece * cut, cut)
        model_copies.append(
            [
                pltpu.make_async_copy(
                    cot_hbm.at[:, part], cot_ref.at[:, part], sem.at[6 + 3 * piece]
                )
            ]
        )
        for place, (_, half) in enumerate(halves):
            model_copies[-1].append(
                pltpu.make_async_copy(
                    weight_hbm.at[at(half, rows), part],
                    weight_ref.at[pl.ds(place * rows, rows), part],
                    sem.at[7 + 3 * piece + place],
                )
            )
        for copy in model_copies[-1]:
            copy.start()
    plain_copies = []
    for place, (target, half) in enumerate(halves):
        first = 0
        for which, source in enumerate((q_hbm, k_hbm, v_hbm)):
            cols = source.shape[1] // 2
            plain_copies.append(
                pltpu.make_async_copy(
                    source.at[:, at(half, cols)],
                    target.at[:, pl.ds(first, cols)],
                    sem.at[3 * place + which],
                )
            )
            plain_copies[-1].start()
            first += cols
    total = None
    for piece in range(pieces):
        for copy in model_copies[piece]:
            copy.wait()
        part = slice(piece * cut, (piece + 1) * cut)
        product = dot_nt(weight_ref[:, part], cot_ref[:, part])
        total = product if total is None else total + product
    for place, (target, _) in enumerate(halves):
        for head in range(rows // HEAD_SIZE):
            row = place * rows + head * HEAD_SIZE
            target[:, first + head * HEAD_SIZE : first + (head + 1) * HEAD_SIZE] = total[
                row : row + HEAD_SIZE
            ].astype(jnp.bfloat16)
    for copy in plain_copies:
        copy.wait()


def turn_kernel(normed_ref, cot_ref, block_ref, _, __, *refs):
    *column_refs, own_ref, turned_ref = refs
    me = lax.axis_index("seq")
    cut = column_refs[0].shape[2]
    own_ref[...] = block_ref[...]
    for which, ref in enumerate((normed_ref, cot_ref)):
        turned_ref[which] = ref[...].astype(jnp.float32).T.astype(jnp.bfloat16)
        for chip, target in enumerate(column_refs):
            for far in range(2):
                target[far, which] = turned_ref[which, at(me ^ (2 * chip + far), cut)]


def pass_on_kernel(_, attn_ref, dv_t_ref, *refs):
    *column_refs, give_ref = refs
    cut, rows = column_refs[0].shape[2:]
    for chip, ref in enumerate(column_refs):
        for which in range(2):
            first = (2 * chip + which) * cut
            give_ref[first : first + cut] = ref[1, which]
    first = 2 * len(column_refs) * cut
    for ref in (attn_ref, dv_t_ref):
        for block in range(ref.shape[1] // rows):
            give_ref[first : first + ref.shape[0]] = ref[:, block * rows : (block + 1) * rows]
            first += ref.shape[0]


def attention_kernel(blocks, *refs):
    attention_body(refs[:blocks], *refs[blocks:])


def attention_body(
    block_refs,
    dx_own_ref,
    dx_far_ref,
    attn_ref,
    prob_ref,
    grad_t_ref,
    gathered_ref,
    score_even_ref,
    score_odd_ref,
    delta_ref,
    query_ref,
    value_t_ref,
    key_t_ref,
    dq_t_ref,
    dk_ref,
    dv_ref,
):
    me = lax.axis_index("seq")
    core, chip = me % 2, me // 2
    rows = dx_own_ref.shape[0]
    for apart, source in enumerate(block_refs):
        gathered_ref[at(me ^ apart, rows)] = source[...]
    tokens = gathered_ref.shape[0]
    size = 2 * rows
    steps = tokens // size
    wide = QUERIES_PER_KEY * size
    heads = QUERIES_PER_KEY
    key_cols = slice(heads * HEAD_SIZE, (heads + 1) * HEAD_SIZE)
    value_cols = slice((heads + 1) * HEAD_SIZE, (heads + 2) * HEAD_SIZE)
    grad_base = (heads + 2) * HEAD_SIZE
    value_t_ref[...] = gathered_ref[:, value_cols].T
    key_t_ref[...] = gathered_ref[:, key_cols].T
    key_place = lax.broadcasted_iota(jnp.int32, (size, wide), 0)
    query_place = lax.broadcasted_iota(jnp.int32, (size, wide), 1) % size
    allowed = key_place <= query_place

    for step in range(steps):
        span = (step + 1) * size
        own = slice(step * size, span)
        lanes = slice(step * wide, (step + 1) * wide)
        score_ref = score_odd_ref if step % 2 else score_even_ref
        queries = jnp.concatenate(
            [gathered_ref[own, h * HEAD_SIZE : (h + 1) * HEAD_SIZE] for h in range(heads)], axis=0
        )
        query_ref[lanes] = queries
        top = None
        for piece in range(step + 1):
            part = slice(piece * size, (piece + 1) * size)
            scores = dot_nt(gathered_ref[part, key_cols], queries)
            if piece == step:
                scores = jnp.where(allowed, scores, excluded)
            score_ref[part] = scores
            largest = jnp.max(scores.reshape(size // 8, 8, wide), axis=0)
            top = largest if top is None else jnp.maximum(top, largest)
        top = jnp.max(top, axis=0, keepdims=True)
        total = None
        for piece in range(step + 1):
            part = slice(piece * size, (piece + 1) * size)
            weights = jnp.exp2((score_ref[part] - top) * log2_scale)
            prob_ref[part, lanes] = weights.astype(jnp.bfloat16)
            summed = jnp.sum(weights.reshape(size // 8, 8, wide), axis=0)
            total = summed if total is None else total + summed
        inverse = 1.0 / jnp.sum(total, axis=0, keepdims=True)
        attn = dot_nn(value_t_ref[:, :span], prob_ref[:span, lanes]) * inverse
        for h in range(heads):
            attn_ref[h * HEAD_SIZE : (h + 1) * HEAD_SIZE, own] = attn[
                :, h * size : (h + 1) * size
            ].astype(jnp.bfloat16)
        grads_t = jnp.concatenate(
            [
                gathered_ref[
                    block * rows : (block + 1) * rows,
                    grad_base + h * HEAD_SIZE : grad_base + (h + 1) * HEAD_SIZE,
                ]
                for h in range(heads)
                for block in (2 * step, 2 * step + 1)
            ],
            axis=1,
        )
        grads_t = (grads_t.astype(jnp.float32) * inverse).astype(jnp.bfloat16)
        grad_t_ref[:, lanes] = grads_t
        delta_ref[:, lanes] = jnp.sum(grads_t.astype(jnp.float32) * attn, axis=0, keepdims=True)

    dq_t_ref[...] = jnp.zeros_like(dq_t_ref)
    dk_ref[...] = jnp.zeros_like(dk_ref)
    dv_ref[...] = jnp.zeros_like(dv_ref)
    for step in range(steps):
        key_step = jnp.minimum(chip, step)
        query_step = jnp.maximum(chip, step)
        dprob = dot_nn(
            gathered_ref[at(key_step, size), value_cols], grad_t_ref[:, at(query_step, wide)]
        )
        prob = prob_ref[at(key_step, size), at(query_step, wide)]
        dscore = (
            prob.astype(jnp.float32)
            * (dprob - delta_ref[:, at(query_step, wide)])
        ).astype(jnp.bfloat16)

        @pl.when(step <= chip)
        def _():
            dq_t_ref[...] += dot_nn(key_t_ref[:, at(key_step, size)], dscore)

        @pl.when(step >= chip)
        def _():
            dk_ref[...] += dot_nn(dscore, query_ref[at(query_step, wide)])
            dv_ref[...] += dot_nt(prob, grad_t_ref[:, at(query_step, wide)])

    for target, half in ((dx_far_ref, 1 - core), (dx_own_ref, core)):
        for h in range(heads):
            target[:, h * HEAD_SIZE : (h + 1) * HEAD_SIZE] = (
                (logit_scale * dq_t_ref[:, at(2 * h + half, rows)])
                .T.astype(jnp.bfloat16)
            )
        target[:, key_cols] = (logit_scale * dk_ref[at(half, rows)]).astype(jnp.bfloat16)
        target[:, value_cols] = dv_ref[at(half, rows)].astype(jnp.bfloat16)


def value_grad_kernel(prob_ref, grad_t_ref, dv_t_ref):
    size = 2 * HEAD_SIZE
    wide = QUERIES_PER_KEY * size
    for step in range(prob_ref.shape[0] // size):
        own = slice(step * size, (step + 1) * size)
        dv_t_ref[:, own] = dot_nt(grad_t_ref[:, step * wide :], prob_ref[own, step * wide :]).astype(
            jnp.bfloat16
        )


def input_terms_kernel(apart_groups, own_ref, far_ref, wq_ref, wk_ref, wv_ref, *refs):
    terms, dx_ref = refs[-1 - len(apart_groups) : -1], refs[-1]
    core = lax.axis_index("seq") % 2
    group = lax.axis_index("head")
    q_cols = wq_ref.shape[1] // 2
    kv_cols = wk_ref.shape[1] // 2
    for source, half in ((own_ref, core), (far_ref, 1 - core)):
        dx_ref[:, at(half, q_cols)] = source[:, :q_cols]
        dx_ref[:, pl.ds(pl.multiple_of(2 * q_cols + half * kv_cols, kv_cols), kv_cols)] = source[
            :, q_cols : q_cols + kv_cols
        ]
        dx_ref[
            :, pl.ds(pl.multiple_of(2 * q_cols + (2 + half) * kv_cols, kv_cols), kv_cols)
        ] = source[:, q_cols + kv_cols :]
    for apart, target in zip(apart_groups, terms):
        cut = target.shape[0]
        place = at(group ^ apart, cut)
        target[...] = (
            dot_nt(wq_ref[place], dx_ref[:, : 2 * q_cols])
            + dot_nt(wk_ref[place], dx_ref[:, 2 * q_cols : 2 * q_cols + 2 * kv_cols])
            + dot_nt(wv_ref[place], dx_ref[:, 2 * q_cols + 2 * kv_cols :])
        ).astype(target.dtype)


def weight_grad_kernel(attn_ref, dv_t_ref, got_ref, *refs):
    column_refs, refs = refs[:-6], refs[-6:]
    wvalue_ref, woutput_ref, done_ref, joined_ref, far_attn_ref, far_dv_ref = refs
    done_ref[...] = jnp.zeros_like(done_ref)
    me = lax.axis_index("seq")
    core = me % 2
    cut, rows = column_refs[0].shape[2:]
    for chip, ref in enumerate(column_refs):
        joined_ref[:, :, at(me ^ (2 * chip), rows)] = ref[0]
        for which in range(2):
            first = (2 * chip + which) * cut
            joined_ref[which, :, at(me ^ (2 * chip + 1), rows)] = got_ref[first : first + cut]
    first = 2 * len(column_refs) * cut
    for ref in (far_attn_ref, far_dv_ref):
        for block in range(ref.shape[1] // rows):
            ref[:, block * rows : (block + 1) * rows] = got_ref[first : first + ref.shape[0]]
            first += ref.shape[0]
    for half, attn, dv_t in ((core, attn_ref, dv_t_ref), (1 - core, far_attn_ref, far_dv_ref)):
        woutput_ref[:, at(half, attn.shape[0])] = dot_nt(joined_ref[1], attn[...])
        wvalue_ref[:, at(half, dv_t.shape[0])] = dot_nt(joined_ref[0], dv_t[...])


def add_kernel(own_ref, arrived_ref, _, sum_ref):
    total = own_ref[...].astype(jnp.float32) + arrived_ref[...].astype(jnp.float32)
    sum_ref[...] = total.astype(jnp.bfloat16)


def far_sum_kernel(_, own_ref, arrived_ref, sum_ref):
    sum_ref[...] = own_ref[...] + arrived_ref[...].astype(jnp.float32)


def sum_kernel(own_ref, *refs):
    total = own_ref[...]
    for arrived_ref in refs[:-1]:
        total = total + arrived_ref[...].astype(jnp.float32)
    refs[-1][...] = total.astype(jnp.bfloat16)


def kernel_call(
    body, outs, operands, in_vmem=(), scratch=(), flops=0, moved=0, room=16
):
    vmem = pl.BlockSpec(memory_space=pltpu.VMEM)
    hbm = pl.BlockSpec(memory_space=pltpu.HBM)
    return pl.pallas_call(
        body,
        out_shape=outs,
        in_specs=[vmem if place in in_vmem else hbm for place in range(len(operands))],
        out_specs=(vmem,) * len(outs),
        scratch_shapes=list(scratch),
        compiler_params=pltpu.CompilerParams(vmem_limit_bytes=room * 1024 * 1024),
        cost_estimate=pl.CostEstimate(flops=flops, bytes_accessed=moved, transcendentals=0),
    )(*operands)


def swapped(value, axis, apart):
    count = lax.axis_size(axis)
    return lax.ppermute(value, axis, [(place, place ^ apart) for place in range(count)])


def gathered_plan(
    normed_input,
    stored_queries,
    stored_keys,
    stored_values,
    query_weight,
    key_matrix,
    value_matrix,
    output_weight,
    out_cotangent,
):
    bf16, f32 = jnp.bfloat16, jnp.float32
    rows, model = normed_input.shape
    blocks = lax.axis_size("seq")
    groups = lax.axis_size("head")
    tokens = rows * blocks
    q_cols = stored_queries.shape[1] // 2
    kv_cols = HEAD_SIZE
    wide = 2 * QUERIES_PER_KEY * rows
    packed_cols = 2 * q_cols + 2 * kv_cols
    pieces = 3 if model % (6 * HEAD_SIZE) == 0 else 1
    shape = jax.ShapeDtypeStruct
    same, other = kernel_call(
        out_grad_kernel,
        (shape((rows, packed_cols), bf16),) * 2,
        (out_cotangent, output_weight, stored_queries, stored_keys, stored_values),
        scratch=(
            pltpu.VMEM(out_cotangent.shape, bf16),
            pltpu.VMEM(output_weight.shape, bf16),
            pltpu.SemaphoreType.DMA((6 + 3 * pieces,)),
        ),
        flops=4 * rows * model * q_cols,
        moved=2 * model * (rows + 2 * q_cols),
        room=63,
    )
    held = {0: same}
    for apart in range(2, blocks):
        lowest, highest = 2, 1 << (apart.bit_length() - 1)
        while not apart & lowest:
            lowest *= 2
        through = lowest if apart % 2 else highest
        if lowest == highest:
            held[apart] = swapped(other if apart % 2 else same, "seq", apart)
        else:
            held[apart] = swapped(held[apart ^ through], "seq", through)
    held[1] = swapped(other, "seq", 1)
    cut = model // blocks
    *columns, held[0] = kernel_call(
        turn_kernel,
        (shape((2, 2, cut, rows), bf16),) * (blocks // 2) + (shape(same.shape, bf16),),
        (normed_input, out_cotangent, same, held[2], held[blocks // 2 + 1]),
        in_vmem=range(3),
        scratch=(pltpu.VMEM((2, model, rows), bf16),),
        moved=8 * rows * model,
        room=8,
    )
    columns = [columns[0]] + [
        swapped(columns[chip], "seq", 2 * chip) for chip in range(1, blocks // 2)
    ]
    dx_own, dx_far, attn, prob, grad_t = kernel_call(
        functools.partial(attention_kernel, blocks),
        (
            shape((rows, q_cols + 2 * kv_cols), bf16),
            shape((rows, q_cols + 2 * kv_cols), bf16),
            shape((q_cols, tokens), bf16),
            shape((tokens, tokens * QUERIES_PER_KEY), bf16),
            shape((HEAD_SIZE, tokens * QUERIES_PER_KEY), bf16),
        ),
        [held[apart] for apart in range(blocks)],
        in_vmem=range(blocks),
        scratch=(
            pltpu.VMEM((tokens, packed_cols), bf16),
            pltpu.VMEM((tokens, wide), f32),
            pltpu.VMEM((tokens, wide), f32),
            pltpu.VMEM((1, tokens * QUERIES_PER_KEY), f32),
            pltpu.VMEM((tokens * QUERIES_PER_KEY, HEAD_SIZE), bf16),
            pltpu.VMEM((HEAD_SIZE, tokens), bf16),
            pltpu.VMEM((HEAD_SIZE, tokens), bf16),
            pltpu.VMEM((HEAD_SIZE, wide), f32),
            pltpu.VMEM((2 * rows, HEAD_SIZE), f32),
            pltpu.VMEM((2 * rows, HEAD_SIZE), f32),
        ),
        flops=8 * tokens * tokens * q_cols,
        moved=2 * tokens * packed_cols,
    )
    dx_got = swapped(dx_far, "seq", 1)
    def terms_of(chosen):
        return kernel_call(
            functools.partial(input_terms_kernel, chosen),
            tuple(shape((model // groups, rows), f32 if not apart else bf16) for apart in chosen),
            (dx_own, dx_got, query_weight, key_matrix, value_matrix),
            in_vmem=range(5),
            scratch=(pltpu.VMEM((rows, 2 * (q_cols + 2 * kv_cols)), bf16),),
            flops=2 * len(chosen) * rows * (model // groups) * 2 * (q_cols + 2 * kv_cols),
            moved=2 * len(chosen) * (model // groups) * 2 * (q_cols + 2 * kv_cols),
            room=4,
        )

    (far_term,) = terms_of((3,))
    pair_term, near_term, own_term = terms_of((2, 1, 0))
    (dv_t,) = kernel_call(
        value_grad_kernel,
        (shape((kv_cols, tokens), bf16),),
        (prob, grad_t),
        in_vmem=range(2),
        flops=tokens * tokens * q_cols,
        moved=2 * tokens * tokens * QUERIES_PER_KEY,
        room=4,
    )
    (pair_sum,) = kernel_call(
        add_kernel,
        (shape(pair_term.shape, bf16),),
        (pair_term, swapped(far_term, "head", 1), dv_t),
        in_vmem=range(2),
        room=4,
    )
    part_rows = q_cols + kv_cols
    (give,) = kernel_call(
        pass_on_kernel,
        (shape((blocks * (cut + part_rows), rows), bf16),),
        (pair_sum, attn, dv_t, *columns),
        in_vmem=range(1, 3 + blocks // 2),
        room=4,
    )
    grad_wvalue, grad_woutput, weights_done = kernel_call(
        weight_grad_kernel,
        (
            shape((model // blocks, 2 * kv_cols), f32),
            shape((model // blocks, 2 * q_cols), f32),
            shape((8, HEAD_SIZE), f32),
        ),
        (attn, dv_t, swapped(give, "seq", 1), *columns),
        in_vmem=range(3 + blocks // 2),
        scratch=(
            pltpu.VMEM((2, model // blocks, tokens), bf16),
            pltpu.VMEM((q_cols, tokens), bf16),
            pltpu.VMEM((kv_cols, tokens), bf16),
        ),
        room=8,
    )
    (far_sum,) = kernel_call(
        far_sum_kernel,
        (shape((model // groups, rows), f32),),
        (weights_done, own_term, swapped(pair_sum, "head", 2)),
        in_vmem=range(1, 3),
        moved=10 * rows * (model // groups),
        room=4,
    )
    (grad_input,) = kernel_call(
        sum_kernel,
        (shape((model // groups, rows), bf16),),
        (far_sum, swapped(near_term, "head", 1)),
        in_vmem=range(2),
        moved=4 * groups * (model // groups) * rows,
    )
    return (grad_input.T, grad_wvalue, grad_woutput.T)


def power_of_two(count):
    return count & (count - 1) == 0


def local(normed_input, stored_queries, stored_keys, *others):
    blocks, groups = lax.axis_size("seq"), lax.axis_size("head")
    whole_window = normed_input.shape[0] * blocks <= WINDOW_LENGTH
    two_heads = stored_keys.shape[1] == 2 * HEAD_SIZE
    paired = blocks >= 4 and power_of_two(blocks) and groups == 4
    plan = gathered_plan if whole_window and two_heads and paired else windowed_plan
    return plan(normed_input, stored_queries, stored_keys, *others)


def windowed_plan(
    normed_input,
    stored_queries,
    stored_keys,
    stored_values,
    query_weight,
    key_matrix,
    value_matrix,
    output_weight,
    out_cotangent,
):
    tok_rows = normed_input.shape[0]
    blocks_seq = lax.axis_size("seq")
    seq_place = lax.axis_index("seq")
    reach_blocks = min(WINDOW_LENGTH // tok_rows, blocks_seq - 1)
    kv_heads = stored_keys.shape[1] // HEAD_SIZE
    output_gradient = jnp.dot(
        out_cotangent, output_weight.T, preferred_element_type=jnp.float32
    ).astype(jnp.bfloat16)
    pieces = [(stored_keys, stored_values)]
    current = (stored_keys, stored_values)
    for relay_step in range(reach_blocks):
        current = passed_along((current[0], current[1]), "seq", 1)
        pieces = [current] + pieces
    key_window = jnp.concatenate([piece[0] for piece in pieces], axis=0)
    value_window = jnp.concatenate([piece[1] for piece in pieces], axis=0)
    key_span = key_window.shape[0]
    query_pos = seq_place * tok_rows + jnp.arange(tok_rows, dtype=jnp.int32)
    key_pos = (seq_place - reach_blocks) * tok_rows + jnp.arange(key_span, dtype=jnp.int32)
    pos_gap = query_pos[:, None] - key_pos[None, :]
    allowed = (pos_gap >= 0) & (pos_gap < WINDOW_LENGTH) & (key_pos >= 0)[None, :]
    allowed_rows = jnp.tile(allowed, (QUERIES_PER_KEY, 1))
    query_stack = (
        stored_queries.reshape(tok_rows, kv_heads, QUERIES_PER_KEY, HEAD_SIZE)
        .transpose(1, 2, 0, 3)
        .reshape(kv_heads, QUERIES_PER_KEY * tok_rows, HEAD_SIZE)
    )
    grad_stack = (
        output_gradient.reshape(tok_rows, kv_heads, QUERIES_PER_KEY, HEAD_SIZE)
        .transpose(1, 2, 0, 3)
        .reshape(kv_heads, QUERIES_PER_KEY * tok_rows, HEAD_SIZE)
    )
    key_stack = key_window.reshape(key_span, kv_heads, HEAD_SIZE).transpose(1, 0, 2)
    value_stack = value_window.reshape(key_span, kv_heads, HEAD_SIZE).transpose(1, 0, 2)

    def per_head(head_items):
        query_head, key_head, value_head, grad_head = head_items
        attention_logits = logit_scale * jnp.dot(
            query_head, key_head.T, preferred_element_type=jnp.float32
        )
        masked = jnp.where(allowed_rows, attention_logits, -jnp.inf)
        row_top = jnp.max(masked, axis=1, keepdims=True)
        exp_scores = jnp.exp(masked - row_top)
        attn_prob = exp_scores / jnp.sum(exp_scores, axis=1, keepdims=True)
        probability_halfwidth = attn_prob.astype(jnp.bfloat16)
        attn_head = jnp.dot(
            probability_halfwidth, value_head, preferred_element_type=jnp.float32
        ).astype(jnp.bfloat16)
        row_delta = jnp.sum(
            grad_head.astype(jnp.float32) * attn_head.astype(jnp.float32), axis=1, keepdims=True
        )
        probability_gradient = jnp.dot(grad_head, value_head.T, preferred_element_type=jnp.float32)
        score_gradient = (attn_prob * (probability_gradient - row_delta)).astype(jnp.bfloat16)
        qgrad_head = (
            logit_scale * jnp.dot(score_gradient, key_head, preferred_element_type=jnp.float32)
        ).astype(jnp.bfloat16)
        key_partial = logit_scale * jnp.dot(
            score_gradient.T, query_head, preferred_element_type=jnp.float32
        )
        value_partial = jnp.dot(
            probability_halfwidth.T, grad_head, preferred_element_type=jnp.float32
        )
        return (attn_head, qgrad_head, key_partial, value_partial)

    attn_all, qgrad_all, key_all, value_all = lax.map(
        per_head, (query_stack, key_stack, value_stack, grad_stack)
    )
    attention_output = (
        attn_all.reshape(kv_heads, QUERIES_PER_KEY, tok_rows, HEAD_SIZE)
        .transpose(2, 0, 1, 3)
        .reshape(tok_rows, kv_heads * QUERIES_PER_KEY * HEAD_SIZE)
    )
    query_gradient = (
        qgrad_all.reshape(kv_heads, QUERIES_PER_KEY, tok_rows, HEAD_SIZE)
        .transpose(2, 0, 1, 3)
        .reshape(tok_rows, kv_heads * QUERIES_PER_KEY * HEAD_SIZE)
    )
    key_terms = key_all.transpose(1, 0, 2).reshape(key_span, kv_heads * HEAD_SIZE)
    value_terms = value_all.transpose(1, 0, 2).reshape(key_span, kv_heads * HEAD_SIZE)

    def take_slot(terms, slot_index):
        return terms[slot_index * tok_rows : (slot_index + 1) * tok_rows]

    key_sum = take_slot(key_terms, reach_blocks)
    value_sum = take_slot(value_terms, reach_blocks)
    for distance in range(1, reach_blocks + 1):
        received = passed_along(
            (
                take_slot(key_terms, reach_blocks - distance),
                take_slot(value_terms, reach_blocks - distance),
            ),
            "seq",
            -distance,
        )
        key_sum = key_sum + received[0]
        value_sum = value_sum + received[1]
    grad_key = key_sum.astype(jnp.bfloat16)
    grad_value = value_sum.astype(jnp.bfloat16)
    input_terms = jnp.dot(query_gradient, query_weight.T, preferred_element_type=jnp.float32)
    input_terms = input_terms + jnp.dot(grad_key, key_matrix.T, preferred_element_type=jnp.float32)
    input_terms = input_terms + jnp.dot(
        grad_value, value_matrix.T, preferred_element_type=jnp.float32
    )
    grad_input = lax.psum_scatter(input_terms, "head", scatter_dimension=1, tiled=True).astype(
        jnp.bfloat16
    )
    value_cols = grad_value.shape[1]
    input_cols = normed_input.T
    cot_cols = out_cotangent.T
    gathered = lax.psum_scatter(
        jnp.concatenate(
            [
                jnp.dot(input_cols, grad_value, preferred_element_type=jnp.float32),
                jnp.dot(cot_cols, attention_output, preferred_element_type=jnp.float32),
            ],
            axis=1,
        ),
        "seq",
        scatter_dimension=0,
        tiled=True,
    )
    grad_wvalue = gathered[:, :value_cols]
    grad_woutput = gathered[:, value_cols:].T
    return (grad_input, grad_wvalue, grad_woutput)


def solution(mesh):
    placed = (
        P("seq", None),
        P("seq", "head"),
        P("seq", "head"),
        P("seq", "head"),
        P(None, "head"),
        P(None, "head"),
        P(None, "head"),
        P("head", None),
        P("seq", None),
    )
    return jax.shard_map(
        local,
        mesh=mesh,
        in_specs=placed,
        out_specs=(P("seq", "head"), P("seq", "head"), P("head", "seq")),
        check_vma=False,
    )
```

```python
import functools

import jax
import jax.numpy as jnp
from jax import lax
from jax.experimental import pallas as pl
from jax.experimental.pallas import tpu as pltpu
from jax.sharding import PartitionSpec as P

HEAD_SIZE = 128
WINDOW_LENGTH = 4096
QUERIES_PER_KEY = 2


logit_scale = 1.0 / 12.0
log2_scale = 1.4426950408889634 / 12.0
excluded = -1e30


def passed_along(value, axis, steps):
    count = lax.axis_size(axis)
    leading, last = (max(0, -steps), min(count, count - steps))
    return lax.ppermute(value, axis, [(source, source + steps) for source in range(leading, last)])


NT = (((1,), (1,)), ((), ()))


def dot_nt(left, right):
    return lax.dot_general(left, right, NT, preferred_element_type=jnp.float32)


def dot_nn(left, right):
    return jnp.dot(left, right, preferred_element_type=jnp.float32)


def at(place, size):
    return pl.ds(pl.multiple_of(place * size, size), size)


def out_grad_kernel(
    cot_hbm, weight_hbm, q_hbm, k_hbm, v_hbm, same_hbm, other_hbm, cot_ref, weight_ref, half_ref, sem
):
    core = lax.axis_index("seq") % 2
    halves = ((other_hbm, 1 - core), (same_hbm, core))
    rows = weight_ref.shape[0] // 2
    pieces = (sem.shape[0] - 10) // 3
    cut = weight_ref.shape[1] // pieces
    model_copies = []
    for piece in range(pieces):
        part = pl.ds(piece * cut, cut)
        model_copies.append(
            [
                pltpu.make_async_copy(
                    cot_hbm.at[:, part], cot_ref.at[:, part], sem.at[6 + 3 * piece]
                )
            ]
        )
        for place, (_, half) in enumerate(halves):
            model_copies[-1].append(
                pltpu.make_async_copy(
                    weight_hbm.at[at(half, rows), part],
                    weight_ref.at[pl.ds(place * rows, rows), part],
                    sem.at[7 + 3 * piece + place],
                )
            )
        for copy in model_copies[-1]:
            copy.start()
    plain_copies = []
    for place, (target, half) in enumerate(halves):
        first = 0
        for which, source in enumerate((q_hbm, k_hbm, v_hbm)):
            cols = source.shape[1] // 2
            plain_copies.append(
                pltpu.make_async_copy(
                    source.at[:, at(half, cols)],
                    half_ref.at[place, :, pl.ds(first, cols)],
                    sem.at[3 * place + which],
                )
            )
            plain_copies[-1].start()
            first += cols
    out_copies = []
    for place, (target, _) in enumerate(halves):
        for which, cols in enumerate((pl.ds(0, first), pl.ds(first, target.shape[1] - first))):
            out_copies.append(
                pltpu.make_async_copy(
                    half_ref.at[place, :, cols],
                    target.at[:, cols],
                    sem.at[6 + 3 * pieces + 2 * place + which],
                )
            )
    total = None
    for piece in range(pieces):
        for copy in model_copies[piece]:
            copy.wait()
        part = slice(piece * cut, (piece + 1) * cut)
        product = dot_nt(weight_ref[:, part], cot_ref[:, part])
        total = product if total is None else total + product
    for copy in plain_copies:
        copy.wait()
    out_copies[0].start()
    out_copies[2].start()
    for place in range(2):
        for head in range(rows // HEAD_SIZE):
            row = place * rows + head * HEAD_SIZE
            half_ref[place, :, first + head * HEAD_SIZE : first + (head + 1) * HEAD_SIZE] = total[
                row : row + HEAD_SIZE
            ].astype(jnp.bfloat16)
        out_copies[2 * place + 1].start()
    for copy in out_copies:
        copy.wait()


def turn_kernel(normed_ref, cot_ref, block_ref, _, __, *refs):
    *column_refs, own_ref, turned_ref = refs
    me = lax.axis_index("seq")
    cut = column_refs[0].shape[2]
    own_ref[...] = block_ref[...]
    for which, ref in enumerate((normed_ref, cot_ref)):
        turned_ref[which] = ref[...].astype(jnp.float32).T.astype(jnp.bfloat16)
        for chip, target in enumerate(column_refs):
            for far in range(2):
                target[far, which] = turned_ref[which, at(me ^ (2 * chip + far), cut)]


def pass_on_kernel(_, attn_ref, dv_t_ref, *refs):
    *column_refs, give_ref = refs
    cut, rows = column_refs[0].shape[2:]
    for chip, ref in enumerate(column_refs):
        for which in range(2):
            first = (2 * chip + which) * cut
            give_ref[first : first + cut] = ref[1, which]
    first = 2 * len(column_refs) * cut
    for ref in (attn_ref, dv_t_ref):
        for block in range(ref.shape[1] // rows):
            give_ref[first : first + ref.shape[0]] = ref[:, block * rows : (block + 1) * rows]
            first += ref.shape[0]


def attention_kernel(blocks, *refs):
    attention_body(refs[:blocks], *refs[blocks:])


def attention_body(
    block_refs,
    dx_own_ref,
    dx_far_ref,
    attn_ref,
    prob_ref,
    grad_t_ref,
    gathered_ref,
    score_even_ref,
    score_odd_ref,
    delta_ref,
    query_ref,
    value_t_ref,
    key_t_ref,
    dq_t_ref,
    dk_ref,
    dv_ref,
):
    me = lax.axis_index("seq")
    core, chip = me % 2, me // 2
    rows = dx_own_ref.shape[0]
    for apart, source in enumerate(block_refs):
        gathered_ref[at(me ^ apart, rows)] = source[...]
    tokens = gathered_ref.shape[0]
    size = 2 * rows
    steps = tokens // size
    wide = QUERIES_PER_KEY * size
    heads = QUERIES_PER_KEY
    key_cols = slice(heads * HEAD_SIZE, (heads + 1) * HEAD_SIZE)
    value_cols = slice((heads + 1) * HEAD_SIZE, (heads + 2) * HEAD_SIZE)
    grad_base = (heads + 2) * HEAD_SIZE
    value_t_ref[...] = gathered_ref[:, value_cols].T
    key_t_ref[...] = gathered_ref[:, key_cols].T
    key_place = lax.broadcasted_iota(jnp.int32, (size, wide), 0)
    query_place = lax.broadcasted_iota(jnp.int32, (size, wide), 1) % size
    allowed = key_place <= query_place

    def scored(step):
        own = slice(step * size, (step + 1) * size)
        score_ref = score_odd_ref if step % 2 else score_even_ref
        queries = jnp.concatenate(
            [gathered_ref[own, h * HEAD_SIZE : (h + 1) * HEAD_SIZE] for h in range(heads)], axis=0
        )
        query_ref[step * wide : (step + 1) * wide] = queries
        top = None
        for piece in range(step + 1):
            part = slice(piece * size, (piece + 1) * size)
            scores = dot_nt(gathered_ref[part, key_cols], queries)
            if piece == step:
                scores = jnp.where(allowed, scores, excluded)
            score_ref[part] = scores
            largest = jnp.max(scores.reshape(size // 8, 8, wide), axis=0)
            top = largest if top is None else jnp.maximum(top, largest)
        return top

    next_top = scored(steps - 1)
    for step in range(steps - 1, -1, -1):
        span = (step + 1) * size
        own = slice(step * size, span)
        lanes = slice(step * wide, (step + 1) * wide)
        score_ref = score_odd_ref if step % 2 else score_even_ref
        top = next_top
        if step:
            next_top = scored(step - 1)
        top = jnp.max(top, axis=0, keepdims=True)
        total = None
        for piece in range(step + 1):
            part = slice(piece * size, (piece + 1) * size)
            weights = jnp.exp2((score_ref[part] - top) * log2_scale)
            prob_ref[part, lanes] = weights.astype(jnp.bfloat16)
            summed = jnp.sum(weights.reshape(size // 8, 8, wide), axis=0)
            total = summed if total is None else total + summed
        inverse = 1.0 / jnp.sum(total, axis=0, keepdims=True)
        attn = dot_nn(value_t_ref[:, :span], prob_ref[:span, lanes]) * inverse
        for h in range(heads):
            attn_ref[h * HEAD_SIZE : (h + 1) * HEAD_SIZE, own] = attn[
                :, h * size : (h + 1) * size
            ].astype(jnp.bfloat16)
        grads_t = jnp.concatenate(
            [
                gathered_ref[
                    block * rows : (block + 1) * rows,
                    grad_base + h * HEAD_SIZE : grad_base + (h + 1) * HEAD_SIZE,
                ]
                for h in range(heads)
                for block in (2 * step, 2 * step + 1)
            ],
            axis=1,
        )
        grads_t = (grads_t.astype(jnp.float32) * inverse).astype(jnp.bfloat16)
        grad_t_ref[:, lanes] = grads_t
        delta_ref[:, lanes] = jnp.sum(grads_t.astype(jnp.float32) * attn, axis=0, keepdims=True)

    dq_t_ref[...] = jnp.zeros_like(dq_t_ref)
    dk_ref[...] = jnp.zeros_like(dk_ref)
    dv_ref[...] = jnp.zeros_like(dv_ref)
    for step in range(steps):
        key_step = jnp.minimum(chip, step)
        query_step = jnp.maximum(chip, step)
        dprob = dot_nn(
            gathered_ref[at(key_step, size), value_cols], grad_t_ref[:, at(query_step, wide)]
        )
        prob = prob_ref[at(key_step, size), at(query_step, wide)]
        dscore = (
            prob.astype(jnp.float32)
            * (dprob - delta_ref[:, at(query_step, wide)])
        ).astype(jnp.bfloat16)

        @pl.when(step <= chip)
        def _():
            dq_t_ref[...] += dot_nn(key_t_ref[:, at(key_step, size)], dscore)

        @pl.when(step >= chip)
        def _():
            dk_ref[...] += dot_nn(dscore, query_ref[at(query_step, wide)])
            dv_ref[...] += dot_nt(prob, grad_t_ref[:, at(query_step, wide)])

    for target, half in ((dx_far_ref, 1 - core), (dx_own_ref, core)):
        for h in range(heads):
            target[:, h * HEAD_SIZE : (h + 1) * HEAD_SIZE] = (
                (logit_scale * dq_t_ref[:, at(2 * h + half, rows)])
                .T.astype(jnp.bfloat16)
            )
        target[:, key_cols] = (logit_scale * dk_ref[at(half, rows)]).astype(jnp.bfloat16)
        target[:, value_cols] = dv_ref[at(half, rows)].astype(jnp.bfloat16)


def value_grad_kernel(prob_ref, grad_t_ref, dv_t_ref):
    size = 2 * HEAD_SIZE
    wide = QUERIES_PER_KEY * size
    for step in range(prob_ref.shape[0] // size):
        own = slice(step * size, (step + 1) * size)
        dv_t_ref[:, own] = dot_nt(grad_t_ref[:, step * wide :], prob_ref[own, step * wide :]).astype(
            jnp.bfloat16
        )


def input_terms_kernel(apart_groups, own_ref, far_ref, wq_ref, wk_ref, wv_ref, *refs):
    terms, dx_ref = refs[-1 - len(apart_groups) : -1], refs[-1]
    core = lax.axis_index("seq") % 2
    group = lax.axis_index("head")
    q_cols = wq_ref.shape[1] // 2
    kv_cols = wk_ref.shape[1] // 2
    for source, half in ((own_ref, core), (far_ref, 1 - core)):
        dx_ref[:, at(half, q_cols)] = source[:, :q_cols]
        dx_ref[:, pl.ds(pl.multiple_of(2 * q_cols + half * kv_cols, kv_cols), kv_cols)] = source[
            :, q_cols : q_cols + kv_cols
        ]
        dx_ref[
            :, pl.ds(pl.multiple_of(2 * q_cols + (2 + half) * kv_cols, kv_cols), kv_cols)
        ] = source[:, q_cols + kv_cols :]
    for apart, target in zip(apart_groups, terms):
        cut = target.shape[0]
        place = at(group ^ apart, cut)
        target[...] = (
            dot_nt(wq_ref[place], dx_ref[:, : 2 * q_cols])
            + dot_nt(wk_ref[place], dx_ref[:, 2 * q_cols : 2 * q_cols + 2 * kv_cols])
            + dot_nt(wv_ref[place], dx_ref[:, 2 * q_cols + 2 * kv_cols :])
        ).astype(target.dtype)


def weight_grad_kernel(attn_ref, dv_t_ref, got_ref, *refs):
    column_refs, refs = refs[:-6], refs[-6:]
    wvalue_ref, woutput_ref, done_ref, joined_ref, far_attn_ref, far_dv_ref = refs
    done_ref[...] = jnp.zeros_like(done_ref)
    me = lax.axis_index("seq")
    core = me % 2
    cut, rows = column_refs[0].shape[2:]
    for chip, ref in enumerate(column_refs):
        joined_ref[:, :, at(me ^ (2 * chip), rows)] = ref[0]
        for which in range(2):
            first = (2 * chip + which) * cut
            joined_ref[which, :, at(me ^ (2 * chip + 1), rows)] = got_ref[first : first + cut]
    first = 2 * len(column_refs) * cut
    for ref in (far_attn_ref, far_dv_ref):
        for block in range(ref.shape[1] // rows):
            ref[:, block * rows : (block + 1) * rows] = got_ref[first : first + ref.shape[0]]
            first += ref.shape[0]
    for half, attn, dv_t in ((core, attn_ref, dv_t_ref), (1 - core, far_attn_ref, far_dv_ref)):
        woutput_ref[:, at(half, attn.shape[0])] = dot_nt(joined_ref[1], attn[...])
        wvalue_ref[:, at(half, dv_t.shape[0])] = dot_nt(joined_ref[0], dv_t[...])


def add_kernel(own_ref, arrived_ref, _, sum_ref):
    total = own_ref[...].astype(jnp.float32) + arrived_ref[...].astype(jnp.float32)
    sum_ref[...] = total.astype(jnp.bfloat16)


def far_sum_kernel(_, own_ref, arrived_ref, sum_ref):
    sum_ref[...] = own_ref[...] + arrived_ref[...].astype(jnp.float32)


def sum_kernel(own_ref, *refs):
    total = own_ref[...]
    for arrived_ref in refs[:-1]:
        total = total + arrived_ref[...].astype(jnp.float32)
    refs[-1][...] = total.astype(jnp.bfloat16)


def kernel_call(
    body, outs, operands, in_vmem=(), scratch=(), flops=0, moved=0, room=16, out_vmem=True
):
    vmem = pl.BlockSpec(memory_space=pltpu.VMEM)
    hbm = pl.BlockSpec(memory_space=pltpu.HBM)
    return pl.pallas_call(
        body,
        out_shape=outs,
        in_specs=[vmem if place in in_vmem else hbm for place in range(len(operands))],
        out_specs=(vmem if out_vmem else hbm,) * len(outs),
        scratch_shapes=list(scratch),
        compiler_params=pltpu.CompilerParams(vmem_limit_bytes=room * 1024 * 1024),
        cost_estimate=pl.CostEstimate(flops=flops, bytes_accessed=moved, transcendentals=0),
    )(*operands)


def swapped(value, axis, apart):
    count = lax.axis_size(axis)
    return lax.ppermute(value, axis, [(place, place ^ apart) for place in range(count)])


def gathered_plan(
    normed_input,
    stored_queries,
    stored_keys,
    stored_values,
    query_weight,
    key_matrix,
    value_matrix,
    output_weight,
    out_cotangent,
):
    bf16, f32 = jnp.bfloat16, jnp.float32
    rows, model = normed_input.shape
    blocks = lax.axis_size("seq")
    groups = lax.axis_size("head")
    tokens = rows * blocks
    q_cols = stored_queries.shape[1] // 2
    kv_cols = HEAD_SIZE
    wide = 2 * QUERIES_PER_KEY * rows
    packed_cols = 2 * q_cols + 2 * kv_cols
    pieces = 3 if model % (6 * HEAD_SIZE) == 0 else 1
    shape = jax.ShapeDtypeStruct
    same, other = kernel_call(
        out_grad_kernel,
        (shape((rows, packed_cols), bf16),) * 2,
        (out_cotangent, output_weight, stored_queries, stored_keys, stored_values),
        scratch=(
            pltpu.VMEM(out_cotangent.shape, bf16),
            pltpu.VMEM(output_weight.shape, bf16),
            pltpu.VMEM((2, rows, packed_cols), bf16),
            pltpu.SemaphoreType.DMA((10 + 3 * pieces,)),
        ),
        flops=4 * rows * model * q_cols,
        moved=2 * model * (rows + 2 * q_cols),
        room=63,
        out_vmem=False,
    )
    held = {0: same}
    for apart in range(2, blocks):
        lowest, highest = 2, 1 << (apart.bit_length() - 1)
        while not apart & lowest:
            lowest *= 2
        through = lowest if apart % 2 else highest
        if lowest == highest:
            held[apart] = swapped(other if apart % 2 else same, "seq", apart)
        else:
            held[apart] = swapped(held[apart ^ through], "seq", through)
    held[1] = swapped(other, "seq", 1)
    cut = model // blocks
    *columns, held[0] = kernel_call(
        turn_kernel,
        (shape((2, 2, cut, rows), bf16),) * (blocks // 2) + (shape(same.shape, bf16),),
        (normed_input, out_cotangent, same, held[2], held[blocks // 2 + 1]),
        in_vmem=range(3),
        scratch=(pltpu.VMEM((2, model, rows), bf16),),
        moved=8 * rows * model,
        room=8,
    )
    columns = [columns[0]] + [
        swapped(columns[chip], "seq", 2 * chip) for chip in range(1, blocks // 2)
    ]
    dx_own, dx_far, attn, prob, grad_t = kernel_call(
        functools.partial(attention_kernel, blocks),
        (
            shape((rows, q_cols + 2 * kv_cols), bf16),
            shape((rows, q_cols + 2 * kv_cols), bf16),
            shape((q_cols, tokens), bf16),
            shape((tokens, tokens * QUERIES_PER_KEY), bf16),
            shape((HEAD_SIZE, tokens * QUERIES_PER_KEY), bf16),
        ),
        [held[apart] for apart in range(blocks)],
        in_vmem=range(blocks),
        scratch=(
            pltpu.VMEM((tokens, packed_cols), bf16),
            pltpu.VMEM((tokens, wide), f32),
            pltpu.VMEM((tokens, wide), f32),
            pltpu.VMEM((1, tokens * QUERIES_PER_KEY), f32),
            pltpu.VMEM((tokens * QUERIES_PER_KEY, HEAD_SIZE), bf16),
            pltpu.VMEM((HEAD_SIZE, tokens), bf16),
            pltpu.VMEM((HEAD_SIZE, tokens), bf16),
            pltpu.VMEM((HEAD_SIZE, wide), f32),
            pltpu.VMEM((2 * rows, HEAD_SIZE), f32),
            pltpu.VMEM((2 * rows, HEAD_SIZE), f32),
        ),
        flops=8 * tokens * tokens * q_cols,
        moved=2 * tokens * packed_cols,
    )
    dx_got = swapped(dx_far, "seq", 1)
    def terms_of(chosen):
        return kernel_call(
            functools.partial(input_terms_kernel, chosen),
            tuple(shape((model // groups, rows), f32 if not apart else bf16) for apart in chosen),
            (dx_own, dx_got, query_weight, key_matrix, value_matrix),
            in_vmem=range(5),
            scratch=(pltpu.VMEM((rows, 2 * (q_cols + 2 * kv_cols)), bf16),),
            flops=2 * len(chosen) * rows * (model // groups) * 2 * (q_cols + 2 * kv_cols),
            moved=2 * len(chosen) * (model // groups) * 2 * (q_cols + 2 * kv_cols),
            room=4,
        )

    (far_term,) = terms_of((3,))
    pair_term, near_term, own_term = terms_of((2, 1, 0))
    (dv_t,) = kernel_call(
        value_grad_kernel,
        (shape((kv_cols, tokens), bf16),),
        (prob, grad_t),
        in_vmem=range(2),
        flops=tokens * tokens * q_cols,
        moved=2 * tokens * tokens * QUERIES_PER_KEY,
        room=4,
    )
    (pair_sum,) = kernel_call(
        add_kernel,
        (shape(pair_term.shape, bf16),),
        (pair_term, swapped(far_term, "head", 1), dv_t),
        in_vmem=range(2),
        room=4,
    )
    part_rows = q_cols + kv_cols
    (give,) = kernel_call(
        pass_on_kernel,
        (shape((blocks * (cut + part_rows), rows), bf16),),
        (pair_sum, attn, dv_t, *columns),
        in_vmem=range(1, 3 + blocks // 2),
        room=4,
    )
    grad_wvalue, grad_woutput, weights_done = kernel_call(
        weight_grad_kernel,
        (
            shape((model // blocks, 2 * kv_cols), f32),
            shape((model // blocks, 2 * q_cols), f32),
            shape((8, HEAD_SIZE), f32),
        ),
        (attn, dv_t, swapped(give, "seq", 1), *columns),
        in_vmem=range(3 + blocks // 2),
        scratch=(
            pltpu.VMEM((2, model // blocks, tokens), bf16),
            pltpu.VMEM((q_cols, tokens), bf16),
            pltpu.VMEM((kv_cols, tokens), bf16),
        ),
        room=8,
    )
    (far_sum,) = kernel_call(
        far_sum_kernel,
        (shape((model // groups, rows), f32),),
        (weights_done, own_term, swapped(pair_sum, "head", 2)),
        in_vmem=range(1, 3),
        moved=10 * rows * (model // groups),
        room=4,
    )
    (grad_input,) = kernel_call(
        sum_kernel,
        (shape((model // groups, rows), bf16),),
        (far_sum, swapped(near_term, "head", 1)),
        in_vmem=range(2),
        moved=4 * groups * (model // groups) * rows,
    )
    return (grad_input.T, grad_wvalue, grad_woutput.T)


def power_of_two(count):
    return count & (count - 1) == 0


def local(normed_input, stored_queries, stored_keys, *others):
    blocks, groups = lax.axis_size("seq"), lax.axis_size("head")
    whole_window = normed_input.shape[0] * blocks <= WINDOW_LENGTH
    two_heads = stored_keys.shape[1] == 2 * HEAD_SIZE
    paired = blocks >= 4 and power_of_two(blocks) and groups == 4
    plan = gathered_plan if whole_window and two_heads and paired else windowed_plan
    return plan(normed_input, stored_queries, stored_keys, *others)


def windowed_plan(
    normed_input,
    stored_queries,
    stored_keys,
    stored_values,
    query_weight,
    key_matrix,
    value_matrix,
    output_weight,
    out_cotangent,
):
    tok_rows = normed_input.shape[0]
    blocks_seq = lax.axis_size("seq")
    seq_place = lax.axis_index("seq")
    reach_blocks = min(WINDOW_LENGTH // tok_rows, blocks_seq - 1)
    kv_heads = stored_keys.shape[1] // HEAD_SIZE
    output_gradient = jnp.dot(
        out_cotangent, output_weight.T, preferred_element_type=jnp.float32
    ).astype(jnp.bfloat16)
    pieces = [(stored_keys, stored_values)]
    current = (stored_keys, stored_values)
    for relay_step in range(reach_blocks):
        current = passed_along((current[0], current[1]), "seq", 1)
        pieces = [current] + pieces
    key_window = jnp.concatenate([piece[0] for piece in pieces], axis=0)
    value_window = jnp.concatenate([piece[1] for piece in pieces], axis=0)
    key_span = key_window.shape[0]
    query_pos = seq_place * tok_rows + jnp.arange(tok_rows, dtype=jnp.int32)
    key_pos = (seq_place - reach_blocks) * tok_rows + jnp.arange(key_span, dtype=jnp.int32)
    pos_gap = query_pos[:, None] - key_pos[None, :]
    allowed = (pos_gap >= 0) & (pos_gap < WINDOW_LENGTH) & (key_pos >= 0)[None, :]
    allowed_rows = jnp.tile(allowed, (QUERIES_PER_KEY, 1))
    query_stack = (
        stored_queries.reshape(tok_rows, kv_heads, QUERIES_PER_KEY, HEAD_SIZE)
        .transpose(1, 2, 0, 3)
        .reshape(kv_heads, QUERIES_PER_KEY * tok_rows, HEAD_SIZE)
    )
    grad_stack = (
        output_gradient.reshape(tok_rows, kv_heads, QUERIES_PER_KEY, HEAD_SIZE)
        .transpose(1, 2, 0, 3)
        .reshape(kv_heads, QUERIES_PER_KEY * tok_rows, HEAD_SIZE)
    )
    key_stack = key_window.reshape(key_span, kv_heads, HEAD_SIZE).transpose(1, 0, 2)
    value_stack = value_window.reshape(key_span, kv_heads, HEAD_SIZE).transpose(1, 0, 2)

    def per_head(head_items):
        query_head, key_head, value_head, grad_head = head_items
        attention_logits = logit_scale * jnp.dot(
            query_head, key_head.T, preferred_element_type=jnp.float32
        )
        masked = jnp.where(allowed_rows, attention_logits, -jnp.inf)
        row_top = jnp.max(masked, axis=1, keepdims=True)
        exp_scores = jnp.exp(masked - row_top)
        attn_prob = exp_scores / jnp.sum(exp_scores, axis=1, keepdims=True)
        probability_halfwidth = attn_prob.astype(jnp.bfloat16)
        attn_head = jnp.dot(
            probability_halfwidth, value_head, preferred_element_type=jnp.float32
        ).astype(jnp.bfloat16)
        row_delta = jnp.sum(
            grad_head.astype(jnp.float32) * attn_head.astype(jnp.float32), axis=1, keepdims=True
        )
        probability_gradient = jnp.dot(grad_head, value_head.T, preferred_element_type=jnp.float32)
        score_gradient = (attn_prob * (probability_gradient - row_delta)).astype(jnp.bfloat16)
        qgrad_head = (
            logit_scale * jnp.dot(score_gradient, key_head, preferred_element_type=jnp.float32)
        ).astype(jnp.bfloat16)
        key_partial = logit_scale * jnp.dot(
            score_gradient.T, query_head, preferred_element_type=jnp.float32
        )
        value_partial = jnp.dot(
            probability_halfwidth.T, grad_head, preferred_element_type=jnp.float32
        )
        return (attn_head, qgrad_head, key_partial, value_partial)

    attn_all, qgrad_all, key_all, value_all = lax.map(
        per_head, (query_stack, key_stack, value_stack, grad_stack)
    )
    attention_output = (
        attn_all.reshape(kv_heads, QUERIES_PER_KEY, tok_rows, HEAD_SIZE)
        .transpose(2, 0, 1, 3)
        .reshape(tok_rows, kv_heads * QUERIES_PER_KEY * HEAD_SIZE)
    )
    query_gradient = (
        qgrad_all.reshape(kv_heads, QUERIES_PER_KEY, tok_rows, HEAD_SIZE)
        .transpose(2, 0, 1, 3)
        .reshape(tok_rows, kv_heads * QUERIES_PER_KEY * HEAD_SIZE)
    )
    key_terms = key_all.transpose(1, 0, 2).reshape(key_span, kv_heads * HEAD_SIZE)
    value_terms = value_all.transpose(1, 0, 2).reshape(key_span, kv_heads * HEAD_SIZE)

    def take_slot(terms, slot_index):
        return terms[slot_index * tok_rows : (slot_index + 1) * tok_rows]

    key_sum = take_slot(key_terms, reach_blocks)
    value_sum = take_slot(value_terms, reach_blocks)
    for distance in range(1, reach_blocks + 1):
        received = passed_along(
            (
                take_slot(key_terms, reach_blocks - distance),
                take_slot(value_terms, reach_blocks - distance),
            ),
            "seq",
            -distance,
        )
        key_sum = key_sum + received[0]
        value_sum = value_sum + received[1]
    grad_key = key_sum.astype(jnp.bfloat16)
    grad_value = value_sum.astype(jnp.bfloat16)
    input_terms = jnp.dot(query_gradient, query_weight.T, preferred_element_type=jnp.float32)
    input_terms = input_terms + jnp.dot(grad_key, key_matrix.T, preferred_element_type=jnp.float32)
    input_terms = input_terms + jnp.dot(
        grad_value, value_matrix.T, preferred_element_type=jnp.float32
    )
    grad_input = lax.psum_scatter(input_terms, "head", scatter_dimension=1, tiled=True).astype(
        jnp.bfloat16
    )
    value_cols = grad_value.shape[1]
    input_cols = normed_input.T
    cot_cols = out_cotangent.T
    gathered = lax.psum_scatter(
        jnp.concatenate(
            [
                jnp.dot(input_cols, grad_value, preferred_element_type=jnp.float32),
                jnp.dot(cot_cols, attention_output, preferred_element_type=jnp.float32),
            ],
            axis=1,
        ),
        "seq",
        scatter_dimension=0,
        tiled=True,
    )
    grad_wvalue = gathered[:, :value_cols]
    grad_woutput = gathered[:, value_cols:].T
    return (grad_input, grad_wvalue, grad_woutput)


def solution(mesh):
    placed = (
        P("seq", None),
        P("seq", "head"),
        P("seq", "head"),
        P("seq", "head"),
        P(None, "head"),
        P(None, "head"),
        P(None, "head"),
        P("head", None),
        P("seq", None),
    )
    return jax.shard_map(
        local,
        mesh=mesh,
        in_specs=placed,
        out_specs=(P("seq", "head"), P("seq", "head"), P("head", "seq")),
        check_vma=False,
    )
```

```python
import functools

import jax
import jax.numpy as jnp
from jax import lax
from jax.experimental import pallas as pl
from jax.experimental.pallas import tpu as pltpu
from jax.sharding import PartitionSpec as P

HEAD_SIZE = 128
WINDOW_LENGTH = 4096
QUERIES_PER_KEY = 2


logit_scale = 1.0 / 12.0
log2_scale = 1.4426950408889634 / 12.0
excluded = -1e30


def passed_along(value, axis, steps):
    count = lax.axis_size(axis)
    leading, last = (max(0, -steps), min(count, count - steps))
    return lax.ppermute(value, axis, [(source, source + steps) for source in range(leading, last)])


NT = (((1,), (1,)), ((), ()))


def dot_nt(left, right):
    return lax.dot_general(left, right, NT, preferred_element_type=jnp.float32)


def dot_nn(left, right):
    return jnp.dot(left, right, preferred_element_type=jnp.float32)


def at(place, size):
    return pl.ds(pl.multiple_of(place * size, size), size)


def out_grad_kernel(
    cot_hbm, weight_hbm, q_hbm, k_hbm, v_hbm, same_ref, other_ref, cot_ref, weight_ref, sem
):
    core = lax.axis_index("seq") % 2
    halves = ((other_ref, 1 - core), (same_ref, core))
    rows = weight_ref.shape[0] // 2
    pieces = (sem.shape[0] - 6) // 3
    cut = weight_ref.shape[1] // pieces
    model_copies = []
    for piece in range(pieces):
        part = pl.ds(piece * cut, cut)
        model_copies.append(
            [
                pltpu.make_async_copy(
                    cot_hbm.at[:, part], cot_ref.at[:, part], sem.at[6 + 3 * piece]
                )
            ]
        )
        for place, (_, half) in enumerate(halves):
            model_copies[-1].append(
                pltpu.make_async_copy(
                    weight_hbm.at[at(half, rows), part],
                    weight_ref.at[pl.ds(place * rows, rows), part],
                    sem.at[7 + 3 * piece + place],
                )
            )
        for copy in model_copies[-1]:
            copy.start()
    plain_copies = []
    for place, (target, half) in enumerate(halves):
        first = 0
        for which, source in enumerate((q_hbm, k_hbm, v_hbm)):
            cols = source.shape[1] // 2
            plain_copies.append(
                pltpu.make_async_copy(
                    source.at[:, at(half, cols)],
                    target.at[:, pl.ds(first, cols)],
                    sem.at[3 * place + which],
                )
            )
            plain_copies[-1].start()
            first += cols
    total = None
    for piece in range(pieces):
        for copy in model_copies[piece]:
            copy.wait()
        part = slice(piece * cut, (piece + 1) * cut)
        product = dot_nt(weight_ref[:, part], cot_ref[:, part])
        total = product if total is None else total + product
    for place, (target, _) in enumerate(halves):
        for head in range(rows // HEAD_SIZE):
            row = place * rows + head * HEAD_SIZE
            target[:, first + head * HEAD_SIZE : first + (head + 1) * HEAD_SIZE] = total[
                row : row + HEAD_SIZE
            ].astype(jnp.bfloat16)
    for copy in plain_copies:
        copy.wait()


def turn_kernel(normed_ref, cot_ref, block_ref, _, __, *refs):
    *column_refs, own_ref, turned_ref = refs
    me = lax.axis_index("seq")
    cut = column_refs[0].shape[2]
    own_ref[...] = block_ref[...]
    for which, ref in enumerate((normed_ref, cot_ref)):
        turned_ref[which] = ref[...].astype(jnp.float32).T.astype(jnp.bfloat16)
        for chip, target in enumerate(column_refs):
            for far in range(2):
                target[far, which] = turned_ref[which, at(me ^ (2 * chip + far), cut)]


def pass_on_kernel(_, attn_ref, dv_t_ref, *refs):
    *column_refs, give_ref = refs
    cut, rows = column_refs[0].shape[2:]
    for chip, ref in enumerate(column_refs):
        for which in range(2):
            first = (2 * chip + which) * cut
            give_ref[first : first + cut] = ref[1, which]
    first = 2 * len(column_refs) * cut
    for ref in (attn_ref, dv_t_ref):
        for block in range(ref.shape[1] // rows):
            give_ref[first : first + ref.shape[0]] = ref[:, block * rows : (block + 1) * rows]
            first += ref.shape[0]


def attention_kernel(blocks, *refs):
    attention_body(refs[:blocks], *refs[blocks:])


def attention_body(
    block_refs,
    dx_own_ref,
    dx_far_ref,
    attn_ref,
    prob_ref,
    grad_t_ref,
    gathered_ref,
    score_even_ref,
    score_odd_ref,
    delta_ref,
    query_ref,
    value_t_ref,
    key_t_ref,
    dq_t_ref,
    dk_ref,
    dv_ref,
):
    me = lax.axis_index("seq")
    core, chip = me % 2, me // 2
    rows = dx_own_ref.shape[0]
    for apart, source in enumerate(block_refs):
        gathered_ref[at(me ^ apart, rows)] = source[...]
    tokens = gathered_ref.shape[0]
    size = 2 * rows
    steps = tokens // size
    wide = QUERIES_PER_KEY * size
    heads = QUERIES_PER_KEY
    key_cols = slice(heads * HEAD_SIZE, (heads + 1) * HEAD_SIZE)
    value_cols = slice((heads + 1) * HEAD_SIZE, (heads + 2) * HEAD_SIZE)
    grad_base = (heads + 2) * HEAD_SIZE
    value_t_ref[...] = gathered_ref[:, value_cols].T
    key_t_ref[...] = gathered_ref[:, key_cols].T
    key_place = lax.broadcasted_iota(jnp.int32, (size, wide), 0)
    query_place = lax.broadcasted_iota(jnp.int32, (size, wide), 1) % size
    allowed = key_place <= query_place

    def scored(step):
        own = slice(step * size, (step + 1) * size)
        score_ref = score_odd_ref if step % 2 else score_even_ref
        queries = jnp.concatenate(
            [gathered_ref[own, h * HEAD_SIZE : (h + 1) * HEAD_SIZE] for h in range(heads)], axis=0
        )
        query_ref[step * wide : (step + 1) * wide] = queries
        top = None
        for piece in range(step + 1):
            part = slice(piece * size, (piece + 1) * size)
            scores = dot_nt(gathered_ref[part, key_cols], queries)
            if piece == step:
                scores = jnp.where(allowed, scores, excluded)
            score_ref[part] = scores
            largest = jnp.max(scores.reshape(size // 8, 8, wide), axis=0)
            top = largest if top is None else jnp.maximum(top, largest)
        return top

    next_top = scored(steps - 1)
    for step in range(steps - 1, -1, -1):
        span = (step + 1) * size
        own = slice(step * size, span)
        lanes = slice(step * wide, (step + 1) * wide)
        score_ref = score_odd_ref if step % 2 else score_even_ref
        top = next_top
        if step:
            next_top = scored(step - 1)
        top = jnp.max(top, axis=0, keepdims=True)
        total = None
        for piece in range(step + 1):
            part = slice(piece * size, (piece + 1) * size)
            weights = jnp.exp2((score_ref[part] - top) * log2_scale)
            prob_ref[part, lanes] = weights.astype(jnp.bfloat16)
            summed = jnp.sum(weights.reshape(size // 8, 8, wide), axis=0)
            total = summed if total is None else total + summed
        inverse = 1.0 / jnp.sum(total, axis=0, keepdims=True)
        attn = dot_nn(value_t_ref[:, :span], prob_ref[:span, lanes]) * inverse
        for h in range(heads):
            attn_ref[h * HEAD_SIZE : (h + 1) * HEAD_SIZE, own] = attn[
                :, h * size : (h + 1) * size
            ].astype(jnp.bfloat16)
        grads_t = jnp.concatenate(
            [
                gathered_ref[
                    block * rows : (block + 1) * rows,
                    grad_base + h * HEAD_SIZE : grad_base + (h + 1) * HEAD_SIZE,
                ]
                for h in range(heads)
                for block in (2 * step, 2 * step + 1)
            ],
            axis=1,
        )
        grads_t = (grads_t.astype(jnp.float32) * inverse).astype(jnp.bfloat16)
        grad_t_ref[:, lanes] = grads_t
        delta_ref[:, lanes] = jnp.sum(grads_t.astype(jnp.float32) * attn, axis=0, keepdims=True)

    dq_t_ref[...] = jnp.zeros_like(dq_t_ref)
    dk_ref[...] = jnp.zeros_like(dk_ref)
    dv_ref[...] = jnp.zeros_like(dv_ref)
    for step in range(steps):
        key_step = jnp.minimum(chip, step)
        query_step = jnp.maximum(chip, step)
        dprob = dot_nn(
            gathered_ref[at(key_step, size), value_cols], grad_t_ref[:, at(query_step, wide)]
        )
        prob = prob_ref[at(key_step, size), at(query_step, wide)]
        dscore = (
            prob.astype(jnp.float32)
            * (dprob - delta_ref[:, at(query_step, wide)])
        ).astype(jnp.bfloat16)

        @pl.when(step <= chip)
        def _():
            dq_t_ref[...] += dot_nn(key_t_ref[:, at(key_step, size)], dscore)

        @pl.when(step >= chip)
        def _():
            dk_ref[...] += dot_nn(dscore, query_ref[at(query_step, wide)])
            dv_ref[...] += dot_nt(prob, grad_t_ref[:, at(query_step, wide)])

    for target, half in ((dx_far_ref, 1 - core), (dx_own_ref, core)):
        for h in range(heads):
            target[:, h * HEAD_SIZE : (h + 1) * HEAD_SIZE] = (
                (logit_scale * dq_t_ref[:, at(2 * h + half, rows)])
                .T.astype(jnp.bfloat16)
            )
        target[:, key_cols] = (logit_scale * dk_ref[at(half, rows)]).astype(jnp.bfloat16)
        target[:, value_cols] = dv_ref[at(half, rows)].astype(jnp.bfloat16)


def value_grad_kernel(prob_ref, grad_t_ref, dv_t_ref):
    size = 2 * HEAD_SIZE
    wide = QUERIES_PER_KEY * size
    for step in range(prob_ref.shape[0] // size):
        own = slice(step * size, (step + 1) * size)
        dv_t_ref[:, own] = dot_nt(grad_t_ref[:, step * wide :], prob_ref[own, step * wide :]).astype(
            jnp.bfloat16
        )


def input_terms_kernel(apart_groups, own_ref, far_ref, wq_ref, wk_ref, wv_ref, *refs):
    terms, dx_ref = refs[-1 - len(apart_groups) : -1], refs[-1]
    core = lax.axis_index("seq") % 2
    group = lax.axis_index("head")
    q_cols = wq_ref.shape[1] // 2
    kv_cols = wk_ref.shape[1] // 2
    for source, half in ((own_ref, core), (far_ref, 1 - core)):
        dx_ref[:, at(half, q_cols)] = source[:, :q_cols]
        dx_ref[:, pl.ds(pl.multiple_of(2 * q_cols + half * kv_cols, kv_cols), kv_cols)] = source[
            :, q_cols : q_cols + kv_cols
        ]
        dx_ref[
            :, pl.ds(pl.multiple_of(2 * q_cols + (2 + half) * kv_cols, kv_cols), kv_cols)
        ] = source[:, q_cols + kv_cols :]
    for apart, target in zip(apart_groups, terms):
        cut = target.shape[0]
        place = at(group ^ apart, cut)
        target[...] = (
            dot_nt(wq_ref[place], dx_ref[:, : 2 * q_cols])
            + dot_nt(wk_ref[place], dx_ref[:, 2 * q_cols : 2 * q_cols + 2 * kv_cols])
            + dot_nt(wv_ref[place], dx_ref[:, 2 * q_cols + 2 * kv_cols :])
        ).astype(target.dtype)


def weight_grad_kernel(attn_ref, dv_t_ref, got_ref, *refs):
    column_refs, refs = refs[:-6], refs[-6:]
    wvalue_ref, woutput_ref, done_ref, joined_ref, far_attn_ref, far_dv_ref = refs
    done_ref[...] = jnp.zeros_like(done_ref)
    me = lax.axis_index("seq")
    core = me % 2
    cut, rows = column_refs[0].shape[2:]
    for chip, ref in enumerate(column_refs):
        joined_ref[:, :, at(me ^ (2 * chip), rows)] = ref[0]
        for which in range(2):
            first = (2 * chip + which) * cut
            joined_ref[which, :, at(me ^ (2 * chip + 1), rows)] = got_ref[first : first + cut]
    first = 2 * len(column_refs) * cut
    for ref in (far_attn_ref, far_dv_ref):
        for block in range(ref.shape[1] // rows):
            ref[:, block * rows : (block + 1) * rows] = got_ref[first : first + ref.shape[0]]
            first += ref.shape[0]
    for half, attn, dv_t in ((core, attn_ref, dv_t_ref), (1 - core, far_attn_ref, far_dv_ref)):
        woutput_ref[:, at(half, attn.shape[0])] = dot_nt(joined_ref[1], attn[...])
        wvalue_ref[:, at(half, dv_t.shape[0])] = dot_nt(joined_ref[0], dv_t[...])


def add_kernel(own_ref, arrived_ref, _, sum_ref):
    total = own_ref[...].astype(jnp.float32) + arrived_ref[...].astype(jnp.float32)
    sum_ref[...] = total.astype(jnp.bfloat16)


def far_sum_kernel(_, own_ref, arrived_ref, sum_ref):
    sum_ref[...] = own_ref[...] + arrived_ref[...].astype(jnp.float32)


def sum_kernel(own_ref, *refs):
    total = own_ref[...]
    for arrived_ref in refs[:-1]:
        total = total + arrived_ref[...].astype(jnp.float32)
    refs[-1][...] = total.astype(jnp.bfloat16)


def kernel_call(
    body, outs, operands, in_vmem=(), scratch=(), flops=0, moved=0, room=16
):
    vmem = pl.BlockSpec(memory_space=pltpu.VMEM)
    hbm = pl.BlockSpec(memory_space=pltpu.HBM)
    return pl.pallas_call(
        body,
        out_shape=outs,
        in_specs=[vmem if place in in_vmem else hbm for place in range(len(operands))],
        out_specs=(vmem,) * len(outs),
        scratch_shapes=list(scratch),
        compiler_params=pltpu.CompilerParams(vmem_limit_bytes=int(room * 1024 * 1024)),
        cost_estimate=pl.CostEstimate(flops=flops, bytes_accessed=moved, transcendentals=0),
    )(*operands)


def swapped(value, axis, apart):
    count = lax.axis_size(axis)
    return lax.ppermute(value, axis, [(place, place ^ apart) for place in range(count)])


def gathered_plan(
    normed_input,
    stored_queries,
    stored_keys,
    stored_values,
    query_weight,
    key_matrix,
    value_matrix,
    output_weight,
    out_cotangent,
):
    bf16, f32 = jnp.bfloat16, jnp.float32
    rows, model = normed_input.shape
    blocks = lax.axis_size("seq")
    groups = lax.axis_size("head")
    tokens = rows * blocks
    q_cols = stored_queries.shape[1] // 2
    kv_cols = HEAD_SIZE
    wide = 2 * QUERIES_PER_KEY * rows
    packed_cols = 2 * q_cols + 2 * kv_cols
    pieces = model // (2 * HEAD_SIZE) if model % (2 * HEAD_SIZE) == 0 else 1
    shape = jax.ShapeDtypeStruct
    same, other = kernel_call(
        out_grad_kernel,
        (shape((rows, packed_cols), bf16),) * 2,
        (out_cotangent, output_weight, stored_queries, stored_keys, stored_values),
        scratch=(
            pltpu.VMEM(out_cotangent.shape, bf16),
            pltpu.VMEM(output_weight.shape, bf16),
            pltpu.SemaphoreType.DMA((6 + 3 * pieces,)),
        ),
        flops=4 * rows * model * q_cols,
        moved=2 * model * (rows + 2 * q_cols),
        room=62,
    )
    held = {0: same}
    for apart in range(2, blocks):
        lowest, highest = 2, 1 << (apart.bit_length() - 1)
        while not apart & lowest:
            lowest *= 2
        through = lowest if apart % 2 else highest
        if lowest == highest:
            held[apart] = swapped(other if apart % 2 else same, "seq", apart)
        else:
            held[apart] = swapped(held[apart ^ through], "seq", through)
    held[1] = swapped(other, "seq", 1)
    cut = model // blocks
    *columns, held[0] = kernel_call(
        turn_kernel,
        (shape((2, 2, cut, rows), bf16),) * (blocks // 2) + (shape(same.shape, bf16),),
        (normed_input, out_cotangent, same, held[2], held[blocks // 2 + 1]),
        in_vmem=range(3),
        scratch=(pltpu.VMEM((2, model, rows), bf16),),
        moved=8 * rows * model,
        room=8,
    )
    columns = [columns[0]] + [
        swapped(columns[chip], "seq", 2 * chip) for chip in range(1, blocks // 2)
    ]
    dx_own, dx_far, attn, prob, grad_t = kernel_call(
        functools.partial(attention_kernel, blocks),
        (
            shape((rows, q_cols + 2 * kv_cols), bf16),
            shape((rows, q_cols + 2 * kv_cols), bf16),
            shape((q_cols, tokens), bf16),
            shape((tokens, tokens * QUERIES_PER_KEY), bf16),
            shape((HEAD_SIZE, tokens * QUERIES_PER_KEY), bf16),
        ),
        [held[apart] for apart in range(blocks)],
        in_vmem=range(blocks),
        scratch=(
            pltpu.VMEM((tokens, packed_cols), bf16),
            pltpu.VMEM((tokens, wide), f32),
            pltpu.VMEM((tokens, wide), f32),
            pltpu.VMEM((1, tokens * QUERIES_PER_KEY), f32),
            pltpu.VMEM((tokens * QUERIES_PER_KEY, HEAD_SIZE), bf16),
            pltpu.VMEM((HEAD_SIZE, tokens), bf16),
            pltpu.VMEM((HEAD_SIZE, tokens), bf16),
            pltpu.VMEM((HEAD_SIZE, wide), f32),
            pltpu.VMEM((2 * rows, HEAD_SIZE), f32),
            pltpu.VMEM((2 * rows, HEAD_SIZE), f32),
        ),
        flops=8 * tokens * tokens * q_cols,
        moved=2 * tokens * packed_cols,
    )
    dx_got = swapped(dx_far, "seq", 1)
    def terms_of(chosen):
        return kernel_call(
            functools.partial(input_terms_kernel, chosen),
            tuple(shape((model // groups, rows), f32 if not apart else bf16) for apart in chosen),
            (dx_own, dx_got, query_weight, key_matrix, value_matrix),
            in_vmem=range(5),
            scratch=(pltpu.VMEM((rows, 2 * (q_cols + 2 * kv_cols)), bf16),),
            flops=2 * len(chosen) * rows * (model // groups) * 2 * (q_cols + 2 * kv_cols),
            moved=2 * len(chosen) * (model // groups) * 2 * (q_cols + 2 * kv_cols),
            room=4,
        )

    (far_term,) = terms_of((3,))
    pair_term, near_term, own_term = terms_of((2, 1, 0))
    (dv_t,) = kernel_call(
        value_grad_kernel,
        (shape((kv_cols, tokens), bf16),),
        (prob, grad_t),
        in_vmem=range(2),
        flops=tokens * tokens * q_cols,
        moved=2 * tokens * tokens * QUERIES_PER_KEY,
        room=4,
    )
    (pair_sum,) = kernel_call(
        add_kernel,
        (shape(pair_term.shape, bf16),),
        (pair_term, swapped(far_term, "head", 1), dv_t),
        in_vmem=range(2),
        room=4,
    )
    part_rows = q_cols + kv_cols
    (give,) = kernel_call(
        pass_on_kernel,
        (shape((blocks * (cut + part_rows), rows), bf16),),
        (pair_sum, attn, dv_t, *columns),
        in_vmem=range(1, 3 + blocks // 2),
        room=4,
    )
    grad_wvalue, grad_woutput, weights_done = kernel_call(
        weight_grad_kernel,
        (
            shape((model // blocks, 2 * kv_cols), f32),
            shape((model // blocks, 2 * q_cols), f32),
            shape((8, HEAD_SIZE), f32),
        ),
        (attn, dv_t, swapped(give, "seq", 1), *columns),
        in_vmem=range(3 + blocks // 2),
        scratch=(
            pltpu.VMEM((2, model // blocks, tokens), bf16),
            pltpu.VMEM((q_cols, tokens), bf16),
            pltpu.VMEM((kv_cols, tokens), bf16),
        ),
        room=8,
    )
    (far_sum,) = kernel_call(
        far_sum_kernel,
        (shape((model // groups, rows), f32),),
        (weights_done, own_term, swapped(pair_sum, "head", 2)),
        in_vmem=range(1, 3),
        moved=10 * rows * (model // groups),
        room=4,
    )
    (grad_input,) = kernel_call(
        sum_kernel,
        (shape((model // groups, rows), bf16),),
        (far_sum, swapped(near_term, "head", 1)),
        in_vmem=range(2),
        moved=4 * groups * (model // groups) * rows,
    )
    return (grad_input.T, grad_wvalue, grad_woutput.T)


def power_of_two(count):
    return count & (count - 1) == 0


def local(normed_input, stored_queries, stored_keys, *others):
    blocks, groups = lax.axis_size("seq"), lax.axis_size("head")
    whole_window = normed_input.shape[0] * blocks <= WINDOW_LENGTH
    two_heads = stored_keys.shape[1] == 2 * HEAD_SIZE
    paired = blocks >= 4 and power_of_two(blocks) and groups == 4
    plan = gathered_plan if whole_window and two_heads and paired else windowed_plan
    return plan(normed_input, stored_queries, stored_keys, *others)


def windowed_plan(
    normed_input,
    stored_queries,
    stored_keys,
    stored_values,
    query_weight,
    key_matrix,
    value_matrix,
    output_weight,
    out_cotangent,
):
    tok_rows = normed_input.shape[0]
    blocks_seq = lax.axis_size("seq")
    seq_place = lax.axis_index("seq")
    reach_blocks = min(WINDOW_LENGTH // tok_rows, blocks_seq - 1)
    kv_heads = stored_keys.shape[1] // HEAD_SIZE
    output_gradient = jnp.dot(
        out_cotangent, output_weight.T, preferred_element_type=jnp.float32
    ).astype(jnp.bfloat16)
    pieces = [(stored_keys, stored_values)]
    current = (stored_keys, stored_values)
    for relay_step in range(reach_blocks):
        current = passed_along((current[0], current[1]), "seq", 1)
        pieces = [current] + pieces
    key_window = jnp.concatenate([piece[0] for piece in pieces], axis=0)
    value_window = jnp.concatenate([piece[1] for piece in pieces], axis=0)
    key_span = key_window.shape[0]
    query_pos = seq_place * tok_rows + jnp.arange(tok_rows, dtype=jnp.int32)
    key_pos = (seq_place - reach_blocks) * tok_rows + jnp.arange(key_span, dtype=jnp.int32)
    pos_gap = query_pos[:, None] - key_pos[None, :]
    allowed = (pos_gap >= 0) & (pos_gap < WINDOW_LENGTH) & (key_pos >= 0)[None, :]
    allowed_rows = jnp.tile(allowed, (QUERIES_PER_KEY, 1))
    query_stack = (
        stored_queries.reshape(tok_rows, kv_heads, QUERIES_PER_KEY, HEAD_SIZE)
        .transpose(1, 2, 0, 3)
        .reshape(kv_heads, QUERIES_PER_KEY * tok_rows, HEAD_SIZE)
    )
    grad_stack = (
        output_gradient.reshape(tok_rows, kv_heads, QUERIES_PER_KEY, HEAD_SIZE)
        .transpose(1, 2, 0, 3)
        .reshape(kv_heads, QUERIES_PER_KEY * tok_rows, HEAD_SIZE)
    )
    key_stack = key_window.reshape(key_span, kv_heads, HEAD_SIZE).transpose(1, 0, 2)
    value_stack = value_window.reshape(key_span, kv_heads, HEAD_SIZE).transpose(1, 0, 2)

    def per_head(head_items):
        query_head, key_head, value_head, grad_head = head_items
        attention_logits = logit_scale * jnp.dot(
            query_head, key_head.T, preferred_element_type=jnp.float32
        )
        masked = jnp.where(allowed_rows, attention_logits, -jnp.inf)
        row_top = jnp.max(masked, axis=1, keepdims=True)
        exp_scores = jnp.exp(masked - row_top)
        attn_prob = exp_scores / jnp.sum(exp_scores, axis=1, keepdims=True)
        probability_halfwidth = attn_prob.astype(jnp.bfloat16)
        attn_head = jnp.dot(
            probability_halfwidth, value_head, preferred_element_type=jnp.float32
        ).astype(jnp.bfloat16)
        row_delta = jnp.sum(
            grad_head.astype(jnp.float32) * attn_head.astype(jnp.float32), axis=1, keepdims=True
        )
        probability_gradient = jnp.dot(grad_head, value_head.T, preferred_element_type=jnp.float32)
        score_gradient = (attn_prob * (probability_gradient - row_delta)).astype(jnp.bfloat16)
        qgrad_head = (
            logit_scale * jnp.dot(score_gradient, key_head, preferred_element_type=jnp.float32)
        ).astype(jnp.bfloat16)
        key_partial = logit_scale * jnp.dot(
            score_gradient.T, query_head, preferred_element_type=jnp.float32
        )
        value_partial = jnp.dot(
            probability_halfwidth.T, grad_head, preferred_element_type=jnp.float32
        )
        return (attn_head, qgrad_head, key_partial, value_partial)

    attn_all, qgrad_all, key_all, value_all = lax.map(
        per_head, (query_stack, key_stack, value_stack, grad_stack)
    )
    attention_output = (
        attn_all.reshape(kv_heads, QUERIES_PER_KEY, tok_rows, HEAD_SIZE)
        .transpose(2, 0, 1, 3)
        .reshape(tok_rows, kv_heads * QUERIES_PER_KEY * HEAD_SIZE)
    )
    query_gradient = (
        qgrad_all.reshape(kv_heads, QUERIES_PER_KEY, tok_rows, HEAD_SIZE)
        .transpose(2, 0, 1, 3)
        .reshape(tok_rows, kv_heads * QUERIES_PER_KEY * HEAD_SIZE)
    )
    key_terms = key_all.transpose(1, 0, 2).reshape(key_span, kv_heads * HEAD_SIZE)
    value_terms = value_all.transpose(1, 0, 2).reshape(key_span, kv_heads * HEAD_SIZE)

    def take_slot(terms, slot_index):
        return terms[slot_index * tok_rows : (slot_index + 1) * tok_rows]

    key_sum = take_slot(key_terms, reach_blocks)
    value_sum = take_slot(value_terms, reach_blocks)
    for distance in range(1, reach_blocks + 1):
        received = passed_along(
            (
                take_slot(key_terms, reach_blocks - distance),
                take_slot(value_terms, reach_blocks - distance),
            ),
            "seq",
            -distance,
        )
        key_sum = key_sum + received[0]
        value_sum = value_sum + received[1]
    grad_key = key_sum.astype(jnp.bfloat16)
    grad_value = value_sum.astype(jnp.bfloat16)
    input_terms = jnp.dot(query_gradient, query_weight.T, preferred_element_type=jnp.float32)
    input_terms = input_terms + jnp.dot(grad_key, key_matrix.T, preferred_element_type=jnp.float32)
    input_terms = input_terms + jnp.dot(
        grad_value, value_matrix.T, preferred_element_type=jnp.float32
    )
    grad_input = lax.psum_scatter(input_terms, "head", scatter_dimension=1, tiled=True).astype(
        jnp.bfloat16
    )
    value_cols = grad_value.shape[1]
    input_cols = normed_input.T
    cot_cols = out_cotangent.T
    gathered = lax.psum_scatter(
        jnp.concatenate(
            [
                jnp.dot(input_cols, grad_value, preferred_element_type=jnp.float32),
                jnp.dot(cot_cols, attention_output, preferred_element_type=jnp.float32),
            ],
            axis=1,
        ),
        "seq",
        scatter_dimension=0,
        tiled=True,
    )
    grad_wvalue = gathered[:, :value_cols]
    grad_woutput = gathered[:, value_cols:].T
    return (grad_input, grad_wvalue, grad_woutput)


def solution(mesh):
    placed = (
        P("seq", None),
        P("seq", "head"),
        P("seq", "head"),
        P("seq", "head"),
        P(None, "head"),
        P(None, "head"),
        P(None, "head"),
        P("head", None),
        P("seq", None),
    )
    return jax.shard_map(
        local,
        mesh=mesh,
        in_specs=placed,
        out_specs=(P("seq", "head"), P("seq", "head"), P("head", "seq")),
        check_vma=False,
    )
```

```python
import functools

import jax
import jax.numpy as jnp
from jax import lax
from jax.experimental import pallas as pl
from jax.experimental.pallas import tpu as pltpu
from jax.sharding import PartitionSpec as P

HEAD_SIZE = 128
WINDOW_LENGTH = 4096
QUERIES_PER_KEY = 2


logit_scale = 1.0 / 12.0
log2_scale = 1.4426950408889634 / 12.0
excluded = -1e30


def passed_along(value, axis, steps):
    count = lax.axis_size(axis)
    leading, last = (max(0, -steps), min(count, count - steps))
    return lax.ppermute(value, axis, [(source, source + steps) for source in range(leading, last)])


NT = (((1,), (1,)), ((), ()))


def dot_nt(left, right):
    return lax.dot_general(left, right, NT, preferred_element_type=jnp.float32)


def dot_nn(left, right):
    return jnp.dot(left, right, preferred_element_type=jnp.float32)


def at(place, size):
    return pl.ds(pl.multiple_of(place * size, size), size)


def out_grad_kernel(
    cot_hbm, weight_hbm, q_hbm, k_hbm, v_hbm, same_ref, other_ref, cot_ref, weight_ref, sem
):
    core = lax.axis_index("seq") % 2
    halves = ((other_ref, 1 - core), (same_ref, core))
    rows = weight_ref.shape[0] // 2
    pieces = (sem.shape[0] - 6) // 3
    cut = weight_ref.shape[1] // pieces
    model_copies = []
    for piece in range(pieces):
        part = pl.ds(piece * cut, cut)
        model_copies.append(
            [
                pltpu.make_async_copy(
                    cot_hbm.at[:, part], cot_ref.at[:, part], sem.at[6 + 3 * piece]
                )
            ]
        )
        for place, (_, half) in enumerate(halves):
            model_copies[-1].append(
                pltpu.make_async_copy(
                    weight_hbm.at[at(half, rows), part],
                    weight_ref.at[pl.ds(place * rows, rows), part],
                    sem.at[7 + 3 * piece + place],
                )
            )
        for copy in model_copies[-1]:
            copy.start()
    plain_copies = []
    for place, (target, half) in enumerate(halves):
        first = 0
        for which, source in enumerate((q_hbm, k_hbm, v_hbm)):
            cols = source.shape[1] // 2
            plain_copies.append(
                pltpu.make_async_copy(
                    source.at[:, at(half, cols)],
                    target.at[:, pl.ds(first, cols)],
                    sem.at[3 * place + which],
                )
            )
            plain_copies[-1].start()
            first += cols
    total = None
    for piece in range(pieces):
        for copy in model_copies[piece]:
            copy.wait()
        part = slice(piece * cut, (piece + 1) * cut)
        product = dot_nt(cot_ref[:, part], weight_ref[:, part])
        total = product if total is None else total + product
    for place, (target, _) in enumerate(halves):
        for head in range(rows // HEAD_SIZE):
            row = place * rows + head * HEAD_SIZE
            target[:, first + head * HEAD_SIZE : first + (head + 1) * HEAD_SIZE] = total[
                :, row : row + HEAD_SIZE
            ].T.astype(jnp.bfloat16)
    for copy in plain_copies:
        copy.wait()


def turn_kernel(normed_ref, cot_ref, block_ref, _, __, *refs):
    *column_refs, own_ref, turned_ref = refs
    me = lax.axis_index("seq")
    cut = column_refs[0].shape[2]
    own_ref[...] = block_ref[...]
    for which, ref in enumerate((normed_ref, cot_ref)):
        turned_ref[which] = ref[...].astype(jnp.float32).T.astype(jnp.bfloat16)
        for chip, target in enumerate(column_refs):
            for far in range(2):
                target[far, which] = turned_ref[which, at(me ^ (2 * chip + far), cut)]


def pass_on_kernel(_, attn_ref, dv_t_ref, *refs):
    *column_refs, give_ref = refs
    cut, rows = column_refs[0].shape[2:]
    for chip, ref in enumerate(column_refs):
        for which in range(2):
            first = (2 * chip + which) * cut
            give_ref[first : first + cut] = ref[1, which]
    first = 2 * len(column_refs) * cut
    for ref in (attn_ref, dv_t_ref):
        for block in range(ref.shape[1] // rows):
            give_ref[first : first + ref.shape[0]] = ref[:, block * rows : (block + 1) * rows]
            first += ref.shape[0]


def attention_kernel(blocks, *refs):
    attention_body(refs[:blocks], *refs[blocks:])


def attention_body(
    block_refs,
    dx_own_ref,
    dx_far_ref,
    attn_ref,
    prob_ref,
    grad_t_ref,
    gathered_ref,
    score_even_ref,
    score_odd_ref,
    delta_ref,
    query_ref,
    value_t_ref,
    key_t_ref,
    dq_t_ref,
    dk_ref,
    dv_ref,
):
    me = lax.axis_index("seq")
    core, chip = me % 2, me // 2
    rows = dx_own_ref.shape[0]
    for apart, source in enumerate(block_refs):
        gathered_ref[at(me ^ apart, rows)] = source[...]
    tokens = gathered_ref.shape[0]
    size = 2 * rows
    steps = tokens // size
    wide = QUERIES_PER_KEY * size
    heads = QUERIES_PER_KEY
    key_cols = slice(heads * HEAD_SIZE, (heads + 1) * HEAD_SIZE)
    value_cols = slice((heads + 1) * HEAD_SIZE, (heads + 2) * HEAD_SIZE)
    grad_base = (heads + 2) * HEAD_SIZE
    value_t_ref[...] = gathered_ref[:, value_cols].T
    key_t_ref[...] = gathered_ref[:, key_cols].T
    key_place = lax.broadcasted_iota(jnp.int32, (size, wide), 0)
    query_place = lax.broadcasted_iota(jnp.int32, (size, wide), 1) % size
    allowed = key_place <= query_place

    def scored(step):
        own = slice(step * size, (step + 1) * size)
        score_ref = score_odd_ref if step % 2 else score_even_ref
        queries = jnp.concatenate(
            [gathered_ref[own, h * HEAD_SIZE : (h + 1) * HEAD_SIZE] for h in range(heads)], axis=0
        )
        query_ref[step * wide : (step + 1) * wide] = queries
        top = None
        for piece in range(step + 1):
            part = slice(piece * size, (piece + 1) * size)
            scores = dot_nt(gathered_ref[part, key_cols], queries)
            if piece == step:
                scores = jnp.where(allowed, scores, excluded)
            score_ref[part] = scores
            largest = jnp.max(scores.reshape(size // 8, 8, wide), axis=0)
            top = largest if top is None else jnp.maximum(top, largest)
        return top

    next_top = scored(steps - 1)
    for step in range(steps - 1, -1, -1):
        span = (step + 1) * size
        own = slice(step * size, span)
        lanes = slice(step * wide, (step + 1) * wide)
        score_ref = score_odd_ref if step % 2 else score_even_ref
        top = next_top
        if step:
            next_top = scored(step - 1)
        top = jnp.max(top, axis=0, keepdims=True)
        total = None
        for piece in range(step + 1):
            part = slice(piece * size, (piece + 1) * size)
            weights = jnp.exp2((score_ref[part] - top) * log2_scale)
            prob_ref[part, lanes] = weights.astype(jnp.bfloat16)
            summed = jnp.sum(weights.reshape(size // 8, 8, wide), axis=0)
            total = summed if total is None else total + summed
        inverse = 1.0 / jnp.sum(total, axis=0, keepdims=True)
        attn = dot_nn(value_t_ref[:, :span], prob_ref[:span, lanes]) * inverse
        for h in range(heads):
            attn_ref[h * HEAD_SIZE : (h + 1) * HEAD_SIZE, own] = attn[
                :, h * size : (h + 1) * size
            ].astype(jnp.bfloat16)
        grads_t = jnp.concatenate(
            [
                gathered_ref[
                    block * rows : (block + 1) * rows,
                    grad_base + h * HEAD_SIZE : grad_base + (h + 1) * HEAD_SIZE,
                ]
                for h in range(heads)
                for block in (2 * step, 2 * step + 1)
            ],
            axis=1,
        )
        grads_t = (grads_t.astype(jnp.float32) * inverse).astype(jnp.bfloat16)
        grad_t_ref[:, lanes] = grads_t
        delta_ref[:, lanes] = jnp.sum(grads_t.astype(jnp.float32) * attn, axis=0, keepdims=True)

    dq_t_ref[...] = jnp.zeros_like(dq_t_ref)
    dk_ref[...] = jnp.zeros_like(dk_ref)
    dv_ref[...] = jnp.zeros_like(dv_ref)
    for step in range(steps):
        key_step = jnp.minimum(chip, step)
        query_step = jnp.maximum(chip, step)
        dprob = dot_nn(
            gathered_ref[at(key_step, size), value_cols], grad_t_ref[:, at(query_step, wide)]
        )
        prob = prob_ref[at(key_step, size), at(query_step, wide)]
        dscore = (
            prob.astype(jnp.float32)
            * (dprob - delta_ref[:, at(query_step, wide)])
        ).astype(jnp.bfloat16)

        @pl.when(step <= chip)
        def _():
            dq_t_ref[...] += dot_nn(key_t_ref[:, at(key_step, size)], dscore)

        @pl.when(step >= chip)
        def _():
            dk_ref[...] += dot_nn(dscore, query_ref[at(query_step, wide)])
            dv_ref[...] += dot_nt(prob, grad_t_ref[:, at(query_step, wide)])

    for target, half in ((dx_far_ref, 1 - core), (dx_own_ref, core)):
        for h in range(heads):
            target[:, h * HEAD_SIZE : (h + 1) * HEAD_SIZE] = (
                (logit_scale * dq_t_ref[:, at(2 * h + half, rows)])
                .T.astype(jnp.bfloat16)
            )
        target[:, key_cols] = (logit_scale * dk_ref[at(half, rows)]).astype(jnp.bfloat16)
        target[:, value_cols] = dv_ref[at(half, rows)].astype(jnp.bfloat16)


def value_grad_kernel(prob_ref, grad_t_ref, dv_t_ref):
    size = 2 * HEAD_SIZE
    wide = QUERIES_PER_KEY * size
    for step in range(prob_ref.shape[0] // size):
        own = slice(step * size, (step + 1) * size)
        dv_t_ref[:, own] = dot_nt(grad_t_ref[:, step * wide :], prob_ref[own, step * wide :]).astype(
            jnp.bfloat16
        )


def input_terms_kernel(apart_groups, own_ref, far_ref, wq_ref, wk_ref, wv_ref, *refs):
    terms, dx_ref = refs[-1 - len(apart_groups) : -1], refs[-1]
    core = lax.axis_index("seq") % 2
    group = lax.axis_index("head")
    q_cols = wq_ref.shape[1] // 2
    kv_cols = wk_ref.shape[1] // 2
    for source, half in ((own_ref, core), (far_ref, 1 - core)):
        dx_ref[:, at(half, q_cols)] = source[:, :q_cols]
        dx_ref[:, pl.ds(pl.multiple_of(2 * q_cols + half * kv_cols, kv_cols), kv_cols)] = source[
            :, q_cols : q_cols + kv_cols
        ]
        dx_ref[
            :, pl.ds(pl.multiple_of(2 * q_cols + (2 + half) * kv_cols, kv_cols), kv_cols)
        ] = source[:, q_cols + kv_cols :]
    for apart, target in zip(apart_groups, terms):
        cut = target.shape[0]
        place = at(group ^ apart, cut)
        target[...] = (
            dot_nt(wq_ref[place], dx_ref[:, : 2 * q_cols])
            + dot_nt(wk_ref[place], dx_ref[:, 2 * q_cols : 2 * q_cols + 2 * kv_cols])
            + dot_nt(wv_ref[place], dx_ref[:, 2 * q_cols + 2 * kv_cols :])
        ).astype(target.dtype)


def weight_grad_kernel(attn_ref, dv_t_ref, got_ref, *refs):
    column_refs, refs = refs[:-6], refs[-6:]
    wvalue_ref, woutput_ref, done_ref, joined_ref, far_attn_ref, far_dv_ref = refs
    done_ref[...] = jnp.zeros_like(done_ref)
    me = lax.axis_index("seq")
    core = me % 2
    cut, rows = column_refs[0].shape[2:]
    for chip, ref in enumerate(column_refs):
        joined_ref[:, :, at(me ^ (2 * chip), rows)] = ref[0]
        for which in range(2):
            first = (2 * chip + which) * cut
            joined_ref[which, :, at(me ^ (2 * chip + 1), rows)] = got_ref[first : first + cut]
    first = 2 * len(column_refs) * cut
    for ref in (far_attn_ref, far_dv_ref):
        for block in range(ref.shape[1] // rows):
            ref[:, block * rows : (block + 1) * rows] = got_ref[first : first + ref.shape[0]]
            first += ref.shape[0]
    for half, attn, dv_t in ((core, attn_ref, dv_t_ref), (1 - core, far_attn_ref, far_dv_ref)):
        woutput_ref[:, at(half, attn.shape[0])] = dot_nt(joined_ref[1], attn[...])
        wvalue_ref[:, at(half, dv_t.shape[0])] = dot_nt(joined_ref[0], dv_t[...])


def add_kernel(own_ref, arrived_ref, _, sum_ref):
    total = own_ref[...].astype(jnp.float32) + arrived_ref[...].astype(jnp.float32)
    sum_ref[...] = total.astype(jnp.bfloat16)


def far_sum_kernel(_, own_ref, arrived_ref, sum_ref):
    sum_ref[...] = own_ref[...] + arrived_ref[...].astype(jnp.float32)


def sum_kernel(own_ref, *refs):
    total = own_ref[...]
    for arrived_ref in refs[:-1]:
        total = total + arrived_ref[...].astype(jnp.float32)
    refs[-1][...] = total.astype(jnp.bfloat16)


def kernel_call(
    body, outs, operands, in_vmem=(), scratch=(), flops=0, moved=0, room=16
):
    vmem = pl.BlockSpec(memory_space=pltpu.VMEM)
    hbm = pl.BlockSpec(memory_space=pltpu.HBM)
    return pl.pallas_call(
        body,
        out_shape=outs,
        in_specs=[vmem if place in in_vmem else hbm for place in range(len(operands))],
        out_specs=(vmem,) * len(outs),
        scratch_shapes=list(scratch),
        compiler_params=pltpu.CompilerParams(vmem_limit_bytes=int(room * 1024 * 1024)),
        cost_estimate=pl.CostEstimate(flops=flops, bytes_accessed=moved, transcendentals=0),
    )(*operands)


def swapped(value, axis, apart):
    count = lax.axis_size(axis)
    return lax.ppermute(value, axis, [(place, place ^ apart) for place in range(count)])


def gathered_plan(
    normed_input,
    stored_queries,
    stored_keys,
    stored_values,
    query_weight,
    key_matrix,
    value_matrix,
    output_weight,
    out_cotangent,
):
    bf16, f32 = jnp.bfloat16, jnp.float32
    rows, model = normed_input.shape
    blocks = lax.axis_size("seq")
    groups = lax.axis_size("head")
    tokens = rows * blocks
    q_cols = stored_queries.shape[1] // 2
    kv_cols = HEAD_SIZE
    wide = 2 * QUERIES_PER_KEY * rows
    packed_cols = 2 * q_cols + 2 * kv_cols
    pieces = 3 if model % (6 * HEAD_SIZE) == 0 else 1
    shape = jax.ShapeDtypeStruct
    same, other = kernel_call(
        out_grad_kernel,
        (shape((rows, packed_cols), bf16),) * 2,
        (out_cotangent, output_weight, stored_queries, stored_keys, stored_values),
        scratch=(
            pltpu.VMEM(out_cotangent.shape, bf16),
            pltpu.VMEM(output_weight.shape, bf16),
            pltpu.SemaphoreType.DMA((6 + 3 * pieces,)),
        ),
        flops=4 * rows * model * q_cols,
        moved=2 * model * (rows + 2 * q_cols),
        room=63,
    )
    held = {0: same}
    for apart in range(2, blocks):
        lowest, highest = 2, 1 << (apart.bit_length() - 1)
        while not apart & lowest:
            lowest *= 2
        through = lowest if apart % 2 else highest
        if lowest == highest:
            held[apart] = swapped(other if apart % 2 else same, "seq", apart)
        else:
            held[apart] = swapped(held[apart ^ through], "seq", through)
    held[1] = swapped(other, "seq", 1)
    cut = model // blocks
    *columns, held[0] = kernel_call(
        turn_kernel,
        (shape((2, 2, cut, rows), bf16),) * (blocks // 2) + (shape(same.shape, bf16),),
        (normed_input, out_cotangent, same, held[2], held[blocks // 2 + 1]),
        in_vmem=range(3),
        scratch=(pltpu.VMEM((2, model, rows), bf16),),
        moved=8 * rows * model,
        room=8,
    )
    columns = [columns[0]] + [
        swapped(columns[chip], "seq", 2 * chip) for chip in range(1, blocks // 2)
    ]
    dx_own, dx_far, attn, prob, grad_t = kernel_call(
        functools.partial(attention_kernel, blocks),
        (
            shape((rows, q_cols + 2 * kv_cols), bf16),
            shape((rows, q_cols + 2 * kv_cols), bf16),
            shape((q_cols, tokens), bf16),
            shape((tokens, tokens * QUERIES_PER_KEY), bf16),
            shape((HEAD_SIZE, tokens * QUERIES_PER_KEY), bf16),
        ),
        [held[apart] for apart in range(blocks)],
        in_vmem=range(blocks),
        scratch=(
            pltpu.VMEM((tokens, packed_cols), bf16),
            pltpu.VMEM((tokens, wide), f32),
            pltpu.VMEM((tokens, wide), f32),
            pltpu.VMEM((1, tokens * QUERIES_PER_KEY), f32),
            pltpu.VMEM((tokens * QUERIES_PER_KEY, HEAD_SIZE), bf16),
            pltpu.VMEM((HEAD_SIZE, tokens), bf16),
            pltpu.VMEM((HEAD_SIZE, tokens), bf16),
            pltpu.VMEM((HEAD_SIZE, wide), f32),
            pltpu.VMEM((2 * rows, HEAD_SIZE), f32),
            pltpu.VMEM((2 * rows, HEAD_SIZE), f32),
        ),
        flops=8 * tokens * tokens * q_cols,
        moved=2 * tokens * packed_cols,
    )
    dx_got = swapped(dx_far, "seq", 1)
    def terms_of(chosen):
        return kernel_call(
            functools.partial(input_terms_kernel, chosen),
            tuple(shape((model // groups, rows), f32 if not apart else bf16) for apart in chosen),
            (dx_own, dx_got, query_weight, key_matrix, value_matrix),
            in_vmem=range(5),
            scratch=(pltpu.VMEM((rows, 2 * (q_cols + 2 * kv_cols)), bf16),),
            flops=2 * len(chosen) * rows * (model // groups) * 2 * (q_cols + 2 * kv_cols),
            moved=2 * len(chosen) * (model // groups) * 2 * (q_cols + 2 * kv_cols),
            room=4,
        )

    (far_term,) = terms_of((3,))
    pair_term, near_term, own_term = terms_of((2, 1, 0))
    (dv_t,) = kernel_call(
        value_grad_kernel,
        (shape((kv_cols, tokens), bf16),),
        (prob, grad_t),
        in_vmem=range(2),
        flops=tokens * tokens * q_cols,
        moved=2 * tokens * tokens * QUERIES_PER_KEY,
        room=4,
    )
    (pair_sum,) = kernel_call(
        add_kernel,
        (shape(pair_term.shape, bf16),),
        (pair_term, swapped(far_term, "head", 1), dv_t),
        in_vmem=range(2),
        room=4,
    )
    part_rows = q_cols + kv_cols
    (give,) = kernel_call(
        pass_on_kernel,
        (shape((blocks * (cut + part_rows), rows), bf16),),
        (pair_sum, attn, dv_t, *columns),
        in_vmem=range(1, 3 + blocks // 2),
        room=4,
    )
    grad_wvalue, grad_woutput, weights_done = kernel_call(
        weight_grad_kernel,
        (
            shape((model // blocks, 2 * kv_cols), f32),
            shape((model // blocks, 2 * q_cols), f32),
            shape((8, HEAD_SIZE), f32),
        ),
        (attn, dv_t, swapped(give, "seq", 1), *columns),
        in_vmem=range(3 + blocks // 2),
        scratch=(
            pltpu.VMEM((2, model // blocks, tokens), bf16),
            pltpu.VMEM((q_cols, tokens), bf16),
            pltpu.VMEM((kv_cols, tokens), bf16),
        ),
        room=8,
    )
    (far_sum,) = kernel_call(
        far_sum_kernel,
        (shape((model // groups, rows), f32),),
        (weights_done, own_term, swapped(pair_sum, "head", 2)),
        in_vmem=range(1, 3),
        moved=10 * rows * (model // groups),
        room=4,
    )
    (grad_input,) = kernel_call(
        sum_kernel,
        (shape((model // groups, rows), bf16),),
        (far_sum, swapped(near_term, "head", 1)),
        in_vmem=range(2),
        moved=4 * groups * (model // groups) * rows,
    )
    return (grad_input.T, grad_wvalue, grad_woutput.T)


def power_of_two(count):
    return count & (count - 1) == 0


def local(normed_input, stored_queries, stored_keys, *others):
    blocks, groups = lax.axis_size("seq"), lax.axis_size("head")
    whole_window = normed_input.shape[0] * blocks <= WINDOW_LENGTH
    two_heads = stored_keys.shape[1] == 2 * HEAD_SIZE
    paired = blocks >= 4 and power_of_two(blocks) and groups == 4
    plan = gathered_plan if whole_window and two_heads and paired else windowed_plan
    return plan(normed_input, stored_queries, stored_keys, *others)


def windowed_plan(
    normed_input,
    stored_queries,
    stored_keys,
    stored_values,
    query_weight,
    key_matrix,
    value_matrix,
    output_weight,
    out_cotangent,
):
    tok_rows = normed_input.shape[0]
    blocks_seq = lax.axis_size("seq")
    seq_place = lax.axis_index("seq")
    reach_blocks = min(WINDOW_LENGTH // tok_rows, blocks_seq - 1)
    kv_heads = stored_keys.shape[1] // HEAD_SIZE
    output_gradient = jnp.dot(
        out_cotangent, output_weight.T, preferred_element_type=jnp.float32
    ).astype(jnp.bfloat16)
    pieces = [(stored_keys, stored_values)]
    current = (stored_keys, stored_values)
    for relay_step in range(reach_blocks):
        current = passed_along((current[0], current[1]), "seq", 1)
        pieces = [current] + pieces
    key_window = jnp.concatenate([piece[0] for piece in pieces], axis=0)
    value_window = jnp.concatenate([piece[1] for piece in pieces], axis=0)
    key_span = key_window.shape[0]
    query_pos = seq_place * tok_rows + jnp.arange(tok_rows, dtype=jnp.int32)
    key_pos = (seq_place - reach_blocks) * tok_rows + jnp.arange(key_span, dtype=jnp.int32)
    pos_gap = query_pos[:, None] - key_pos[None, :]
    allowed = (pos_gap >= 0) & (pos_gap < WINDOW_LENGTH) & (key_pos >= 0)[None, :]
    allowed_rows = jnp.tile(allowed, (QUERIES_PER_KEY, 1))
    query_stack = (
        stored_queries.reshape(tok_rows, kv_heads, QUERIES_PER_KEY, HEAD_SIZE)
        .transpose(1, 2, 0, 3)
        .reshape(kv_heads, QUERIES_PER_KEY * tok_rows, HEAD_SIZE)
    )
    grad_stack = (
        output_gradient.reshape(tok_rows, kv_heads, QUERIES_PER_KEY, HEAD_SIZE)
        .transpose(1, 2, 0, 3)
        .reshape(kv_heads, QUERIES_PER_KEY * tok_rows, HEAD_SIZE)
    )
    key_stack = key_window.reshape(key_span, kv_heads, HEAD_SIZE).transpose(1, 0, 2)
    value_stack = value_window.reshape(key_span, kv_heads, HEAD_SIZE).transpose(1, 0, 2)

    def per_head(head_items):
        query_head, key_head, value_head, grad_head = head_items
        attention_logits = logit_scale * jnp.dot(
            query_head, key_head.T, preferred_element_type=jnp.float32
        )
        masked = jnp.where(allowed_rows, attention_logits, -jnp.inf)
        row_top = jnp.max(masked, axis=1, keepdims=True)
        exp_scores = jnp.exp(masked - row_top)
        attn_prob = exp_scores / jnp.sum(exp_scores, axis=1, keepdims=True)
        probability_halfwidth = attn_prob.astype(jnp.bfloat16)
        attn_head = jnp.dot(
            probability_halfwidth, value_head, preferred_element_type=jnp.float32
        ).astype(jnp.bfloat16)
        row_delta = jnp.sum(
            grad_head.astype(jnp.float32) * attn_head.astype(jnp.float32), axis=1, keepdims=True
        )
        probability_gradient = jnp.dot(grad_head, value_head.T, preferred_element_type=jnp.float32)
        score_gradient = (attn_prob * (probability_gradient - row_delta)).astype(jnp.bfloat16)
        qgrad_head = (
            logit_scale * jnp.dot(score_gradient, key_head, preferred_element_type=jnp.float32)
        ).astype(jnp.bfloat16)
        key_partial = logit_scale * jnp.dot(
            score_gradient.T, query_head, preferred_element_type=jnp.float32
        )
        value_partial = jnp.dot(
            probability_halfwidth.T, grad_head, preferred_element_type=jnp.float32
        )
        return (attn_head, qgrad_head, key_partial, value_partial)

    attn_all, qgrad_all, key_all, value_all = lax.map(
        per_head, (query_stack, key_stack, value_stack, grad_stack)
    )
    attention_output = (
        attn_all.reshape(kv_heads, QUERIES_PER_KEY, tok_rows, HEAD_SIZE)
        .transpose(2, 0, 1, 3)
        .reshape(tok_rows, kv_heads * QUERIES_PER_KEY * HEAD_SIZE)
    )
    query_gradient = (
        qgrad_all.reshape(kv_heads, QUERIES_PER_KEY, tok_rows, HEAD_SIZE)
        .transpose(2, 0, 1, 3)
        .reshape(tok_rows, kv_heads * QUERIES_PER_KEY * HEAD_SIZE)
    )
    key_terms = key_all.transpose(1, 0, 2).reshape(key_span, kv_heads * HEAD_SIZE)
    value_terms = value_all.transpose(1, 0, 2).reshape(key_span, kv_heads * HEAD_SIZE)

    def take_slot(terms, slot_index):
        return terms[slot_index * tok_rows : (slot_index + 1) * tok_rows]

    key_sum = take_slot(key_terms, reach_blocks)
    value_sum = take_slot(value_terms, reach_blocks)
    for distance in range(1, reach_blocks + 1):
        received = passed_along(
            (
                take_slot(key_terms, reach_blocks - distance),
                take_slot(value_terms, reach_blocks - distance),
            ),
            "seq",
            -distance,
        )
        key_sum = key_sum + received[0]
        value_sum = value_sum + received[1]
    grad_key = key_sum.astype(jnp.bfloat16)
    grad_value = value_sum.astype(jnp.bfloat16)
    input_terms = jnp.dot(query_gradient, query_weight.T, preferred_element_type=jnp.float32)
    input_terms = input_terms + jnp.dot(grad_key, key_matrix.T, preferred_element_type=jnp.float32)
    input_terms = input_terms + jnp.dot(
        grad_value, value_matrix.T, preferred_element_type=jnp.float32
    )
    grad_input = lax.psum_scatter(input_terms, "head", scatter_dimension=1, tiled=True).astype(
        jnp.bfloat16
    )
    value_cols = grad_value.shape[1]
    input_cols = normed_input.T
    cot_cols = out_cotangent.T
    gathered = lax.psum_scatter(
        jnp.concatenate(
            [
                jnp.dot(input_cols, grad_value, preferred_element_type=jnp.float32),
                jnp.dot(cot_cols, attention_output, preferred_element_type=jnp.float32),
            ],
            axis=1,
        ),
        "seq",
        scatter_dimension=0,
        tiled=True,
    )
    grad_wvalue = gathered[:, :value_cols]
    grad_woutput = gathered[:, value_cols:].T
    return (grad_input, grad_wvalue, grad_woutput)


def solution(mesh):
    placed = (
        P("seq", None),
        P("seq", "head"),
        P("seq", "head"),
        P("seq", "head"),
        P(None, "head"),
        P(None, "head"),
        P(None, "head"),
        P("head", None),
        P("seq", None),
    )
    return jax.shard_map(
        local,
        mesh=mesh,
        in_specs=placed,
        out_specs=(P("seq", "head"), P("seq", "head"), P("head", "seq")),
        check_vma=False,
    )
```

```python
import functools

import jax
import jax.numpy as jnp
from jax import lax
from jax.experimental import pallas as pl
from jax.experimental.pallas import tpu as pltpu
from jax.sharding import PartitionSpec as P

HEAD_SIZE = 128
WINDOW_LENGTH = 4096
QUERIES_PER_KEY = 2


logit_scale = 1.0 / 12.0
log2_scale = 1.4426950408889634 / 12.0
excluded = -1e30


def passed_along(value, axis, steps):
    count = lax.axis_size(axis)
    leading, last = (max(0, -steps), min(count, count - steps))
    return lax.ppermute(value, axis, [(source, source + steps) for source in range(leading, last)])


NT = (((1,), (1,)), ((), ()))


def dot_nt(left, right):
    return lax.dot_general(left, right, NT, preferred_element_type=jnp.float32)


def dot_nn(left, right):
    return jnp.dot(left, right, preferred_element_type=jnp.float32)


def at(place, size):
    return pl.ds(pl.multiple_of(place * size, size), size)


def out_grad_kernel(
    cot_hbm, weight_hbm, q_hbm, k_hbm, v_hbm, same_ref, other_ref, cot_ref, weight_ref, sem
):
    core = lax.axis_index("seq") % 2
    halves = ((other_ref, 1 - core), (same_ref, core))
    rows = weight_ref.shape[0] // 2
    pieces = (sem.shape[0] - 6) // 3
    cut = weight_ref.shape[1] // pieces
    model_copies = []
    for piece in range(pieces):
        part = pl.ds(piece * cut, cut)
        model_copies.append(
            [
                pltpu.make_async_copy(
                    cot_hbm.at[:, part], cot_ref.at[:, part], sem.at[6 + 3 * piece]
                )
            ]
        )
        for place, (_, half) in enumerate(halves):
            model_copies[-1].append(
                pltpu.make_async_copy(
                    weight_hbm.at[at(half, rows), part],
                    weight_ref.at[pl.ds(place * rows, rows), part],
                    sem.at[7 + 3 * piece + place],
                )
            )
        for copy in model_copies[-1]:
            copy.start()
    plain_copies = []
    for place, (target, half) in enumerate(halves):
        first = 0
        for which, source in enumerate((q_hbm, k_hbm, v_hbm)):
            cols = source.shape[1] // 2
            plain_copies.append(
                pltpu.make_async_copy(
                    source.at[:, at(half, cols)],
                    target.at[:, pl.ds(first, cols)],
                    sem.at[3 * place + which],
                )
            )
            plain_copies[-1].start()
            first += cols
    total = None
    for piece in range(pieces):
        for copy in model_copies[piece]:
            copy.wait()
        part = slice(piece * cut, (piece + 1) * cut)
        product = dot_nt(cot_ref[:, part], weight_ref[:, part])
        total = product if total is None else total + product
    for place, (target, _) in enumerate(halves):
        for head in range(rows // HEAD_SIZE):
            row = place * rows + head * HEAD_SIZE
            target[:, first + head * HEAD_SIZE : first + (head + 1) * HEAD_SIZE] = total[
                :, row : row + HEAD_SIZE
            ].T.astype(jnp.bfloat16)
    for copy in plain_copies:
        copy.wait()


def turn_kernel(normed_ref, cot_ref, block_ref, _, __, *refs):
    *column_refs, own_ref, turned_ref = refs
    me = lax.axis_index("seq")
    cut = column_refs[0].shape[2]
    own_ref[...] = block_ref[...]
    for which, ref in enumerate((normed_ref, cot_ref)):
        turned_ref[which] = ref[...].astype(jnp.float32).T.astype(jnp.bfloat16)
        for chip, target in enumerate(column_refs):
            for far in range(2):
                target[far, which] = turned_ref[which, at(me ^ (2 * chip + far), cut)]


def pass_on_kernel(_, __, attn_ref, dv_t_ref, *refs):
    *column_refs, give_ref = refs
    cut, rows = column_refs[0].shape[2:]
    for chip, ref in enumerate(column_refs):
        for which in range(2):
            first = (2 * chip + which) * cut
            give_ref[first : first + cut] = ref[1, which]
    first = 2 * len(column_refs) * cut
    for ref in (attn_ref, dv_t_ref):
        for block in range(ref.shape[1] // rows):
            give_ref[first : first + ref.shape[0]] = ref[:, block * rows : (block + 1) * rows]
            first += ref.shape[0]


def attention_kernel(blocks, *refs):
    attention_body(refs[:blocks], *refs[blocks:])


def attention_body(
    block_refs,
    dx_own_ref,
    dx_far_ref,
    attn_ref,
    prob_ref,
    grad_t_ref,
    gathered_ref,
    score_even_ref,
    score_odd_ref,
    delta_ref,
    query_ref,
    value_t_ref,
    key_t_ref,
    dq_t_ref,
    dk_ref,
    dv_ref,
):
    me = lax.axis_index("seq")
    core, chip = me % 2, me // 2
    rows = dx_own_ref.shape[0]
    for apart, source in enumerate(block_refs):
        gathered_ref[at(me ^ apart, rows)] = source[...]
    tokens = gathered_ref.shape[0]
    size = 2 * rows
    steps = tokens // size
    wide = QUERIES_PER_KEY * size
    heads = QUERIES_PER_KEY
    key_cols = slice(heads * HEAD_SIZE, (heads + 1) * HEAD_SIZE)
    value_cols = slice((heads + 1) * HEAD_SIZE, (heads + 2) * HEAD_SIZE)
    grad_base = (heads + 2) * HEAD_SIZE
    value_t_ref[...] = gathered_ref[:, value_cols].T
    key_t_ref[...] = gathered_ref[:, key_cols].T
    key_place = lax.broadcasted_iota(jnp.int32, (size, wide), 0)
    query_place = lax.broadcasted_iota(jnp.int32, (size, wide), 1) % size
    allowed = key_place <= query_place

    def scored(step):
        own = slice(step * size, (step + 1) * size)
        score_ref = score_odd_ref if step % 2 else score_even_ref
        queries = jnp.concatenate(
            [gathered_ref[own, h * HEAD_SIZE : (h + 1) * HEAD_SIZE] for h in range(heads)], axis=0
        )
        query_ref[step * wide : (step + 1) * wide] = queries
        top = None
        for piece in range(step + 1):
            part = slice(piece * size, (piece + 1) * size)
            scores = dot_nt(gathered_ref[part, key_cols], queries)
            if piece == step:
                scores = jnp.where(allowed, scores, excluded)
            score_ref[part] = scores
            largest = jnp.max(scores.reshape(size // 8, 8, wide), axis=0)
            top = largest if top is None else jnp.maximum(top, largest)
        return top

    next_top = scored(steps - 1)
    for step in range(steps - 1, -1, -1):
        span = (step + 1) * size
        own = slice(step * size, span)
        lanes = slice(step * wide, (step + 1) * wide)
        score_ref = score_odd_ref if step % 2 else score_even_ref
        top = next_top
        if step:
            next_top = scored(step - 1)
        top = jnp.max(top, axis=0, keepdims=True)
        total = None
        for piece in range(step + 1):
            part = slice(piece * size, (piece + 1) * size)
            weights = jnp.exp2((score_ref[part] - top) * log2_scale)
            prob_ref[part, lanes] = weights.astype(jnp.bfloat16)
            summed = jnp.sum(weights.reshape(size // 8, 8, wide), axis=0)
            total = summed if total is None else total + summed
        inverse = 1.0 / jnp.sum(total, axis=0, keepdims=True)
        attn = dot_nn(value_t_ref[:, :span], prob_ref[:span, lanes]) * inverse
        for h in range(heads):
            attn_ref[h * HEAD_SIZE : (h + 1) * HEAD_SIZE, own] = attn[
                :, h * size : (h + 1) * size
            ].astype(jnp.bfloat16)
        grads_t = jnp.concatenate(
            [
                gathered_ref[
                    block * rows : (block + 1) * rows,
                    grad_base + h * HEAD_SIZE : grad_base + (h + 1) * HEAD_SIZE,
                ]
                for h in range(heads)
                for block in (2 * step, 2 * step + 1)
            ],
            axis=1,
        )
        grads_t = (grads_t.astype(jnp.float32) * inverse).astype(jnp.bfloat16)
        grad_t_ref[:, lanes] = grads_t
        delta_ref[:, lanes] = jnp.sum(grads_t.astype(jnp.float32) * attn, axis=0, keepdims=True)

    dq_t_ref[...] = jnp.zeros_like(dq_t_ref)
    dk_ref[...] = jnp.zeros_like(dk_ref)
    dv_ref[...] = jnp.zeros_like(dv_ref)
    for step in range(steps):
        key_step = jnp.minimum(chip, step)
        query_step = jnp.maximum(chip, step)
        dprob = dot_nn(
            gathered_ref[at(key_step, size), value_cols], grad_t_ref[:, at(query_step, wide)]
        )
        prob = prob_ref[at(key_step, size), at(query_step, wide)]
        dscore = (
            prob.astype(jnp.float32)
            * (dprob - delta_ref[:, at(query_step, wide)])
        ).astype(jnp.bfloat16)

        @pl.when(step <= chip)
        def _():
            dq_t_ref[...] += dot_nn(key_t_ref[:, at(key_step, size)], dscore)

        @pl.when(step >= chip)
        def _():
            dk_ref[...] += dot_nn(dscore, query_ref[at(query_step, wide)])
            dv_ref[...] += dot_nt(prob, grad_t_ref[:, at(query_step, wide)])

    for target, half in ((dx_far_ref, 1 - core), (dx_own_ref, core)):
        for h in range(heads):
            target[:, h * HEAD_SIZE : (h + 1) * HEAD_SIZE] = (
                (logit_scale * dq_t_ref[:, at(2 * h + half, rows)])
                .T.astype(jnp.bfloat16)
            )
        target[:, key_cols] = (logit_scale * dk_ref[at(half, rows)]).astype(jnp.bfloat16)
        target[:, value_cols] = dv_ref[at(half, rows)].astype(jnp.bfloat16)


def value_grad_kernel(prob_ref, grad_t_ref, dv_t_ref):
    size = 2 * HEAD_SIZE
    wide = QUERIES_PER_KEY * size
    for step in range(prob_ref.shape[0] // size):
        own = slice(step * size, (step + 1) * size)
        dv_t_ref[:, own] = dot_nt(grad_t_ref[:, step * wide :], prob_ref[own, step * wide :]).astype(
            jnp.bfloat16
        )


def input_terms_kernel(apart_groups, own_ref, far_ref, wq_ref, wk_ref, wv_ref, *refs):
    terms, dx_ref = refs[-1 - len(apart_groups) : -1], refs[-1]
    core = lax.axis_index("seq") % 2
    group = lax.axis_index("head")
    q_cols = wq_ref.shape[1] // 2
    kv_cols = wk_ref.shape[1] // 2
    for source, half in ((own_ref, core), (far_ref, 1 - core)):
        dx_ref[:, at(half, q_cols)] = source[:, :q_cols]
        dx_ref[:, pl.ds(pl.multiple_of(2 * q_cols + half * kv_cols, kv_cols), kv_cols)] = source[
            :, q_cols : q_cols + kv_cols
        ]
        dx_ref[
            :, pl.ds(pl.multiple_of(2 * q_cols + (2 + half) * kv_cols, kv_cols), kv_cols)
        ] = source[:, q_cols + kv_cols :]
    for apart, target in zip(apart_groups, terms):
        cut = target.shape[0]
        place = at(group ^ apart, cut)
        target[...] = (
            dot_nt(wq_ref[place], dx_ref[:, : 2 * q_cols])
            + dot_nt(wk_ref[place], dx_ref[:, 2 * q_cols : 2 * q_cols + 2 * kv_cols])
            + dot_nt(wv_ref[place], dx_ref[:, 2 * q_cols + 2 * kv_cols :])
        ).astype(target.dtype)


def weight_grad_kernel(attn_ref, dv_t_ref, got_ref, *refs):
    column_refs, refs = refs[:-6], refs[-6:]
    wvalue_ref, woutput_ref, done_ref, joined_ref, far_attn_ref, far_dv_ref = refs
    done_ref[...] = jnp.zeros_like(done_ref)
    me = lax.axis_index("seq")
    core = me % 2
    cut, rows = column_refs[0].shape[2:]
    for chip, ref in enumerate(column_refs):
        joined_ref[:, :, at(me ^ (2 * chip), rows)] = ref[0]
        for which in range(2):
            first = (2 * chip + which) * cut
            joined_ref[which, :, at(me ^ (2 * chip + 1), rows)] = got_ref[first : first + cut]
    first = 2 * len(column_refs) * cut
    for ref in (far_attn_ref, far_dv_ref):
        for block in range(ref.shape[1] // rows):
            ref[:, block * rows : (block + 1) * rows] = got_ref[first : first + ref.shape[0]]
            first += ref.shape[0]
    for half, attn, dv_t in ((core, attn_ref, dv_t_ref), (1 - core, far_attn_ref, far_dv_ref)):
        woutput_ref[:, at(half, attn.shape[0])] = dot_nt(joined_ref[1], attn[...])
        wvalue_ref[:, at(half, dv_t.shape[0])] = dot_nt(joined_ref[0], dv_t[...])


def add_kernel(own_ref, arrived_ref, _, sum_ref):
    total = own_ref[...].astype(jnp.float32) + arrived_ref[...].astype(jnp.float32)
    sum_ref[...] = total.astype(jnp.bfloat16)


def sum_kernel(_, own_ref, *refs):
    total = own_ref[...]
    for arrived_ref in refs[:-1]:
        total = total + arrived_ref[...].astype(jnp.float32)
    refs[-1][...] = total.astype(jnp.bfloat16)


def kernel_call(
    body, outs, operands, in_vmem=(), scratch=(), flops=0, moved=0, room=16
):
    vmem = pl.BlockSpec(memory_space=pltpu.VMEM)
    hbm = pl.BlockSpec(memory_space=pltpu.HBM)
    return pl.pallas_call(
        body,
        out_shape=outs,
        in_specs=[vmem if place in in_vmem else hbm for place in range(len(operands))],
        out_specs=(vmem,) * len(outs),
        scratch_shapes=list(scratch),
        compiler_params=pltpu.CompilerParams(vmem_limit_bytes=int(room * 1024 * 1024)),
        cost_estimate=pl.CostEstimate(flops=flops, bytes_accessed=moved, transcendentals=0),
    )(*operands)


def swapped(value, axis, apart):
    count = lax.axis_size(axis)
    return lax.ppermute(value, axis, [(place, place ^ apart) for place in range(count)])


def gathered_plan(
    normed_input,
    stored_queries,
    stored_keys,
    stored_values,
    query_weight,
    key_matrix,
    value_matrix,
    output_weight,
    out_cotangent,
):
    bf16, f32 = jnp.bfloat16, jnp.float32
    rows, model = normed_input.shape
    blocks = lax.axis_size("seq")
    groups = lax.axis_size("head")
    tokens = rows * blocks
    q_cols = stored_queries.shape[1] // 2
    kv_cols = HEAD_SIZE
    wide = 2 * QUERIES_PER_KEY * rows
    packed_cols = 2 * q_cols + 2 * kv_cols
    pieces = 3 if model % (6 * HEAD_SIZE) == 0 else 1
    shape = jax.ShapeDtypeStruct
    same, other = kernel_call(
        out_grad_kernel,
        (shape((rows, packed_cols), bf16),) * 2,
        (out_cotangent, output_weight, stored_queries, stored_keys, stored_values),
        scratch=(
            pltpu.VMEM(out_cotangent.shape, bf16),
            pltpu.VMEM(output_weight.shape, bf16),
            pltpu.SemaphoreType.DMA((6 + 3 * pieces,)),
        ),
        flops=4 * rows * model * q_cols,
        moved=2 * model * (rows + 2 * q_cols),
        room=63,
    )
    held = {0: same}
    for apart in range(2, blocks):
        lowest, highest = 2, 1 << (apart.bit_length() - 1)
        while not apart & lowest:
            lowest *= 2
        through = lowest if apart % 2 else highest
        if lowest == highest:
            held[apart] = swapped(other if apart % 2 else same, "seq", apart)
        else:
            held[apart] = swapped(held[apart ^ through], "seq", through)
    held[1] = swapped(other, "seq", 1)
    cut = model // blocks
    *columns, held[0] = kernel_call(
        turn_kernel,
        (shape((2, 2, cut, rows), bf16),) * (blocks // 2) + (shape(same.shape, bf16),),
        (normed_input, out_cotangent, same, held[2], held[blocks // 2 + 1]),
        in_vmem=range(3),
        scratch=(pltpu.VMEM((2, model, rows), bf16),),
        moved=8 * rows * model,
        room=8,
    )
    columns = [columns[0]] + [
        swapped(columns[chip], "seq", 2 * chip) for chip in range(1, blocks // 2)
    ]
    dx_own, dx_far, attn, prob, grad_t = kernel_call(
        functools.partial(attention_kernel, blocks),
        (
            shape((rows, q_cols + 2 * kv_cols), bf16),
            shape((rows, q_cols + 2 * kv_cols), bf16),
            shape((q_cols, tokens), bf16),
            shape((tokens, tokens * QUERIES_PER_KEY), bf16),
            shape((HEAD_SIZE, tokens * QUERIES_PER_KEY), bf16),
        ),
        [held[apart] for apart in range(blocks)],
        in_vmem=range(blocks),
        scratch=(
            pltpu.VMEM((tokens, packed_cols), bf16),
            pltpu.VMEM((tokens, wide), f32),
            pltpu.VMEM((tokens, wide), f32),
            pltpu.VMEM((1, tokens * QUERIES_PER_KEY), f32),
            pltpu.VMEM((tokens * QUERIES_PER_KEY, HEAD_SIZE), bf16),
            pltpu.VMEM((HEAD_SIZE, tokens), bf16),
            pltpu.VMEM((HEAD_SIZE, tokens), bf16),
            pltpu.VMEM((HEAD_SIZE, wide), f32),
            pltpu.VMEM((2 * rows, HEAD_SIZE), f32),
            pltpu.VMEM((2 * rows, HEAD_SIZE), f32),
        ),
        flops=8 * tokens * tokens * q_cols,
        moved=2 * tokens * packed_cols,
    )
    dx_got = swapped(dx_far, "seq", 1)
    def terms_of(chosen):
        return kernel_call(
            functools.partial(input_terms_kernel, chosen),
            tuple(shape((model // groups, rows), f32 if not apart else bf16) for apart in chosen),
            (dx_own, dx_got, query_weight, key_matrix, value_matrix),
            in_vmem=range(5),
            scratch=(pltpu.VMEM((rows, 2 * (q_cols + 2 * kv_cols)), bf16),),
            flops=2 * len(chosen) * rows * (model // groups) * 2 * (q_cols + 2 * kv_cols),
            moved=2 * len(chosen) * (model // groups) * 2 * (q_cols + 2 * kv_cols),
            room=4,
        )

    (far_term,) = terms_of((3,))
    pair_term, near_term, own_term = terms_of((2, 1, 0))
    (dv_t,) = kernel_call(
        value_grad_kernel,
        (shape((kv_cols, tokens), bf16),),
        (prob, grad_t),
        in_vmem=range(2),
        flops=tokens * tokens * q_cols,
        moved=2 * tokens * tokens * QUERIES_PER_KEY,
        room=4,
    )
    (pair_sum,) = kernel_call(
        add_kernel,
        (shape(pair_term.shape, bf16),),
        (pair_term, swapped(far_term, "head", 1), dv_t),
        in_vmem=range(2),
        room=4,
    )
    near_got = swapped(near_term, "head", 1)
    part_rows = q_cols + kv_cols
    (give,) = kernel_call(
        pass_on_kernel,
        (shape((blocks * (cut + part_rows), rows), bf16),),
        (pair_sum, near_got, attn, dv_t, *columns),
        in_vmem=range(2, 4 + blocks // 2),
        room=4,
    )
    grad_wvalue, grad_woutput, weights_done = kernel_call(
        weight_grad_kernel,
        (
            shape((model // blocks, 2 * kv_cols), f32),
            shape((model // blocks, 2 * q_cols), f32),
            shape((8, HEAD_SIZE), f32),
        ),
        (attn, dv_t, swapped(give, "seq", 1), *columns),
        in_vmem=range(3 + blocks // 2),
        scratch=(
            pltpu.VMEM((2, model // blocks, tokens), bf16),
            pltpu.VMEM((q_cols, tokens), bf16),
            pltpu.VMEM((kv_cols, tokens), bf16),
        ),
        room=8,
    )
    (grad_input,) = kernel_call(
        sum_kernel,
        (shape((model // groups, rows), bf16),),
        (weights_done, own_term, near_got, swapped(pair_sum, "head", 2)),
        in_vmem=range(1, 4),
        moved=4 * groups * (model // groups) * rows,
    )
    return (grad_input.T, grad_wvalue, grad_woutput.T)


def power_of_two(count):
    return count & (count - 1) == 0


def local(normed_input, stored_queries, stored_keys, *others):
    blocks, groups = lax.axis_size("seq"), lax.axis_size("head")
    whole_window = normed_input.shape[0] * blocks <= WINDOW_LENGTH
    two_heads = stored_keys.shape[1] == 2 * HEAD_SIZE
    paired = blocks >= 4 and power_of_two(blocks) and groups == 4
    plan = gathered_plan if whole_window and two_heads and paired else windowed_plan
    return plan(normed_input, stored_queries, stored_keys, *others)


def windowed_plan(
    normed_input,
    stored_queries,
    stored_keys,
    stored_values,
    query_weight,
    key_matrix,
    value_matrix,
    output_weight,
    out_cotangent,
):
    tok_rows = normed_input.shape[0]
    blocks_seq = lax.axis_size("seq")
    seq_place = lax.axis_index("seq")
    reach_blocks = min(WINDOW_LENGTH // tok_rows, blocks_seq - 1)
    kv_heads = stored_keys.shape[1] // HEAD_SIZE
    output_gradient = jnp.dot(
        out_cotangent, output_weight.T, preferred_element_type=jnp.float32
    ).astype(jnp.bfloat16)
    pieces = [(stored_keys, stored_values)]
    current = (stored_keys, stored_values)
    for relay_step in range(reach_blocks):
        current = passed_along((current[0], current[1]), "seq", 1)
        pieces = [current] + pieces
    key_window = jnp.concatenate([piece[0] for piece in pieces], axis=0)
    value_window = jnp.concatenate([piece[1] for piece in pieces], axis=0)
    key_span = key_window.shape[0]
    query_pos = seq_place * tok_rows + jnp.arange(tok_rows, dtype=jnp.int32)
    key_pos = (seq_place - reach_blocks) * tok_rows + jnp.arange(key_span, dtype=jnp.int32)
    pos_gap = query_pos[:, None] - key_pos[None, :]
    allowed = (pos_gap >= 0) & (pos_gap < WINDOW_LENGTH) & (key_pos >= 0)[None, :]
    allowed_rows = jnp.tile(allowed, (QUERIES_PER_KEY, 1))
    query_stack = (
        stored_queries.reshape(tok_rows, kv_heads, QUERIES_PER_KEY, HEAD_SIZE)
        .transpose(1, 2, 0, 3)
        .reshape(kv_heads, QUERIES_PER_KEY * tok_rows, HEAD_SIZE)
    )
    grad_stack = (
        output_gradient.reshape(tok_rows, kv_heads, QUERIES_PER_KEY, HEAD_SIZE)
        .transpose(1, 2, 0, 3)
        .reshape(kv_heads, QUERIES_PER_KEY * tok_rows, HEAD_SIZE)
    )
    key_stack = key_window.reshape(key_span, kv_heads, HEAD_SIZE).transpose(1, 0, 2)
    value_stack = value_window.reshape(key_span, kv_heads, HEAD_SIZE).transpose(1, 0, 2)

    def per_head(head_items):
        query_head, key_head, value_head, grad_head = head_items
        attention_logits = logit_scale * jnp.dot(
            query_head, key_head.T, preferred_element_type=jnp.float32
        )
        masked = jnp.where(allowed_rows, attention_logits, -jnp.inf)
        row_top = jnp.max(masked, axis=1, keepdims=True)
        exp_scores = jnp.exp(masked - row_top)
        attn_prob = exp_scores / jnp.sum(exp_scores, axis=1, keepdims=True)
        probability_halfwidth = attn_prob.astype(jnp.bfloat16)
        attn_head = jnp.dot(
            probability_halfwidth, value_head, preferred_element_type=jnp.float32
        ).astype(jnp.bfloat16)
        row_delta = jnp.sum(
            grad_head.astype(jnp.float32) * attn_head.astype(jnp.float32), axis=1, keepdims=True
        )
        probability_gradient = jnp.dot(grad_head, value_head.T, preferred_element_type=jnp.float32)
        score_gradient = (attn_prob * (probability_gradient - row_delta)).astype(jnp.bfloat16)
        qgrad_head = (
            logit_scale * jnp.dot(score_gradient, key_head, preferred_element_type=jnp.float32)
        ).astype(jnp.bfloat16)
        key_partial = logit_scale * jnp.dot(
            score_gradient.T, query_head, preferred_element_type=jnp.float32
        )
        value_partial = jnp.dot(
            probability_halfwidth.T, grad_head, preferred_element_type=jnp.float32
        )
        return (attn_head, qgrad_head, key_partial, value_partial)

    attn_all, qgrad_all, key_all, value_all = lax.map(
        per_head, (query_stack, key_stack, value_stack, grad_stack)
    )
    attention_output = (
        attn_all.reshape(kv_heads, QUERIES_PER_KEY, tok_rows, HEAD_SIZE)
        .transpose(2, 0, 1, 3)
        .reshape(tok_rows, kv_heads * QUERIES_PER_KEY * HEAD_SIZE)
    )
    query_gradient = (
        qgrad_all.reshape(kv_heads, QUERIES_PER_KEY, tok_rows, HEAD_SIZE)
        .transpose(2, 0, 1, 3)
        .reshape(tok_rows, kv_heads * QUERIES_PER_KEY * HEAD_SIZE)
    )
    key_terms = key_all.transpose(1, 0, 2).reshape(key_span, kv_heads * HEAD_SIZE)
    value_terms = value_all.transpose(1, 0, 2).reshape(key_span, kv_heads * HEAD_SIZE)

    def take_slot(terms, slot_index):
        return terms[slot_index * tok_rows : (slot_index + 1) * tok_rows]

    key_sum = take_slot(key_terms, reach_blocks)
    value_sum = take_slot(value_terms, reach_blocks)
    for distance in range(1, reach_blocks + 1):
        received = passed_along(
            (
                take_slot(key_terms, reach_blocks - distance),
                take_slot(value_terms, reach_blocks - distance),
            ),
            "seq",
            -distance,
        )
        key_sum = key_sum + received[0]
        value_sum = value_sum + received[1]
    grad_key = key_sum.astype(jnp.bfloat16)
    grad_value = value_sum.astype(jnp.bfloat16)
    input_terms = jnp.dot(query_gradient, query_weight.T, preferred_element_type=jnp.float32)
    input_terms = input_terms + jnp.dot(grad_key, key_matrix.T, preferred_element_type=jnp.float32)
    input_terms = input_terms + jnp.dot(
        grad_value, value_matrix.T, preferred_element_type=jnp.float32
    )
    grad_input = lax.psum_scatter(input_terms, "head", scatter_dimension=1, tiled=True).astype(
        jnp.bfloat16
    )
    value_cols = grad_value.shape[1]
    input_cols = normed_input.T
    cot_cols = out_cotangent.T
    gathered = lax.psum_scatter(
        jnp.concatenate(
            [
                jnp.dot(input_cols, grad_value, preferred_element_type=jnp.float32),
                jnp.dot(cot_cols, attention_output, preferred_element_type=jnp.float32),
            ],
            axis=1,
        ),
        "seq",
        scatter_dimension=0,
        tiled=True,
    )
    grad_wvalue = gathered[:, :value_cols]
    grad_woutput = gathered[:, value_cols:].T
    return (grad_input, grad_wvalue, grad_woutput)


def solution(mesh):
    placed = (
        P("seq", None),
        P("seq", "head"),
        P("seq", "head"),
        P("seq", "head"),
        P(None, "head"),
        P(None, "head"),
        P(None, "head"),
        P("head", None),
        P("seq", None),
    )
    return jax.shard_map(
        local,
        mesh=mesh,
        in_specs=placed,
        out_specs=(P("seq", "head"), P("seq", "head"), P("head", "seq")),
        check_vma=False,
    )
```

```python
import functools

import jax
import jax.numpy as jnp
from jax import lax
from jax.experimental import pallas as pl
from jax.experimental.pallas import tpu as pltpu
from jax.sharding import PartitionSpec as P

HEAD_SIZE = 128
WINDOW_LENGTH = 4096
QUERIES_PER_KEY = 2


logit_scale = 1.0 / 12.0
log2_scale = 1.4426950408889634 / 12.0
excluded = -1e30


def passed_along(value, axis, steps):
    count = lax.axis_size(axis)
    leading, last = (max(0, -steps), min(count, count - steps))
    return lax.ppermute(value, axis, [(source, source + steps) for source in range(leading, last)])


NT = (((1,), (1,)), ((), ()))


def dot_nt(left, right):
    return lax.dot_general(left, right, NT, preferred_element_type=jnp.float32)


def dot_nn(left, right):
    return jnp.dot(left, right, preferred_element_type=jnp.float32)


def at(place, size):
    return pl.ds(pl.multiple_of(place * size, size), size)


def out_grad_kernel(
    cot_hbm, weight_hbm, q_hbm, k_hbm, v_hbm, same_ref, other_ref, cot_ref, weight_ref, sem
):
    core = lax.axis_index("seq") % 2
    halves = ((other_ref, 1 - core), (same_ref, core))
    rows = weight_ref.shape[0] // 2
    pieces = (sem.shape[0] - 6) // 3
    cut = weight_ref.shape[1] // pieces
    model_copies = []
    for piece in range(pieces):
        part = pl.ds(piece * cut, cut)
        model_copies.append(
            [
                pltpu.make_async_copy(
                    cot_hbm.at[:, part], cot_ref.at[:, part], sem.at[6 + 3 * piece]
                )
            ]
        )
        for place, (_, half) in enumerate(halves):
            model_copies[-1].append(
                pltpu.make_async_copy(
                    weight_hbm.at[at(half, rows), part],
                    weight_ref.at[pl.ds(place * rows, rows), part],
                    sem.at[7 + 3 * piece + place],
                )
            )
        for copy in model_copies[-1]:
            copy.start()
    plain_copies = []
    for place, (target, half) in enumerate(halves):
        first = 0
        for which, source in enumerate((q_hbm, k_hbm, v_hbm)):
            cols = source.shape[1] // 2
            plain_copies.append(
                pltpu.make_async_copy(
                    source.at[:, at(half, cols)],
                    target.at[:, pl.ds(first, cols)],
                    sem.at[3 * place + which],
                )
            )
            plain_copies[-1].start()
            first += cols
    total = None
    for piece in range(pieces):
        for copy in model_copies[piece]:
            copy.wait()
        part = slice(piece * cut, (piece + 1) * cut)
        product = dot_nt(cot_ref[:, part], weight_ref[:, part])
        total = product if total is None else total + product
    for place, (target, _) in enumerate(halves):
        for head in range(rows // HEAD_SIZE):
            row = place * rows + head * HEAD_SIZE
            target[:, first + head * HEAD_SIZE : first + (head + 1) * HEAD_SIZE] = total[
                :, row : row + HEAD_SIZE
            ].T.astype(jnp.bfloat16)
    for copy in plain_copies:
        copy.wait()


def turn_kernel(normed_ref, cot_ref, block_ref, _, __, *refs):
    *column_refs, own_ref, turned_ref = refs
    me = lax.axis_index("seq")
    cut = column_refs[0].shape[2]
    own_ref[...] = block_ref[...]
    for which, ref in enumerate((normed_ref, cot_ref)):
        turned_ref[which] = ref[...].astype(jnp.float32).T.astype(jnp.bfloat16)
        for chip, target in enumerate(column_refs):
            for far in range(2):
                target[far, which] = turned_ref[which, at(me ^ (2 * chip + far), cut)]


def pass_on_kernel(_, attn_ref, dv_t_ref, *refs):
    *column_refs, give_ref = refs
    cut, rows = column_refs[0].shape[2:]
    for chip, ref in enumerate(column_refs):
        for which in range(2):
            first = (2 * chip + which) * cut
            give_ref[first : first + cut] = ref[1, which]
    first = 2 * len(column_refs) * cut
    for ref in (attn_ref, dv_t_ref):
        for block in range(ref.shape[1] // rows):
            give_ref[first : first + ref.shape[0]] = ref[:, block * rows : (block + 1) * rows]
            first += ref.shape[0]


def attention_kernel(blocks, late, *refs):
    first = blocks + late
    attention_body(refs[:blocks], *refs[first : first + 5], *refs[first + 5 + late :])


def attention_body(
    block_refs,
    dx_own_ref,
    dx_far_ref,
    attn_ref,
    prob_ref,
    grad_t_ref,
    gathered_ref,
    score_even_ref,
    score_odd_ref,
    delta_ref,
    query_ref,
    value_t_ref,
    key_t_ref,
    dq_t_ref,
    dk_ref,
    dv_ref,
):
    me = lax.axis_index("seq")
    core, chip = me % 2, me // 2
    rows = dx_own_ref.shape[0]
    for apart, source in enumerate(block_refs):
        gathered_ref[at(me ^ apart, rows)] = source[...]
    tokens = gathered_ref.shape[0]
    size = 2 * rows
    steps = tokens // size
    wide = QUERIES_PER_KEY * size
    heads = QUERIES_PER_KEY
    key_cols = slice(heads * HEAD_SIZE, (heads + 1) * HEAD_SIZE)
    value_cols = slice((heads + 1) * HEAD_SIZE, (heads + 2) * HEAD_SIZE)
    grad_base = (heads + 2) * HEAD_SIZE
    value_t_ref[...] = gathered_ref[:, value_cols].T
    key_t_ref[...] = gathered_ref[:, key_cols].T
    key_place = lax.broadcasted_iota(jnp.int32, (size, wide), 0)
    query_place = lax.broadcasted_iota(jnp.int32, (size, wide), 1) % size
    allowed = key_place <= query_place

    def scored(step):
        own = slice(step * size, (step + 1) * size)
        score_ref = score_odd_ref if step % 2 else score_even_ref
        queries = jnp.concatenate(
            [gathered_ref[own, h * HEAD_SIZE : (h + 1) * HEAD_SIZE] for h in range(heads)], axis=0
        )
        query_ref[step * wide : (step + 1) * wide] = queries
        top = None
        for piece in range(step + 1):
            part = slice(piece * size, (piece + 1) * size)
            scores = dot_nt(gathered_ref[part, key_cols], queries)
            if piece == step:
                scores = jnp.where(allowed, scores, excluded)
            score_ref[part] = scores
            largest = jnp.max(scores.reshape(size // 8, 8, wide), axis=0)
            top = largest if top is None else jnp.maximum(top, largest)
        return top

    next_top = scored(steps - 1)
    for step in range(steps - 1, -1, -1):
        span = (step + 1) * size
        own = slice(step * size, span)
        lanes = slice(step * wide, (step + 1) * wide)
        score_ref = score_odd_ref if step % 2 else score_even_ref
        top = next_top
        if step:
            next_top = scored(step - 1)
        top = jnp.max(top, axis=0, keepdims=True)
        total = None
        for piece in range(step + 1):
            part = slice(piece * size, (piece + 1) * size)
            weights = jnp.exp2((score_ref[part] - top) * log2_scale)
            prob_ref[part, lanes] = weights.astype(jnp.bfloat16)
            summed = jnp.sum(weights.reshape(size // 8, 8, wide), axis=0)
            total = summed if total is None else total + summed
        inverse = 1.0 / jnp.sum(total, axis=0, keepdims=True)
        attn = dot_nn(value_t_ref[:, :span], prob_ref[:span, lanes]) * inverse
        for h in range(heads):
            attn_ref[h * HEAD_SIZE : (h + 1) * HEAD_SIZE, own] = attn[
                :, h * size : (h + 1) * size
            ].astype(jnp.bfloat16)
        grads_t = jnp.concatenate(
            [
                gathered_ref[
                    block * rows : (block + 1) * rows,
                    grad_base + h * HEAD_SIZE : grad_base + (h + 1) * HEAD_SIZE,
                ]
                for h in range(heads)
                for block in (2 * step, 2 * step + 1)
            ],
            axis=1,
        )
        grads_t = (grads_t.astype(jnp.float32) * inverse).astype(jnp.bfloat16)
        grad_t_ref[:, lanes] = grads_t
        delta_ref[:, lanes] = jnp.sum(grads_t.astype(jnp.float32) * attn, axis=0, keepdims=True)

    dq_t_ref[...] = jnp.zeros_like(dq_t_ref)
    dk_ref[...] = jnp.zeros_like(dk_ref)
    dv_ref[...] = jnp.zeros_like(dv_ref)
    for step in range(steps):
        key_step = jnp.minimum(chip, step)
        query_step = jnp.maximum(chip, step)
        dprob = dot_nn(
            gathered_ref[at(key_step, size), value_cols], grad_t_ref[:, at(query_step, wide)]
        )
        prob = prob_ref[at(key_step, size), at(query_step, wide)]
        dscore = (
            prob.astype(jnp.float32)
            * (dprob - delta_ref[:, at(query_step, wide)])
        ).astype(jnp.bfloat16)

        @pl.when(step <= chip)
        def _():
            dq_t_ref[...] += dot_nn(key_t_ref[:, at(key_step, size)], dscore)

        @pl.when(step >= chip)
        def _():
            dk_ref[...] += dot_nn(dscore, query_ref[at(query_step, wide)])
            dv_ref[...] += dot_nt(prob, grad_t_ref[:, at(query_step, wide)])

    for target, half in ((dx_far_ref, 1 - core), (dx_own_ref, core)):
        for h in range(heads):
            target[:, h * HEAD_SIZE : (h + 1) * HEAD_SIZE] = (
                (logit_scale * dq_t_ref[:, at(2 * h + half, rows)])
                .T.astype(jnp.bfloat16)
            )
        target[:, key_cols] = (logit_scale * dk_ref[at(half, rows)]).astype(jnp.bfloat16)
        target[:, value_cols] = dv_ref[at(half, rows)].astype(jnp.bfloat16)


def value_grad_kernel(prob_ref, grad_t_ref, dv_t_ref):
    size = 2 * HEAD_SIZE
    wide = QUERIES_PER_KEY * size
    for step in range(prob_ref.shape[0] // size):
        own = slice(step * size, (step + 1) * size)
        dv_t_ref[:, own] = dot_nt(grad_t_ref[:, step * wide :], prob_ref[own, step * wide :]).astype(
            jnp.bfloat16
        )


def input_terms_kernel(apart_groups, own_ref, far_ref, wq_ref, wk_ref, wv_ref, *refs):
    terms, dx_ref = refs[-1 - len(apart_groups) : -1], refs[-1]
    core = lax.axis_index("seq") % 2
    group = lax.axis_index("head")
    q_cols = wq_ref.shape[1] // 2
    kv_cols = wk_ref.shape[1] // 2
    for source, half in ((own_ref, core), (far_ref, 1 - core)):
        dx_ref[:, at(half, q_cols)] = source[:, :q_cols]
        dx_ref[:, pl.ds(pl.multiple_of(2 * q_cols + half * kv_cols, kv_cols), kv_cols)] = source[
            :, q_cols : q_cols + kv_cols
        ]
        dx_ref[
            :, pl.ds(pl.multiple_of(2 * q_cols + (2 + half) * kv_cols, kv_cols), kv_cols)
        ] = source[:, q_cols + kv_cols :]
    for apart, target in zip(apart_groups, terms):
        cut = target.shape[0]
        place = at(group ^ apart, cut)
        target[...] = (
            dot_nt(wq_ref[place], dx_ref[:, : 2 * q_cols])
            + dot_nt(wk_ref[place], dx_ref[:, 2 * q_cols : 2 * q_cols + 2 * kv_cols])
            + dot_nt(wv_ref[place], dx_ref[:, 2 * q_cols + 2 * kv_cols :])
        ).astype(target.dtype)


def weight_grad_kernel(attn_ref, dv_t_ref, got_ref, *refs):
    column_refs, refs = refs[:-6], refs[-6:]
    wvalue_ref, woutput_ref, done_ref, joined_ref, far_attn_ref, far_dv_ref = refs
    done_ref[...] = jnp.zeros_like(done_ref)
    me = lax.axis_index("seq")
    core = me % 2
    cut, rows = column_refs[0].shape[2:]
    for chip, ref in enumerate(column_refs):
        joined_ref[:, :, at(me ^ (2 * chip), rows)] = ref[0]
        for which in range(2):
            first = (2 * chip + which) * cut
            joined_ref[which, :, at(me ^ (2 * chip + 1), rows)] = got_ref[first : first + cut]
    first = 2 * len(column_refs) * cut
    for ref in (far_attn_ref, far_dv_ref):
        for block in range(ref.shape[1] // rows):
            ref[:, block * rows : (block + 1) * rows] = got_ref[first : first + ref.shape[0]]
            first += ref.shape[0]
    for half, attn, dv_t in ((core, attn_ref, dv_t_ref), (1 - core, far_attn_ref, far_dv_ref)):
        woutput_ref[:, at(half, attn.shape[0])] = dot_nt(joined_ref[1], attn[...])
        wvalue_ref[:, at(half, dv_t.shape[0])] = dot_nt(joined_ref[0], dv_t[...])


def add_kernel(own_ref, arrived_ref, _, sum_ref):
    total = own_ref[...].astype(jnp.float32) + arrived_ref[...].astype(jnp.float32)
    sum_ref[...] = total.astype(jnp.bfloat16)


def far_sum_kernel(_, own_ref, arrived_ref, sum_ref):
    sum_ref[...] = own_ref[...] + arrived_ref[...].astype(jnp.float32)


def sum_kernel(own_ref, *refs):
    total = own_ref[...]
    for arrived_ref in refs[:-1]:
        total = total + arrived_ref[...].astype(jnp.float32)
    refs[-1][...] = total.astype(jnp.bfloat16)


def kernel_call(
    body, outs, operands, in_vmem=(), scratch=(), flops=0, moved=0, room=16, aliases={}
):
    vmem = pl.BlockSpec(memory_space=pltpu.VMEM)
    hbm = pl.BlockSpec(memory_space=pltpu.HBM)
    return pl.pallas_call(
        body,
        out_shape=outs,
        in_specs=[vmem if place in in_vmem else hbm for place in range(len(operands))],
        out_specs=tuple(hbm if place in aliases.values() else vmem for place in range(len(outs))),
        input_output_aliases=aliases,
        scratch_shapes=list(scratch),
        compiler_params=pltpu.CompilerParams(vmem_limit_bytes=int(room * 1024 * 1024)),
        cost_estimate=pl.CostEstimate(flops=flops, bytes_accessed=moved, transcendentals=0),
    )(*operands)


def swapped(value, axis, apart):
    count = lax.axis_size(axis)
    return lax.ppermute(value, axis, [(place, place ^ apart) for place in range(count)])


def gathered_plan(
    normed_input,
    stored_queries,
    stored_keys,
    stored_values,
    query_weight,
    key_matrix,
    value_matrix,
    output_weight,
    out_cotangent,
):
    bf16, f32 = jnp.bfloat16, jnp.float32
    rows, model = normed_input.shape
    blocks = lax.axis_size("seq")
    groups = lax.axis_size("head")
    tokens = rows * blocks
    q_cols = stored_queries.shape[1] // 2
    kv_cols = HEAD_SIZE
    wide = 2 * QUERIES_PER_KEY * rows
    packed_cols = 2 * q_cols + 2 * kv_cols
    pieces = 3 if model % (6 * HEAD_SIZE) == 0 else 1
    shape = jax.ShapeDtypeStruct
    same, other = kernel_call(
        out_grad_kernel,
        (shape((rows, packed_cols), bf16),) * 2,
        (out_cotangent, output_weight, stored_queries, stored_keys, stored_values),
        scratch=(
            pltpu.VMEM(out_cotangent.shape, bf16),
            pltpu.VMEM(output_weight.shape, bf16),
            pltpu.SemaphoreType.DMA((6 + 3 * pieces,)),
        ),
        flops=4 * rows * model * q_cols,
        moved=2 * model * (rows + 2 * q_cols),
        room=63,
    )
    held = {0: same}
    for apart in range(2, blocks):
        lowest, highest = 2, 1 << (apart.bit_length() - 1)
        while not apart & lowest:
            lowest *= 2
        through = lowest if apart % 2 else highest
        if lowest == highest:
            held[apart] = swapped(other if apart % 2 else same, "seq", apart)
        else:
            held[apart] = swapped(held[apart ^ through], "seq", through)
    held[1] = swapped(other, "seq", 1)
    cut = model // blocks
    *columns, held[0] = kernel_call(
        turn_kernel,
        (shape((2, 2, cut, rows), bf16),) * (blocks // 2) + (shape(same.shape, bf16),),
        (normed_input, out_cotangent, same, held[2], held[blocks // 2 + 1]),
        in_vmem=range(3),
        scratch=(pltpu.VMEM((2, model, rows), bf16),),
        moved=8 * rows * model,
        room=8,
    )
    late = [chip for chip in range(1, blocks // 2) if not power_of_two(chip)]
    dx_own, dx_far, attn, prob, grad_t, *passed = kernel_call(
        functools.partial(attention_kernel, blocks, len(late)),
        (
            shape((rows, q_cols + 2 * kv_cols), bf16),
            shape((rows, q_cols + 2 * kv_cols), bf16),
            shape((q_cols, tokens), bf16),
            shape((tokens, tokens * QUERIES_PER_KEY), bf16),
            shape((HEAD_SIZE, tokens * QUERIES_PER_KEY), bf16),
        )
        + tuple(shape(columns[chip].shape, bf16) for chip in late),
        [held[apart] for apart in range(blocks)] + [columns[chip] for chip in late],
        in_vmem=range(blocks),
        aliases={blocks + place: 5 + place for place in range(len(late))},
        scratch=(
            pltpu.VMEM((tokens, packed_cols), bf16),
            pltpu.VMEM((tokens, wide), f32),
            pltpu.VMEM((tokens, wide), f32),
            pltpu.VMEM((1, tokens * QUERIES_PER_KEY), f32),
            pltpu.VMEM((tokens * QUERIES_PER_KEY, HEAD_SIZE), bf16),
            pltpu.VMEM((HEAD_SIZE, tokens), bf16),
            pltpu.VMEM((HEAD_SIZE, tokens), bf16),
            pltpu.VMEM((HEAD_SIZE, wide), f32),
            pltpu.VMEM((2 * rows, HEAD_SIZE), f32),
            pltpu.VMEM((2 * rows, HEAD_SIZE), f32),
        ),
        flops=8 * tokens * tokens * q_cols,
        moved=2 * tokens * packed_cols,
    )
    dx_got = swapped(dx_far, "seq", 1)
    for place, chip in enumerate(late):
        columns[chip] = passed[place]
    columns = [columns[0]] + [
        swapped(columns[chip], "seq", 2 * chip) for chip in range(1, blocks // 2)
    ]
    def terms_of(chosen):
        return kernel_call(
            functools.partial(input_terms_kernel, chosen),
            tuple(shape((model // groups, rows), f32 if not apart else bf16) for apart in chosen),
            (dx_own, dx_got, query_weight, key_matrix, value_matrix),
            in_vmem=range(5),
            scratch=(pltpu.VMEM((rows, 2 * (q_cols + 2 * kv_cols)), bf16),),
            flops=2 * len(chosen) * rows * (model // groups) * 2 * (q_cols + 2 * kv_cols),
            moved=2 * len(chosen) * (model // groups) * 2 * (q_cols + 2 * kv_cols),
            room=4,
        )

    (far_term,) = terms_of((3,))
    pair_term, near_term, own_term = terms_of((2, 1, 0))
    (dv_t,) = kernel_call(
        value_grad_kernel,
        (shape((kv_cols, tokens), bf16),),
        (prob, grad_t),
        in_vmem=range(2),
        flops=tokens * tokens * q_cols,
        moved=2 * tokens * tokens * QUERIES_PER_KEY,
        room=4,
    )
    (pair_sum,) = kernel_call(
        add_kernel,
        (shape(pair_term.shape, bf16),),
        (pair_term, swapped(far_term, "head", 1), dv_t),
        in_vmem=range(2),
        room=4,
    )
    part_rows = q_cols + kv_cols
    (give,) = kernel_call(
        pass_on_kernel,
        (shape((blocks * (cut + part_rows), rows), bf16),),
        (pair_sum, attn, dv_t, *columns),
        in_vmem=range(1, 3 + blocks // 2),
        room=4,
    )
    grad_wvalue, grad_woutput, weights_done = kernel_call(
        weight_grad_kernel,
        (
            shape((model // blocks, 2 * kv_cols), f32),
            shape((model // blocks, 2 * q_cols), f32),
            shape((8, HEAD_SIZE), f32),
        ),
        (attn, dv_t, swapped(give, "seq", 1), *columns),
        in_vmem=range(3 + blocks // 2),
        scratch=(
            pltpu.VMEM((2, model // blocks, tokens), bf16),
            pltpu.VMEM((q_cols, tokens), bf16),
            pltpu.VMEM((kv_cols, tokens), bf16),
        ),
        room=8,
    )
    (far_sum,) = kernel_call(
        far_sum_kernel,
        (shape((model // groups, rows), f32),),
        (weights_done, own_term, swapped(pair_sum, "head", 2)),
        in_vmem=range(1, 3),
        moved=10 * rows * (model // groups),
        room=4,
    )
    (grad_input,) = kernel_call(
        sum_kernel,
        (shape((model // groups, rows), bf16),),
        (far_sum, swapped(near_term, "head", 1)),
        in_vmem=range(2),
        moved=4 * groups * (model // groups) * rows,
    )
    return (grad_input.T, grad_wvalue, grad_woutput.T)


def power_of_two(count):
    return count & (count - 1) == 0


def local(normed_input, stored_queries, stored_keys, *others):
    blocks, groups = lax.axis_size("seq"), lax.axis_size("head")
    whole_window = normed_input.shape[0] * blocks <= WINDOW_LENGTH
    two_heads = stored_keys.shape[1] == 2 * HEAD_SIZE
    paired = blocks >= 4 and power_of_two(blocks) and groups == 4
    plan = gathered_plan if whole_window and two_heads and paired else windowed_plan
    return plan(normed_input, stored_queries, stored_keys, *others)


def windowed_plan(
    normed_input,
    stored_queries,
    stored_keys,
    stored_values,
    query_weight,
    key_matrix,
    value_matrix,
    output_weight,
    out_cotangent,
):
    tok_rows = normed_input.shape[0]
    blocks_seq = lax.axis_size("seq")
    seq_place = lax.axis_index("seq")
    reach_blocks = min(WINDOW_LENGTH // tok_rows, blocks_seq - 1)
    kv_heads = stored_keys.shape[1] // HEAD_SIZE
    output_gradient = jnp.dot(
        out_cotangent, output_weight.T, preferred_element_type=jnp.float32
    ).astype(jnp.bfloat16)
    pieces = [(stored_keys, stored_values)]
    current = (stored_keys, stored_values)
    for relay_step in range(reach_blocks):
        current = passed_along((current[0], current[1]), "seq", 1)
        pieces = [current] + pieces
    key_window = jnp.concatenate([piece[0] for piece in pieces], axis=0)
    value_window = jnp.concatenate([piece[1] for piece in pieces], axis=0)
    key_span = key_window.shape[0]
    query_pos = seq_place * tok_rows + jnp.arange(tok_rows, dtype=jnp.int32)
    key_pos = (seq_place - reach_blocks) * tok_rows + jnp.arange(key_span, dtype=jnp.int32)
    pos_gap = query_pos[:, None] - key_pos[None, :]
    allowed = (pos_gap >= 0) & (pos_gap < WINDOW_LENGTH) & (key_pos >= 0)[None, :]
    allowed_rows = jnp.tile(allowed, (QUERIES_PER_KEY, 1))
    query_stack = (
        stored_queries.reshape(tok_rows, kv_heads, QUERIES_PER_KEY, HEAD_SIZE)
        .transpose(1, 2, 0, 3)
        .reshape(kv_heads, QUERIES_PER_KEY * tok_rows, HEAD_SIZE)
    )
    grad_stack = (
        output_gradient.reshape(tok_rows, kv_heads, QUERIES_PER_KEY, HEAD_SIZE)
        .transpose(1, 2, 0, 3)
        .reshape(kv_heads, QUERIES_PER_KEY * tok_rows, HEAD_SIZE)
    )
    key_stack = key_window.reshape(key_span, kv_heads, HEAD_SIZE).transpose(1, 0, 2)
    value_stack = value_window.reshape(key_span, kv_heads, HEAD_SIZE).transpose(1, 0, 2)

    def per_head(head_items):
        query_head, key_head, value_head, grad_head = head_items
        attention_logits = logit_scale * jnp.dot(
            query_head, key_head.T, preferred_element_type=jnp.float32
        )
        masked = jnp.where(allowed_rows, attention_logits, -jnp.inf)
        row_top = jnp.max(masked, axis=1, keepdims=True)
        exp_scores = jnp.exp(masked - row_top)
        attn_prob = exp_scores / jnp.sum(exp_scores, axis=1, keepdims=True)
        probability_halfwidth = attn_prob.astype(jnp.bfloat16)
        attn_head = jnp.dot(
            probability_halfwidth, value_head, preferred_element_type=jnp.float32
        ).astype(jnp.bfloat16)
        row_delta = jnp.sum(
            grad_head.astype(jnp.float32) * attn_head.astype(jnp.float32), axis=1, keepdims=True
        )
        probability_gradient = jnp.dot(grad_head, value_head.T, preferred_element_type=jnp.float32)
        score_gradient = (attn_prob * (probability_gradient - row_delta)).astype(jnp.bfloat16)
        qgrad_head = (
            logit_scale * jnp.dot(score_gradient, key_head, preferred_element_type=jnp.float32)
        ).astype(jnp.bfloat16)
        key_partial = logit_scale * jnp.dot(
            score_gradient.T, query_head, preferred_element_type=jnp.float32
        )
        value_partial = jnp.dot(
            probability_halfwidth.T, grad_head, preferred_element_type=jnp.float32
        )
        return (attn_head, qgrad_head, key_partial, value_partial)

    attn_all, qgrad_all, key_all, value_all = lax.map(
        per_head, (query_stack, key_stack, value_stack, grad_stack)
    )
    attention_output = (
        attn_all.reshape(kv_heads, QUERIES_PER_KEY, tok_rows, HEAD_SIZE)
        .transpose(2, 0, 1, 3)
        .reshape(tok_rows, kv_heads * QUERIES_PER_KEY * HEAD_SIZE)
    )
    query_gradient = (
        qgrad_all.reshape(kv_heads, QUERIES_PER_KEY, tok_rows, HEAD_SIZE)
        .transpose(2, 0, 1, 3)
        .reshape(tok_rows, kv_heads * QUERIES_PER_KEY * HEAD_SIZE)
    )
    key_terms = key_all.transpose(1, 0, 2).reshape(key_span, kv_heads * HEAD_SIZE)
    value_terms = value_all.transpose(1, 0, 2).reshape(key_span, kv_heads * HEAD_SIZE)

    def take_slot(terms, slot_index):
        return terms[slot_index * tok_rows : (slot_index + 1) * tok_rows]

    key_sum = take_slot(key_terms, reach_blocks)
    value_sum = take_slot(value_terms, reach_blocks)
    for distance in range(1, reach_blocks + 1):
        received = passed_along(
            (
                take_slot(key_terms, reach_blocks - distance),
                take_slot(value_terms, reach_blocks - distance),
            ),
            "seq",
            -distance,
        )
        key_sum = key_sum + received[0]
        value_sum = value_sum + received[1]
    grad_key = key_sum.astype(jnp.bfloat16)
    grad_value = value_sum.astype(jnp.bfloat16)
    input_terms = jnp.dot(query_gradient, query_weight.T, preferred_element_type=jnp.float32)
    input_terms = input_terms + jnp.dot(grad_key, key_matrix.T, preferred_element_type=jnp.float32)
    input_terms = input_terms + jnp.dot(
        grad_value, value_matrix.T, preferred_element_type=jnp.float32
    )
    grad_input = lax.psum_scatter(input_terms, "head", scatter_dimension=1, tiled=True).astype(
        jnp.bfloat16
    )
    value_cols = grad_value.shape[1]
    input_cols = normed_input.T
    cot_cols = out_cotangent.T
    gathered = lax.psum_scatter(
        jnp.concatenate(
            [
                jnp.dot(input_cols, grad_value, preferred_element_type=jnp.float32),
                jnp.dot(cot_cols, attention_output, preferred_element_type=jnp.float32),
            ],
            axis=1,
        ),
        "seq",
        scatter_dimension=0,
        tiled=True,
    )
    grad_wvalue = gathered[:, :value_cols]
    grad_woutput = gathered[:, value_cols:].T
    return (grad_input, grad_wvalue, grad_woutput)


def solution(mesh):
    placed = (
        P("seq", None),
        P("seq", "head"),
        P("seq", "head"),
        P("seq", "head"),
        P(None, "head"),
        P(None, "head"),
        P(None, "head"),
        P("head", None),
        P("seq", None),
    )
    return jax.shard_map(
        local,
        mesh=mesh,
        in_specs=placed,
        out_specs=(P("seq", "head"), P("seq", "head"), P("head", "seq")),
        check_vma=False,
    )
```

```python
import functools

import jax
import jax.numpy as jnp
from jax import lax
from jax.experimental import pallas as pl
from jax.experimental.pallas import tpu as pltpu
from jax.sharding import PartitionSpec as P

HEAD_SIZE = 128
WINDOW_LENGTH = 4096
QUERIES_PER_KEY = 2


logit_scale = 1.0 / 12.0
log2_scale = 1.4426950408889634 / 12.0
excluded = -1e30


def passed_along(value, axis, steps):
    count = lax.axis_size(axis)
    leading, last = (max(0, -steps), min(count, count - steps))
    return lax.ppermute(value, axis, [(source, source + steps) for source in range(leading, last)])


NT = (((1,), (1,)), ((), ()))
ones_rows = 16


def dot_nt(left, right):
    return lax.dot_general(left, right, NT, preferred_element_type=jnp.float32)


def dot_nn(left, right):
    return jnp.dot(left, right, preferred_element_type=jnp.float32)


def at(place, size):
    return pl.ds(pl.multiple_of(place * size, size), size)


def out_grad_kernel(
    cot_hbm, weight_hbm, q_hbm, k_hbm, v_hbm, same_ref, other_ref, cot_ref, weight_ref, sem
):
    core = lax.axis_index("seq") % 2
    halves = ((other_ref, 1 - core), (same_ref, core))
    rows = weight_ref.shape[0] // 2
    pieces = (sem.shape[0] - 6) // 3
    cut = weight_ref.shape[1] // pieces
    model_copies = []
    for piece in range(pieces):
        part = pl.ds(piece * cut, cut)
        model_copies.append(
            [
                pltpu.make_async_copy(
                    cot_hbm.at[:, part], cot_ref.at[:, part], sem.at[6 + 3 * piece]
                )
            ]
        )
        for place, (_, half) in enumerate(halves):
            model_copies[-1].append(
                pltpu.make_async_copy(
                    weight_hbm.at[at(half, rows), part],
                    weight_ref.at[pl.ds(place * rows, rows), part],
                    sem.at[7 + 3 * piece + place],
                )
            )
        for copy in model_copies[-1]:
            copy.start()
    plain_copies = []
    for place, (target, half) in enumerate(halves):
        first = 0
        for which, source in enumerate((q_hbm, k_hbm, v_hbm)):
            cols = source.shape[1] // 2
            plain_copies.append(
                pltpu.make_async_copy(
                    source.at[:, at(half, cols)],
                    target.at[:, pl.ds(first, cols)],
                    sem.at[3 * place + which],
                )
            )
            plain_copies[-1].start()
            first += cols
    total = None
    for piece in range(pieces):
        for copy in model_copies[piece]:
            copy.wait()
        part = slice(piece * cut, (piece + 1) * cut)
        product = dot_nt(cot_ref[:, part], weight_ref[:, part])
        total = product if total is None else total + product
    for place, (target, _) in enumerate(halves):
        for head in range(rows // HEAD_SIZE):
            row = place * rows + head * HEAD_SIZE
            target[:, first + head * HEAD_SIZE : first + (head + 1) * HEAD_SIZE] = total[
                :, row : row + HEAD_SIZE
            ].T.astype(jnp.bfloat16)
    for copy in plain_copies:
        copy.wait()


def turn_kernel(normed_ref, cot_ref, block_ref, _, __, *refs):
    *column_refs, own_ref, turned_ref = refs
    me = lax.axis_index("seq")
    cut = column_refs[0].shape[2]
    own_ref[...] = block_ref[...]
    for which, ref in enumerate((normed_ref, cot_ref)):
        turned_ref[which] = ref[...].astype(jnp.float32).T.astype(jnp.bfloat16)
        for chip, target in enumerate(column_refs):
            for far in range(2):
                target[far, which] = turned_ref[which, at(me ^ (2 * chip + far), cut)]


def pass_on_kernel(_, attn_ref, dv_t_ref, *refs):
    *column_refs, give_ref = refs
    cut, rows = column_refs[0].shape[2:]
    for chip, ref in enumerate(column_refs):
        for which in range(2):
            first = (2 * chip + which) * cut
            give_ref[first : first + cut] = ref[1, which]
    first = 2 * len(column_refs) * cut
    for ref in (attn_ref, dv_t_ref):
        for block in range(ref.shape[1] // rows):
            give_ref[first : first + ref.shape[0]] = ref[:, block * rows : (block + 1) * rows]
            first += ref.shape[0]


def attention_kernel(blocks, *refs):
    attention_body(refs[:blocks], *refs[blocks:])


def attention_body(
    block_refs,
    dx_own_ref,
    dx_far_ref,
    attn_ref,
    prob_ref,
    grad_t_ref,
    gathered_ref,
    score_even_ref,
    score_odd_ref,
    delta_ref,
    query_ref,
    value_t_ref,
    key_t_ref,
    dq_t_ref,
    dk_ref,
    dv_ref,
):
    me = lax.axis_index("seq")
    core, chip = me % 2, me // 2
    rows = dx_own_ref.shape[0]
    for apart, source in enumerate(block_refs):
        gathered_ref[at(me ^ apart, rows)] = source[...]
    tokens = gathered_ref.shape[0]
    size = 2 * rows
    steps = tokens // size
    wide = QUERIES_PER_KEY * size
    heads = QUERIES_PER_KEY
    key_cols = slice(heads * HEAD_SIZE, (heads + 1) * HEAD_SIZE)
    value_cols = slice((heads + 1) * HEAD_SIZE, (heads + 2) * HEAD_SIZE)
    grad_base = (heads + 2) * HEAD_SIZE
    value_t_ref[:HEAD_SIZE] = gathered_ref[:, value_cols].T
    value_t_ref[HEAD_SIZE:] = jnp.ones((ones_rows, tokens), jnp.bfloat16)
    key_t_ref[...] = gathered_ref[:, key_cols].T
    key_place = lax.broadcasted_iota(jnp.int32, (size, wide), 0)
    query_place = lax.broadcasted_iota(jnp.int32, (size, wide), 1) % size
    allowed = key_place <= query_place

    def scored(step):
        own = slice(step * size, (step + 1) * size)
        score_ref = score_odd_ref if step % 2 else score_even_ref
        queries = jnp.concatenate(
            [gathered_ref[own, h * HEAD_SIZE : (h + 1) * HEAD_SIZE] for h in range(heads)], axis=0
        )
        query_ref[step * wide : (step + 1) * wide] = queries
        top = None
        for piece in range(step + 1):
            part = slice(piece * size, (piece + 1) * size)
            scores = dot_nt(gathered_ref[part, key_cols], queries)
            if piece == step:
                scores = jnp.where(allowed, scores, excluded)
            score_ref[part] = scores
            largest = jnp.max(scores.reshape(size // 8, 8, wide), axis=0)
            top = largest if top is None else jnp.maximum(top, largest)
        return top

    next_top = scored(steps - 1)
    for step in range(steps - 1, -1, -1):
        span = (step + 1) * size
        own = slice(step * size, span)
        lanes = slice(step * wide, (step + 1) * wide)
        score_ref = score_odd_ref if step % 2 else score_even_ref
        top = next_top
        if step:
            next_top = scored(step - 1)
        top = jnp.max(top, axis=0, keepdims=True)
        for piece in range(step + 1):
            part = slice(piece * size, (piece + 1) * size)
            weights = jnp.exp2((score_ref[part] - top) * log2_scale)
            prob_ref[part, lanes] = weights.astype(jnp.bfloat16)
        product = dot_nn(value_t_ref[:, :span], prob_ref[:span, lanes])
        inverse = 1.0 / product[HEAD_SIZE : HEAD_SIZE + 1]
        attn = product[:HEAD_SIZE] * inverse
        for h in range(heads):
            attn_ref[h * HEAD_SIZE : (h + 1) * HEAD_SIZE, own] = attn[
                :, h * size : (h + 1) * size
            ].astype(jnp.bfloat16)
        grads_t = jnp.concatenate(
            [
                gathered_ref[
                    block * rows : (block + 1) * rows,
                    grad_base + h * HEAD_SIZE : grad_base + (h + 1) * HEAD_SIZE,
                ]
                for h in range(heads)
                for block in (2 * step, 2 * step + 1)
            ],
            axis=1,
        )
        grads_t = (grads_t.astype(jnp.float32) * inverse).astype(jnp.bfloat16)
        grad_t_ref[:, lanes] = grads_t
        delta_ref[:, lanes] = jnp.sum(grads_t.astype(jnp.float32) * attn, axis=0, keepdims=True)

    dq_t_ref[...] = jnp.zeros_like(dq_t_ref)
    dk_ref[...] = jnp.zeros_like(dk_ref)
    dv_ref[...] = jnp.zeros_like(dv_ref)
    for step in range(steps):
        key_step = jnp.minimum(chip, step)
        query_step = jnp.maximum(chip, step)
        dprob = dot_nn(
            gathered_ref[at(key_step, size), value_cols], grad_t_ref[:, at(query_step, wide)]
        )
        prob = prob_ref[at(key_step, size), at(query_step, wide)]
        dscore = (
            prob.astype(jnp.float32)
            * (dprob - delta_ref[:, at(query_step, wide)])
        ).astype(jnp.bfloat16)

        @pl.when(step <= chip)
        def _():
            dq_t_ref[...] += dot_nn(key_t_ref[:, at(key_step, size)], dscore)

        @pl.when(step >= chip)
        def _():
            dk_ref[...] += dot_nn(dscore, query_ref[at(query_step, wide)])
            dv_ref[...] += dot_nt(prob, grad_t_ref[:, at(query_step, wide)])

    for target, half in ((dx_far_ref, 1 - core), (dx_own_ref, core)):
        for h in range(heads):
            target[:, h * HEAD_SIZE : (h + 1) * HEAD_SIZE] = (
                (logit_scale * dq_t_ref[:, at(2 * h + half, rows)])
                .T.astype(jnp.bfloat16)
            )
        target[:, key_cols] = (logit_scale * dk_ref[at(half, rows)]).astype(jnp.bfloat16)
        target[:, value_cols] = dv_ref[at(half, rows)].astype(jnp.bfloat16)


def value_grad_kernel(prob_ref, grad_t_ref, dv_t_ref):
    size = 2 * HEAD_SIZE
    wide = QUERIES_PER_KEY * size
    for step in range(prob_ref.shape[0] // size):
        own = slice(step * size, (step + 1) * size)
        dv_t_ref[:, own] = dot_nt(grad_t_ref[:, step * wide :], prob_ref[own, step * wide :]).astype(
            jnp.bfloat16
        )


def input_terms_kernel(apart_groups, own_ref, far_ref, wq_ref, wk_ref, wv_ref, *refs):
    terms, dx_ref = refs[-1 - len(apart_groups) : -1], refs[-1]
    core = lax.axis_index("seq") % 2
    group = lax.axis_index("head")
    q_cols = wq_ref.shape[1] // 2
    kv_cols = wk_ref.shape[1] // 2
    for source, half in ((own_ref, core), (far_ref, 1 - core)):
        dx_ref[:, at(half, q_cols)] = source[:, :q_cols]
        dx_ref[:, pl.ds(pl.multiple_of(2 * q_cols + half * kv_cols, kv_cols), kv_cols)] = source[
            :, q_cols : q_cols + kv_cols
        ]
        dx_ref[
            :, pl.ds(pl.multiple_of(2 * q_cols + (2 + half) * kv_cols, kv_cols), kv_cols)
        ] = source[:, q_cols + kv_cols :]
    for apart, target in zip(apart_groups, terms):
        cut = target.shape[0]
        place = at(group ^ apart, cut)
        target[...] = (
            dot_nt(wq_ref[place], dx_ref[:, : 2 * q_cols])
            + dot_nt(wk_ref[place], dx_ref[:, 2 * q_cols : 2 * q_cols + 2 * kv_cols])
            + dot_nt(wv_ref[place], dx_ref[:, 2 * q_cols + 2 * kv_cols :])
        ).astype(target.dtype)


def weight_grad_kernel(attn_ref, dv_t_ref, got_ref, *refs):
    column_refs, refs = refs[:-6], refs[-6:]
    wvalue_ref, woutput_ref, done_ref, joined_ref, far_attn_ref, far_dv_ref = refs
    done_ref[...] = jnp.zeros_like(done_ref)
    me = lax.axis_index("seq")
    core = me % 2
    cut, rows = column_refs[0].shape[2:]
    for chip, ref in enumerate(column_refs):
        joined_ref[:, :, at(me ^ (2 * chip), rows)] = ref[0]
        for which in range(2):
            first = (2 * chip + which) * cut
            joined_ref[which, :, at(me ^ (2 * chip + 1), rows)] = got_ref[first : first + cut]
    first = 2 * len(column_refs) * cut
    for ref in (far_attn_ref, far_dv_ref):
        for block in range(ref.shape[1] // rows):
            ref[:, block * rows : (block + 1) * rows] = got_ref[first : first + ref.shape[0]]
            first += ref.shape[0]
    for half, attn, dv_t in ((core, attn_ref, dv_t_ref), (1 - core, far_attn_ref, far_dv_ref)):
        woutput_ref[:, at(half, attn.shape[0])] = dot_nt(joined_ref[1], attn[...])
        wvalue_ref[:, at(half, dv_t.shape[0])] = dot_nt(joined_ref[0], dv_t[...])


def add_kernel(own_ref, arrived_ref, _, sum_ref):
    total = own_ref[...].astype(jnp.float32) + arrived_ref[...].astype(jnp.float32)
    sum_ref[...] = total.astype(jnp.bfloat16)


def far_sum_kernel(_, own_ref, arrived_ref, sum_ref):
    sum_ref[...] = own_ref[...] + arrived_ref[...].astype(jnp.float32)


def sum_kernel(own_ref, *refs):
    total = own_ref[...]
    for arrived_ref in refs[:-1]:
        total = total + arrived_ref[...].astype(jnp.float32)
    refs[-1][...] = total.astype(jnp.bfloat16)


def kernel_call(
    body, outs, operands, in_vmem=(), scratch=(), flops=0, moved=0, room=16
):
    vmem = pl.BlockSpec(memory_space=pltpu.VMEM)
    hbm = pl.BlockSpec(memory_space=pltpu.HBM)
    return pl.pallas_call(
        body,
        out_shape=outs,
        in_specs=[vmem if place in in_vmem else hbm for place in range(len(operands))],
        out_specs=(vmem,) * len(outs),
        scratch_shapes=list(scratch),
        compiler_params=pltpu.CompilerParams(vmem_limit_bytes=int(room * 1024 * 1024)),
        cost_estimate=pl.CostEstimate(flops=flops, bytes_accessed=moved, transcendentals=0),
    )(*operands)


def swapped(value, axis, apart):
    count = lax.axis_size(axis)
    return lax.ppermute(value, axis, [(place, place ^ apart) for place in range(count)])


def gathered_plan(
    normed_input,
    stored_queries,
    stored_keys,
    stored_values,
    query_weight,
    key_matrix,
    value_matrix,
    output_weight,
    out_cotangent,
):
    bf16, f32 = jnp.bfloat16, jnp.float32
    rows, model = normed_input.shape
    blocks = lax.axis_size("seq")
    groups = lax.axis_size("head")
    tokens = rows * blocks
    q_cols = stored_queries.shape[1] // 2
    kv_cols = HEAD_SIZE
    wide = 2 * QUERIES_PER_KEY * rows
    packed_cols = 2 * q_cols + 2 * kv_cols
    pieces = 3 if model % (6 * HEAD_SIZE) == 0 else 1
    shape = jax.ShapeDtypeStruct
    same, other = kernel_call(
        out_grad_kernel,
        (shape((rows, packed_cols), bf16),) * 2,
        (out_cotangent, output_weight, stored_queries, stored_keys, stored_values),
        scratch=(
            pltpu.VMEM(out_cotangent.shape, bf16),
            pltpu.VMEM(output_weight.shape, bf16),
            pltpu.SemaphoreType.DMA((6 + 3 * pieces,)),
        ),
        flops=4 * rows * model * q_cols,
        moved=2 * model * (rows + 2 * q_cols),
        room=63,
    )
    held = {0: same}
    for apart in range(2, blocks):
        lowest, highest = 2, 1 << (apart.bit_length() - 1)
        while not apart & lowest:
            lowest *= 2
        through = lowest if apart % 2 else highest
        if lowest == highest:
            held[apart] = swapped(other if apart % 2 else same, "seq", apart)
        else:
            held[apart] = swapped(held[apart ^ through], "seq", through)
    held[1] = swapped(other, "seq", 1)
    cut = model // blocks
    *columns, held[0] = kernel_call(
        turn_kernel,
        (shape((2, 2, cut, rows), bf16),) * (blocks // 2) + (shape(same.shape, bf16),),
        (normed_input, out_cotangent, same, held[2], held[blocks // 2 + 1]),
        in_vmem=range(3),
        scratch=(pltpu.VMEM((2, model, rows), bf16),),
        moved=8 * rows * model,
        room=8,
    )
    columns = [columns[0]] + [
        swapped(columns[chip], "seq", 2 * chip) for chip in range(1, blocks // 2)
    ]
    dx_own, dx_far, attn, prob, grad_t = kernel_call(
        functools.partial(attention_kernel, blocks),
        (
            shape((rows, q_cols + 2 * kv_cols), bf16),
            shape((rows, q_cols + 2 * kv_cols), bf16),
            shape((q_cols, tokens), bf16),
            shape((tokens, tokens * QUERIES_PER_KEY), bf16),
            shape((HEAD_SIZE, tokens * QUERIES_PER_KEY), bf16),
        ),
        [held[apart] for apart in range(blocks)],
        in_vmem=range(blocks),
        scratch=(
            pltpu.VMEM((tokens, packed_cols), bf16),
            pltpu.VMEM((tokens, wide), f32),
            pltpu.VMEM((tokens, wide), f32),
            pltpu.VMEM((1, tokens * QUERIES_PER_KEY), f32),
            pltpu.VMEM((tokens * QUERIES_PER_KEY, HEAD_SIZE), bf16),
            pltpu.VMEM((HEAD_SIZE + ones_rows, tokens), bf16),
            pltpu.VMEM((HEAD_SIZE, tokens), bf16),
            pltpu.VMEM((HEAD_SIZE, wide), f32),
            pltpu.VMEM((2 * rows, HEAD_SIZE), f32),
            pltpu.VMEM((2 * rows, HEAD_SIZE), f32),
        ),
        flops=8 * tokens * tokens * q_cols,
        moved=2 * tokens * packed_cols,
    )
    dx_got = swapped(dx_far, "seq", 1)
    def terms_of(chosen):
        return kernel_call(
            functools.partial(input_terms_kernel, chosen),
            tuple(shape((model // groups, rows), f32 if not apart else bf16) for apart in chosen),
            (dx_own, dx_got, query_weight, key_matrix, value_matrix),
            in_vmem=range(5),
            scratch=(pltpu.VMEM((rows, 2 * (q_cols + 2 * kv_cols)), bf16),),
            flops=2 * len(chosen) * rows * (model // groups) * 2 * (q_cols + 2 * kv_cols),
            moved=2 * len(chosen) * (model // groups) * 2 * (q_cols + 2 * kv_cols),
            room=4,
        )

    (far_term,) = terms_of((3,))
    pair_term, near_term, own_term = terms_of((2, 1, 0))
    (dv_t,) = kernel_call(
        value_grad_kernel,
        (shape((kv_cols, tokens), bf16),),
        (prob, grad_t),
        in_vmem=range(2),
        flops=tokens * tokens * q_cols,
        moved=2 * tokens * tokens * QUERIES_PER_KEY,
        room=4,
    )
    (pair_sum,) = kernel_call(
        add_kernel,
        (shape(pair_term.shape, bf16),),
        (pair_term, swapped(far_term, "head", 1), dv_t),
        in_vmem=range(2),
        room=4,
    )
    part_rows = q_cols + kv_cols
    (give,) = kernel_call(
        pass_on_kernel,
        (shape((blocks * (cut + part_rows), rows), bf16),),
        (pair_sum, attn, dv_t, *columns),
        in_vmem=range(1, 3 + blocks // 2),
        room=4,
    )
    grad_wvalue, grad_woutput, weights_done = kernel_call(
        weight_grad_kernel,
        (
            shape((model // blocks, 2 * kv_cols), f32),
            shape((model // blocks, 2 * q_cols), f32),
            shape((8, HEAD_SIZE), f32),
        ),
        (attn, dv_t, swapped(give, "seq", 1), *columns),
        in_vmem=range(3 + blocks // 2),
        scratch=(
            pltpu.VMEM((2, model // blocks, tokens), bf16),
            pltpu.VMEM((q_cols, tokens), bf16),
            pltpu.VMEM((kv_cols, tokens), bf16),
        ),
        room=8,
    )
    (far_sum,) = kernel_call(
        far_sum_kernel,
        (shape((model // groups, rows), f32),),
        (weights_done, own_term, swapped(pair_sum, "head", 2)),
        in_vmem=range(1, 3),
        moved=10 * rows * (model // groups),
        room=4,
    )
    (grad_input,) = kernel_call(
        sum_kernel,
        (shape((model // groups, rows), bf16),),
        (far_sum, swapped(near_term, "head", 1)),
        in_vmem=range(2),
        moved=4 * groups * (model // groups) * rows,
    )
    return (grad_input.T, grad_wvalue, grad_woutput.T)


def power_of_two(count):
    return count & (count - 1) == 0


def local(normed_input, stored_queries, stored_keys, *others):
    blocks, groups = lax.axis_size("seq"), lax.axis_size("head")
    whole_window = normed_input.shape[0] * blocks <= WINDOW_LENGTH
    two_heads = stored_keys.shape[1] == 2 * HEAD_SIZE
    paired = blocks >= 4 and power_of_two(blocks) and groups == 4
    plan = gathered_plan if whole_window and two_heads and paired else windowed_plan
    return plan(normed_input, stored_queries, stored_keys, *others)


def windowed_plan(
    normed_input,
    stored_queries,
    stored_keys,
    stored_values,
    query_weight,
    key_matrix,
    value_matrix,
    output_weight,
    out_cotangent,
):
    tok_rows = normed_input.shape[0]
    blocks_seq = lax.axis_size("seq")
    seq_place = lax.axis_index("seq")
    reach_blocks = min(WINDOW_LENGTH // tok_rows, blocks_seq - 1)
    kv_heads = stored_keys.shape[1] // HEAD_SIZE
    output_gradient = jnp.dot(
        out_cotangent, output_weight.T, preferred_element_type=jnp.float32
    ).astype(jnp.bfloat16)
    pieces = [(stored_keys, stored_values)]
    current = (stored_keys, stored_values)
    for relay_step in range(reach_blocks):
        current = passed_along((current[0], current[1]), "seq", 1)
        pieces = [current] + pieces
    key_window = jnp.concatenate([piece[0] for piece in pieces], axis=0)
    value_window = jnp.concatenate([piece[1] for piece in pieces], axis=0)
    key_span = key_window.shape[0]
    query_pos = seq_place * tok_rows + jnp.arange(tok_rows, dtype=jnp.int32)
    key_pos = (seq_place - reach_blocks) * tok_rows + jnp.arange(key_span, dtype=jnp.int32)
    pos_gap = query_pos[:, None] - key_pos[None, :]
    allowed = (pos_gap >= 0) & (pos_gap < WINDOW_LENGTH) & (key_pos >= 0)[None, :]
    allowed_rows = jnp.tile(allowed, (QUERIES_PER_KEY, 1))
    query_stack = (
        stored_queries.reshape(tok_rows, kv_heads, QUERIES_PER_KEY, HEAD_SIZE)
        .transpose(1, 2, 0, 3)
        .reshape(kv_heads, QUERIES_PER_KEY * tok_rows, HEAD_SIZE)
    )
    grad_stack = (
        output_gradient.reshape(tok_rows, kv_heads, QUERIES_PER_KEY, HEAD_SIZE)
        .transpose(1, 2, 0, 3)
        .reshape(kv_heads, QUERIES_PER_KEY * tok_rows, HEAD_SIZE)
    )
    key_stack = key_window.reshape(key_span, kv_heads, HEAD_SIZE).transpose(1, 0, 2)
    value_stack = value_window.reshape(key_span, kv_heads, HEAD_SIZE).transpose(1, 0, 2)

    def per_head(head_items):
        query_head, key_head, value_head, grad_head = head_items
        attention_logits = logit_scale * jnp.dot(
            query_head, key_head.T, preferred_element_type=jnp.float32
        )
        masked = jnp.where(allowed_rows, attention_logits, -jnp.inf)
        row_top = jnp.max(masked, axis=1, keepdims=True)
        exp_scores = jnp.exp(masked - row_top)
        attn_prob = exp_scores / jnp.sum(exp_scores, axis=1, keepdims=True)
        probability_halfwidth = attn_prob.astype(jnp.bfloat16)
        attn_head = jnp.dot(
            probability_halfwidth, value_head, preferred_element_type=jnp.float32
        ).astype(jnp.bfloat16)
        row_delta = jnp.sum(
            grad_head.astype(jnp.float32) * attn_head.astype(jnp.float32), axis=1, keepdims=True
        )
        probability_gradient = jnp.dot(grad_head, value_head.T, preferred_element_type=jnp.float32)
        score_gradient = (attn_prob * (probability_gradient - row_delta)).astype(jnp.bfloat16)
        qgrad_head = (
            logit_scale * jnp.dot(score_gradient, key_head, preferred_element_type=jnp.float32)
        ).astype(jnp.bfloat16)
        key_partial = logit_scale * jnp.dot(
            score_gradient.T, query_head, preferred_element_type=jnp.float32
        )
        value_partial = jnp.dot(
            probability_halfwidth.T, grad_head, preferred_element_type=jnp.float32
        )
        return (attn_head, qgrad_head, key_partial, value_partial)

    attn_all, qgrad_all, key_all, value_all = lax.map(
        per_head, (query_stack, key_stack, value_stack, grad_stack)
    )
    attention_output = (
        attn_all.reshape(kv_heads, QUERIES_PER_KEY, tok_rows, HEAD_SIZE)
        .transpose(2, 0, 1, 3)
        .reshape(tok_rows, kv_heads * QUERIES_PER_KEY * HEAD_SIZE)
    )
    query_gradient = (
        qgrad_all.reshape(kv_heads, QUERIES_PER_KEY, tok_rows, HEAD_SIZE)
        .transpose(2, 0, 1, 3)
        .reshape(tok_rows, kv_heads * QUERIES_PER_KEY * HEAD_SIZE)
    )
    key_terms = key_all.transpose(1, 0, 2).reshape(key_span, kv_heads * HEAD_SIZE)
    value_terms = value_all.transpose(1, 0, 2).reshape(key_span, kv_heads * HEAD_SIZE)

    def take_slot(terms, slot_index):
        return terms[slot_index * tok_rows : (slot_index + 1) * tok_rows]

    key_sum = take_slot(key_terms, reach_blocks)
    value_sum = take_slot(value_terms, reach_blocks)
    for distance in range(1, reach_blocks + 1):
        received = passed_along(
            (
                take_slot(key_terms, reach_blocks - distance),
                take_slot(value_terms, reach_blocks - distance),
            ),
            "seq",
            -distance,
        )
        key_sum = key_sum + received[0]
        value_sum = value_sum + received[1]
    grad_key = key_sum.astype(jnp.bfloat16)
    grad_value = value_sum.astype(jnp.bfloat16)
    input_terms = jnp.dot(query_gradient, query_weight.T, preferred_element_type=jnp.float32)
    input_terms = input_terms + jnp.dot(grad_key, key_matrix.T, preferred_element_type=jnp.float32)
    input_terms = input_terms + jnp.dot(
        grad_value, value_matrix.T, preferred_element_type=jnp.float32
    )
    grad_input = lax.psum_scatter(input_terms, "head", scatter_dimension=1, tiled=True).astype(
        jnp.bfloat16
    )
    value_cols = grad_value.shape[1]
    input_cols = normed_input.T
    cot_cols = out_cotangent.T
    gathered = lax.psum_scatter(
        jnp.concatenate(
            [
                jnp.dot(input_cols, grad_value, preferred_element_type=jnp.float32),
                jnp.dot(cot_cols, attention_output, preferred_element_type=jnp.float32),
            ],
            axis=1,
        ),
        "seq",
        scatter_dimension=0,
        tiled=True,
    )
    grad_wvalue = gathered[:, :value_cols]
    grad_woutput = gathered[:, value_cols:].T
    return (grad_input, grad_wvalue, grad_woutput)


def solution(mesh):
    placed = (
        P("seq", None),
        P("seq", "head"),
        P("seq", "head"),
        P("seq", "head"),
        P(None, "head"),
        P(None, "head"),
        P(None, "head"),
        P("head", None),
        P("seq", None),
    )
    return jax.shard_map(
        local,
        mesh=mesh,
        in_specs=placed,
        out_specs=(P("seq", "head"), P("seq", "head"), P("head", "seq")),
        check_vma=False,
    )
```

```python
import functools

import jax
import jax.numpy as jnp
from jax import lax
from jax.experimental import pallas as pl
from jax.experimental.pallas import tpu as pltpu
from jax.sharding import PartitionSpec as P

HEAD_SIZE = 128
WINDOW_LENGTH = 4096
QUERIES_PER_KEY = 2


logit_scale = 1.0 / 12.0
log2_scale = 1.4426950408889634 / 12.0
excluded = -1e30


def passed_along(value, axis, steps):
    count = lax.axis_size(axis)
    leading, last = (max(0, -steps), min(count, count - steps))
    return lax.ppermute(value, axis, [(source, source + steps) for source in range(leading, last)])


NT = (((1,), (1,)), ((), ()))


def dot_nt(left, right):
    return lax.dot_general(left, right, NT, preferred_element_type=jnp.float32)


def dot_nn(left, right):
    return jnp.dot(left, right, preferred_element_type=jnp.float32)


def at(place, size):
    return pl.ds(pl.multiple_of(place * size, size), size)


def out_grad_kernel(
    cot_hbm, weight_hbm, q_hbm, k_hbm, v_hbm, same_hbm, other_hbm, cot_ref, weight_ref, half_ref, sem
):
    core = lax.axis_index("seq") % 2
    halves = ((other_hbm, 1 - core), (same_hbm, core))
    rows = weight_ref.shape[0] // 2
    pieces = (sem.shape[0] - 10) // 3
    cut = weight_ref.shape[1] // pieces
    model_copies = []
    for piece in range(pieces):
        part = pl.ds(piece * cut, cut)
        model_copies.append(
            [
                pltpu.make_async_copy(
                    cot_hbm.at[:, part], cot_ref.at[:, part], sem.at[6 + 3 * piece]
                )
            ]
        )
        for place, (_, half) in enumerate(halves):
            model_copies[-1].append(
                pltpu.make_async_copy(
                    weight_hbm.at[at(half, rows), part],
                    weight_ref.at[pl.ds(place * rows, rows), part],
                    sem.at[7 + 3 * piece + place],
                )
            )
        for copy in model_copies[-1]:
            copy.start()
    plain_copies = []
    for place, (target, half) in enumerate(halves):
        first = 0
        for which, source in enumerate((q_hbm, k_hbm, v_hbm)):
            cols = source.shape[1] // 2
            plain_copies.append(
                pltpu.make_async_copy(
                    source.at[:, at(half, cols)],
                    half_ref.at[place, :, pl.ds(first, cols)],
                    sem.at[3 * place + which],
                )
            )
            plain_copies[-1].start()
            first += cols
    out_copies = []
    for place, (target, _) in enumerate(halves):
        for which, cols in enumerate((pl.ds(0, first), pl.ds(first, target.shape[1] - first))):
            out_copies.append(
                pltpu.make_async_copy(
                    half_ref.at[place, :, cols],
                    target.at[:, cols],
                    sem.at[6 + 3 * pieces + 2 * place + which],
                )
            )
    total = None
    for piece in range(pieces):
        for copy in model_copies[piece]:
            copy.wait()
        part = slice(piece * cut, (piece + 1) * cut)
        product = dot_nt(cot_ref[:, part], weight_ref[:, part])
        total = product if total is None else total + product
        if piece == 0:
            for copy in plain_copies:
                copy.wait()
            out_copies[0].start()
            out_copies[2].start()
    for place in range(2):
        for head in range(rows // HEAD_SIZE):
            row = place * rows + head * HEAD_SIZE
            half_ref[place, :, first + head * HEAD_SIZE : first + (head + 1) * HEAD_SIZE] = total[
                :, row : row + HEAD_SIZE
            ].T.astype(jnp.bfloat16)
        out_copies[2 * place + 1].start()
    for copy in out_copies:
        copy.wait()


def turn_kernel(normed_ref, cot_ref, block_ref, _, __, *refs):
    *column_refs, own_ref, turned_ref = refs
    me = lax.axis_index("seq")
    cut = column_refs[0].shape[2]
    own_ref[...] = block_ref[...]
    for which, ref in enumerate((normed_ref, cot_ref)):
        turned_ref[which] = ref[...].astype(jnp.float32).T.astype(jnp.bfloat16)
        for chip, target in enumerate(column_refs):
            for far in range(2):
                target[far, which] = turned_ref[which, at(me ^ (2 * chip + far), cut)]


def pass_on_kernel(_, attn_ref, dv_t_ref, *refs):
    *column_refs, give_ref = refs
    cut, rows = column_refs[0].shape[2:]
    for chip, ref in enumerate(column_refs):
        for which in range(2):
            first = (2 * chip + which) * cut
            give_ref[first : first + cut] = ref[1, which]
    first = 2 * len(column_refs) * cut
    for ref in (attn_ref, dv_t_ref):
        for block in range(ref.shape[1] // rows):
            give_ref[first : first + ref.shape[0]] = ref[:, block * rows : (block + 1) * rows]
            first += ref.shape[0]


def attention_kernel(blocks, *refs):
    attention_body(refs[:blocks], *refs[blocks:])


def attention_body(
    block_refs,
    dx_own_ref,
    dx_far_ref,
    attn_ref,
    prob_ref,
    grad_t_ref,
    gathered_ref,
    score_even_ref,
    score_odd_ref,
    delta_ref,
    query_ref,
    value_t_ref,
    key_t_ref,
    dq_t_ref,
    dk_ref,
    dv_ref,
):
    me = lax.axis_index("seq")
    core, chip = me % 2, me // 2
    rows = dx_own_ref.shape[0]
    for apart, source in enumerate(block_refs):
        gathered_ref[at(me ^ apart, rows)] = source[...]
    tokens = gathered_ref.shape[0]
    size = 2 * rows
    steps = tokens // size
    wide = QUERIES_PER_KEY * size
    heads = QUERIES_PER_KEY
    key_cols = slice(heads * HEAD_SIZE, (heads + 1) * HEAD_SIZE)
    value_cols = slice((heads + 1) * HEAD_SIZE, (heads + 2) * HEAD_SIZE)
    grad_base = (heads + 2) * HEAD_SIZE
    value_t_ref[...] = gathered_ref[:, value_cols].T
    key_t_ref[...] = gathered_ref[:, key_cols].T
    key_place = lax.broadcasted_iota(jnp.int32, (size, wide), 0)
    query_place = lax.broadcasted_iota(jnp.int32, (size, wide), 1) % size
    allowed = key_place <= query_place

    def scored(step):
        own = slice(step * size, (step + 1) * size)
        score_ref = score_odd_ref if step % 2 else score_even_ref
        queries = jnp.concatenate(
            [gathered_ref[own, h * HEAD_SIZE : (h + 1) * HEAD_SIZE] for h in range(heads)], axis=0
        )
        query_ref[step * wide : (step + 1) * wide] = queries
        top = None
        for piece in range(step + 1):
            part = slice(piece * size, (piece + 1) * size)
            scores = dot_nt(gathered_ref[part, key_cols], queries)
            if piece == step:
                scores = jnp.where(allowed, scores, excluded)
            score_ref[part] = scores
            largest = jnp.max(scores.reshape(size // 8, 8, wide), axis=0)
            top = largest if top is None else jnp.maximum(top, largest)
        return top

    next_top = scored(steps - 1)
    for step in range(steps - 1, -1, -1):
        span = (step + 1) * size
        own = slice(step * size, span)
        lanes = slice(step * wide, (step + 1) * wide)
        score_ref = score_odd_ref if step % 2 else score_even_ref
        top = next_top
        if step:
            next_top = scored(step - 1)
        top = jnp.max(top, axis=0, keepdims=True)
        total = None
        for piece in range(step + 1):
            part = slice(piece * size, (piece + 1) * size)
            weights = jnp.exp2((score_ref[part] - top) * log2_scale)
            prob_ref[part, lanes] = weights.astype(jnp.bfloat16)
            summed = jnp.sum(weights.reshape(size // 8, 8, wide), axis=0)
            total = summed if total is None else total + summed
        inverse = 1.0 / jnp.sum(total, axis=0, keepdims=True)
        attn = dot_nn(value_t_ref[:, :span], prob_ref[:span, lanes]) * inverse
        for h in range(heads):
            attn_ref[h * HEAD_SIZE : (h + 1) * HEAD_SIZE, own] = attn[
                :, h * size : (h + 1) * size
            ].astype(jnp.bfloat16)
        grads_t = jnp.concatenate(
            [
                gathered_ref[
                    block * rows : (block + 1) * rows,
                    grad_base + h * HEAD_SIZE : grad_base + (h + 1) * HEAD_SIZE,
                ]
                for h in range(heads)
                for block in (2 * step, 2 * step + 1)
            ],
            axis=1,
        )
        grads_t = (grads_t.astype(jnp.float32) * inverse).astype(jnp.bfloat16)
        grad_t_ref[:, lanes] = grads_t
        delta_ref[:, lanes] = jnp.sum(grads_t.astype(jnp.float32) * attn, axis=0, keepdims=True)

    dq_t_ref[...] = jnp.zeros_like(dq_t_ref)
    dk_ref[...] = jnp.zeros_like(dk_ref)
    dv_ref[...] = jnp.zeros_like(dv_ref)
    for step in range(steps):
        key_step = jnp.minimum(chip, step)
        query_step = jnp.maximum(chip, step)
        dprob = dot_nn(
            gathered_ref[at(key_step, size), value_cols], grad_t_ref[:, at(query_step, wide)]
        )
        prob = prob_ref[at(key_step, size), at(query_step, wide)]
        dscore = (
            prob.astype(jnp.float32)
            * (dprob - delta_ref[:, at(query_step, wide)])
        ).astype(jnp.bfloat16)

        @pl.when(step <= chip)
        def _():
            dq_t_ref[...] += dot_nn(key_t_ref[:, at(key_step, size)], dscore)

        @pl.when(step >= chip)
        def _():
            dk_ref[...] += dot_nn(dscore, query_ref[at(query_step, wide)])
            dv_ref[...] += dot_nt(prob, grad_t_ref[:, at(query_step, wide)])

    for target, half in ((dx_far_ref, 1 - core), (dx_own_ref, core)):
        for h in range(heads):
            target[:, h * HEAD_SIZE : (h + 1) * HEAD_SIZE] = (
                (logit_scale * dq_t_ref[:, at(2 * h + half, rows)])
                .T.astype(jnp.bfloat16)
            )
        target[:, key_cols] = (logit_scale * dk_ref[at(half, rows)]).astype(jnp.bfloat16)
        target[:, value_cols] = dv_ref[at(half, rows)].astype(jnp.bfloat16)


def value_grad_kernel(prob_ref, grad_t_ref, dv_t_ref):
    size = 2 * HEAD_SIZE
    wide = QUERIES_PER_KEY * size
    for step in range(prob_ref.shape[0] // size):
        own = slice(step * size, (step + 1) * size)
        dv_t_ref[:, own] = dot_nt(grad_t_ref[:, step * wide :], prob_ref[own, step * wide :]).astype(
            jnp.bfloat16
        )


def input_terms_kernel(apart_groups, own_ref, far_ref, wq_ref, wk_ref, wv_ref, *refs):
    terms, dx_ref = refs[-1 - len(apart_groups) : -1], refs[-1]
    core = lax.axis_index("seq") % 2
    group = lax.axis_index("head")
    q_cols = wq_ref.shape[1] // 2
    kv_cols = wk_ref.shape[1] // 2
    for source, half in ((own_ref, core), (far_ref, 1 - core)):
        dx_ref[:, at(half, q_cols)] = source[:, :q_cols]
        dx_ref[:, pl.ds(pl.multiple_of(2 * q_cols + half * kv_cols, kv_cols), kv_cols)] = source[
            :, q_cols : q_cols + kv_cols
        ]
        dx_ref[
            :, pl.ds(pl.multiple_of(2 * q_cols + (2 + half) * kv_cols, kv_cols), kv_cols)
        ] = source[:, q_cols + kv_cols :]
    for apart, target in zip(apart_groups, terms):
        cut = target.shape[0]
        place = at(group ^ apart, cut)
        target[...] = (
            dot_nt(wq_ref[place], dx_ref[:, : 2 * q_cols])
            + dot_nt(wk_ref[place], dx_ref[:, 2 * q_cols : 2 * q_cols + 2 * kv_cols])
            + dot_nt(wv_ref[place], dx_ref[:, 2 * q_cols + 2 * kv_cols :])
        ).astype(target.dtype)


def weight_grad_kernel(attn_ref, dv_t_ref, got_ref, *refs):
    column_refs, refs = refs[:-6], refs[-6:]
    wvalue_ref, woutput_ref, done_ref, joined_ref, far_attn_ref, far_dv_ref = refs
    done_ref[...] = jnp.zeros_like(done_ref)
    me = lax.axis_index("seq")
    core = me % 2
    cut, rows = column_refs[0].shape[2:]
    for chip, ref in enumerate(column_refs):
        joined_ref[:, :, at(me ^ (2 * chip), rows)] = ref[0]
        for which in range(2):
            first = (2 * chip + which) * cut
            joined_ref[which, :, at(me ^ (2 * chip + 1), rows)] = got_ref[first : first + cut]
    first = 2 * len(column_refs) * cut
    for ref in (far_attn_ref, far_dv_ref):
        for block in range(ref.shape[1] // rows):
            ref[:, block * rows : (block + 1) * rows] = got_ref[first : first + ref.shape[0]]
            first += ref.shape[0]
    for half, attn, dv_t in ((core, attn_ref, dv_t_ref), (1 - core, far_attn_ref, far_dv_ref)):
        woutput_ref[:, at(half, attn.shape[0])] = dot_nt(joined_ref[1], attn[...])
        wvalue_ref[:, at(half, dv_t.shape[0])] = dot_nt(joined_ref[0], dv_t[...])


def add_kernel(own_ref, arrived_ref, _, sum_ref):
    total = own_ref[...].astype(jnp.float32) + arrived_ref[...].astype(jnp.float32)
    sum_ref[...] = total.astype(jnp.bfloat16)


def far_sum_kernel(_, own_ref, arrived_ref, sum_ref):
    sum_ref[...] = own_ref[...] + arrived_ref[...].astype(jnp.float32)


def sum_kernel(own_ref, *refs):
    total = own_ref[...]
    for arrived_ref in refs[:-1]:
        total = total + arrived_ref[...].astype(jnp.float32)
    refs[-1][...] = total.astype(jnp.bfloat16)


def kernel_call(
    body, outs, operands, in_vmem=(), scratch=(), flops=0, moved=0, room=16, out_vmem=True
):
    vmem = pl.BlockSpec(memory_space=pltpu.VMEM)
    hbm = pl.BlockSpec(memory_space=pltpu.HBM)
    return pl.pallas_call(
        body,
        out_shape=outs,
        in_specs=[vmem if place in in_vmem else hbm for place in range(len(operands))],
        out_specs=(vmem if out_vmem else hbm,) * len(outs),
        scratch_shapes=list(scratch),
        compiler_params=pltpu.CompilerParams(vmem_limit_bytes=int(room * 1024 * 1024)),
        cost_estimate=pl.CostEstimate(flops=flops, bytes_accessed=moved, transcendentals=0),
    )(*operands)


def swapped(value, axis, apart):
    count = lax.axis_size(axis)
    return lax.ppermute(value, axis, [(place, place ^ apart) for place in range(count)])


def gathered_plan(
    normed_input,
    stored_queries,
    stored_keys,
    stored_values,
    query_weight,
    key_matrix,
    value_matrix,
    output_weight,
    out_cotangent,
):
    bf16, f32 = jnp.bfloat16, jnp.float32
    rows, model = normed_input.shape
    blocks = lax.axis_size("seq")
    groups = lax.axis_size("head")
    tokens = rows * blocks
    q_cols = stored_queries.shape[1] // 2
    kv_cols = HEAD_SIZE
    wide = 2 * QUERIES_PER_KEY * rows
    packed_cols = 2 * q_cols + 2 * kv_cols
    pieces = 3 if model % (6 * HEAD_SIZE) == 0 else 1
    shape = jax.ShapeDtypeStruct
    same, other = kernel_call(
        out_grad_kernel,
        (shape((rows, packed_cols), bf16),) * 2,
        (out_cotangent, output_weight, stored_queries, stored_keys, stored_values),
        scratch=(
            pltpu.VMEM(out_cotangent.shape, bf16),
            pltpu.VMEM(output_weight.shape, bf16),
            pltpu.VMEM((2, rows, packed_cols), bf16),
            pltpu.SemaphoreType.DMA((10 + 3 * pieces,)),
        ),
        flops=4 * rows * model * q_cols,
        moved=2 * model * (rows + 2 * q_cols),
        room=63,
        out_vmem=False,
    )
    held = {0: same}
    for apart in range(2, blocks):
        lowest, highest = 2, 1 << (apart.bit_length() - 1)
        while not apart & lowest:
            lowest *= 2
        through = lowest if apart % 2 else highest
        if lowest == highest:
            held[apart] = swapped(other if apart % 2 else same, "seq", apart)
        else:
            held[apart] = swapped(held[apart ^ through], "seq", through)
    held[1] = swapped(other, "seq", 1)
    cut = model // blocks
    *columns, held[0] = kernel_call(
        turn_kernel,
        (shape((2, 2, cut, rows), bf16),) * (blocks // 2) + (shape(same.shape, bf16),),
        (normed_input, out_cotangent, same, held[2], held[blocks // 2 + 1]),
        in_vmem=range(3),
        scratch=(pltpu.VMEM((2, model, rows), bf16),),
        moved=8 * rows * model,
        room=8,
    )
    columns = [columns[0]] + [
        swapped(columns[chip], "seq", 2 * chip) for chip in range(1, blocks // 2)
    ]
    dx_own, dx_far, attn, prob, grad_t = kernel_call(
        functools.partial(attention_kernel, blocks),
        (
            shape((rows, q_cols + 2 * kv_cols), bf16),
            shape((rows, q_cols + 2 * kv_cols), bf16),
            shape((q_cols, tokens), bf16),
            shape((tokens, tokens * QUERIES_PER_KEY), bf16),
            shape((HEAD_SIZE, tokens * QUERIES_PER_KEY), bf16),
        ),
        [held[apart] for apart in range(blocks)],
        in_vmem=range(blocks),
        scratch=(
            pltpu.VMEM((tokens, packed_cols), bf16),
            pltpu.VMEM((tokens, wide), f32),
            pltpu.VMEM((tokens, wide), f32),
            pltpu.VMEM((1, tokens * QUERIES_PER_KEY), f32),
            pltpu.VMEM((tokens * QUERIES_PER_KEY, HEAD_SIZE), bf16),
            pltpu.VMEM((HEAD_SIZE, tokens), bf16),
            pltpu.VMEM((HEAD_SIZE, tokens), bf16),
            pltpu.VMEM((HEAD_SIZE, wide), f32),
            pltpu.VMEM((2 * rows, HEAD_SIZE), f32),
            pltpu.VMEM((2 * rows, HEAD_SIZE), f32),
        ),
        flops=8 * tokens * tokens * q_cols,
        moved=2 * tokens * packed_cols,
    )
    dx_got = swapped(dx_far, "seq", 1)
    def terms_of(chosen):
        return kernel_call(
            functools.partial(input_terms_kernel, chosen),
            tuple(shape((model // groups, rows), f32 if not apart else bf16) for apart in chosen),
            (dx_own, dx_got, query_weight, key_matrix, value_matrix),
            in_vmem=range(5),
            scratch=(pltpu.VMEM((rows, 2 * (q_cols + 2 * kv_cols)), bf16),),
            flops=2 * len(chosen) * rows * (model // groups) * 2 * (q_cols + 2 * kv_cols),
            moved=2 * len(chosen) * (model // groups) * 2 * (q_cols + 2 * kv_cols),
            room=4,
        )

    (far_term,) = terms_of((3,))
    pair_term, near_term, own_term = terms_of((2, 1, 0))
    (dv_t,) = kernel_call(
        value_grad_kernel,
        (shape((kv_cols, tokens), bf16),),
        (prob, grad_t),
        in_vmem=range(2),
        flops=tokens * tokens * q_cols,
        moved=2 * tokens * tokens * QUERIES_PER_KEY,
        room=4,
    )
    (pair_sum,) = kernel_call(
        add_kernel,
        (shape(pair_term.shape, bf16),),
        (pair_term, swapped(far_term, "head", 1), dv_t),
        in_vmem=range(2),
        room=4,
    )
    part_rows = q_cols + kv_cols
    (give,) = kernel_call(
        pass_on_kernel,
        (shape((blocks * (cut + part_rows), rows), bf16),),
        (pair_sum, attn, dv_t, *columns),
        in_vmem=range(1, 3 + blocks // 2),
        room=4,
    )
    grad_wvalue, grad_woutput, weights_done = kernel_call(
        weight_grad_kernel,
        (
            shape((model // blocks, 2 * kv_cols), f32),
            shape((model // blocks, 2 * q_cols), f32),
            shape((8, HEAD_SIZE), f32),
        ),
        (attn, dv_t, swapped(give, "seq", 1), *columns),
        in_vmem=range(3 + blocks // 2),
        scratch=(
            pltpu.VMEM((2, model // blocks, tokens), bf16),
            pltpu.VMEM((q_cols, tokens), bf16),
            pltpu.VMEM((kv_cols, tokens), bf16),
        ),
        room=8,
    )
    (far_sum,) = kernel_call(
        far_sum_kernel,
        (shape((model // groups, rows), f32),),
        (weights_done, own_term, swapped(pair_sum, "head", 2)),
        in_vmem=range(1, 3),
        moved=10 * rows * (model // groups),
        room=4,
    )
    (grad_input,) = kernel_call(
        sum_kernel,
        (shape((model // groups, rows), bf16),),
        (far_sum, swapped(near_term, "head", 1)),
        in_vmem=range(2),
        moved=4 * groups * (model // groups) * rows,
    )
    return (grad_input.T, grad_wvalue, grad_woutput.T)


def power_of_two(count):
    return count & (count - 1) == 0


def local(normed_input, stored_queries, stored_keys, *others):
    blocks, groups = lax.axis_size("seq"), lax.axis_size("head")
    whole_window = normed_input.shape[0] * blocks <= WINDOW_LENGTH
    two_heads = stored_keys.shape[1] == 2 * HEAD_SIZE
    paired = blocks >= 4 and power_of_two(blocks) and groups == 4
    plan = gathered_plan if whole_window and two_heads and paired else windowed_plan
    return plan(normed_input, stored_queries, stored_keys, *others)


def windowed_plan(
    normed_input,
    stored_queries,
    stored_keys,
    stored_values,
    query_weight,
    key_matrix,
    value_matrix,
    output_weight,
    out_cotangent,
):
    tok_rows = normed_input.shape[0]
    blocks_seq = lax.axis_size("seq")
    seq_place = lax.axis_index("seq")
    reach_blocks = min(WINDOW_LENGTH // tok_rows, blocks_seq - 1)
    kv_heads = stored_keys.shape[1] // HEAD_SIZE
    output_gradient = jnp.dot(
        out_cotangent, output_weight.T, preferred_element_type=jnp.float32
    ).astype(jnp.bfloat16)
    pieces = [(stored_keys, stored_values)]
    current = (stored_keys, stored_values)
    for relay_step in range(reach_blocks):
        current = passed_along((current[0], current[1]), "seq", 1)
        pieces = [current] + pieces
    key_window = jnp.concatenate([piece[0] for piece in pieces], axis=0)
    value_window = jnp.concatenate([piece[1] for piece in pieces], axis=0)
    key_span = key_window.shape[0]
    query_pos = seq_place * tok_rows + jnp.arange(tok_rows, dtype=jnp.int32)
    key_pos = (seq_place - reach_blocks) * tok_rows + jnp.arange(key_span, dtype=jnp.int32)
    pos_gap = query_pos[:, None] - key_pos[None, :]
    allowed = (pos_gap >= 0) & (pos_gap < WINDOW_LENGTH) & (key_pos >= 0)[None, :]
    allowed_rows = jnp.tile(allowed, (QUERIES_PER_KEY, 1))
    query_stack = (
        stored_queries.reshape(tok_rows, kv_heads, QUERIES_PER_KEY, HEAD_SIZE)
        .transpose(1, 2, 0, 3)
        .reshape(kv_heads, QUERIES_PER_KEY * tok_rows, HEAD_SIZE)
    )
    grad_stack = (
        output_gradient.reshape(tok_rows, kv_heads, QUERIES_PER_KEY, HEAD_SIZE)
        .transpose(1, 2, 0, 3)
        .reshape(kv_heads, QUERIES_PER_KEY * tok_rows, HEAD_SIZE)
    )
    key_stack = key_window.reshape(key_span, kv_heads, HEAD_SIZE).transpose(1, 0, 2)
    value_stack = value_window.reshape(key_span, kv_heads, HEAD_SIZE).transpose(1, 0, 2)

    def per_head(head_items):
        query_head, key_head, value_head, grad_head = head_items
        attention_logits = logit_scale * jnp.dot(
            query_head, key_head.T, preferred_element_type=jnp.float32
        )
        masked = jnp.where(allowed_rows, attention_logits, -jnp.inf)
        row_top = jnp.max(masked, axis=1, keepdims=True)
        exp_scores = jnp.exp(masked - row_top)
        attn_prob = exp_scores / jnp.sum(exp_scores, axis=1, keepdims=True)
        probability_halfwidth = attn_prob.astype(jnp.bfloat16)
        attn_head = jnp.dot(
            probability_halfwidth, value_head, preferred_element_type=jnp.float32
        ).astype(jnp.bfloat16)
        row_delta = jnp.sum(
            grad_head.astype(jnp.float32) * attn_head.astype(jnp.float32), axis=1, keepdims=True
        )
        probability_gradient = jnp.dot(grad_head, value_head.T, preferred_element_type=jnp.float32)
        score_gradient = (attn_prob * (probability_gradient - row_delta)).astype(jnp.bfloat16)
        qgrad_head = (
            logit_scale * jnp.dot(score_gradient, key_head, preferred_element_type=jnp.float32)
        ).astype(jnp.bfloat16)
        key_partial = logit_scale * jnp.dot(
            score_gradient.T, query_head, preferred_element_type=jnp.float32
        )
        value_partial = jnp.dot(
            probability_halfwidth.T, grad_head, preferred_element_type=jnp.float32
        )
        return (attn_head, qgrad_head, key_partial, value_partial)

    attn_all, qgrad_all, key_all, value_all = lax.map(
        per_head, (query_stack, key_stack, value_stack, grad_stack)
    )
    attention_output = (
        attn_all.reshape(kv_heads, QUERIES_PER_KEY, tok_rows, HEAD_SIZE)
        .transpose(2, 0, 1, 3)
        .reshape(tok_rows, kv_heads * QUERIES_PER_KEY * HEAD_SIZE)
    )
    query_gradient = (
        qgrad_all.reshape(kv_heads, QUERIES_PER_KEY, tok_rows, HEAD_SIZE)
        .transpose(2, 0, 1, 3)
        .reshape(tok_rows, kv_heads * QUERIES_PER_KEY * HEAD_SIZE)
    )
    key_terms = key_all.transpose(1, 0, 2).reshape(key_span, kv_heads * HEAD_SIZE)
    value_terms = value_all.transpose(1, 0, 2).reshape(key_span, kv_heads * HEAD_SIZE)

    def take_slot(terms, slot_index):
        return terms[slot_index * tok_rows : (slot_index + 1) * tok_rows]

    key_sum = take_slot(key_terms, reach_blocks)
    value_sum = take_slot(value_terms, reach_blocks)
    for distance in range(1, reach_blocks + 1):
        received = passed_along(
            (
                take_slot(key_terms, reach_blocks - distance),
                take_slot(value_terms, reach_blocks - distance),
            ),
            "seq",
            -distance,
        )
        key_sum = key_sum + received[0]
        value_sum = value_sum + received[1]
    grad_key = key_sum.astype(jnp.bfloat16)
    grad_value = value_sum.astype(jnp.bfloat16)
    input_terms = jnp.dot(query_gradient, query_weight.T, preferred_element_type=jnp.float32)
    input_terms = input_terms + jnp.dot(grad_key, key_matrix.T, preferred_element_type=jnp.float32)
    input_terms = input_terms + jnp.dot(
        grad_value, value_matrix.T, preferred_element_type=jnp.float32
    )
    grad_input = lax.psum_scatter(input_terms, "head", scatter_dimension=1, tiled=True).astype(
        jnp.bfloat16
    )
    value_cols = grad_value.shape[1]
    input_cols = normed_input.T
    cot_cols = out_cotangent.T
    gathered = lax.psum_scatter(
        jnp.concatenate(
            [
                jnp.dot(input_cols, grad_value, preferred_element_type=jnp.float32),
                jnp.dot(cot_cols, attention_output, preferred_element_type=jnp.float32),
            ],
            axis=1,
        ),
        "seq",
        scatter_dimension=0,
        tiled=True,
    )
    grad_wvalue = gathered[:, :value_cols]
    grad_woutput = gathered[:, value_cols:].T
    return (grad_input, grad_wvalue, grad_woutput)


def solution(mesh):
    placed = (
        P("seq", None),
        P("seq", "head"),
        P("seq", "head"),
        P("seq", "head"),
        P(None, "head"),
        P(None, "head"),
        P(None, "head"),
        P("head", None),
        P("seq", None),
    )
    return jax.shard_map(
        local,
        mesh=mesh,
        in_specs=placed,
        out_specs=(P("seq", "head"), P("seq", "head"), P("head", "seq")),
        check_vma=False,
    )
```

```python
import functools

import jax
import jax.numpy as jnp
from jax import lax
from jax.experimental import pallas as pl
from jax.experimental.pallas import tpu as pltpu
from jax.sharding import PartitionSpec as P

HEAD_SIZE = 128
WINDOW_LENGTH = 4096
QUERIES_PER_KEY = 2


logit_scale = 1.0 / 12.0
log2_scale = 1.4426950408889634 / 12.0
excluded = -1e30


def passed_along(value, axis, steps):
    count = lax.axis_size(axis)
    leading, last = (max(0, -steps), min(count, count - steps))
    return lax.ppermute(value, axis, [(source, source + steps) for source in range(leading, last)])


NT = (((1,), (1,)), ((), ()))


def dot_nt(left, right):
    return lax.dot_general(left, right, NT, preferred_element_type=jnp.float32)


def dot_nn(left, right):
    return jnp.dot(left, right, preferred_element_type=jnp.float32)


def at(place, size):
    return pl.ds(pl.multiple_of(place * size, size), size)


def out_grad_kernel(
    cot_hbm, weight_hbm, q_hbm, k_hbm, v_hbm, same_ref, other_ref, cot_ref, weight_ref, sem
):
    core = lax.axis_index("seq") % 2
    halves = ((other_ref, 1 - core), (same_ref, core))
    rows = weight_ref.shape[0] // 2
    pieces = (sem.shape[0] - 6) // 3
    cut = weight_ref.shape[1] // pieces
    model_copies = []
    for piece in range(pieces):
        part = pl.ds(piece * cut, cut)
        model_copies.append(
            [
                pltpu.make_async_copy(
                    cot_hbm.at[:, part], cot_ref.at[:, part], sem.at[6 + 3 * piece]
                )
            ]
        )
        for place, (_, half) in enumerate(halves):
            model_copies[-1].append(
                pltpu.make_async_copy(
                    weight_hbm.at[at(half, rows), part],
                    weight_ref.at[pl.ds(place * rows, rows), part],
                    sem.at[7 + 3 * piece + place],
                )
            )
        for copy in model_copies[-1]:
            copy.start()
    plain_copies = []
    for place, (target, half) in enumerate(halves):
        first = 0
        for which, source in enumerate((q_hbm, k_hbm, v_hbm)):
            cols = source.shape[1] // 2
            plain_copies.append(
                pltpu.make_async_copy(
                    source.at[:, at(half, cols)],
                    target.at[:, pl.ds(first, cols)],
                    sem.at[3 * place + which],
                )
            )
            plain_copies[-1].start()
            first += cols
    total = None
    for piece in range(pieces):
        for copy in model_copies[piece]:
            copy.wait()
        part = slice(piece * cut, (piece + 1) * cut)
        product = dot_nt(cot_ref[:, part], weight_ref[:, part])
        total = product if total is None else total + product
    for place, (target, _) in enumerate(halves):
        for head in range(rows // HEAD_SIZE):
            row = place * rows + head * HEAD_SIZE
            target[:, first + head * HEAD_SIZE : first + (head + 1) * HEAD_SIZE] = total[
                :, row : row + HEAD_SIZE
            ].T.astype(jnp.bfloat16)
    for copy in plain_copies:
        copy.wait()


def hold_kernel(same_ref, other_ref, kept_same_ref, kept_other_ref):
    kept_same_ref[...] = same_ref[...]
    kept_other_ref[...] = other_ref[...]


def turn_kernel(normed_ref, cot_ref, _, __, *refs):
    *column_refs, turned_ref = refs
    me = lax.axis_index("seq")
    cut = column_refs[0].shape[2]
    for which, ref in enumerate((normed_ref, cot_ref)):
        turned_ref[which] = ref[...].astype(jnp.float32).T.astype(jnp.bfloat16)
        for chip, target in enumerate(column_refs):
            for far in range(2):
                target[far, which] = turned_ref[which, at(me ^ (2 * chip + far), cut)]


def pass_on_kernel(_, attn_ref, dv_t_ref, *refs):
    *column_refs, give_ref = refs
    cut, rows = column_refs[0].shape[2:]
    for chip, ref in enumerate(column_refs):
        for which in range(2):
            first = (2 * chip + which) * cut
            give_ref[first : first + cut] = ref[1, which]
    first = 2 * len(column_refs) * cut
    for ref in (attn_ref, dv_t_ref):
        for block in range(ref.shape[1] // rows):
            give_ref[first : first + ref.shape[0]] = ref[:, block * rows : (block + 1) * rows]
            first += ref.shape[0]


def attention_kernel(blocks, *refs):
    attention_body(refs[:blocks], *refs[blocks:])


def attention_body(
    block_refs,
    dx_own_ref,
    dx_far_ref,
    attn_ref,
    prob_ref,
    grad_t_ref,
    gathered_ref,
    score_even_ref,
    score_odd_ref,
    delta_ref,
    query_ref,
    value_t_ref,
    key_t_ref,
    dq_t_ref,
    dk_ref,
    dv_ref,
):
    me = lax.axis_index("seq")
    core, chip = me % 2, me // 2
    rows = dx_own_ref.shape[0]
    for apart, source in enumerate(block_refs):
        gathered_ref[at(me ^ apart, rows)] = source[...]
    tokens = gathered_ref.shape[0]
    size = 2 * rows
    steps = tokens // size
    wide = QUERIES_PER_KEY * size
    heads = QUERIES_PER_KEY
    key_cols = slice(heads * HEAD_SIZE, (heads + 1) * HEAD_SIZE)
    value_cols = slice((heads + 1) * HEAD_SIZE, (heads + 2) * HEAD_SIZE)
    grad_base = (heads + 2) * HEAD_SIZE
    value_t_ref[...] = gathered_ref[:, value_cols].T
    key_t_ref[...] = gathered_ref[:, key_cols].T
    key_place = lax.broadcasted_iota(jnp.int32, (size, wide), 0)
    query_place = lax.broadcasted_iota(jnp.int32, (size, wide), 1) % size
    allowed = key_place <= query_place

    def scored(step):
        own = slice(step * size, (step + 1) * size)
        score_ref = score_odd_ref if step % 2 else score_even_ref
        queries = jnp.concatenate(
            [gathered_ref[own, h * HEAD_SIZE : (h + 1) * HEAD_SIZE] for h in range(heads)], axis=0
        )
        query_ref[step * wide : (step + 1) * wide] = queries
        top = None
        for piece in range(step + 1):
            part = slice(piece * size, (piece + 1) * size)
            scores = dot_nt(gathered_ref[part, key_cols], queries)
            if piece == step:
                scores = jnp.where(allowed, scores, excluded)
            score_ref[part] = scores
            largest = jnp.max(scores.reshape(size // 8, 8, wide), axis=0)
            top = largest if top is None else jnp.maximum(top, largest)
        return top

    next_top = scored(steps - 1)
    for step in range(steps - 1, -1, -1):
        span = (step + 1) * size
        own = slice(step * size, span)
        lanes = slice(step * wide, (step + 1) * wide)
        score_ref = score_odd_ref if step % 2 else score_even_ref
        top = next_top
        if step:
            next_top = scored(step - 1)
        top = jnp.max(top, axis=0, keepdims=True)
        total = None
        for piece in range(step + 1):
            part = slice(piece * size, (piece + 1) * size)
            weights = jnp.exp2((score_ref[part] - top) * log2_scale)
            prob_ref[part, lanes] = weights.astype(jnp.bfloat16)
            summed = jnp.sum(weights.reshape(size // 8, 8, wide), axis=0)
            total = summed if total is None else total + summed
        inverse = 1.0 / jnp.sum(total, axis=0, keepdims=True)
        attn = dot_nn(value_t_ref[:, :span], prob_ref[:span, lanes]) * inverse
        for h in range(heads):
            attn_ref[h * HEAD_SIZE : (h + 1) * HEAD_SIZE, own] = attn[
                :, h * size : (h + 1) * size
            ].astype(jnp.bfloat16)
        grads_t = jnp.concatenate(
            [
                gathered_ref[
                    block * rows : (block + 1) * rows,
                    grad_base + h * HEAD_SIZE : grad_base + (h + 1) * HEAD_SIZE,
                ]
                for h in range(heads)
                for block in (2 * step, 2 * step + 1)
            ],
            axis=1,
        )
        grads_t = (grads_t.astype(jnp.float32) * inverse).astype(jnp.bfloat16)
        grad_t_ref[:, lanes] = grads_t
        delta_ref[:, lanes] = jnp.sum(grads_t.astype(jnp.float32) * attn, axis=0, keepdims=True)

    dq_t_ref[...] = jnp.zeros_like(dq_t_ref)
    dk_ref[...] = jnp.zeros_like(dk_ref)
    dv_ref[...] = jnp.zeros_like(dv_ref)
    for step in range(steps):
        key_step = jnp.minimum(chip, step)
        query_step = jnp.maximum(chip, step)
        dprob = dot_nn(
            gathered_ref[at(key_step, size), value_cols], grad_t_ref[:, at(query_step, wide)]
        )
        prob = prob_ref[at(key_step, size), at(query_step, wide)]
        dscore = (
            prob.astype(jnp.float32)
            * (dprob - delta_ref[:, at(query_step, wide)])
        ).astype(jnp.bfloat16)

        @pl.when(step <= chip)
        def _():
            dq_t_ref[...] += dot_nn(key_t_ref[:, at(key_step, size)], dscore)

        @pl.when(step >= chip)
        def _():
            dk_ref[...] += dot_nn(dscore, query_ref[at(query_step, wide)])
            dv_ref[...] += dot_nt(prob, grad_t_ref[:, at(query_step, wide)])

    for target, half in ((dx_far_ref, 1 - core), (dx_own_ref, core)):
        for h in range(heads):
            target[:, h * HEAD_SIZE : (h + 1) * HEAD_SIZE] = (
                (logit_scale * dq_t_ref[:, at(2 * h + half, rows)])
                .T.astype(jnp.bfloat16)
            )
        target[:, key_cols] = (logit_scale * dk_ref[at(half, rows)]).astype(jnp.bfloat16)
        target[:, value_cols] = dv_ref[at(half, rows)].astype(jnp.bfloat16)


def value_grad_kernel(prob_ref, grad_t_ref, dv_t_ref):
    size = 2 * HEAD_SIZE
    wide = QUERIES_PER_KEY * size
    for step in range(prob_ref.shape[0] // size):
        own = slice(step * size, (step + 1) * size)
        dv_t_ref[:, own] = dot_nt(grad_t_ref[:, step * wide :], prob_ref[own, step * wide :]).astype(
            jnp.bfloat16
        )


def input_terms_kernel(apart_groups, own_ref, far_ref, wq_ref, wk_ref, wv_ref, *refs):
    terms, dx_ref = refs[-1 - len(apart_groups) : -1], refs[-1]
    core = lax.axis_index("seq") % 2
    group = lax.axis_index("head")
    q_cols = wq_ref.shape[1] // 2
    kv_cols = wk_ref.shape[1] // 2
    for source, half in ((own_ref, core), (far_ref, 1 - core)):
        dx_ref[:, at(half, q_cols)] = source[:, :q_cols]
        dx_ref[:, pl.ds(pl.multiple_of(2 * q_cols + half * kv_cols, kv_cols), kv_cols)] = source[
            :, q_cols : q_cols + kv_cols
        ]
        dx_ref[
            :, pl.ds(pl.multiple_of(2 * q_cols + (2 + half) * kv_cols, kv_cols), kv_cols)
        ] = source[:, q_cols + kv_cols :]
    for apart, target in zip(apart_groups, terms):
        cut = target.shape[0]
        place = at(group ^ apart, cut)
        target[...] = (
            dot_nt(wq_ref[place], dx_ref[:, : 2 * q_cols])
            + dot_nt(wk_ref[place], dx_ref[:, 2 * q_cols : 2 * q_cols + 2 * kv_cols])
            + dot_nt(wv_ref[place], dx_ref[:, 2 * q_cols + 2 * kv_cols :])
        ).astype(target.dtype)


def weight_grad_kernel(attn_ref, dv_t_ref, got_ref, *refs):
    column_refs, refs = refs[:-6], refs[-6:]
    wvalue_ref, woutput_ref, done_ref, joined_ref, far_attn_ref, far_dv_ref = refs
    done_ref[...] = jnp.zeros_like(done_ref)
    me = lax.axis_index("seq")
    core = me % 2
    cut, rows = column_refs[0].shape[2:]
    for chip, ref in enumerate(column_refs):
        joined_ref[:, :, at(me ^ (2 * chip), rows)] = ref[0]
        for which in range(2):
            first = (2 * chip + which) * cut
            joined_ref[which, :, at(me ^ (2 * chip + 1), rows)] = got_ref[first : first + cut]
    first = 2 * len(column_refs) * cut
    for ref in (far_attn_ref, far_dv_ref):
        for block in range(ref.shape[1] // rows):
            ref[:, block * rows : (block + 1) * rows] = got_ref[first : first + ref.shape[0]]
            first += ref.shape[0]
    for half, attn, dv_t in ((core, attn_ref, dv_t_ref), (1 - core, far_attn_ref, far_dv_ref)):
        woutput_ref[:, at(half, attn.shape[0])] = dot_nt(joined_ref[1], attn[...])
        wvalue_ref[:, at(half, dv_t.shape[0])] = dot_nt(joined_ref[0], dv_t[...])


def add_kernel(own_ref, arrived_ref, _, sum_ref):
    total = own_ref[...].astype(jnp.float32) + arrived_ref[...].astype(jnp.float32)
    sum_ref[...] = total.astype(jnp.bfloat16)


def far_sum_kernel(_, own_ref, arrived_ref, sum_ref):
    sum_ref[...] = own_ref[...] + arrived_ref[...].astype(jnp.float32)


def sum_kernel(own_ref, *refs):
    total = own_ref[...]
    for arrived_ref in refs[:-1]:
        total = total + arrived_ref[...].astype(jnp.float32)
    refs[-1][...] = total.astype(jnp.bfloat16)


def kernel_call(
    body, outs, operands, in_vmem=(), scratch=(), flops=0, moved=0, room=16
):
    vmem = pl.BlockSpec(memory_space=pltpu.VMEM)
    hbm = pl.BlockSpec(memory_space=pltpu.HBM)
    return pl.pallas_call(
        body,
        out_shape=outs,
        in_specs=[vmem if place in in_vmem else hbm for place in range(len(operands))],
        out_specs=(vmem,) * len(outs),
        scratch_shapes=list(scratch),
        compiler_params=pltpu.CompilerParams(vmem_limit_bytes=int(room * 1024 * 1024)),
        cost_estimate=pl.CostEstimate(flops=flops, bytes_accessed=moved, transcendentals=0),
    )(*operands)


def swapped(value, axis, apart):
    count = lax.axis_size(axis)
    return lax.ppermute(value, axis, [(place, place ^ apart) for place in range(count)])


def gathered_plan(
    normed_input,
    stored_queries,
    stored_keys,
    stored_values,
    query_weight,
    key_matrix,
    value_matrix,
    output_weight,
    out_cotangent,
):
    bf16, f32 = jnp.bfloat16, jnp.float32
    rows, model = normed_input.shape
    blocks = lax.axis_size("seq")
    groups = lax.axis_size("head")
    tokens = rows * blocks
    q_cols = stored_queries.shape[1] // 2
    kv_cols = HEAD_SIZE
    wide = 2 * QUERIES_PER_KEY * rows
    packed_cols = 2 * q_cols + 2 * kv_cols
    pieces = 3 if model % (6 * HEAD_SIZE) == 0 else 1
    shape = jax.ShapeDtypeStruct
    same, other = kernel_call(
        out_grad_kernel,
        (shape((rows, packed_cols), bf16),) * 2,
        (out_cotangent, output_weight, stored_queries, stored_keys, stored_values),
        scratch=(
            pltpu.VMEM(out_cotangent.shape, bf16),
            pltpu.VMEM(output_weight.shape, bf16),
            pltpu.SemaphoreType.DMA((6 + 3 * pieces,)),
        ),
        flops=4 * rows * model * q_cols,
        moved=2 * model * (rows + 2 * q_cols),
        room=63,
    )
    kept_same, kept_other = kernel_call(
        hold_kernel,
        (shape(same.shape, bf16),) * 2,
        (same, other),
        in_vmem=range(2),
        moved=8 * rows * packed_cols,
        room=4,
    )
    held = {0: kept_same}
    for apart in range(2, blocks):
        lowest, highest = 2, 1 << (apart.bit_length() - 1)
        while not apart & lowest:
            lowest *= 2
        through = lowest if apart % 2 else highest
        if lowest == highest:
            first = apart in (2, blocks // 2 + 1)
            even, odd = (same, other) if first else (kept_same, kept_other)
            held[apart] = swapped(odd if apart % 2 else even, "seq", apart)
        else:
            held[apart] = swapped(held[apart ^ through], "seq", through)
    held[1] = swapped(other, "seq", 1)
    cut = model // blocks
    columns = kernel_call(
        turn_kernel,
        (shape((2, 2, cut, rows), bf16),) * (blocks // 2),
        (normed_input, out_cotangent, held[2], held[blocks // 2 + 1]),
        in_vmem=range(2),
        scratch=(pltpu.VMEM((2, model, rows), bf16),),
        moved=8 * rows * model,
        room=8,
    )
    columns = [columns[0]] + [
        swapped(columns[chip], "seq", 2 * chip) for chip in range(1, blocks // 2)
    ]
    dx_own, dx_far, attn, prob, grad_t = kernel_call(
        functools.partial(attention_kernel, blocks),
        (
            shape((rows, q_cols + 2 * kv_cols), bf16),
            shape((rows, q_cols + 2 * kv_cols), bf16),
            shape((q_cols, tokens), bf16),
            shape((tokens, tokens * QUERIES_PER_KEY), bf16),
            shape((HEAD_SIZE, tokens * QUERIES_PER_KEY), bf16),
        ),
        [held[apart] for apart in range(blocks)],
        in_vmem=range(blocks),
        scratch=(
            pltpu.VMEM((tokens, packed_cols), bf16),
            pltpu.VMEM((tokens, wide), f32),
            pltpu.VMEM((tokens, wide), f32),
            pltpu.VMEM((1, tokens * QUERIES_PER_KEY), f32),
            pltpu.VMEM((tokens * QUERIES_PER_KEY, HEAD_SIZE), bf16),
            pltpu.VMEM((HEAD_SIZE, tokens), bf16),
            pltpu.VMEM((HEAD_SIZE, tokens), bf16),
            pltpu.VMEM((HEAD_SIZE, wide), f32),
            pltpu.VMEM((2 * rows, HEAD_SIZE), f32),
            pltpu.VMEM((2 * rows, HEAD_SIZE), f32),
        ),
        flops=8 * tokens * tokens * q_cols,
        moved=2 * tokens * packed_cols,
    )
    dx_got = swapped(dx_far, "seq", 1)
    def terms_of(chosen):
        return kernel_call(
            functools.partial(input_terms_kernel, chosen),
            tuple(shape((model // groups, rows), f32 if not apart else bf16) for apart in chosen),
            (dx_own, dx_got, query_weight, key_matrix, value_matrix),
            in_vmem=range(5),
            scratch=(pltpu.VMEM((rows, 2 * (q_cols + 2 * kv_cols)), bf16),),
            flops=2 * len(chosen) * rows * (model // groups) * 2 * (q_cols + 2 * kv_cols),
            moved=2 * len(chosen) * (model // groups) * 2 * (q_cols + 2 * kv_cols),
            room=4,
        )

    (far_term,) = terms_of((3,))
    pair_term, near_term, own_term = terms_of((2, 1, 0))
    (dv_t,) = kernel_call(
        value_grad_kernel,
        (shape((kv_cols, tokens), bf16),),
        (prob, grad_t),
        in_vmem=range(2),
        flops=tokens * tokens * q_cols,
        moved=2 * tokens * tokens * QUERIES_PER_KEY,
        room=4,
    )
    (pair_sum,) = kernel_call(
        add_kernel,
        (shape(pair_term.shape, bf16),),
        (pair_term, swapped(far_term, "head", 1), dv_t),
        in_vmem=range(2),
        room=4,
    )
    part_rows = q_cols + kv_cols
    (give,) = kernel_call(
        pass_on_kernel,
        (shape((blocks * (cut + part_rows), rows), bf16),),
        (pair_sum, attn, dv_t, *columns),
        in_vmem=range(1, 3 + blocks // 2),
        room=4,
    )
    grad_wvalue, grad_woutput, weights_done = kernel_call(
        weight_grad_kernel,
        (
            shape((model // blocks, 2 * kv_cols), f32),
            shape((model // blocks, 2 * q_cols), f32),
            shape((8, HEAD_SIZE), f32),
        ),
        (attn, dv_t, swapped(give, "seq", 1), *columns),
        in_vmem=range(3 + blocks // 2),
        scratch=(
            pltpu.VMEM((2, model // blocks, tokens), bf16),
            pltpu.VMEM((q_cols, tokens), bf16),
            pltpu.VMEM((kv_cols, tokens), bf16),
        ),
        room=8,
    )
    (far_sum,) = kernel_call(
        far_sum_kernel,
        (shape((model // groups, rows), f32),),
        (weights_done, own_term, swapped(pair_sum, "head", 2)),
        in_vmem=range(1, 3),
        moved=10 * rows * (model // groups),
        room=4,
    )
    (grad_input,) = kernel_call(
        sum_kernel,
        (shape((model // groups, rows), bf16),),
        (far_sum, swapped(near_term, "head", 1)),
        in_vmem=range(2),
        moved=4 * groups * (model // groups) * rows,
    )
    return (grad_input.T, grad_wvalue, grad_woutput.T)


def power_of_two(count):
    return count & (count - 1) == 0


def local(normed_input, stored_queries, stored_keys, *others):
    blocks, groups = lax.axis_size("seq"), lax.axis_size("head")
    whole_window = normed_input.shape[0] * blocks <= WINDOW_LENGTH
    two_heads = stored_keys.shape[1] == 2 * HEAD_SIZE
    paired = blocks >= 4 and power_of_two(blocks) and groups == 4
    plan = gathered_plan if whole_window and two_heads and paired else windowed_plan
    return plan(normed_input, stored_queries, stored_keys, *others)


def windowed_plan(
    normed_input,
    stored_queries,
    stored_keys,
    stored_values,
    query_weight,
    key_matrix,
    value_matrix,
    output_weight,
    out_cotangent,
):
    tok_rows = normed_input.shape[0]
    blocks_seq = lax.axis_size("seq")
    seq_place = lax.axis_index("seq")
    reach_blocks = min(WINDOW_LENGTH // tok_rows, blocks_seq - 1)
    kv_heads = stored_keys.shape[1] // HEAD_SIZE
    output_gradient = jnp.dot(
        out_cotangent, output_weight.T, preferred_element_type=jnp.float32
    ).astype(jnp.bfloat16)
    pieces = [(stored_keys, stored_values)]
    current = (stored_keys, stored_values)
    for relay_step in range(reach_blocks):
        current = passed_along((current[0], current[1]), "seq", 1)
        pieces = [current] + pieces
    key_window = jnp.concatenate([piece[0] for piece in pieces], axis=0)
    value_window = jnp.concatenate([piece[1] for piece in pieces], axis=0)
    key_span = key_window.shape[0]
    query_pos = seq_place * tok_rows + jnp.arange(tok_rows, dtype=jnp.int32)
    key_pos = (seq_place - reach_blocks) * tok_rows + jnp.arange(key_span, dtype=jnp.int32)
    pos_gap = query_pos[:, None] - key_pos[None, :]
    allowed = (pos_gap >= 0) & (pos_gap < WINDOW_LENGTH) & (key_pos >= 0)[None, :]
    allowed_rows = jnp.tile(allowed, (QUERIES_PER_KEY, 1))
    query_stack = (
        stored_queries.reshape(tok_rows, kv_heads, QUERIES_PER_KEY, HEAD_SIZE)
        .transpose(1, 2, 0, 3)
        .reshape(kv_heads, QUERIES_PER_KEY * tok_rows, HEAD_SIZE)
    )
    grad_stack = (
        output_gradient.reshape(tok_rows, kv_heads, QUERIES_PER_KEY, HEAD_SIZE)
        .transpose(1, 2, 0, 3)
        .reshape(kv_heads, QUERIES_PER_KEY * tok_rows, HEAD_SIZE)
    )
    key_stack = key_window.reshape(key_span, kv_heads, HEAD_SIZE).transpose(1, 0, 2)
    value_stack = value_window.reshape(key_span, kv_heads, HEAD_SIZE).transpose(1, 0, 2)

    def per_head(head_items):
        query_head, key_head, value_head, grad_head = head_items
        attention_logits = logit_scale * jnp.dot(
            query_head, key_head.T, preferred_element_type=jnp.float32
        )
        masked = jnp.where(allowed_rows, attention_logits, -jnp.inf)
        row_top = jnp.max(masked, axis=1, keepdims=True)
        exp_scores = jnp.exp(masked - row_top)
        attn_prob = exp_scores / jnp.sum(exp_scores, axis=1, keepdims=True)
        probability_halfwidth = attn_prob.astype(jnp.bfloat16)
        attn_head = jnp.dot(
            probability_halfwidth, value_head, preferred_element_type=jnp.float32
        ).astype(jnp.bfloat16)
        row_delta = jnp.sum(
            grad_head.astype(jnp.float32) * attn_head.astype(jnp.float32), axis=1, keepdims=True
        )
        probability_gradient = jnp.dot(grad_head, value_head.T, preferred_element_type=jnp.float32)
        score_gradient = (attn_prob * (probability_gradient - row_delta)).astype(jnp.bfloat16)
        qgrad_head = (
            logit_scale * jnp.dot(score_gradient, key_head, preferred_element_type=jnp.float32)
        ).astype(jnp.bfloat16)
        key_partial = logit_scale * jnp.dot(
            score_gradient.T, query_head, preferred_element_type=jnp.float32
        )
        value_partial = jnp.dot(
            probability_halfwidth.T, grad_head, preferred_element_type=jnp.float32
        )
        return (attn_head, qgrad_head, key_partial, value_partial)

    attn_all, qgrad_all, key_all, value_all = lax.map(
        per_head, (query_stack, key_stack, value_stack, grad_stack)
    )
    attention_output = (
        attn_all.reshape(kv_heads, QUERIES_PER_KEY, tok_rows, HEAD_SIZE)
        .transpose(2, 0, 1, 3)
        .reshape(tok_rows, kv_heads * QUERIES_PER_KEY * HEAD_SIZE)
    )
    query_gradient = (
        qgrad_all.reshape(kv_heads, QUERIES_PER_KEY, tok_rows, HEAD_SIZE)
        .transpose(2, 0, 1, 3)
        .reshape(tok_rows, kv_heads * QUERIES_PER_KEY * HEAD_SIZE)
    )
    key_terms = key_all.transpose(1, 0, 2).reshape(key_span, kv_heads * HEAD_SIZE)
    value_terms = value_all.transpose(1, 0, 2).reshape(key_span, kv_heads * HEAD_SIZE)

    def take_slot(terms, slot_index):
        return terms[slot_index * tok_rows : (slot_index + 1) * tok_rows]

    key_sum = take_slot(key_terms, reach_blocks)
    value_sum = take_slot(value_terms, reach_blocks)
    for distance in range(1, reach_blocks + 1):
        received = passed_along(
            (
                take_slot(key_terms, reach_blocks - distance),
                take_slot(value_terms, reach_blocks - distance),
            ),
            "seq",
            -distance,
        )
        key_sum = key_sum + received[0]
        value_sum = value_sum + received[1]
    grad_key = key_sum.astype(jnp.bfloat16)
    grad_value = value_sum.astype(jnp.bfloat16)
    input_terms = jnp.dot(query_gradient, query_weight.T, preferred_element_type=jnp.float32)
    input_terms = input_terms + jnp.dot(grad_key, key_matrix.T, preferred_element_type=jnp.float32)
    input_terms = input_terms + jnp.dot(
        grad_value, value_matrix.T, preferred_element_type=jnp.float32
    )
    grad_input = lax.psum_scatter(input_terms, "head", scatter_dimension=1, tiled=True).astype(
        jnp.bfloat16
    )
    value_cols = grad_value.shape[1]
    input_cols = normed_input.T
    cot_cols = out_cotangent.T
    gathered = lax.psum_scatter(
        jnp.concatenate(
            [
                jnp.dot(input_cols, grad_value, preferred_element_type=jnp.float32),
                jnp.dot(cot_cols, attention_output, preferred_element_type=jnp.float32),
            ],
            axis=1,
        ),
        "seq",
        scatter_dimension=0,
        tiled=True,
    )
    grad_wvalue = gathered[:, :value_cols]
    grad_woutput = gathered[:, value_cols:].T
    return (grad_input, grad_wvalue, grad_woutput)


def solution(mesh):
    placed = (
        P("seq", None),
        P("seq", "head"),
        P("seq", "head"),
        P("seq", "head"),
        P(None, "head"),
        P(None, "head"),
        P(None, "head"),
        P("head", None),
        P("seq", None),
    )
    return jax.shard_map(
        local,
        mesh=mesh,
        in_specs=placed,
        out_specs=(P("seq", "head"), P("seq", "head"), P("head", "seq")),
        check_vma=False,
    )
```

```python
import functools

import jax
import jax.numpy as jnp
from jax import lax
from jax.experimental import pallas as pl
from jax.experimental.pallas import tpu as pltpu
from jax.sharding import PartitionSpec as P

HEAD_SIZE = 128
WINDOW_LENGTH = 4096
QUERIES_PER_KEY = 2


logit_scale = 1.0 / 12.0
log2_scale = 1.4426950408889634 / 12.0
excluded = -1e30


def passed_along(value, axis, steps):
    count = lax.axis_size(axis)
    leading, last = (max(0, -steps), min(count, count - steps))
    return lax.ppermute(value, axis, [(source, source + steps) for source in range(leading, last)])


NT = (((1,), (1,)), ((), ()))


def dot_nt(left, right):
    return lax.dot_general(left, right, NT, preferred_element_type=jnp.float32)


def dot_nn(left, right):
    return jnp.dot(left, right, preferred_element_type=jnp.float32)


def at(place, size):
    return pl.ds(pl.multiple_of(place * size, size), size)


def out_grad_kernel(
    cot_hbm, weight_hbm, q_hbm, k_hbm, v_hbm, same_ref, other_ref, cot_ref, weight_ref, sem
):
    core = lax.axis_index("seq") % 2
    halves = ((other_ref, 1 - core), (same_ref, core))
    rows = weight_ref.shape[0] // 2
    pieces = (sem.shape[0] - 6) // 3
    cut = weight_ref.shape[1] // pieces
    model_copies = []
    for piece in range(pieces):
        part = pl.ds(piece * cut, cut)
        model_copies.append(
            [
                pltpu.make_async_copy(
                    cot_hbm.at[:, part], cot_ref.at[:, part], sem.at[6 + 3 * piece]
                )
            ]
        )
        for place, (_, half) in enumerate(halves):
            model_copies[-1].append(
                pltpu.make_async_copy(
                    weight_hbm.at[at(half, rows), part],
                    weight_ref.at[pl.ds(place * rows, rows), part],
                    sem.at[7 + 3 * piece + place],
                )
            )
        for copy in model_copies[-1]:
            copy.start()
    plain_copies = []
    for place, (target, half) in enumerate(halves):
        first = 0
        for which, source in enumerate((q_hbm, k_hbm, v_hbm)):
            cols = source.shape[1] // 2
            plain_copies.append(
                pltpu.make_async_copy(
                    source.at[:, at(half, cols)],
                    target.at[:, pl.ds(first, cols)],
                    sem.at[3 * place + which],
                )
            )
            plain_copies[-1].start()
            first += cols
    total = None
    for piece in range(pieces):
        for copy in model_copies[piece]:
            copy.wait()
        part = slice(piece * cut, (piece + 1) * cut)
        product = dot_nt(cot_ref[:, part], weight_ref[:, part])
        total = product if total is None else total + product
    for place, (target, _) in enumerate(halves):
        for head in range(rows // HEAD_SIZE):
            row = place * rows + head * HEAD_SIZE
            target[:, first + head * HEAD_SIZE : first + (head + 1) * HEAD_SIZE] = total[
                :, row : row + HEAD_SIZE
            ].T.astype(jnp.bfloat16)
    for copy in plain_copies:
        copy.wait()


def hold_kernel(same_ref, other_ref, kept_same_ref, kept_other_ref):
    kept_same_ref[...] = same_ref[...]
    kept_other_ref[...] = other_ref[...]


def turn_kernel(normed_ref, cot_ref, _, __, *refs):
    *column_refs, turned_ref = refs
    me = lax.axis_index("seq")
    cut = column_refs[0].shape[2]
    for which, ref in enumerate((normed_ref, cot_ref)):
        turned_ref[which] = ref[...].astype(jnp.float32).T.astype(jnp.bfloat16)
        for chip, target in enumerate(column_refs):
            for far in range(2):
                target[far, which] = turned_ref[which, at(me ^ (2 * chip + far), cut)]


def pass_on_kernel(_, attn_ref, dv_t_ref, *refs):
    *column_refs, give_ref = refs
    cut, rows = column_refs[0].shape[2:]
    for chip, ref in enumerate(column_refs):
        for which in range(2):
            first = (2 * chip + which) * cut
            give_ref[first : first + cut] = ref[1, which]
    first = 2 * len(column_refs) * cut
    for ref in (attn_ref, dv_t_ref):
        for block in range(ref.shape[1] // rows):
            give_ref[first : first + ref.shape[0]] = ref[:, block * rows : (block + 1) * rows]
            first += ref.shape[0]


def attention_kernel(blocks, *refs):
    attention_body(refs[:blocks], *refs[blocks:])


def attention_body(
    block_refs,
    dx_own_ref,
    dx_far_ref,
    attn_ref,
    prob_ref,
    grad_t_ref,
    gathered_ref,
    score_even_ref,
    score_odd_ref,
    delta_ref,
    query_ref,
    value_t_ref,
    key_t_ref,
    dq_t_ref,
    dk_ref,
    dv_ref,
):
    me = lax.axis_index("seq")
    core, chip = me % 2, me // 2
    rows = dx_own_ref.shape[0]
    for apart, source in enumerate(block_refs):
        gathered_ref[at(me ^ apart, rows)] = source[...]
    tokens = gathered_ref.shape[0]
    size = 2 * rows
    steps = tokens // size
    wide = QUERIES_PER_KEY * size
    heads = QUERIES_PER_KEY
    key_cols = slice(heads * HEAD_SIZE, (heads + 1) * HEAD_SIZE)
    value_cols = slice((heads + 1) * HEAD_SIZE, (heads + 2) * HEAD_SIZE)
    grad_base = (heads + 2) * HEAD_SIZE
    value_t_ref[...] = gathered_ref[:, value_cols].T
    key_t_ref[...] = gathered_ref[:, key_cols].T
    key_place = lax.broadcasted_iota(jnp.int32, (size, wide), 0)
    query_place = lax.broadcasted_iota(jnp.int32, (size, wide), 1) % size
    allowed = key_place <= query_place

    def scored(step):
        own = slice(step * size, (step + 1) * size)
        score_ref = score_odd_ref if step % 2 else score_even_ref
        queries = jnp.concatenate(
            [gathered_ref[own, h * HEAD_SIZE : (h + 1) * HEAD_SIZE] for h in range(heads)], axis=0
        )
        query_ref[step * wide : (step + 1) * wide] = queries
        top = None
        for piece in range(step + 1):
            part = slice(piece * size, (piece + 1) * size)
            scores = dot_nt(gathered_ref[part, key_cols], queries)
            if piece == step:
                scores = jnp.where(allowed, scores, excluded)
            score_ref[part] = scores
            largest = jnp.max(scores.reshape(size // 8, 8, wide), axis=0)
            top = largest if top is None else jnp.maximum(top, largest)
        return top

    next_top = scored(steps - 1)
    for step in range(steps - 1, -1, -1):
        span = (step + 1) * size
        own = slice(step * size, span)
        lanes = slice(step * wide, (step + 1) * wide)
        score_ref = score_odd_ref if step % 2 else score_even_ref
        top = next_top
        if step:
            next_top = scored(step - 1)
        top = jnp.max(top, axis=0, keepdims=True)
        total = None
        for piece in range(step + 1):
            part = slice(piece * size, (piece + 1) * size)
            weights = jnp.exp2((score_ref[part] - top) * log2_scale)
            prob_ref[part, lanes] = weights.astype(jnp.bfloat16)
            summed = jnp.sum(weights.reshape(size // 8, 8, wide), axis=0)
            total = summed if total is None else total + summed
        inverse = 1.0 / jnp.sum(total, axis=0, keepdims=True)
        attn = dot_nn(value_t_ref[:, :span], prob_ref[:span, lanes]) * inverse
        for h in range(heads):
            attn_ref[h * HEAD_SIZE : (h + 1) * HEAD_SIZE, own] = attn[
                :, h * size : (h + 1) * size
            ].astype(jnp.bfloat16)
        grads_t = jnp.concatenate(
            [
                gathered_ref[
                    block * rows : (block + 1) * rows,
                    grad_base + h * HEAD_SIZE : grad_base + (h + 1) * HEAD_SIZE,
                ]
                for h in range(heads)
                for block in (2 * step, 2 * step + 1)
            ],
            axis=1,
        )
        grads_t = (grads_t.astype(jnp.float32) * inverse).astype(jnp.bfloat16)
        grad_t_ref[:, lanes] = grads_t
        delta_ref[:, lanes] = jnp.sum(grads_t.astype(jnp.float32) * attn, axis=0, keepdims=True)

    dq_t_ref[...] = jnp.zeros_like(dq_t_ref)
    dk_ref[...] = jnp.zeros_like(dk_ref)
    dv_ref[...] = jnp.zeros_like(dv_ref)
    for step in range(steps):
        key_step = jnp.minimum(chip, step)
        query_step = jnp.maximum(chip, step)
        dprob = dot_nn(
            gathered_ref[at(key_step, size), value_cols], grad_t_ref[:, at(query_step, wide)]
        )
        prob = prob_ref[at(key_step, size), at(query_step, wide)]
        dscore = (
            prob.astype(jnp.float32)
            * (dprob - delta_ref[:, at(query_step, wide)])
        ).astype(jnp.bfloat16)

        @pl.when(step <= chip)
        def _():
            dq_t_ref[...] += dot_nn(key_t_ref[:, at(key_step, size)], dscore)

        @pl.when(step >= chip)
        def _():
            dk_ref[...] += dot_nn(dscore, query_ref[at(query_step, wide)])
            dv_ref[...] += dot_nt(prob, grad_t_ref[:, at(query_step, wide)])

    for target, half in ((dx_far_ref, 1 - core), (dx_own_ref, core)):
        for h in range(heads):
            target[:, h * HEAD_SIZE : (h + 1) * HEAD_SIZE] = (
                (logit_scale * dq_t_ref[:, at(2 * h + half, rows)])
                .T.astype(jnp.bfloat16)
            )
        target[:, key_cols] = (logit_scale * dk_ref[at(half, rows)]).astype(jnp.bfloat16)
        target[:, value_cols] = dv_ref[at(half, rows)].astype(jnp.bfloat16)


def value_grad_kernel(prob_ref, grad_t_ref, dv_t_ref):
    size = 2 * HEAD_SIZE
    wide = QUERIES_PER_KEY * size
    for step in range(prob_ref.shape[0] // size):
        own = slice(step * size, (step + 1) * size)
        dv_t_ref[:, own] = dot_nt(grad_t_ref[:, step * wide :], prob_ref[own, step * wide :]).astype(
            jnp.bfloat16
        )


def input_terms_kernel(apart_groups, own_ref, far_ref, wq_ref, wk_ref, wv_ref, *refs):
    terms, dx_ref = refs[-1 - len(apart_groups) : -1], refs[-1]
    core = lax.axis_index("seq") % 2
    group = lax.axis_index("head")
    q_cols = wq_ref.shape[1] // 2
    kv_cols = wk_ref.shape[1] // 2
    for source, half in ((own_ref, core), (far_ref, 1 - core)):
        dx_ref[:, at(half, q_cols)] = source[:, :q_cols]
        dx_ref[:, pl.ds(pl.multiple_of(2 * q_cols + half * kv_cols, kv_cols), kv_cols)] = source[
            :, q_cols : q_cols + kv_cols
        ]
        dx_ref[
            :, pl.ds(pl.multiple_of(2 * q_cols + (2 + half) * kv_cols, kv_cols), kv_cols)
        ] = source[:, q_cols + kv_cols :]
    for apart, target in zip(apart_groups, terms):
        cut = target.shape[0]
        place = at(group ^ apart, cut)
        target[...] = (
            dot_nt(wq_ref[place], dx_ref[:, : 2 * q_cols])
            + dot_nt(wk_ref[place], dx_ref[:, 2 * q_cols : 2 * q_cols + 2 * kv_cols])
            + dot_nt(wv_ref[place], dx_ref[:, 2 * q_cols + 2 * kv_cols :])
        ).astype(target.dtype)


def weight_grad_kernel(attn_ref, dv_t_ref, got_ref, *refs):
    column_refs, refs = refs[:-6], refs[-6:]
    wvalue_ref, woutput_ref, done_ref, joined_ref, far_attn_ref, far_dv_ref = refs
    done_ref[...] = jnp.zeros_like(done_ref)
    me = lax.axis_index("seq")
    core = me % 2
    cut, rows = column_refs[0].shape[2:]
    for chip, ref in enumerate(column_refs):
        joined_ref[:, :, at(me ^ (2 * chip), rows)] = ref[0]
        for which in range(2):
            first = (2 * chip + which) * cut
            joined_ref[which, :, at(me ^ (2 * chip + 1), rows)] = got_ref[first : first + cut]
    first = 2 * len(column_refs) * cut
    for ref in (far_attn_ref, far_dv_ref):
        for block in range(ref.shape[1] // rows):
            ref[:, block * rows : (block + 1) * rows] = got_ref[first : first + ref.shape[0]]
            first += ref.shape[0]
    for half, attn, dv_t in ((core, attn_ref, dv_t_ref), (1 - core, far_attn_ref, far_dv_ref)):
        woutput_ref[:, at(half, attn.shape[0])] = dot_nt(joined_ref[1], attn[...])
        wvalue_ref[:, at(half, dv_t.shape[0])] = dot_nt(joined_ref[0], dv_t[...])


def add_kernel(own_ref, arrived_ref, _, sum_ref):
    total = own_ref[...].astype(jnp.float32) + arrived_ref[...].astype(jnp.float32)
    sum_ref[...] = total.astype(jnp.bfloat16)


def far_sum_kernel(_, own_ref, arrived_ref, sum_ref):
    sum_ref[...] = own_ref[...] + arrived_ref[...].astype(jnp.float32)


def sum_kernel(own_ref, *refs):
    total = own_ref[...]
    for arrived_ref in refs[:-1]:
        total = total + arrived_ref[...].astype(jnp.float32)
    refs[-1][...] = total.astype(jnp.bfloat16)


def kernel_call(
    body, outs, operands, in_vmem=(), scratch=(), flops=0, moved=0, room=16
):
    vmem = pl.BlockSpec(memory_space=pltpu.VMEM)
    hbm = pl.BlockSpec(memory_space=pltpu.HBM)
    return pl.pallas_call(
        body,
        out_shape=outs,
        in_specs=[vmem if place in in_vmem else hbm for place in range(len(operands))],
        out_specs=(vmem,) * len(outs),
        scratch_shapes=list(scratch),
        compiler_params=pltpu.CompilerParams(vmem_limit_bytes=int(room * 1024 * 1024)),
        cost_estimate=pl.CostEstimate(flops=flops, bytes_accessed=moved, transcendentals=0),
    )(*operands)


def swapped(value, axis, apart):
    count = lax.axis_size(axis)
    return lax.ppermute(value, axis, [(place, place ^ apart) for place in range(count)])


def gathered_plan(
    normed_input,
    stored_queries,
    stored_keys,
    stored_values,
    query_weight,
    key_matrix,
    value_matrix,
    output_weight,
    out_cotangent,
):
    bf16, f32 = jnp.bfloat16, jnp.float32
    rows, model = normed_input.shape
    blocks = lax.axis_size("seq")
    groups = lax.axis_size("head")
    tokens = rows * blocks
    q_cols = stored_queries.shape[1] // 2
    kv_cols = HEAD_SIZE
    wide = 2 * QUERIES_PER_KEY * rows
    packed_cols = 2 * q_cols + 2 * kv_cols
    pieces = 3 if model % (6 * HEAD_SIZE) == 0 else 1
    shape = jax.ShapeDtypeStruct
    same, other = kernel_call(
        out_grad_kernel,
        (shape((rows, packed_cols), bf16),) * 2,
        (out_cotangent, output_weight, stored_queries, stored_keys, stored_values),
        scratch=(
            pltpu.VMEM(out_cotangent.shape, bf16),
            pltpu.VMEM(output_weight.shape, bf16),
            pltpu.SemaphoreType.DMA((6 + 3 * pieces,)),
        ),
        flops=4 * rows * model * q_cols,
        moved=2 * model * (rows + 2 * q_cols),
        room=63,
    )
    kept_same, kept_other = kernel_call(
        hold_kernel,
        (shape(same.shape, bf16),) * 2,
        (same, other),
        in_vmem=range(2),
        moved=8 * rows * packed_cols,
        room=4,
    )
    held = {0: kept_same}
    for apart in range(2, blocks):
        lowest, highest = 2, 1 << (apart.bit_length() - 1)
        while not apart & lowest:
            lowest *= 2
        through = lowest if apart % 2 else highest
        if lowest == highest:
            first = apart in (2, blocks // 2 + 1)
            even, odd = (same, other) if first else (kept_same, kept_other)
            held[apart] = swapped(odd if apart % 2 else even, "seq", apart)
        else:
            held[apart] = swapped(held[apart ^ through], "seq", through)
    held[1] = swapped(other, "seq", 1)
    cut = model // blocks
    columns = kernel_call(
        turn_kernel,
        (shape((2, 2, cut, rows), bf16),) * (blocks // 2),
        (normed_input, out_cotangent, held[3], held[blocks // 2]),
        in_vmem=range(2),
        scratch=(pltpu.VMEM((2, model, rows), bf16),),
        moved=8 * rows * model,
        room=8,
    )
    columns = [columns[0]] + [
        swapped(columns[chip], "seq", 2 * chip) for chip in range(1, blocks // 2)
    ]
    dx_own, dx_far, attn, prob, grad_t = kernel_call(
        functools.partial(attention_kernel, blocks),
        (
            shape((rows, q_cols + 2 * kv_cols), bf16),
            shape((rows, q_cols + 2 * kv_cols), bf16),
            shape((q_cols, tokens), bf16),
            shape((tokens, tokens * QUERIES_PER_KEY), bf16),
            shape((HEAD_SIZE, tokens * QUERIES_PER_KEY), bf16),
        ),
        [held[apart] for apart in range(blocks)],
        in_vmem=range(blocks),
        scratch=(
            pltpu.VMEM((tokens, packed_cols), bf16),
            pltpu.VMEM((tokens, wide), f32),
            pltpu.VMEM((tokens, wide), f32),
            pltpu.VMEM((1, tokens * QUERIES_PER_KEY), f32),
            pltpu.VMEM((tokens * QUERIES_PER_KEY, HEAD_SIZE), bf16),
            pltpu.VMEM((HEAD_SIZE, tokens), bf16),
            pltpu.VMEM((HEAD_SIZE, tokens), bf16),
            pltpu.VMEM((HEAD_SIZE, wide), f32),
            pltpu.VMEM((2 * rows, HEAD_SIZE), f32),
            pltpu.VMEM((2 * rows, HEAD_SIZE), f32),
        ),
        flops=8 * tokens * tokens * q_cols,
        moved=2 * tokens * packed_cols,
    )
    dx_got = swapped(dx_far, "seq", 1)
    def terms_of(chosen):
        return kernel_call(
            functools.partial(input_terms_kernel, chosen),
            tuple(shape((model // groups, rows), f32 if not apart else bf16) for apart in chosen),
            (dx_own, dx_got, query_weight, key_matrix, value_matrix),
            in_vmem=range(5),
            scratch=(pltpu.VMEM((rows, 2 * (q_cols + 2 * kv_cols)), bf16),),
            flops=2 * len(chosen) * rows * (model // groups) * 2 * (q_cols + 2 * kv_cols),
            moved=2 * len(chosen) * (model // groups) * 2 * (q_cols + 2 * kv_cols),
            room=4,
        )

    (far_term,) = terms_of((3,))
    pair_term, near_term, own_term = terms_of((2, 1, 0))
    (dv_t,) = kernel_call(
        value_grad_kernel,
        (shape((kv_cols, tokens), bf16),),
        (prob, grad_t),
        in_vmem=range(2),
        flops=tokens * tokens * q_cols,
        moved=2 * tokens * tokens * QUERIES_PER_KEY,
        room=4,
    )
    (pair_sum,) = kernel_call(
        add_kernel,
        (shape(pair_term.shape, bf16),),
        (pair_term, swapped(far_term, "head", 1), dv_t),
        in_vmem=range(2),
        room=4,
    )
    part_rows = q_cols + kv_cols
    (give,) = kernel_call(
        pass_on_kernel,
        (shape((blocks * (cut + part_rows), rows), bf16),),
        (pair_sum, attn, dv_t, *columns),
        in_vmem=range(1, 3 + blocks // 2),
        room=4,
    )
    grad_wvalue, grad_woutput, weights_done = kernel_call(
        weight_grad_kernel,
        (
            shape((model // blocks, 2 * kv_cols), f32),
            shape((model // blocks, 2 * q_cols), f32),
            shape((8, HEAD_SIZE), f32),
        ),
        (attn, dv_t, swapped(give, "seq", 1), *columns),
        in_vmem=range(3 + blocks // 2),
        scratch=(
            pltpu.VMEM((2, model // blocks, tokens), bf16),
            pltpu.VMEM((q_cols, tokens), bf16),
            pltpu.VMEM((kv_cols, tokens), bf16),
        ),
        room=8,
    )
    (far_sum,) = kernel_call(
        far_sum_kernel,
        (shape((model // groups, rows), f32),),
        (weights_done, own_term, swapped(pair_sum, "head", 2)),
        in_vmem=range(1, 3),
        moved=10 * rows * (model // groups),
        room=4,
    )
    (grad_input,) = kernel_call(
        sum_kernel,
        (shape((model // groups, rows), bf16),),
        (far_sum, swapped(near_term, "head", 1)),
        in_vmem=range(2),
        moved=4 * groups * (model // groups) * rows,
    )
    return (grad_input.T, grad_wvalue, grad_woutput.T)


def power_of_two(count):
    return count & (count - 1) == 0


def local(normed_input, stored_queries, stored_keys, *others):
    blocks, groups = lax.axis_size("seq"), lax.axis_size("head")
    whole_window = normed_input.shape[0] * blocks <= WINDOW_LENGTH
    two_heads = stored_keys.shape[1] == 2 * HEAD_SIZE
    paired = blocks >= 4 and power_of_two(blocks) and groups == 4
    plan = gathered_plan if whole_window and two_heads and paired else windowed_plan
    return plan(normed_input, stored_queries, stored_keys, *others)


def windowed_plan(
    normed_input,
    stored_queries,
    stored_keys,
    stored_values,
    query_weight,
    key_matrix,
    value_matrix,
    output_weight,
    out_cotangent,
):
    tok_rows = normed_input.shape[0]
    blocks_seq = lax.axis_size("seq")
    seq_place = lax.axis_index("seq")
    reach_blocks = min(WINDOW_LENGTH // tok_rows, blocks_seq - 1)
    kv_heads = stored_keys.shape[1] // HEAD_SIZE
    output_gradient = jnp.dot(
        out_cotangent, output_weight.T, preferred_element_type=jnp.float32
    ).astype(jnp.bfloat16)
    pieces = [(stored_keys, stored_values)]
    current = (stored_keys, stored_values)
    for relay_step in range(reach_blocks):
        current = passed_along((current[0], current[1]), "seq", 1)
        pieces = [current] + pieces
    key_window = jnp.concatenate([piece[0] for piece in pieces], axis=0)
    value_window = jnp.concatenate([piece[1] for piece in pieces], axis=0)
    key_span = key_window.shape[0]
    query_pos = seq_place * tok_rows + jnp.arange(tok_rows, dtype=jnp.int32)
    key_pos = (seq_place - reach_blocks) * tok_rows + jnp.arange(key_span, dtype=jnp.int32)
    pos_gap = query_pos[:, None] - key_pos[None, :]
    allowed = (pos_gap >= 0) & (pos_gap < WINDOW_LENGTH) & (key_pos >= 0)[None, :]
    allowed_rows = jnp.tile(allowed, (QUERIES_PER_KEY, 1))
    query_stack = (
        stored_queries.reshape(tok_rows, kv_heads, QUERIES_PER_KEY, HEAD_SIZE)
        .transpose(1, 2, 0, 3)
        .reshape(kv_heads, QUERIES_PER_KEY * tok_rows, HEAD_SIZE)
    )
    grad_stack = (
        output_gradient.reshape(tok_rows, kv_heads, QUERIES_PER_KEY, HEAD_SIZE)
        .transpose(1, 2, 0, 3)
        .reshape(kv_heads, QUERIES_PER_KEY * tok_rows, HEAD_SIZE)
    )
    key_stack = key_window.reshape(key_span, kv_heads, HEAD_SIZE).transpose(1, 0, 2)
    value_stack = value_window.reshape(key_span, kv_heads, HEAD_SIZE).transpose(1, 0, 2)

    def per_head(head_items):
        query_head, key_head, value_head, grad_head = head_items
        attention_logits = logit_scale * jnp.dot(
            query_head, key_head.T, preferred_element_type=jnp.float32
        )
        masked = jnp.where(allowed_rows, attention_logits, -jnp.inf)
        row_top = jnp.max(masked, axis=1, keepdims=True)
        exp_scores = jnp.exp(masked - row_top)
        attn_prob = exp_scores / jnp.sum(exp_scores, axis=1, keepdims=True)
        probability_halfwidth = attn_prob.astype(jnp.bfloat16)
        attn_head = jnp.dot(
            probability_halfwidth, value_head, preferred_element_type=jnp.float32
        ).astype(jnp.bfloat16)
        row_delta = jnp.sum(
            grad_head.astype(jnp.float32) * attn_head.astype(jnp.float32), axis=1, keepdims=True
        )
        probability_gradient = jnp.dot(grad_head, value_head.T, preferred_element_type=jnp.float32)
        score_gradient = (attn_prob * (probability_gradient - row_delta)).astype(jnp.bfloat16)
        qgrad_head = (
            logit_scale * jnp.dot(score_gradient, key_head, preferred_element_type=jnp.float32)
        ).astype(jnp.bfloat16)
        key_partial = logit_scale * jnp.dot(
            score_gradient.T, query_head, preferred_element_type=jnp.float32
        )
        value_partial = jnp.dot(
            probability_halfwidth.T, grad_head, preferred_element_type=jnp.float32
        )
        return (attn_head, qgrad_head, key_partial, value_partial)

    attn_all, qgrad_all, key_all, value_all = lax.map(
        per_head, (query_stack, key_stack, value_stack, grad_stack)
    )
    attention_output = (
        attn_all.reshape(kv_heads, QUERIES_PER_KEY, tok_rows, HEAD_SIZE)
        .transpose(2, 0, 1, 3)
        .reshape(tok_rows, kv_heads * QUERIES_PER_KEY * HEAD_SIZE)
    )
    query_gradient = (
        qgrad_all.reshape(kv_heads, QUERIES_PER_KEY, tok_rows, HEAD_SIZE)
        .transpose(2, 0, 1, 3)
        .reshape(tok_rows, kv_heads * QUERIES_PER_KEY * HEAD_SIZE)
    )
    key_terms = key_all.transpose(1, 0, 2).reshape(key_span, kv_heads * HEAD_SIZE)
    value_terms = value_all.transpose(1, 0, 2).reshape(key_span, kv_heads * HEAD_SIZE)

    def take_slot(terms, slot_index):
        return terms[slot_index * tok_rows : (slot_index + 1) * tok_rows]

    key_sum = take_slot(key_terms, reach_blocks)
    value_sum = take_slot(value_terms, reach_blocks)
    for distance in range(1, reach_blocks + 1):
        received = passed_along(
            (
                take_slot(key_terms, reach_blocks - distance),
                take_slot(value_terms, reach_blocks - distance),
            ),
            "seq",
            -distance,
        )
        key_sum = key_sum + received[0]
        value_sum = value_sum + received[1]
    grad_key = key_sum.astype(jnp.bfloat16)
    grad_value = value_sum.astype(jnp.bfloat16)
    input_terms = jnp.dot(query_gradient, query_weight.T, preferred_element_type=jnp.float32)
    input_terms = input_terms + jnp.dot(grad_key, key_matrix.T, preferred_element_type=jnp.float32)
    input_terms = input_terms + jnp.dot(
        grad_value, value_matrix.T, preferred_element_type=jnp.float32
    )
    grad_input = lax.psum_scatter(input_terms, "head", scatter_dimension=1, tiled=True).astype(
        jnp.bfloat16
    )
    value_cols = grad_value.shape[1]
    input_cols = normed_input.T
    cot_cols = out_cotangent.T
    gathered = lax.psum_scatter(
        jnp.concatenate(
            [
                jnp.dot(input_cols, grad_value, preferred_element_type=jnp.float32),
                jnp.dot(cot_cols, attention_output, preferred_element_type=jnp.float32),
            ],
            axis=1,
        ),
        "seq",
        scatter_dimension=0,
        tiled=True,
    )
    grad_wvalue = gathered[:, :value_cols]
    grad_woutput = gathered[:, value_cols:].T
    return (grad_input, grad_wvalue, grad_woutput)


def solution(mesh):
    placed = (
        P("seq", None),
        P("seq", "head"),
        P("seq", "head"),
        P("seq", "head"),
        P(None, "head"),
        P(None, "head"),
        P(None, "head"),
        P("head", None),
        P("seq", None),
    )
    return jax.shard_map(
        local,
        mesh=mesh,
        in_specs=placed,
        out_specs=(P("seq", "head"), P("seq", "head"), P("head", "seq")),
        check_vma=False,
    )
```
